32 devices in a mesh: dp: 4 (over y, core), seq: 8 (over z, x).
Axes of the slice: x: 2, y: 2, z: 4, core: 2. Of those that a mesh axis runs over, the one named last changes fastest.
Arguments:
- inputs: bfloat16 [20480, 512], P(('dp', 'seq')), may hold values from -6 to 6
- cotangent: bfloat16 [20480, 512], P(('dp', 'seq')), may hold values from -6 to 6
- block_segment: int32 [160], P('dp'), may hold values from 0 to 39, as said below
- segment_parent: int32 [160], P('dp'), may hold values from -1 to 39, as said below
- query_weight: bfloat16 [512, 512], P(('dp', 'seq')), may hold values from -0.5 to 0.5
- key_weight: bfloat16 [512, 512], P(('dp', 'seq')), may hold values from -0.25 to 0.25
- value_weight: bfloat16 [512, 512], P(('dp', 'seq')), may hold values from -0.25 to 0.25
- output_weight: bfloat16 [512, 512], P(('dp', 'seq')), may hold values from -1 to 1
- gate_weight: bfloat16 [512, 512], P(('dp', 'seq')), may hold values from -0.25 to 0.25
- gate_bias: bfloat16 [512], P(('dp', 'seq')), may hold values from -3 to 3
- up_weight: bfloat16 [512, 2048], P(('dp', 'seq')), may hold values from -0.25 to 0.25
- up_bias: bfloat16 [2048], P(('dp', 'seq')), may hold values from -3 to 3
- down_weight: bfloat16 [2048, 512], P(('dp', 'seq')), may hold values from -0.125 to 0.125
- down_bias: bfloat16 [512], P(('dp', 'seq')), may hold values from -3 to 3
- carry_weight: bfloat16 [512, 512], P(('dp', 'seq')), may hold values from -0.25 to 0.25
- carry_bias: bfloat16 [512], P(('dp', 'seq')), may hold values from -3 to 3
- first_gain: bfloat16 [512], P(('dp', 'seq')), may hold values from 0.25 to 1.75
- first_shift: bfloat16 [512], P(('dp', 'seq')), may hold values from -2 to 2
- second_gain: bfloat16 [512], P(('dp', 'seq')), may hold values from 0.25 to 1.75
- second_shift: bfloat16 [512], P(('dp', 'seq')), may hold values from -2 to 2
Outputs:
- output: bfloat16 [20480, 512], P(('dp', 'seq'))
- input_grad: float32 [20480, 512], P(('dp', 'seq'))
- query_weight_grad: float32 [512, 512], P(('dp', 'seq'))
- key_weight_grad: float32 [512, 512], P(('dp', 'seq'))
- value_weight_grad: float32 [512, 512], P(('dp', 'seq'))
- output_weight_grad: float32 [512, 512], P(('dp', 'seq'))
- gate_weight_grad: float32 [512, 512], P(('dp', 'seq'))
- gate_bias_grad: float32 [512], P(('dp', 'seq'))
- up_weight_grad: float32 [512, 2048], P(('dp', 'seq'))
- up_bias_grad: float32 [2048], P(('dp', 'seq'))
- down_weight_grad: float32 [2048, 512], P(('dp', 'seq'))
- down_bias_grad: float32 [512], P(('dp', 'seq'))
- carry_weight_grad: float32 [512, 512], P(('dp', 'seq'))
- carry_bias_grad: float32 [512], P(('dp', 'seq'))
- first_gain_grad: float32 [512], P(('dp', 'seq'))
- first_shift_grad: float32 [512], P(('dp', 'seq'))
- second_gain_grad: float32 [512], P(('dp', 'seq'))
- second_shift_grad: float32 [512], P(('dp', 'seq'))
The draws below stay inside these ranges and needn't reach their ends.
Inputs may be any that keep to these rules, and one draw needn't show every extreme that they name: `segment_parent`: entry s of a dp group's 40 entries is the parent of segment s of that group, or -1 for a root. The group's segments form 2 trees of 20 segments: a chain of 8 from the root, 4 children of the chain's last segment, and 2 children of each of those. `block_segment`: each dp group's 40 entries are a permutation of its segment numbers; entry j names the segment held in slot j, on the device of index j // 5 along seq.
All inputs are finite; a program needn't handle non-finite values.
Results may differ from the reference program's by a relative error of at most 0.035.
Values may be sent and summed in bfloat16 or wider, within the bound.
No kernel may reach another device: no remote copies, remote signals or barrier semaphores. Data moves between devices by JAX's collectives and lax.ppermute only.
A program may use at most 256 MiB of HBM per device.

```python
from functools import partial
import jax
import jax.numpy as jnp
from jax import lax

D = 512
HD = 64
FF = 2048
BLK = 128
TRUNK = 8
BRANCHES = 4
LEAVES = 2
TREE_BLOCKS = 20
DEPTH = 10
GROUP_BLOCKS = 40
ALL_BLOCKS = 160
TOKENS = 20480


def parent_offsets():
    member = jnp.arange(TREE_BLOCKS, dtype=jnp.int32)
    branch_parent = jnp.full_like(member, TRUNK - 1)
    leaf_parent = TRUNK + (member - TRUNK - BRANCHES) // LEAVES
    return jnp.where(member < TRUNK, member - 1, jnp.where(member < TRUNK + BRANCHES, branch_parent, leaf_parent)).astype(jnp.int32)


def draw_segment_parent(key, part):
    groups = ALL_BLOCKS // GROUP_BLOCKS
    offsets = parent_offsets()

    def one_group(group_index):
        labels = jax.random.permutation(jax.random.fold_in(jax.random.fold_in(key, 11), group_index), GROUP_BLOCKS).astype(jnp.int32)
        member = jnp.arange(GROUP_BLOCKS, dtype=jnp.int32)
        inside = offsets[member % TREE_BLOCKS]
        target = jnp.where(inside >= 0, member // TREE_BLOCKS * TREE_BLOCKS + inside, 0)
        linked = jnp.where(inside >= 0, labels[target], -1).astype(jnp.int32)
        return jnp.zeros((GROUP_BLOCKS,), jnp.int32).at[labels].set(linked)
    return jax.vmap(one_group)(jnp.arange(groups)).reshape(-1).astype(jnp.int32)


def draw_block_segment(key, part):
    groups = ALL_BLOCKS // GROUP_BLOCKS

    def one_group(group_index):
        return jax.random.permutation(jax.random.fold_in(jax.random.fold_in(key, 23), group_index), GROUP_BLOCKS).astype(jnp.int32)
    return jax.vmap(one_group)(jnp.arange(groups)).reshape(-1).astype(jnp.int32)


def steps_of(own_key, shape, shards, least, high):
    def one(dim, blocks):
        draws = jax.random.uniform(jax.random.fold_in(jax.random.fold_in(own_key, 6), dim), (blocks,), jnp.float32, least / len(shards), high / len(shards))
        return jnp.repeat(jnp.exp(draws), shape[dim] // blocks).reshape((-1,) + (1,) * (len(shape) - dim - 1))

    gain = one(*shards[0])
    for cut in shards[1:]:
        gain = gain * one(*cut)
    return gain


def noise(stream_key, shape, width, most, pieces=(), kind=jnp.bfloat16):
    drawn = jax.random.normal(stream_key, shape, jnp.float32) * width
    if len(pieces) > 0:
        drawn = steps_of(stream_key, shape, pieces, -0.22, 0.18) * drawn
    return jnp.clip(drawn, min=-most, max=most).astype(kind)


def setup_inputs(seed: int = 0) -> dict:
    key_of = jax.random.split(jax.random.key(seed), 21)
    return {
        "inputs": noise(key_of[0], (TOKENS, D), 1.0, 6.0, ((0, 32),)),
        "cotangent": noise(key_of[1], (TOKENS, D), 1.0, 6.0, ((0, 32),)),
        "block_segment": draw_block_segment(jax.random.fold_in(key_of[20], 71), 0),
        "segment_parent": draw_segment_parent(jax.random.fold_in(key_of[20], 71), 0),
        "query_weight": noise(key_of[4], (D, D), (D // 4) ** -0.5, 0.5, ((0, 32),)),
        "key_weight": noise(key_of[5], (D, D), D ** -0.5, 0.25, ((0, 32),)),
        "value_weight": noise(key_of[6], (D, D), D ** -0.5, 0.25, ((0, 32),)),
        "output_weight": noise(key_of[7], (D, D), (D // 16) ** -0.5, 1.0, ((0, 32),)),
        "gate_weight": noise(key_of[8], (D, D), D ** -0.5, 0.25, ((0, 32),)),
        "gate_bias": noise(key_of[9], (D,), 0.5, 3.0, ((0, 32),)),
        "up_weight": noise(key_of[10], (D, FF), D ** -0.5, 0.25, ((0, 32),)),
        "up_bias": noise(key_of[11], (FF,), 0.5, 3.0, ((0, 32),)),
        "down_weight": noise(key_of[12], (FF, D), FF ** -0.5, 0.125, ((0, 32),)),
        "down_bias": noise(key_of[13], (D,), 0.5, 3.0, ((0, 32),)),
        "carry_weight": noise(key_of[14], (D, D), D ** -0.5, 0.25, ((0, 32),)),
        "carry_bias": noise(key_of[15], (D,), 0.5, 3.0, ((0, 32),)),
        "first_gain": jnp.clip(1.0 + 0.15 * jax.random.normal(key_of[16], (D,), jnp.float32), 0.25, 1.75).astype(jnp.bfloat16),
        "first_shift": noise(key_of[17], (D,), 0.3, 2.0, ((0, 32),)),
        "second_gain": jnp.clip(1.0 + 0.15 * jax.random.normal(key_of[18], (D,), jnp.float32), 0.25, 1.75).astype(jnp.bfloat16),
        "second_shift": noise(key_of[19], (D,), 0.3, 2.0, ((0, 32),)),
    }


@jax.custom_vjp
def low(v):
    return lax.optimization_barrier(v.astype(jnp.bfloat16)).astype(jnp.float32)

@jax.custom_vjp
def low_back(v):
    return v

def low_keep(v):
    return (low(v), None)

def low_pass(kept, grad):
    return (grad,)

def back_keep(v):
    return (v, None)

def back_low(kept, grad):
    return (low(grad),)
low.defvjp(low_keep, low_pass)
low_back.defvjp(back_keep, back_low)
PRECISE = lax.Precision.HIGHEST
EPSILON = 1e-05
NEGATIVE = -1e+30

def normalize(values, norm_gain, norm_shift):
    center = values - lax.optimization_barrier(jnp.mean(values, axis=-1, keepdims=True))
    spread = lax.optimization_barrier(jnp.mean(center * center, axis=-1, keepdims=True))
    return center * lax.rsqrt(spread + EPSILON) * norm_gain + norm_shift

def matmul(left_side, right_side):
    return jnp.dot(left_side, right_side, precision=PRECISE, preferred_element_type=jnp.float32)

def lookup(lookup_table, wanted):
    entries = jnp.arange(lookup_table.shape[0], dtype=jnp.int32)
    matches = wanted[..., None].astype(jnp.int32) == entries
    located = lax.optimization_barrier(jnp.sum(jnp.where(matches, lookup_table.astype(jnp.int32), jnp.int32(0)), axis=-1, dtype=jnp.int32))
    return jnp.where(wanted >= 0, located, jnp.int32(-1)).astype(jnp.int32)

def ancestor_slots(block_segment, segment_parent, own_segments):
    entries = jnp.arange(block_segment.shape[0], dtype=jnp.int32)
    placed = block_segment.astype(jnp.int32)[None, :] == entries[:, None]
    slot_of = lax.optimization_barrier(jnp.sum(jnp.where(placed, entries[None, :], jnp.int32(0)), axis=1, dtype=jnp.int32))
    current = own_segments.astype(jnp.int32)
    lineage = []
    for depth_step in range(DEPTH):
        lineage.append(current)
        current = lookup(segment_parent, current)
    lineage = jnp.stack(lineage, axis=-1).astype(jnp.int32)
    usable = lineage >= 0
    return (jnp.where(usable, lookup(slot_of, lineage), jnp.int32(0)).astype(jnp.int32), usable)

def key_mask(usable):
    query_row = jnp.arange(BLK, dtype=jnp.int32)[:, None]
    key_index = jnp.arange(DEPTH * BLK, dtype=jnp.int32)
    key_row = (key_index % BLK)[None, :]
    earlier = key_row <= query_row
    level_open = jnp.repeat(usable, BLK, axis=-1)
    own_level = (key_index < BLK)[None, :]
    return jnp.where(own_level, earlier, level_open[..., None, :])

def attend_block(keys_blocks, values_blocks, queries, slot_list, usable):
    head_count = queries.shape[-1] // HD
    keys_here = keys_blocks[slot_list.astype(jnp.int32)].reshape(DEPTH * BLK, head_count, HD)
    values_here = values_blocks[slot_list.astype(jnp.int32)].reshape(DEPTH * BLK, head_count, HD)
    query_heads = queries.reshape(BLK, head_count, HD)
    scores = jnp.einsum('qhd,khd->hqk', query_heads, keys_here, precision=PRECISE) * HD ** (-0.5)
    scores = low_back(scores)
    visible = key_mask(usable)[None]
    masked = jnp.where(visible, scores, jnp.asarray(NEGATIVE, dtype=jnp.float32))
    highest = lax.optimization_barrier(jnp.max(masked, axis=-1, keepdims=True))
    raised = jnp.where(visible, jnp.exp(masked - highest), jnp.asarray(0.0, dtype=jnp.float32))
    attention_weight = low(raised / lax.optimization_barrier(jnp.sum(raised, axis=-1, keepdims=True)))
    attended = jnp.einsum('hqk,khd->qhd', attention_weight, values_here, precision=PRECISE)
    return attended.reshape(BLK, head_count * HD)

def group_forward(inputs, params, ancestor_slot, usable):
    query_weight, key_weight, value_weight, output_weight, gate_weight, gate_bias, up_weight, up_bias, down_weight, down_bias, carry_weight, carry_bias, first_gain, first_shift, second_gain, second_shift = params
    model_width = inputs.shape[-1]
    normed = low(normalize(inputs, first_gain, first_shift))
    queries = low_back(low(matmul(normed, query_weight)))
    key_rows = low_back(low(matmul(normed, key_weight)))
    value_rows = low_back(low(matmul(normed, value_weight)))
    gate_open = jax.nn.sigmoid(low_back(matmul(normed, gate_weight) + gate_bias))
    blocks_total = ancestor_slot.shape[0]
    keys_blocks = key_rows.reshape(blocks_total, BLK, model_width)
    values_blocks = value_rows.reshape(blocks_total, BLK, model_width)
    block_step = jax.checkpoint(partial(attend_block, keys_blocks, values_blocks))
    attended = lax.map(lambda packed: block_step(packed[0], packed[1], packed[2]), (queries.reshape(blocks_total, BLK, model_width), ancestor_slot, usable))
    attended = low_back(low(attended.reshape(-1, model_width)))
    branch = low_back(matmul(attended, output_weight))
    middle = inputs + gate_open * branch
    normed_second = low(normalize(middle, second_gain, second_shift))
    up_pre = low_back(matmul(normed_second, up_weight) + up_bias)
    hidden = low(up_pre * jax.nn.sigmoid(up_pre))
    update = low_back(matmul(hidden, down_weight) + down_bias)
    carry_open = jax.nn.sigmoid(low_back(matmul(normed_second, carry_weight) + carry_bias))
    return middle + carry_open * update

def reference(inputs, cotangent, block_segment, segment_parent, query_weight, key_weight, value_weight, output_weight, gate_weight, gate_bias, up_weight, up_bias, down_weight, down_bias, carry_weight, carry_bias, first_gain, first_shift, second_gain, second_shift):
    params = tuple((weight.astype(jnp.float32) for weight in (query_weight, key_weight, value_weight, output_weight, gate_weight, gate_bias, up_weight, up_bias, down_weight, down_bias, carry_weight, carry_bias, first_gain, first_shift, second_gain, second_shift)))
    model_width = inputs.shape[-1]
    groups = block_segment.shape[0] // GROUP_BLOCKS
    group_rows = GROUP_BLOCKS * BLK
    packed_all = (inputs.astype(jnp.float32).reshape(groups, group_rows, model_width), cotangent.astype(jnp.float32).reshape(groups, group_rows, model_width), block_segment.astype(jnp.int32).reshape(groups, GROUP_BLOCKS), segment_parent.astype(jnp.int32).reshape(groups, GROUP_BLOCKS))

    def one_group(totals, packed):
        group_inputs, group_cotangent, segments, parents = packed
        ancestor_slot, usable = ancestor_slots(segments, parents, segments)
        result, pullback = jax.vjp(lambda values, weight_set: group_forward(values, weight_set, ancestor_slot, usable), group_inputs, params)
        input_grad, weight_grads = pullback(group_cotangent)
        totals = jax.tree.map(lambda running, addend: running + addend.astype(jnp.float32), totals, weight_grads)
        return (totals, (result.astype(jnp.bfloat16), input_grad.astype(jnp.float32)))
    start_totals = tuple((jnp.zeros(weight.shape, dtype=jnp.float32) for weight in params))
    totals, (outputs, input_grads) = lax.scan(one_group, start_totals, packed_all)
    return (outputs.reshape(-1, model_width), input_grads.reshape(-1, model_width), totals[0], totals[1], totals[2], totals[3], totals[4], totals[5], totals[6], totals[7], totals[8], totals[9], totals[10], totals[11], totals[12], totals[13], totals[14], totals[15])
```

```python
import functools

import jax
import jax.numpy as jnp
from jax import lax
from jax.experimental import pallas as pl
from jax.experimental.pallas import tpu as pltpu
from jax.sharding import PartitionSpec as P

HD = 64
BLK = 128
DEPTH = 10
PAIR = 2 * HD

EPSILON = 1e-05
NEGATIVE = -1e30
BOTH = ("dp", "seq")
VMEM_BYTES = 60 * 1024 * 1024


def normalize(values, norm_gain, norm_shift):
    center = values - jnp.mean(values, axis=-1, keepdims=True)
    spread = jnp.mean(center * center, axis=-1, keepdims=True)
    return center * lax.rsqrt(spread + EPSILON) * norm_gain + norm_shift


def matmul(left_side, right_side):
    return jnp.dot(left_side, right_side, preferred_element_type=jnp.float32)


def inner_rows(left_side, right_side):
    return lax.dot_general(
        left_side, right_side, (((0,), (0,)), ((), ())), preferred_element_type=jnp.float32
    )


def against(left_side, right_side):
    return lax.dot_general(
        left_side, right_side, (((1,), (1,)), ((), ())), preferred_element_type=jnp.float32
    )


def column_sums(values):
    return jnp.sum(values.astype(jnp.float32), axis=0)


def lookup(lookup_table, wanted):
    entries = jnp.arange(lookup_table.shape[0], dtype=jnp.int32)
    matches = wanted[..., None] == entries
    located = jnp.sum(jnp.where(matches, lookup_table, jnp.int32(0)), axis=-1, dtype=jnp.int32)
    return jnp.where(wanted >= 0, located, jnp.int32(-1))


def ancestor_slots(block_segment, segment_parent, own_segments):
    entries = jnp.arange(block_segment.shape[0], dtype=jnp.int32)
    placed = block_segment[None, :] == entries[:, None]
    slot_of = jnp.sum(jnp.where(placed, entries[None, :], jnp.int32(0)), axis=1, dtype=jnp.int32)
    current = own_segments
    lineage = []
    for depth_step in range(DEPTH):
        lineage.append(current)
        current = lookup(segment_parent, current)
    lineage = jnp.stack(lineage, axis=-1)
    usable = lineage >= 0
    return (jnp.where(usable, lookup(slot_of, lineage), jnp.int32(0)), usable)


def stack_heads(rows):
    lane = lax.broadcasted_iota(jnp.int32, rows.shape, 1)
    low = lane < HD
    zero = jnp.zeros_like(rows)
    return jnp.concatenate([jnp.where(low, rows, zero), jnp.where(low, zero, rows)], axis=0)


def unstack_heads(rows):
    half = rows.shape[0] // 2
    lane = lax.broadcasted_iota(jnp.int32, (half, rows.shape[1]), 1)
    return jnp.where(lane < HD, rows[:half], rows[half:])


def make_bias(levels, bias_ref):
    row = lax.broadcasted_iota(jnp.int32, (BLK, DEPTH * BLK), 0)
    col = lax.broadcasted_iota(jnp.int32, (BLK, DEPTH * BLK), 1)
    limit = jnp.where(col < BLK, row + 1, levels * BLK)
    bias = jnp.where(col < limit, jnp.float32(0.0), jnp.float32(NEGATIVE))
    bias_ref[:BLK, :] = bias
    bias_ref[BLK:, :] = bias


def fetch_levels(slots_ref, slot, source_ref, target_ref):
    for level in range(DEPTH):
        start = pl.multiple_of(slots_ref[slot, level] * BLK, BLK)
        target_ref[level * BLK : (level + 1) * BLK, :] = source_ref[pl.ds(start, BLK), :]


def forward_kernel(slots_ref, query_ref, key_ref, value_ref, mixed_ref, logsum_ref, key_here, value_here, bias_ref):
    width = query_ref.shape[1]

    def one_slot(slot, carry):
        rows = pl.ds(pl.multiple_of(slot * BLK, BLK), BLK)
        fetch_levels(slots_ref, slot, key_ref, key_here)
        fetch_levels(slots_ref, slot, value_ref, value_here)
        make_bias(slots_ref[slot, DEPTH], bias_ref)
        lane = lax.broadcasted_iota(jnp.int32, (BLK, PAIR), 1)
        logsums = jnp.zeros((BLK, PAIR), jnp.float32)
        for pair in range(width // PAIR):
            cols = slice(pair * PAIR, (pair + 1) * PAIR)
            stacked = stack_heads(query_ref[rows, cols])
            scores = against(stacked, key_here[:, cols]) + bias_ref[...]
            highest = jnp.max(scores, axis=-1, keepdims=True)
            raised = jnp.exp(scores - highest)
            total = jnp.sum(raised, axis=-1, keepdims=True)
            mixed = matmul(raised.astype(jnp.bfloat16), value_here[:, cols]) / total
            mixed_ref[rows, cols] = unstack_heads(mixed).astype(jnp.bfloat16)
            logsum = highest + jnp.log(total)
            logsums = jnp.where(lane == 2 * pair, logsum[:BLK], logsums)
            logsums = jnp.where(lane == 2 * pair + 1, logsum[BLK:], logsums)
        logsum_ref[rows, :] = logsums
        return carry

    lax.fori_loop(0, query_ref.shape[0] // BLK, one_slot, 0)


def backward_kernel(
    slots_ref,
    query_ref,
    key_ref,
    value_ref,
    logsum_ref,
    mixed_ref,
    mixed_grad_ref,
    query_grad_ref,
    sums_ref,
    key_here,
    value_here,
    bias_ref,
    key_sums,
    value_sums,
):
    width = query_ref.shape[1]
    key_sums[...] = jnp.zeros_like(key_sums)
    value_sums[...] = jnp.zeros_like(value_sums)

    def one_slot(slot, carry):
        rows = pl.ds(pl.multiple_of(slot * BLK, BLK), BLK)
        fetch_levels(slots_ref, slot, key_ref, key_here)
        fetch_levels(slots_ref, slot, value_ref, value_here)
        make_bias(slots_ref[slot, DEPTH], bias_ref)
        for pair in range(width // PAIR):
            cols = slice(pair * PAIR, (pair + 1) * PAIR)
            stacked = stack_heads(query_ref[rows, cols])
            grad_rows = mixed_grad_ref[rows, cols]
            grad_stacked = stack_heads(grad_rows)
            products = grad_rows.astype(jnp.float32) * mixed_ref[rows, cols].astype(jnp.float32)
            row_dot = jnp.sum(stack_heads(products), axis=-1, keepdims=True)
            logsum = jnp.concatenate(
                [logsum_ref[rows, 2 * pair : 2 * pair + 1], logsum_ref[rows, 2 * pair + 1 : 2 * pair + 2]], axis=0
            )
            key_rows = key_here[:, cols]
            shares = jnp.exp(against(stacked, key_rows) + bias_ref[...] - logsum)
            share_grad = against(grad_stacked, value_here[:, cols])
            score_grad = (shares * (share_grad - row_dot)).astype(jnp.bfloat16)
            query_grad = unstack_heads(matmul(score_grad, key_rows)) * (HD ** (-0.5))
            query_grad_ref[rows, cols] = query_grad.astype(jnp.bfloat16)
            key_part = inner_rows(stacked, score_grad)
            value_part = inner_rows(grad_stacked, shares.astype(jnp.bfloat16))
            for level in range(DEPTH):
                start = pl.multiple_of(slots_ref[slot, level] * BLK, BLK)
                here = slice(level * BLK, (level + 1) * BLK)
                key_sums[cols, pl.ds(start, BLK)] += key_part[:, here]
                value_sums[cols, pl.ds(start, BLK)] += value_part[:, here]
        return carry

    lax.fori_loop(0, query_ref.shape[0] // BLK, one_slot, 0)
    sums_ref[:width, :] = key_sums[...].astype(jnp.bfloat16)
    sums_ref[width:, :] = value_sums[...].astype(jnp.bfloat16)


def in_vmem():
    return pl.BlockSpec(memory_space=pltpu.VMEM)


def in_smem():
    return pl.BlockSpec(memory_space=pltpu.SMEM)


def attend(slots, query_rows, key_group, value_group):
    rows, width = query_rows.shape
    return pl.pallas_call(
        forward_kernel,
        out_shape=(
            jax.ShapeDtypeStruct((rows, width), jnp.bfloat16),
            jax.ShapeDtypeStruct((rows, PAIR), jnp.float32),
        ),
        in_specs=[in_smem(), in_vmem(), in_vmem(), in_vmem()],
        out_specs=(in_vmem(), in_vmem()),
        scratch_shapes=[
            pltpu.VMEM((DEPTH * BLK, width), jnp.bfloat16),
            pltpu.VMEM((DEPTH * BLK, width), jnp.bfloat16),
            pltpu.VMEM((2 * BLK, DEPTH * BLK), jnp.float32),
        ],
        compiler_params=pltpu.CompilerParams(vmem_limit_bytes=VMEM_BYTES),
    )(slots, query_rows, key_group, value_group)


def attend_backward(slots, query_rows, key_group, value_group, logsum, mixed, mixed_grad):
    rows, width = query_rows.shape
    keys = key_group.shape[0]
    return pl.pallas_call(
        backward_kernel,
        out_shape=(
            jax.ShapeDtypeStruct((rows, width), jnp.bfloat16),
            jax.ShapeDtypeStruct((2 * width, keys), jnp.bfloat16),
        ),
        in_specs=[in_smem()] + [in_vmem()] * 6,
        out_specs=(in_vmem(), in_vmem()),
        scratch_shapes=[
            pltpu.VMEM((DEPTH * BLK, width), jnp.bfloat16),
            pltpu.VMEM((DEPTH * BLK, width), jnp.bfloat16),
            pltpu.VMEM((2 * BLK, DEPTH * BLK), jnp.float32),
            pltpu.VMEM((width, keys), jnp.float32),
            pltpu.VMEM((width, keys), jnp.float32),
        ],
        compiler_params=pltpu.CompilerParams(vmem_limit_bytes=VMEM_BYTES),
    )(slots, query_rows, key_group, value_group, logsum, mixed, mixed_grad)


def pack_rows(pieces, width):
    blocks = []
    for piece in pieces:
        for start in range(0, piece.shape[1], width):
            blocks.append(piece[:, start : start + width])
    return blocks


def pack_vectors(pieces, width):
    joined = jnp.concatenate(pieces)
    count = -(-joined.shape[0] // width)
    return jnp.pad(joined, (0, count * width - joined.shape[0])).reshape(count, width)


def joined(pieces, axis):
    return pieces[0] if len(pieces) == 1 else jnp.concatenate(pieces, axis=axis)


def shards(
    inputs,
    cotangent,
    block_segment,
    segment_parent,
    query_weight,
    key_weight,
    value_weight,
    output_weight,
    gate_weight,
    gate_bias,
    up_weight,
    up_bias,
    down_weight,
    down_bias,
    carry_weight,
    carry_bias,
    first_gain,
    first_shift,
    second_gain,
    second_shift,
):
    width = inputs.shape[1]
    devices = lax.axis_size(BOTH)
    block_count = inputs.shape[0] // BLK
    group_blocks = block_segment.shape[0]

    vectors = (gate_bias, up_bias, down_bias, carry_bias, first_gain, first_shift, second_gain, second_shift)
    early = pack_rows((query_weight, key_weight, value_weight, gate_weight), width)
    late = pack_rows((output_weight, up_weight, down_weight, carry_weight), width)
    early = jnp.concatenate(early + [pack_vectors(vectors, width)])
    late = jnp.concatenate(late)
    early = jnp.pad(early, ((0, -early.shape[0] % 16), (0, 0)))
    early_rows = lax.all_gather(early, BOTH)
    input_group = lax.all_gather(inputs, "seq", axis=0, tiled=True)
    late_rows = lax.all_gather(late, BOTH)

    def take(source, start, piece):
        rows = piece.shape[0]
        parts = piece.shape[1] // width
        blocks = [
            source[:, start + part * rows : start + (part + 1) * rows].reshape(devices * rows, width)
            for part in range(parts)
        ]
        return (jnp.concatenate(blocks, axis=1) if parts > 1 else blocks[0]), start + parts * rows

    place = 0
    full_query, place = take(early_rows, place, query_weight)
    full_key, place = take(early_rows, place, key_weight)
    full_value, place = take(early_rows, place, value_weight)
    full_gate, place = take(early_rows, place, gate_weight)
    vector_rows = early_rows[:, place : place + -(-sum(v.shape[0] for v in vectors) // width)].reshape(devices, -1)
    full_vectors = []
    start = 0
    for vector in vectors:
        piece = vector_rows[:, start : start + vector.shape[0]].reshape(-1)
        full_vectors.append(piece.astype(jnp.float32))
        start += vector.shape[0]
    gate_b, up_b, down_b, carry_b, gain_one, shift_one, gain_two, shift_two = full_vectors
    place = 0
    full_output, place = take(late_rows, place, output_weight)
    full_up, place = take(late_rows, place, up_weight)
    full_down, place = take(late_rows, place, down_weight)
    full_carry, place = take(late_rows, place, carry_weight)

    own_start = lax.axis_index("seq") * block_count
    own_segments = lax.dynamic_slice_in_dim(block_segment, own_start, block_count)
    ancestor_slot, usable = ancestor_slots(block_segment, segment_parent, own_segments)
    slots = jnp.concatenate(
        [ancestor_slot, jnp.sum(usable, axis=-1, keepdims=True, dtype=jnp.int32)], axis=-1
    )

    values_in = inputs.astype(jnp.float32)
    normed_low = normalize(values_in, gain_one, shift_one).astype(jnp.bfloat16)
    query_low = (matmul(normed_low, full_query).astype(jnp.bfloat16) * (HD ** (-0.5))).astype(jnp.bfloat16)
    gate_open = jax.nn.sigmoid(matmul(normed_low, full_gate) + gate_b)
    normed_group = normalize(input_group.astype(jnp.float32), gain_one, shift_one).astype(jnp.bfloat16)
    key_group = matmul(normed_group, full_key).astype(jnp.bfloat16)
    value_group = matmul(normed_group, full_value).astype(jnp.bfloat16)

    cuts = max(1, group_blocks // 40)
    heads = [slice(cut * width // cuts, (cut + 1) * width // cuts) for cut in range(cuts)]
    forward = [
        attend(slots, query_low[:, cols], key_group[:, cols], value_group[:, cols]) for cols in heads
    ]
    attended_low = joined([mixed for mixed, logsum in forward], 1)

    branch = matmul(attended_low, full_output)
    middle = values_in + gate_open * branch
    normed_second = normalize(middle, gain_two, shift_two).astype(jnp.bfloat16)
    up_pre = matmul(normed_second, full_up) + up_b
    up_sigmoid = jax.nn.sigmoid(up_pre)
    hidden_low = (up_pre * up_sigmoid).astype(jnp.bfloat16)
    update = matmul(hidden_low, full_down) + down_b
    carry_open = jax.nn.sigmoid(matmul(normed_second, full_carry) + carry_b)
    output = (middle + carry_open * update).astype(jnp.bfloat16)

    grad_out = cotangent.astype(jnp.float32)
    update_grad = (carry_open * grad_out).astype(jnp.bfloat16)
    carry_pre_grad = (grad_out * update * carry_open * (1.0 - carry_open)).astype(jnp.bfloat16)
    grad_down = inner_rows(hidden_low, update_grad)
    grad_down_bias = column_sums(update_grad)
    grad_carry = inner_rows(normed_second, carry_pre_grad)
    grad_carry_bias = column_sums(carry_pre_grad)
    silu_slope = up_sigmoid * (1.0 + up_pre * (1.0 - up_sigmoid))
    up_pre_grad = (against(update_grad, full_down) * silu_slope).astype(jnp.bfloat16)
    grad_up = inner_rows(normed_second, up_pre_grad)
    grad_up_bias = column_sums(up_pre_grad)
    second_norm_grad = against(up_pre_grad, full_up) + against(carry_pre_grad, full_carry)
    second_pull = jax.vjp(normalize, middle, gain_two, shift_two)[1]
    middle_part, grad_second_gain, grad_second_shift = second_pull(second_norm_grad)
    middle_grad = grad_out + middle_part

    def spread(grad, piece):
        rows = piece.shape[0]
        return [
            grad[:, start : start + width].astype(jnp.bfloat16).reshape(devices, rows, width)
            for start in range(0, grad.shape[1], width)
        ]

    def own(summed, start, piece):
        rows = piece.shape[0]
        parts = piece.shape[1] // width
        blocks = [summed[start + part * rows : start + (part + 1) * rows] for part in range(parts)]
        return (jnp.concatenate(blocks, axis=1) if parts > 1 else blocks[0]), start + parts * rows

    first_pack = jnp.concatenate(
        spread(grad_up, up_weight) + spread(grad_down, down_weight) + spread(grad_carry, carry_weight), axis=1
    )
    first_sum = lax.psum_scatter(first_pack, BOTH, scatter_dimension=0, tiled=True)[0].astype(jnp.float32)

    branch_grad = (gate_open * middle_grad).astype(jnp.bfloat16)
    gate_pre_grad = (middle_grad * branch * gate_open * (1.0 - gate_open)).astype(jnp.bfloat16)
    grad_output = inner_rows(attended_low, branch_grad)
    grad_gate = inner_rows(normed_low, gate_pre_grad)
    grad_gate_bias = column_sums(gate_pre_grad)
    attended_grad = against(branch_grad, full_output).astype(jnp.bfloat16)

    backward = [
        attend_backward(
            slots,
            query_low[:, cols],
            key_group[:, cols],
            value_group[:, cols],
            logsum,
            attended_low[:, cols],
            attended_grad[:, cols],
        )
        for cols, (mixed, logsum) in zip(heads, forward)
    ]
    query_rows_grad = joined([query_part for query_part, sums in backward], 1)
    part = width // cuts
    sums = backward[0][1]
    if cuts > 1:
        sums = jnp.concatenate([sums[:part] for _, sums in backward] + [sums[part:] for _, sums in backward])

    both_weight = jnp.concatenate([full_key, full_value], axis=1)
    shared_grad = lax.dot_general(
        sums, both_weight, (((0,), (1,)), ((), ())), preferred_element_type=jnp.float32
    ).astype(jnp.bfloat16)
    shared_sum = lax.psum_scatter(shared_grad, "seq", scatter_dimension=0, tiled=True).astype(jnp.float32)
    grad_both = matmul(sums, normed_group)
    grad_key = jnp.transpose(grad_both[:width])
    grad_value = jnp.transpose(grad_both[width:])
    grad_query = inner_rows(normed_low, query_rows_grad)
    first_norm_grad = (
        against(query_rows_grad, full_query) + shared_sum + against(gate_pre_grad, full_gate)
    )
    first_pull = jax.vjp(normalize, values_in, gain_one, shift_one)[1]
    input_part, grad_first_gain, grad_first_shift = first_pull(first_norm_grad)
    input_grad = middle_grad + input_part

    vector_grads = (
        grad_gate_bias,
        grad_up_bias,
        grad_down_bias,
        grad_carry_bias,
        grad_first_gain,
        grad_first_shift,
        grad_second_gain,
        grad_second_shift,
    )
    vector_pack = jnp.concatenate([grad.reshape(devices, -1) for grad in vector_grads], axis=1)
    count = -(-vector_pack.shape[1] // width)
    vector_pack = jnp.pad(vector_pack, ((0, 0), (0, count * width - vector_pack.shape[1])))
    second_pack = (
        spread(grad_query, query_weight)
        + spread(grad_key, key_weight)
        + spread(grad_value, value_weight)
        + spread(grad_output, output_weight)
        + spread(grad_gate, gate_weight)
        + [vector_pack.astype(jnp.bfloat16).reshape(devices, count, width)]
    )
    second_pack = jnp.concatenate(second_pack, axis=1)
    second_pack = jnp.pad(second_pack, ((0, 0), (0, -second_pack.shape[1] % 16), (0, 0)))
    second_sum = lax.psum_scatter(second_pack, BOTH, scatter_dimension=0, tiled=True)[0].astype(jnp.float32)

    place = 0
    own_up, place = own(first_sum, place, up_weight)
    own_down, place = own(first_sum, place, down_weight)
    own_carry, place = own(first_sum, place, carry_weight)
    place = 0
    own_query, place = own(second_sum, place, query_weight)
    own_key, place = own(second_sum, place, key_weight)
    own_value, place = own(second_sum, place, value_weight)
    own_output, place = own(second_sum, place, output_weight)
    own_gate, place = own(second_sum, place, gate_weight)
    own_vectors = second_sum[place : place + count].reshape(-1)
    vector_out = []
    start = 0
    for vector in vectors:
        vector_out.append(own_vectors[start : start + vector.shape[0]])
        start += vector.shape[0]
    gate_bg, up_bg, down_bg, carry_bg, gain_one_g, shift_one_g, gain_two_g, shift_two_g = vector_out
    return (
        output,
        input_grad,
        own_query,
        own_key,
        own_value,
        own_output,
        own_gate,
        gate_bg,
        own_up,
        up_bg,
        own_down,
        down_bg,
        own_carry,
        carry_bg,
        gain_one_g,
        shift_one_g,
        gain_two_g,
        shift_two_g,
    )


def solution(mesh):
    rows = P(BOTH, None)
    line = P(BOTH)
    matrix_or_line = (rows,) * 5 + (line, rows, line, rows, line, rows) + (line,) * 5
    return jax.shard_map(
        shards,
        mesh=mesh,
        in_specs=(rows, rows, P("dp"), P("dp")) + matrix_or_line,
        out_specs=(rows, rows) + matrix_or_line,
        check_vma=False,
    )
```

```python
import functools

import jax
import jax.numpy as jnp
from jax import lax
from jax.experimental import pallas as pl
from jax.experimental.pallas import tpu as pltpu
from jax.sharding import PartitionSpec as P

HD = 64
BLK = 128
DEPTH = 10
PAIR = 2 * HD

EPSILON = 1e-05
NEGATIVE = -1e30
BOTH = ("dp", "seq")
VMEM_BYTES = 60 * 1024 * 1024


def normalize(values, norm_gain, norm_shift):
    center = values - jnp.mean(values, axis=-1, keepdims=True)
    spread = jnp.mean(center * center, axis=-1, keepdims=True)
    return center * lax.rsqrt(spread + EPSILON) * norm_gain + norm_shift


def matmul(left_side, right_side):
    return jnp.dot(left_side, right_side, preferred_element_type=jnp.float32)


def inner_rows(left_side, right_side):
    return lax.dot_general(
        left_side, right_side, (((0,), (0,)), ((), ())), preferred_element_type=jnp.float32
    )


def against(left_side, right_side):
    return lax.dot_general(
        left_side, right_side, (((1,), (1,)), ((), ())), preferred_element_type=jnp.float32
    )


def column_sums(values):
    return jnp.sum(values.astype(jnp.float32), axis=0)


def lookup(lookup_table, wanted):
    entries = jnp.arange(lookup_table.shape[0], dtype=jnp.int32)
    matches = wanted[..., None] == entries
    located = jnp.sum(jnp.where(matches, lookup_table, jnp.int32(0)), axis=-1, dtype=jnp.int32)
    return jnp.where(wanted >= 0, located, jnp.int32(-1))


def ancestor_slots(block_segment, segment_parent, own_segments):
    entries = jnp.arange(block_segment.shape[0], dtype=jnp.int32)
    placed = block_segment[None, :] == entries[:, None]
    slot_of = jnp.sum(jnp.where(placed, entries[None, :], jnp.int32(0)), axis=1, dtype=jnp.int32)
    current = own_segments
    lineage = []
    for depth_step in range(DEPTH):
        lineage.append(current)
        current = lookup(segment_parent, current)
    lineage = jnp.stack(lineage, axis=-1)
    usable = lineage >= 0
    return (jnp.where(usable, lookup(slot_of, lineage), jnp.int32(0)), usable)


def stack_heads(rows):
    lane = lax.broadcasted_iota(jnp.int32, rows.shape, 1)
    low = lane < HD
    zero = jnp.zeros_like(rows)
    return jnp.concatenate([jnp.where(low, rows, zero), jnp.where(low, zero, rows)], axis=0)


def unstack_heads(rows):
    half = rows.shape[0] // 2
    lane = lax.broadcasted_iota(jnp.int32, (half, rows.shape[1]), 1)
    return jnp.where(lane < HD, rows[:half], rows[half:])


def make_bias(levels, bias_ref):
    row = lax.broadcasted_iota(jnp.int32, (BLK, DEPTH * BLK), 0)
    col = lax.broadcasted_iota(jnp.int32, (BLK, DEPTH * BLK), 1)
    limit = jnp.where(col < BLK, row + 1, levels * BLK)
    bias = jnp.where(col < limit, jnp.float32(0.0), jnp.float32(NEGATIVE))
    bias_ref[:BLK, :] = bias
    bias_ref[BLK:, :] = bias


def fetch_levels(slots_ref, slot, source_ref, target_ref):
    for level in range(DEPTH):
        start = pl.multiple_of(slots_ref[slot, level] * BLK, BLK)
        target_ref[level * BLK : (level + 1) * BLK, :] = source_ref[pl.ds(start, BLK), :]


def forward_kernel(slots_ref, query_ref, key_ref, value_ref, mixed_ref, logsum_ref, key_here, value_here, bias_ref):
    width = query_ref.shape[1]

    def one_slot(slot, carry):
        rows = pl.ds(pl.multiple_of(slot * BLK, BLK), BLK)
        fetch_levels(slots_ref, slot, key_ref, key_here)
        fetch_levels(slots_ref, slot, value_ref, value_here)
        make_bias(slots_ref[slot, DEPTH], bias_ref)
        lane = lax.broadcasted_iota(jnp.int32, (BLK, PAIR), 1)
        logsums = jnp.zeros((BLK, PAIR), jnp.float32)
        for pair in range(width // PAIR):
            cols = slice(pair * PAIR, (pair + 1) * PAIR)
            stacked = stack_heads(query_ref[rows, cols])
            scores = against(stacked, key_here[:, cols]) + bias_ref[...]
            highest = jnp.max(scores, axis=-1, keepdims=True)
            raised = jnp.exp(scores - highest)
            total = jnp.sum(raised, axis=-1, keepdims=True)
            mixed = matmul(raised.astype(jnp.bfloat16), value_here[:, cols]) / total
            mixed_ref[rows, cols] = unstack_heads(mixed).astype(jnp.bfloat16)
            logsum = highest + jnp.log(total)
            logsums = jnp.where(lane == 2 * pair, logsum[:BLK], logsums)
            logsums = jnp.where(lane == 2 * pair + 1, logsum[BLK:], logsums)
        logsum_ref[rows, :] = logsums
        return carry

    lax.fori_loop(0, query_ref.shape[0] // BLK, one_slot, 0)


def backward_kernel(
    slots_ref,
    query_ref,
    key_source,
    value_source,
    logsum_ref,
    mixed_ref,
    mixed_grad_ref,
    normed_source,
    weight_ref,
    *refs,
):
    query_grad_ref, grads_ref, lanes_ref = refs[:3]
    shared_refs = refs[3:-9]
    key_ref, value_ref, normed_ref, key_here, value_here, bias_ref, key_sums, value_sums, copies = refs[-9:]
    width = query_ref.shape[1]
    fetches = [
        pltpu.make_async_copy(source, target, copies.at[index])
        for index, (source, target) in enumerate(
            ((key_source, key_ref), (value_source, value_ref), (normed_source, normed_ref))
        )
    ]
    for fetch in fetches:
        fetch.start()
    key_sums[...] = jnp.zeros_like(key_sums)
    value_sums[...] = jnp.zeros_like(value_sums)
    fetches[0].wait()
    fetches[1].wait()

    def one_slot(slot, carry):
        rows = pl.ds(pl.multiple_of(slot * BLK, BLK), BLK)
        fetch_levels(slots_ref, slot, key_ref, key_here)
        fetch_levels(slots_ref, slot, value_ref, value_here)
        make_bias(slots_ref[slot, DEPTH], bias_ref)
        for pair in range(width // PAIR):
            cols = slice(pair * PAIR, (pair + 1) * PAIR)
            stacked = stack_heads(query_ref[rows, cols])
            grad_rows = mixed_grad_ref[rows, cols]
            grad_stacked = stack_heads(grad_rows)
            products = grad_rows.astype(jnp.float32) * mixed_ref[rows, cols].astype(jnp.float32)
            row_dot = jnp.sum(stack_heads(products), axis=-1, keepdims=True)
            logsum = jnp.concatenate(
                [logsum_ref[rows, 2 * pair : 2 * pair + 1], logsum_ref[rows, 2 * pair + 1 : 2 * pair + 2]], axis=0
            )
            key_rows = key_here[:, cols]
            shares = jnp.exp(against(stacked, key_rows) + bias_ref[...] - logsum)
            share_grad = against(grad_stacked, value_here[:, cols])
            score_grad = (shares * (share_grad - row_dot)).astype(jnp.bfloat16)
            query_grad = unstack_heads(matmul(score_grad, key_rows)) * (HD ** (-0.5))
            query_grad_ref[rows, cols] = query_grad.astype(jnp.bfloat16)
            key_part = inner_rows(stacked, score_grad)
            value_part = inner_rows(grad_stacked, shares.astype(jnp.bfloat16))
            for level in range(DEPTH):
                start = pl.multiple_of(slots_ref[slot, level] * BLK, BLK)
                here = slice(level * BLK, (level + 1) * BLK)
                key_sums[cols, pl.ds(start, BLK)] += key_part[:, here]
                value_sums[cols, pl.ds(start, BLK)] += value_part[:, here]
        return carry

    lax.fori_loop(0, query_ref.shape[0] // BLK, one_slot, 0)

    fetches[2].wait()
    piece = key_sums.shape[1] // len(shared_refs)
    for index in range(len(shared_refs)):
        here = slice(index * piece, (index + 1) * piece)
        shared = None
        for part, part_sums in enumerate((key_sums, value_sums)):
            lines = slice(part * width, (part + 1) * width)
            block = part_sums[:, here]
            tiles = [block[:, start : start + BLK] for start in range(0, piece, BLK)]
            lane_sums = functools.reduce(lambda left, right: left + right, tiles)
            low = block.astype(jnp.bfloat16)
            product = matmul(weight_ref[:, lines], low)
            shared = product if shared is None else shared + product
            grad = matmul(low, normed_ref[here, :])
            if index == 0:
                grads_ref[lines, :] = grad
                lanes_ref[lines, :] = lane_sums
            else:
                grads_ref[lines, :] += grad
                lanes_ref[lines, :] += lane_sums
        shared_refs[index][...] = shared.astype(jnp.bfloat16)


def about(cost):
    return pl.CostEstimate(flops=int(cost * 1e9), bytes_accessed=int(cost * 1e6), transcendentals=0)


def in_vmem():
    return pl.BlockSpec(memory_space=pltpu.VMEM)


def in_smem():
    return pl.BlockSpec(memory_space=pltpu.SMEM)


def attend(slots, query_rows, key_group, value_group):
    rows, width = query_rows.shape
    return pl.pallas_call(
        forward_kernel,
        cost_estimate=about(18),
        out_shape=(
            jax.ShapeDtypeStruct((rows, width), jnp.bfloat16),
            jax.ShapeDtypeStruct((rows, PAIR), jnp.float32),
        ),
        in_specs=[in_smem(), in_vmem(), in_vmem(), in_vmem()],
        out_specs=(in_vmem(), in_vmem()),
        scratch_shapes=[
            pltpu.VMEM((DEPTH * BLK, width), jnp.bfloat16),
            pltpu.VMEM((DEPTH * BLK, width), jnp.bfloat16),
            pltpu.VMEM((2 * BLK, DEPTH * BLK), jnp.float32),
        ],
        compiler_params=pltpu.CompilerParams(vmem_limit_bytes=VMEM_BYTES),
    )(slots, query_rows, key_group, value_group)


def attend_backward(slots, query_rows, key_group, value_group, logsum, mixed, mixed_grad, normed_group, both_weight):
    rows, width = query_rows.shape
    keys, model_width = normed_group.shape
    pieces = keys // rows

    anywhere = pl.BlockSpec(memory_space=pl.ANY)
    return pl.pallas_call(
        backward_kernel,
        cost_estimate=about(40),
        out_shape=(
            jax.ShapeDtypeStruct((rows, width), jnp.bfloat16),
            jax.ShapeDtypeStruct((2 * width, model_width), jnp.float32),
            jax.ShapeDtypeStruct((2 * width, BLK), jnp.float32),
        )
        + (jax.ShapeDtypeStruct((model_width, rows), jnp.bfloat16),) * pieces,
        in_specs=[in_smem(), in_vmem(), anywhere, anywhere, in_vmem(), in_vmem(), in_vmem(), anywhere, in_vmem()],
        out_specs=(in_vmem(),) * (3 + pieces),
        scratch_shapes=[
            pltpu.VMEM((keys, width), jnp.bfloat16),
            pltpu.VMEM((keys, width), jnp.bfloat16),
            pltpu.VMEM((keys, model_width), jnp.bfloat16),
            pltpu.VMEM((DEPTH * BLK, width), jnp.bfloat16),
            pltpu.VMEM((DEPTH * BLK, width), jnp.bfloat16),
            pltpu.VMEM((2 * BLK, DEPTH * BLK), jnp.float32),
            pltpu.VMEM((width, keys), jnp.float32),
            pltpu.VMEM((width, keys), jnp.float32),
            pltpu.SemaphoreType.DMA((3,)),
        ],
        compiler_params=pltpu.CompilerParams(vmem_limit_bytes=VMEM_BYTES),
    )(slots, query_rows, key_group, value_group, logsum, mixed, mixed_grad, normed_group, both_weight)


def project_kernel(pieces, vectors_ref, key_weight_ref, value_weight_ref, refs):
    normed_ref, key_ref, value_ref = refs[-3:]
    gain = vectors_ref[GAIN_ONE : GAIN_ONE + 1, :]
    shift = vectors_ref[SHIFT_ONE : SHIFT_ONE + 1, :]
    for index, piece in enumerate(pieces):
        rows = slice(index * piece.shape[0], (index + 1) * piece.shape[0])
        normed = normalize(piece[...].astype(jnp.float32), gain, shift).astype(jnp.bfloat16)
        normed_ref[rows, :] = normed
        key_ref[rows, :] = matmul(normed, key_weight_ref[...]).astype(jnp.bfloat16)
        value_ref[rows, :] = matmul(normed, value_weight_ref[...]).astype(jnp.bfloat16)


def project(pieces, vectors, key_weight, value_weight, group_rows, step, carried):
    count = len(pieces)
    rows, width = pieces[0].shape

    def body(*refs):
        project_kernel(refs[:count], *refs[count : count + 3], refs)

    block = pl.BlockSpec((count * rows, width), lambda index: (step, 0))
    whole = jax.ShapeDtypeStruct((group_rows, width), jnp.bfloat16)
    extra = [] if carried is None else list(carried)
    return pl.pallas_call(
        body,
        cost_estimate=about(4),
        grid=(1,),
        out_shape=(whole,) * 3,
        in_specs=[in_vmem()] * (count + 3) + [pl.BlockSpec(memory_space=pl.ANY)] * len(extra),
        out_specs=(block,) * 3,
        input_output_aliases={count + 3 + index: index for index in range(len(extra))},
        compiler_params=pltpu.CompilerParams(vmem_limit_bytes=VMEM_BYTES),
    )(*pieces, vectors, key_weight, value_weight, *extra)


class Axis:
    def __init__(self, name, size, stride):
        self.name = name
        self.size = size
        self.stride = stride

    def position(self):
        return lax.axis_index(self.name) // self.stride % self.size

    def rotate(self, values, shift):
        pairs = []
        for index in range(lax.axis_size(self.name)):
            here = index // self.stride % self.size
            there = (here + shift) % self.size
            pairs.append((index, index + (there - here) * self.stride))
        return lax.ppermute(values, self.name, pairs)


def axes():
    seq = lax.axis_size("seq")
    dp = lax.axis_size("dp")
    along_z = 4 if seq % 4 == 0 else 1
    cores = 2 if dp % 2 == 0 else 1
    return (
        Axis("seq", along_z, seq // along_z),
        Axis("seq", seq // along_z, 1),
        Axis("dp", dp // cores, cores),
        Axis("dp", cores, 1),
    )


def relative_devices():
    axis_z, axis_x, axis_y, axis_core = axes()

    def place(axis, dim):
        back = lax.broadcasted_iota(jnp.int32, (axis_core.size, axis_y.size, axis_x.size, axis_z.size), dim)
        return (axis.position() - back + axis.size) % axis.size

    dp_index = place(axis_y, 1) * axis_core.size + place(axis_core, 0)
    seq_index = place(axis_z, 3) * axis_x.size + place(axis_x, 2)
    return (dp_index * lax.axis_size("seq") + seq_index).reshape(-1)


def add_low(left_side, right_side):
    return (left_side.astype(jnp.float32) + right_side.astype(jnp.float32)).astype(jnp.bfloat16)


def ring_scatter(entry, axis):
    running = entry(axis.size - 1)
    for back in range(axis.size - 1, 0, -1):
        running = add_low(axis.rotate(running, -1), entry(back - 1))
    return running


def pair_scatter(keep, send, axis):
    arrived = axis.rotate(send, -1)
    return lambda index: add_low(arrived[index], keep[index])


GATE_B, DOWN_B, CARRY_B, GAIN_ONE, SHIFT_ONE, GAIN_TWO, SHIFT_TWO, UP_B = range(8)
VECTOR_ROWS = 16


def pack_kernel(place_ref, *refs):
    early_sources, late_sources, vector_refs, (early_ref, late_ref) = refs[:4], refs[4:8], refs[8:16], refs[16:]
    width = early_ref.shape[1]
    for target, sources in ((early_ref, early_sources), (late_ref, late_sources)):
        start = 0
        for source in sources:
            rows = source.shape[0]
            for column in range(0, source.shape[1], width):
                target[start : start + rows, :] = source[:, column : column + width]
                start += rows
    block = jnp.zeros((VECTOR_ROWS, width), jnp.float32)
    line = lax.broadcasted_iota(jnp.int32, block.shape, 0)
    for index, source in enumerate(vector_refs):
        count = source.shape[1]
        feature = lax.broadcasted_iota(jnp.int32, (count, width), 0) + place_ref[0] * count
        column = lax.broadcasted_iota(jnp.int32, (count, width), 1)
        for part in range(count * place_ref.shape[0] // width):
            spot = jnp.where(feature == column + part * width, jnp.float32(1.0), jnp.float32(0.0))
            spread = matmul(source[...], spot.astype(jnp.bfloat16))
            block += jnp.where(line == index + part, spread, jnp.float32(0.0))
    early_ref[early_ref.shape[0] - VECTOR_ROWS :, :] = block.astype(jnp.bfloat16)


def unpack_kernel(place_ref, mine_ref, other_ref, query_ref, key_ref, value_ref, gate_ref, vectors_ref):
    half = mine_ref.shape[0]
    rows = (mine_ref.shape[1] - VECTOR_ROWS) // 4
    vectors = jnp.zeros(vectors_ref.shape, jnp.float32)
    for index in range(2 * half):
        source = (mine_ref if index < half else other_ref).at[index % half]
        target = pl.ds(pl.multiple_of(place_ref[index] * rows, rows), rows)
        for part, weight_ref in enumerate((query_ref, key_ref, value_ref, gate_ref)):
            weight_ref[target, :] = source[part * rows : (part + 1) * rows, :]
        vectors += source[4 * rows :, :].astype(jnp.float32)
    vectors_ref[...] = vectors


def unpack_late_kernel(
    place_ref, line_ref, line_other_ref, plane_ref, plane_other_ref, output_ref, up_ref, down_ref, carry_ref
):
    half = line_ref.shape[0]
    width = output_ref.shape[1]
    rows = output_ref.shape[0] // (2 * half)
    down_rows = down_ref.shape[0] // (2 * half)
    for index in range(2 * half):
        source = (line_ref if index < half else line_other_ref).at[index % half]
        target = pl.ds(pl.multiple_of(place_ref[0, index] * rows, rows), rows)
        output_ref[target, :] = source[:rows, :]
        for part in range(up_ref.shape[1] // width):
            up_ref[target, part * width : (part + 1) * width] = source[(part + 1) * rows : (part + 2) * rows, :]
        source = (plane_ref if index < half else plane_other_ref).at[index % half]
        target = pl.ds(pl.multiple_of(place_ref[1, index] * down_rows, down_rows), down_rows)
        down_ref[target, :] = source[:down_rows, :]
        target = pl.ds(pl.multiple_of(place_ref[1, index] * rows, rows), rows)
        carry_ref[target, :] = source[down_rows:, :]


def spread_rows(place_ref, grad_ref, keep_ref, send_ref, start, rows):
    half = keep_ref.shape[0]
    for index in range(2 * half):
        source = pl.ds(pl.multiple_of(place_ref[index] * rows, rows), rows)
        target = (keep_ref if index < half else send_ref).at[index % half]
        target[start : start + rows, :] = grad_ref[source, :].astype(jnp.bfloat16)


def first_grads_kernel(
    place_ref,
    hidden_ref,
    update_grad_ref,
    normed_second_ref,
    up_pre_ref,
    carry_pre_ref,
    attended_ref,
    branch_grad_ref,
    normed_ref,
    gate_pre_ref,
    keep_ref,
    send_ref,
    up_grad,
    down_grad,
    square_grads,
):
    width = keep_ref.shape[2]
    rows = width // (2 * keep_ref.shape[0])
    start = 0
    for part in range(up_pre_ref.shape[1] // width):
        grad = up_grad.at[part]
        grad[...] = inner_rows(normed_second_ref[...], up_pre_ref[:, part * width : (part + 1) * width])
        spread_rows(place_ref, grad, keep_ref, send_ref, start, rows)
        start += rows
    for part in range(hidden_ref.shape[1] // width):
        here = slice(part * width, (part + 1) * width)
        down_grad[here, :] = inner_rows(hidden_ref[:, here], update_grad_ref[...])
    down_rows = hidden_ref.shape[1] // (2 * keep_ref.shape[0])
    spread_rows(place_ref, down_grad, keep_ref, send_ref, start, down_rows)
    start += down_rows
    pairs = ((normed_second_ref, carry_pre_ref), (attended_ref, branch_grad_ref), (normed_ref, gate_pre_ref))
    for index, (left_ref, right_ref) in enumerate(pairs):
        grad = square_grads.at[index]
        grad[...] = inner_rows(left_ref[...], right_ref[...])
        spread_rows(place_ref, grad, keep_ref, send_ref, start, rows)
        start += rows


def second_grads_kernel(
    place_ref,
    both_grads_ref,
    normed_ref,
    query_grad_ref,
    gate_pre_ref,
    lanes_ref,
    query_weight_ref,
    key_weight_ref,
    value_weight_ref,
    gate_weight_ref,
    vectors_ref,
    block_ref,
    keep_ref,
    send_ref,
    grads,
):
    width = keep_ref.shape[2]
    rows = width // (2 * keep_ref.shape[0])
    grads[0] = inner_rows(normed_ref[...], query_grad_ref[...])
    grads[1] = jnp.transpose(both_grads_ref[:width, :])
    grads[2] = jnp.transpose(both_grads_ref[width:, :])
    for index in range(3):
        spread_rows(place_ref, grads.at[index], keep_ref, send_ref, index * rows, rows)
    gate_grad = inner_rows(normed_ref[...], gate_pre_ref[...])

    def line_sums(ref):
        return jnp.sum(ref[...].astype(jnp.float32), axis=0, keepdims=True)

    def as_line(column):
        return jnp.transpose(jnp.broadcast_to(column, (width, BLK)))[:1, :]

    lines = (
        line_sums(query_grad_ref),
        jnp.sum(jnp.transpose(lanes_ref[:width, :]), axis=0, keepdims=True),
        jnp.sum(jnp.transpose(lanes_ref[width:, :]), axis=0, keepdims=True),
        line_sums(gate_pre_ref),
    )
    weighted = jnp.zeros((width, width), jnp.float32)
    shifted = jnp.zeros((width, width), jnp.float32)
    weight_refs = (query_weight_ref, key_weight_ref, value_weight_ref, gate_weight_ref)
    for weight_ref, line, grad in zip(weight_refs, lines, (grads[0], grads[1], grads[2], gate_grad)):
        weight = weight_ref[...].astype(jnp.float32)
        weighted += weight * grad
        shifted += weight * line
    shift_line = as_line(jnp.sum(shifted, axis=1, keepdims=True))
    gain_line = (
        as_line(jnp.sum(weighted, axis=1, keepdims=True)) - vectors_ref[SHIFT_ONE : SHIFT_ONE + 1, :] * shift_line
    ) / vectors_ref[GAIN_ONE : GAIN_ONE + 1, :]
    place = lax.broadcasted_iota(jnp.int32, block_ref.shape, 0)
    block = jnp.where(place == GAIN_ONE, gain_line, block_ref[...])
    block = jnp.where(place == SHIFT_ONE, shift_line, block).astype(jnp.bfloat16)
    for index in range(keep_ref.shape[0]):
        keep_ref[index, 3 * rows :, :] = block
        send_ref[index, 3 * rows :, :] = block


def local_call(kernel, cost, outs, smem, args, scratch=()):
    return pl.pallas_call(
        kernel,
        cost_estimate=about(cost),
        out_shape=outs,
        in_specs=[in_smem()] + [in_vmem()] * len(args),
        out_specs=jax.tree.map(lambda out: in_vmem(), outs),
        scratch_shapes=list(scratch),
        compiler_params=pltpu.CompilerParams(vmem_limit_bytes=VMEM_BYTES),
    )(smem, *args)


def joined(pieces, axis):
    return pieces[0] if len(pieces) == 1 else jnp.concatenate(pieces, axis=axis)


def shards(
    inputs,
    cotangent,
    block_segment,
    segment_parent,
    query_weight,
    key_weight,
    value_weight,
    output_weight,
    gate_weight,
    gate_bias,
    up_weight,
    up_bias,
    down_weight,
    down_bias,
    carry_weight,
    carry_bias,
    first_gain,
    first_shift,
    second_gain,
    second_shift,
):
    width = inputs.shape[1]
    devices = lax.axis_size(BOTH)
    block_count = inputs.shape[0] // BLK
    group_blocks = block_segment.shape[0]

    axis_z, axis_x, axis_y, axis_core = axes()
    rows_each = query_weight.shape[0]
    sizes = (axis_z.size, axis_x.size, axis_y.size, axis_core.size)
    direct = sizes == (4, 2, 2, 2) and rows_each % 16 == 0
    places = relative_devices()
    device = lax.axis_index(BOTH)
    vectors = (gate_bias, down_bias, carry_bias, first_gain, first_shift, second_gain, second_shift, up_bias)
    early_set = (query_weight, key_weight, value_weight, gate_weight)
    late_set = (output_weight, up_weight, down_weight, carry_weight)
    low = jnp.bfloat16

    def struct(*shape, dtype=low):
        return jax.ShapeDtypeStruct(shape, dtype)

    def take(source, start, piece):
        rows = piece.shape[0]
        parts = piece.shape[1] // width
        blocks = [
            source[:, start + part * rows : start + (part + 1) * rows].reshape(devices * rows, width)
            for part in range(parts)
        ]
        return joined(blocks, 1), start + parts * rows

    def flat_rows(pieces):
        return [piece[:, start : start + width] for piece in pieces for start in range(0, piece.shape[1], width)]

    if direct:
        early_count = 4 * rows_each + VECTOR_ROWS
        late_count = sum(piece.shape[0] * piece.shape[1] // width for piece in late_set)
        early, late = local_call(
            pack_kernel,
            2,
            (struct(early_count, width), struct(late_count, width)),
            jnp.full((devices,), device, jnp.int32),
            early_set + late_set + tuple(vector.reshape(1, -1) for vector in vectors),
        )
        late_line = [late]
        early_one = axis_z.rotate(early, 1)
        z_one = axis_z.rotate(inputs, 1)
        x_zero = axis_x.rotate(inputs, 1)
        late_line.append(axis_z.rotate(late, 1))
        early_two = axis_z.rotate(early_one, 1)
        early_two, z_one, x_zero, late_line[1] = lax.optimization_barrier((early_two, z_one, x_zero, late_line[1]))
        early_three = axis_z.rotate(early_two, 1)
        z_two = axis_z.rotate(z_one, 1)
        x_one = axis_x.rotate(z_one, 1)
        late_line.append(axis_z.rotate(late_line[1], 1))
        early_line = jnp.stack([early, early_one, early_two, early_three])
        early_other = axis_x.rotate(early_line, 1)
        early_other, z_two, x_one, late_line[2] = lax.optimization_barrier((early_other, z_two, x_one, late_line[2]))
        early_plane = jnp.stack([early_line, early_other])
        early_other = axis_y.rotate(early_plane, 1)
        z_three = axis_z.rotate(z_two, 1)
        x_two = axis_x.rotate(z_two, 1)
        late_line.append(axis_z.rotate(late_line[2], 1))
        early_all = jnp.stack([early_plane, early_other]).reshape(devices // 2, early_count, width)
        early_other = axis_core.rotate(early_all, 1)
        early_other, z_three, x_two, late_line[3] = lax.optimization_barrier(
            (early_other, z_three, x_two, late_line[3])
        )
        x_three = axis_x.rotate(z_three, 1)
        late_half = late_count // 2
        late_x = jnp.stack([rows[:late_half] for rows in late_line])
        late_y = jnp.stack([rows[late_half:] for rows in late_line])
        late_x_other = axis_x.rotate(late_x, 1)
        late_y_other = axis_y.rotate(late_y, 1)
        x_three, late_x_other, late_y_other = lax.optimization_barrier((x_three, late_x_other, late_y_other))
        late_x = jnp.stack([late_x, late_x_other])
        late_y = jnp.stack([late_y, late_y_other])
        late_x = jnp.stack([late_x, axis_y.rotate(late_x, 1)]).reshape(devices // 2, late_half, width)
        late_y = jnp.stack([late_y, axis_x.rotate(late_y, 1)]).reshape(devices // 2, late_half, width)
        late_x_other = axis_core.rotate(late_x, 1)
        late_y_other = axis_core.rotate(late_y, 1)
        other_places = jnp.transpose(places.reshape(2, 2, 2, 4), (0, 2, 1, 3)).reshape(-1)
        full_output, full_up, full_down, full_carry = local_call(
            unpack_late_kernel,
            5,
            (struct(width, width), struct(width, up_weight.shape[1]), struct(up_weight.shape[1], width), struct(width, width)),
            jnp.stack([places, other_places]),
            (late_x, late_x_other, late_y, late_y_other),
        )
        input_pieces = [[inputs, x_zero], [z_one, x_one], [z_two, x_two], [z_three, x_three]]
        square = struct(width, width)
        full_query, full_key, full_value, full_gate, vector_rows = local_call(
            unpack_kernel,
            3,
            (square, square, square, square, struct(VECTOR_ROWS, width, dtype=jnp.float32)),
            places,
            (early_all, early_other),
        )
    else:
        early_rows = lax.all_gather(jnp.concatenate(early_set), BOTH)
        late_rows = lax.all_gather(jnp.concatenate(flat_rows(late_set)), BOTH)
        place = 0
        full_query, place = take(early_rows, place, query_weight)
        full_key, place = take(early_rows, place, key_weight)
        full_value, place = take(early_rows, place, value_weight)
        full_gate, place = take(early_rows, place, gate_weight)
        place = 0
        full_output, place = take(late_rows, place, output_weight)
        full_up, place = take(late_rows, place, up_weight)
        full_down, place = take(late_rows, place, down_weight)
        full_carry, place = take(late_rows, place, carry_weight)
        lines = [lax.all_gather(vector, BOTH, tiled=True).reshape(-1, width) for vector in vectors]
        lines = jnp.concatenate(lines).astype(jnp.float32)
        vector_rows = jnp.pad(lines, ((0, VECTOR_ROWS - lines.shape[0]), (0, 0)))
        input_pieces = []
        along_z = inputs
        for step_z in range(axis_z.size):
            along_x = along_z
            row = []
            for step_x in range(axis_x.size):
                row.append(along_x)
                along_x = axis_x.rotate(along_x, 1) if step_x + 1 < axis_x.size else None
            input_pieces.append(row)
            along_z = axis_z.rotate(along_z, 1) if step_z + 1 < axis_z.size else None

    carried = None
    for step, row in enumerate(input_pieces):
        carried = project(row, vector_rows, full_key, full_value, group_blocks * BLK, step, carried)
    normed_group, key_group, value_group = carried
    normed_low = normed_group[: inputs.shape[0]]

    gate_b, down_b, carry_b, gain_one, shift_one, gain_two, shift_two = [vector_rows[line] for line in range(UP_B)]
    up_b = vector_rows[UP_B : UP_B + up_weight.shape[1] // width].reshape(-1)

    own_start = lax.axis_index("seq") * block_count
    own_segments = lax.dynamic_slice_in_dim(block_segment, own_start, block_count)
    ancestor_slot, usable = ancestor_slots(block_segment, segment_parent, own_segments)
    owner = ancestor_slot // block_count
    away_z = (axis_z.position() - owner // axis_x.size) % axis_z.size
    away_x = (axis_x.position() - owner % axis_x.size) % axis_x.size
    relative_slot = (away_z * axis_x.size + away_x) * block_count + ancestor_slot % block_count
    slots = jnp.concatenate(
        [relative_slot, jnp.sum(usable, axis=-1, keepdims=True, dtype=jnp.int32)], axis=-1
    )

    values_in = inputs.astype(jnp.float32)
    query_low = (matmul(normed_low, full_query).astype(jnp.bfloat16) * (HD ** (-0.5))).astype(jnp.bfloat16)
    gate_open = jax.nn.sigmoid(matmul(normed_low, full_gate) + gate_b)

    cuts = min(4, max(1, group_blocks // 40) ** 2)
    heads = [slice(cut * width // cuts, (cut + 1) * width // cuts) for cut in range(cuts)]
    forward = [
        attend(slots, query_low[:, cols], key_group[:, cols], value_group[:, cols]) for cols in heads
    ]
    attended_low = joined([mixed for mixed, logsum in forward], 1)

    branch = matmul(attended_low, full_output)
    middle = values_in + gate_open * branch
    normed_second = normalize(middle, gain_two, shift_two).astype(jnp.bfloat16)
    up_pre = matmul(normed_second, full_up) + up_b
    up_sigmoid = jax.nn.sigmoid(up_pre)
    hidden_low = (up_pre * up_sigmoid).astype(jnp.bfloat16)
    update = matmul(hidden_low, full_down) + down_b
    carry_open = jax.nn.sigmoid(matmul(normed_second, full_carry) + carry_b)
    output = (middle + carry_open * update).astype(jnp.bfloat16)

    grad_out = cotangent.astype(jnp.float32)
    update_grad = (carry_open * grad_out).astype(jnp.bfloat16)
    carry_pre_grad = (grad_out * update * carry_open * (1.0 - carry_open)).astype(jnp.bfloat16)
    grad_down_bias = column_sums(update_grad)
    grad_carry_bias = column_sums(carry_pre_grad)
    silu_slope = up_sigmoid * (1.0 + up_pre * (1.0 - up_sigmoid))
    up_pre_grad = (against(update_grad, full_down) * silu_slope).astype(jnp.bfloat16)
    grad_up_bias = column_sums(up_pre_grad)
    second_norm_grad = against(up_pre_grad, full_up) + against(carry_pre_grad, full_carry)
    second_pull = jax.vjp(normalize, middle, gain_two, shift_two)[1]
    middle_part, grad_second_gain, grad_second_shift = second_pull(second_norm_grad)
    middle_grad = grad_out + middle_part

    branch_grad = (gate_open * middle_grad).astype(jnp.bfloat16)
    gate_pre_grad = (middle_grad * branch * gate_open * (1.0 - gate_open)).astype(jnp.bfloat16)
    grad_gate_bias = column_sums(gate_pre_grad)
    attended_grad = against(branch_grad, full_output).astype(jnp.bfloat16)
    if direct:
        first_rows = late_count + rows_each
        half = struct(devices // 2, first_rows, width)
        first_keep, first_send = local_call(
            first_grads_kernel,
            9,
            (half, half),
            places,
            (
                hidden_low,
                update_grad,
                normed_second,
                up_pre_grad,
                carry_pre_grad,
                attended_low,
                branch_grad,
                normed_low,
                gate_pre_grad,
            ),
            (
                pltpu.VMEM((up_weight.shape[1] // width, width, width), jnp.float32),
                pltpu.VMEM((up_weight.shape[1], width), jnp.float32),
                pltpu.VMEM((3, width, width), jnp.float32),
            ),
        )
        near = (2, 2, 4, first_rows, width)
        first_entry = pair_scatter(first_keep.reshape(near), first_send.reshape(near), axis_core)
        first_keep, first_send = first_entry(0), first_entry(1)
        attended_grad, first_keep, first_send = lax.optimization_barrier((attended_grad, first_keep, first_send))
        first_y = pair_scatter(first_keep, first_send, axis_y)

    backward = [
        attend_backward(
            slots,
            query_low[:, cols],
            key_group[:, cols],
            value_group[:, cols],
            logsum,
            attended_low[:, cols],
            attended_grad[:, cols],
            normed_group,
            jnp.concatenate([full_key[:, cols], full_value[:, cols]], axis=1),
        )
        for cols, (mixed, logsum) in zip(heads, forward)
    ]
    query_rows_grad = joined([parts[0] for parts in backward], 1)
    part = width // cuts
    both_grads, lanes = [
        joined([parts[index][:part] for parts in backward] + [parts[index][part:] for parts in backward], 0)
        if cuts > 1
        else backward[0][index]
        for index in (1, 2)
    ]

    shared_parts = [functools.reduce(add_low, pieces) for pieces in zip(*[parts[3:] for parts in backward])]

    def over_x(step_z):
        return ring_scatter(lambda step_x: shared_parts[step_z * axis_x.size + step_x], axis_x)

    shared_sum = jnp.transpose(ring_scatter(over_x, axis_z).astype(jnp.float32))

    zero_line = jnp.zeros((width,), jnp.float32)
    local_lines = (
        grad_gate_bias,
        grad_down_bias,
        grad_carry_bias,
        zero_line,
        zero_line,
        grad_second_gain,
        grad_second_shift,
        grad_up_bias,
    )
    block = jnp.concatenate([line.reshape(-1, width) for line in local_lines])
    block = jnp.pad(block, ((0, VECTOR_ROWS - block.shape[0]), (0, 0)))
    if direct:
        second_rows = 3 * rows_each + VECTOR_ROWS
        half = struct(devices // 2, second_rows, width)
        second_keep, second_send = local_call(
            second_grads_kernel,
            6,
            (half, half),
            places,
            (
                both_grads,
                normed_low,
                query_rows_grad,
                gate_pre_grad,
                lanes,
                full_query,
                full_key,
                full_value,
                full_gate,
                vector_rows,
                block,
            ),
            (pltpu.VMEM((3, width, width), jnp.float32),),
        )
        near = (2, 2, 4, second_rows, width)
        second_entry = pair_scatter(second_keep.reshape(near), second_send.reshape(near), axis_core)
        second_y = pair_scatter(second_entry(0), second_entry(1), axis_y)

        def far(y_entry):
            along = [y_entry(index) for index in range(2)]
            over_z = ring_scatter(lambda back: jnp.stack([along[0][back], along[1][back]]), axis_z)
            return ring_scatter(lambda back: over_z[back], axis_x)

        weight_sum = jnp.concatenate([far(first_y), far(second_y)]).astype(jnp.float32)
    else:
        grad_key = jnp.transpose(both_grads[:width])
        grad_value = jnp.transpose(both_grads[width:])
        grad_query = inner_rows(normed_low, query_rows_grad)
        grad_gate = inner_rows(normed_low, gate_pre_grad)
        both_sums = jnp.sum(lanes, axis=1)
        weights = [weight.astype(jnp.float32) for weight in (full_query, full_key, full_value, full_gate)]
        line_sums = (column_sums(query_rows_grad), both_sums[:width], both_sums[width:], grad_gate_bias)
        shift_line = sum(jnp.sum(weight * line, axis=1) for weight, line in zip(weights, line_sums))
        weighted = sum(
            jnp.sum(weight * grad, axis=1)
            for weight, grad in zip(weights, (grad_query, grad_key, grad_value, grad_gate))
        )
        block = block.at[GAIN_ONE].set((weighted - shift_one * shift_line) / gain_one).at[SHIFT_ONE].set(shift_line)
        grads = (
            (inner_rows(normed_second, up_pre_grad), up_weight),
            (inner_rows(hidden_low, update_grad), down_weight),
            (inner_rows(normed_second, carry_pre_grad), carry_weight),
            (inner_rows(attended_low, branch_grad), output_weight),
            (grad_gate, gate_weight),
            (grad_query, query_weight),
            (grad_key, key_weight),
            (grad_value, value_weight),
        )
        pack = [
            cut.astype(low).reshape(devices, piece.shape[0], width)
            for grad, piece in grads
            for cut in flat_rows((grad,))
        ]
        pack.append(jnp.broadcast_to(block.astype(low), (devices, VECTOR_ROWS, width)))
        pack = jnp.concatenate(pack, axis=1)
        pack = jnp.pad(pack, ((0, 0), (0, -pack.shape[1] % 16), (0, 0)))
        weight_sum = lax.psum_scatter(pack, BOTH, scatter_dimension=0, tiled=True)[0].astype(jnp.float32)

    def own(start, piece):
        rows = piece.shape[0]
        parts = piece.shape[1] // width
        blocks = [weight_sum[start + part * rows : start + (part + 1) * rows] for part in range(parts)]
        return joined(blocks, 1), start + parts * rows

    local_grad = against(query_rows_grad, full_query) + against(gate_pre_grad, full_gate)
    centered = values_in - jnp.mean(values_in, axis=-1, keepdims=True)
    scale = lax.rsqrt(jnp.mean(centered * centered, axis=-1, keepdims=True) + EPSILON)
    hat = centered * scale
    pull = (local_grad + shared_sum) * gain_one
    input_grad = middle_grad + scale * (
        pull - jnp.mean(pull, axis=-1, keepdims=True) - hat * jnp.mean(pull * hat, axis=-1, keepdims=True)
    )

    place = 0
    own_up, place = own(place, up_weight)
    own_down, place = own(place, down_weight)
    own_carry, place = own(place, carry_weight)
    own_output, place = own(place, output_weight)
    own_gate, place = own(place, gate_weight)
    own_query, place = own(place, query_weight)
    own_key, place = own(place, key_weight)
    own_value, place = own(place, value_weight)
    vector_out = []
    for index, vector in enumerate(vectors):
        count = vector.shape[0]
        lines = weight_sum[place + index : place + index + count * devices // width].reshape(-1)
        vector_out.append(lax.dynamic_slice_in_dim(lines, device * count, count))
    gate_bg, down_bg, carry_bg, gain_one_g, shift_one_g, gain_two_g, shift_two_g, up_bg = vector_out
    return (
        output,
        input_grad,
        own_query,
        own_key,
        own_value,
        own_output,
        own_gate,
        gate_bg,
        own_up,
        up_bg,
        own_down,
        down_bg,
        own_carry,
        carry_bg,
        gain_one_g,
        shift_one_g,
        gain_two_g,
        shift_two_g,
    )


def solution(mesh):
    rows = P(BOTH, None)
    line = P(BOTH)
    matrix_or_line = (rows,) * 5 + (line, rows, line, rows, line, rows) + (line,) * 5
    return jax.shard_map(
        shards,
        mesh=mesh,
        in_specs=(rows, rows, P("dp"), P("dp")) + matrix_or_line,
        out_specs=(rows, rows) + matrix_or_line,
        check_vma=False,
    )
```

```python
import functools

import jax
import jax.numpy as jnp
from jax import lax
from jax.experimental import pallas as pl
from jax.experimental.pallas import tpu as pltpu
from jax.sharding import PartitionSpec as P

HD = 64
BLK = 128
DEPTH = 10
PAIR = 2 * HD

EPSILON = 1e-05
NEGATIVE = -1e30
BOTH = ("dp", "seq")
VMEM_BYTES = 60 * 1024 * 1024


def normalize(values, norm_gain, norm_shift):
    center = values - jnp.mean(values, axis=-1, keepdims=True)
    spread = jnp.mean(center * center, axis=-1, keepdims=True)
    return center * lax.rsqrt(spread + EPSILON) * norm_gain + norm_shift


def matmul(left_side, right_side):
    return jnp.dot(left_side, right_side, preferred_element_type=jnp.float32)


def inner_rows(left_side, right_side):
    return lax.dot_general(
        left_side, right_side, (((0,), (0,)), ((), ())), preferred_element_type=jnp.float32
    )


def against(left_side, right_side):
    return lax.dot_general(
        left_side, right_side, (((1,), (1,)), ((), ())), preferred_element_type=jnp.float32
    )


def column_sums(values):
    return jnp.sum(values.astype(jnp.float32), axis=0)


def lookup(lookup_table, wanted):
    entries = jnp.arange(lookup_table.shape[0], dtype=jnp.int32)
    matches = wanted[..., None] == entries
    located = jnp.sum(jnp.where(matches, lookup_table, jnp.int32(0)), axis=-1, dtype=jnp.int32)
    return jnp.where(wanted >= 0, located, jnp.int32(-1))


def ancestor_slots(block_segment, segment_parent, own_segments):
    entries = jnp.arange(block_segment.shape[0], dtype=jnp.int32)
    placed = block_segment[None, :] == entries[:, None]
    slot_of = jnp.sum(jnp.where(placed, entries[None, :], jnp.int32(0)), axis=1, dtype=jnp.int32)
    current = own_segments
    lineage = []
    for depth_step in range(DEPTH):
        lineage.append(current)
        current = lookup(segment_parent, current)
    lineage = jnp.stack(lineage, axis=-1)
    usable = lineage >= 0
    return (jnp.where(usable, lookup(slot_of, lineage), jnp.int32(0)), usable)


def stack_heads(rows):
    lane = lax.broadcasted_iota(jnp.int32, rows.shape, 1)
    low = lane < HD
    zero = jnp.zeros_like(rows)
    return jnp.concatenate([jnp.where(low, rows, zero), jnp.where(low, zero, rows)], axis=0)


def unstack_heads(rows):
    half = rows.shape[0] // 2
    lane = lax.broadcasted_iota(jnp.int32, (half, rows.shape[1]), 1)
    return jnp.where(lane < HD, rows[:half], rows[half:])


def make_bias(levels, bias_ref):
    row = lax.broadcasted_iota(jnp.int32, (BLK, DEPTH * BLK), 0)
    col = lax.broadcasted_iota(jnp.int32, (BLK, DEPTH * BLK), 1)
    limit = jnp.where(col < BLK, row + 1, levels * BLK)
    bias = jnp.where(col < limit, jnp.float32(0.0), jnp.float32(NEGATIVE))
    bias_ref[:BLK, :] = bias
    bias_ref[BLK:, :] = bias


def fetch_levels(slots_ref, slot, source_ref, target_ref):
    for level in range(DEPTH):
        start = pl.multiple_of(slots_ref[slot, level] * BLK, BLK)
        target_ref[level * BLK : (level + 1) * BLK, :] = source_ref[pl.ds(start, BLK), :]


def forward_kernel(slots_ref, query_ref, key_ref, value_ref, mixed_ref, logsum_ref, key_here, value_here, bias_ref):
    width = query_ref.shape[1]

    def one_slot(slot, carry):
        rows = pl.ds(pl.multiple_of(slot * BLK, BLK), BLK)
        fetch_levels(slots_ref, slot, key_ref, key_here)
        fetch_levels(slots_ref, slot, value_ref, value_here)
        make_bias(slots_ref[slot, DEPTH], bias_ref)
        lane = lax.broadcasted_iota(jnp.int32, (BLK, PAIR), 1)
        logsums = jnp.zeros((BLK, PAIR), jnp.float32)
        for pair in range(width // PAIR):
            cols = slice(pair * PAIR, (pair + 1) * PAIR)
            stacked = stack_heads(query_ref[rows, cols])
            scores = against(stacked, key_here[:, cols]) + bias_ref[...]
            highest = jnp.max(scores, axis=-1, keepdims=True)
            raised = jnp.exp(scores - highest)
            total = jnp.sum(raised, axis=-1, keepdims=True)
            mixed = matmul(raised.astype(jnp.bfloat16), value_here[:, cols]) / total
            mixed_ref[rows, cols] = unstack_heads(mixed).astype(jnp.bfloat16)
            logsum = highest + jnp.log(total)
            logsums = jnp.where(lane == 2 * pair, logsum[:BLK], logsums)
            logsums = jnp.where(lane == 2 * pair + 1, logsum[BLK:], logsums)
        logsum_ref[rows, :] = logsums
        return carry

    lax.fori_loop(0, query_ref.shape[0] // BLK, one_slot, 0)


def backward_kernel(
    slots_ref,
    query_ref,
    key_source,
    value_source,
    logsum_ref,
    mixed_ref,
    mixed_grad_ref,
    normed_source,
    weight_ref,
    *refs,
):
    query_grad_ref, grads_ref, lanes_ref = refs[:3]
    shared_refs = refs[3:-9]
    key_ref, value_ref, normed_ref, key_here, value_here, bias_ref, key_sums, value_sums, copies = refs[-9:]
    width = query_ref.shape[1]
    fetches = [
        pltpu.make_async_copy(source, target, copies.at[index])
        for index, (source, target) in enumerate(
            ((key_source, key_ref), (value_source, value_ref), (normed_source, normed_ref))
        )
    ]
    for fetch in fetches:
        fetch.start()
    key_sums[...] = jnp.zeros_like(key_sums)
    value_sums[...] = jnp.zeros_like(value_sums)
    fetches[0].wait()
    fetches[1].wait()

    def one_slot(slot, carry):
        rows = pl.ds(pl.multiple_of(slot * BLK, BLK), BLK)
        fetch_levels(slots_ref, slot, key_ref, key_here)
        fetch_levels(slots_ref, slot, value_ref, value_here)
        make_bias(slots_ref[slot, DEPTH], bias_ref)
        for pair in range(width // PAIR):
            cols = slice(pair * PAIR, (pair + 1) * PAIR)
            stacked = stack_heads(query_ref[rows, cols])
            grad_rows = mixed_grad_ref[rows, cols]
            grad_stacked = stack_heads(grad_rows)
            products = grad_rows.astype(jnp.float32) * mixed_ref[rows, cols].astype(jnp.float32)
            row_dot = jnp.sum(stack_heads(products), axis=-1, keepdims=True)
            logsum = jnp.concatenate(
                [logsum_ref[rows, 2 * pair : 2 * pair + 1], logsum_ref[rows, 2 * pair + 1 : 2 * pair + 2]], axis=0
            )
            key_rows = key_here[:, cols]
            shares = jnp.exp(against(stacked, key_rows) + bias_ref[...] - logsum)
            share_grad = against(grad_stacked, value_here[:, cols])
            score_grad = (shares * (share_grad - row_dot)).astype(jnp.bfloat16)
            query_grad = unstack_heads(matmul(score_grad, key_rows)) * (HD ** (-0.5))
            query_grad_ref[rows, cols] = query_grad.astype(jnp.bfloat16)
            key_part = inner_rows(stacked, score_grad)
            value_part = inner_rows(grad_stacked, shares.astype(jnp.bfloat16))
            for level in range(DEPTH):
                start = pl.multiple_of(slots_ref[slot, level] * BLK, BLK)
                here = slice(level * BLK, (level + 1) * BLK)
                key_sums[cols, pl.ds(start, BLK)] += key_part[:, here]
                value_sums[cols, pl.ds(start, BLK)] += value_part[:, here]
        return carry

    lax.fori_loop(0, query_ref.shape[0] // BLK, one_slot, 0)

    fetches[2].wait()
    piece = key_sums.shape[1] // len(shared_refs)
    for index in range(len(shared_refs)):
        here = slice(index * piece, (index + 1) * piece)
        shared = None
        for part, part_sums in enumerate((key_sums, value_sums)):
            lines = slice(part * width, (part + 1) * width)
            block = part_sums[:, here]
            tiles = [block[:, start : start + BLK] for start in range(0, piece, BLK)]
            lane_sums = functools.reduce(lambda left, right: left + right, tiles)
            low = block.astype(jnp.bfloat16)
            product = matmul(weight_ref[:, lines], low)
            shared = product if shared is None else shared + product
            grad = matmul(low, normed_ref[here, :])
            if index == 0:
                grads_ref[lines, :] = grad
                lanes_ref[lines, :] = lane_sums
            else:
                grads_ref[lines, :] += grad
                lanes_ref[lines, :] += lane_sums
        shared_refs[index][...] = shared.astype(jnp.bfloat16)


def about(cost):
    return pl.CostEstimate(flops=int(cost * 1e9), bytes_accessed=int(cost * 1e6), transcendentals=0)


def in_vmem():
    return pl.BlockSpec(memory_space=pltpu.VMEM)


def in_smem():
    return pl.BlockSpec(memory_space=pltpu.SMEM)


def attend(slots, query_rows, key_group, value_group):
    rows, width = query_rows.shape
    return pl.pallas_call(
        forward_kernel,
        cost_estimate=about(18),
        out_shape=(
            jax.ShapeDtypeStruct((rows, width), jnp.bfloat16),
            jax.ShapeDtypeStruct((rows, PAIR), jnp.float32),
        ),
        in_specs=[in_smem(), in_vmem(), in_vmem(), in_vmem()],
        out_specs=(in_vmem(), in_vmem()),
        scratch_shapes=[
            pltpu.VMEM((DEPTH * BLK, width), jnp.bfloat16),
            pltpu.VMEM((DEPTH * BLK, width), jnp.bfloat16),
            pltpu.VMEM((2 * BLK, DEPTH * BLK), jnp.float32),
        ],
        compiler_params=pltpu.CompilerParams(vmem_limit_bytes=VMEM_BYTES),
    )(slots, query_rows, key_group, value_group)


def attend_backward(slots, query_rows, key_group, value_group, logsum, mixed, mixed_grad, normed_group, both_weight):
    rows, width = query_rows.shape
    keys, model_width = normed_group.shape
    pieces = keys // rows

    anywhere = pl.BlockSpec(memory_space=pl.ANY)
    return pl.pallas_call(
        backward_kernel,
        cost_estimate=about(40),
        out_shape=(
            jax.ShapeDtypeStruct((rows, width), jnp.bfloat16),
            jax.ShapeDtypeStruct((2 * width, model_width), jnp.float32),
            jax.ShapeDtypeStruct((2 * width, BLK), jnp.float32),
        )
        + (jax.ShapeDtypeStruct((model_width, rows), jnp.bfloat16),) * pieces,
        in_specs=[in_smem(), in_vmem(), anywhere, anywhere, in_vmem(), in_vmem(), in_vmem(), anywhere, in_vmem()],
        out_specs=(in_vmem(),) * (3 + pieces),
        scratch_shapes=[
            pltpu.VMEM((keys, width), jnp.bfloat16),
            pltpu.VMEM((keys, width), jnp.bfloat16),
            pltpu.VMEM((keys, model_width), jnp.bfloat16),
            pltpu.VMEM((DEPTH * BLK, width), jnp.bfloat16),
            pltpu.VMEM((DEPTH * BLK, width), jnp.bfloat16),
            pltpu.VMEM((2 * BLK, DEPTH * BLK), jnp.float32),
            pltpu.VMEM((width, keys), jnp.float32),
            pltpu.VMEM((width, keys), jnp.float32),
            pltpu.SemaphoreType.DMA((3,)),
        ],
        compiler_params=pltpu.CompilerParams(vmem_limit_bytes=VMEM_BYTES),
    )(slots, query_rows, key_group, value_group, logsum, mixed, mixed_grad, normed_group, both_weight)


def project(pieces, vectors, key_weight, value_weight, group_rows, step, carried, query_weight=None):
    count = len(pieces)
    rows, width = pieces[0].shape
    weights = [key_weight, value_weight] + ([] if query_weight is None else [query_weight])
    extra = [] if carried is None else list(carried)

    def body(*refs):
        piece_refs, vectors_ref = refs[:count], refs[count]
        weight_refs = refs[count + 1 : count + 1 + len(weights)]
        outs = refs[count + 1 + len(weights) + len(extra) :]
        normed_ref, key_ref, value_ref = outs[:3]
        gain = vectors_ref[GAIN_ONE : GAIN_ONE + 1, :]
        shift = vectors_ref[SHIFT_ONE : SHIFT_ONE + 1, :]
        for index, piece in enumerate(piece_refs):
            here = slice(index * rows, (index + 1) * rows)
            normed = normalize(piece[...].astype(jnp.float32), gain, shift).astype(jnp.bfloat16)
            normed_ref[here, :] = normed
            key_ref[here, :] = matmul(normed, weight_refs[0][...]).astype(jnp.bfloat16)
            value_ref[here, :] = matmul(normed, weight_refs[1][...]).astype(jnp.bfloat16)
            if index == 0 and len(outs) > 3:
                outs[3][...] = normed
                queries = matmul(normed, weight_refs[2][...]).astype(jnp.bfloat16)
                outs[4][...] = (queries.astype(jnp.float32) * (HD ** (-0.5))).astype(jnp.bfloat16)

    block = pl.BlockSpec((count * rows, width), lambda index: (step, 0))
    whole = jax.ShapeDtypeStruct((group_rows, width), jnp.bfloat16)
    own = [] if query_weight is None else [jax.ShapeDtypeStruct((rows, width), jnp.bfloat16)] * 2
    first = count + 1 + len(weights)
    return pl.pallas_call(
        body,
        cost_estimate=about(4),
        grid=(1,),
        out_shape=[whole] * 3 + own,
        in_specs=[in_vmem()] * first + [pl.BlockSpec(memory_space=pl.ANY)] * len(extra),
        out_specs=[block] * 3 + [in_vmem()] * len(own),
        input_output_aliases={first + index: index for index in range(len(extra))},
        compiler_params=pltpu.CompilerParams(vmem_limit_bytes=VMEM_BYTES),
    )(*pieces, vectors, *weights, *extra)


class Axis:
    def __init__(self, name, size, stride):
        self.name = name
        self.size = size
        self.stride = stride

    def position(self):
        return lax.axis_index(self.name) // self.stride % self.size

    def rotate(self, values, shift):
        pairs = []
        for index in range(lax.axis_size(self.name)):
            here = index // self.stride % self.size
            there = (here + shift) % self.size
            pairs.append((index, index + (there - here) * self.stride))
        return lax.ppermute(values, self.name, pairs)


def axes():
    seq = lax.axis_size("seq")
    dp = lax.axis_size("dp")
    along_z = 4 if seq % 4 == 0 else 1
    cores = 2 if dp % 2 == 0 else 1
    return (
        Axis("seq", along_z, seq // along_z),
        Axis("seq", seq // along_z, 1),
        Axis("dp", dp // cores, cores),
        Axis("dp", cores, 1),
    )


def relative_devices():
    axis_z, axis_x, axis_y, axis_core = axes()

    def place(axis, dim):
        back = lax.broadcasted_iota(jnp.int32, (axis_core.size, axis_y.size, axis_x.size, axis_z.size), dim)
        return (axis.position() - back + axis.size) % axis.size

    dp_index = place(axis_y, 1) * axis_core.size + place(axis_core, 0)
    seq_index = place(axis_z, 3) * axis_x.size + place(axis_x, 2)
    return (dp_index * lax.axis_size("seq") + seq_index).reshape(-1)


def scatter_devices():
    axis_z, axis_x, axis_y, axis_core = axes()
    entries = relative_devices().reshape(-1, axis_x.size, axis_z.size)
    return jnp.swapaxes(entries, 1, 2).reshape(-1)


def add_low(left_side, right_side):
    return (left_side.astype(jnp.float32) + right_side.astype(jnp.float32)).astype(jnp.bfloat16)


def add_three(first, second, third):
    total = first.astype(jnp.float32) + second.astype(jnp.float32) + third.astype(jnp.float32)
    return total.astype(jnp.bfloat16)


def tied(values, after):
    return lax.optimization_barrier((values, after))[0]


def ring_scatter(entry, axis):
    running = entry(axis.size - 1)
    for back in range(axis.size - 1, 0, -1):
        running = add_low(axis.rotate(running, -1), entry(back - 1))
    return running


def pair_scatter(keep, send, axis):
    arrived = axis.rotate(send, -1)
    return lambda index: add_low(arrived[index], keep[index])


GATE_B, DOWN_B, CARRY_B, GAIN_ONE, SHIFT_ONE, GAIN_TWO, SHIFT_TWO, UP_B = range(8)
VECTOR_ROWS = 16


def pack_kernel(devices, place_ref, *refs):
    early_sources, late_sources, vector_refs, (early_ref, late_ref) = refs[:4], refs[4:8], refs[8:16], refs[16:]
    width = early_ref.shape[1]
    for target, sources in ((early_ref, early_sources), (late_ref, late_sources)):
        start = 0
        for source in sources:
            rows = source.shape[0]
            for column in range(0, source.shape[1], width):
                target[start : start + rows, :] = source[:, column : column + width]
                start += rows
    block = jnp.zeros((VECTOR_ROWS, width), jnp.float32)
    line = lax.broadcasted_iota(jnp.int32, block.shape, 0)
    for index, source in enumerate(vector_refs):
        count = source.shape[1]
        feature = lax.broadcasted_iota(jnp.int32, (count, width), 0) + place_ref[0] * count
        column = lax.broadcasted_iota(jnp.int32, (count, width), 1)
        for part in range(count * devices // width):
            spot = jnp.where(feature == column + part * width, jnp.float32(1.0), jnp.float32(0.0))
            spread = matmul(source[...], spot.astype(jnp.bfloat16))
            block += jnp.where(line == index + part, spread, jnp.float32(0.0))
    early_ref[early_ref.shape[0] - VECTOR_ROWS :, :] = block.astype(jnp.bfloat16)


def unpack_kernel(place_ref, mine_ref, other_ref, query_ref, key_ref, value_ref, gate_ref, vectors_ref):
    half = mine_ref.shape[0]
    rows = (mine_ref.shape[1] - VECTOR_ROWS) // 4
    vectors = jnp.zeros(vectors_ref.shape, jnp.float32)
    for index in range(2 * half):
        source = (mine_ref if index < half else other_ref).at[index % half]
        target = pl.ds(pl.multiple_of(place_ref[index] * rows, rows), rows)
        for part, weight_ref in enumerate((query_ref, key_ref, value_ref, gate_ref)):
            weight_ref[target, :] = source[part * rows : (part + 1) * rows, :]
        vectors += source[4 * rows :, :].astype(jnp.float32)
    vectors_ref[...] = vectors


def unpack_late_kernel(
    place_ref, line_ref, line_other_ref, plane_ref, plane_other_ref, output_ref, up_ref, down_ref, carry_ref
):
    half = line_ref.shape[0]
    width = output_ref.shape[1]
    rows = output_ref.shape[0] // (2 * half)
    down_rows = down_ref.shape[0] // (2 * half)
    for index in range(2 * half):
        source = (line_ref if index < half else line_other_ref).at[index % half]
        target = pl.ds(pl.multiple_of(place_ref[0, index] * rows, rows), rows)
        output_ref[target, :] = source[:rows, :]
        for part in range(up_ref.shape[1] // width):
            up_ref[target, part * width : (part + 1) * width] = source[(part + 1) * rows : (part + 2) * rows, :]
        source = (plane_ref if index < half else plane_other_ref).at[index % half]
        target = pl.ds(pl.multiple_of(place_ref[1, index] * down_rows, down_rows), down_rows)
        down_ref[target, :] = source[:down_rows, :]
        target = pl.ds(pl.multiple_of(place_ref[1, index] * rows, rows), rows)
        carry_ref[target, :] = source[down_rows:, :]


def spread_rows(place_ref, grad_ref, keep_ref, send_ref, start, rows):
    half = keep_ref.shape[0]
    for index in range(2 * half):
        source = pl.ds(pl.multiple_of(place_ref[index] * rows, rows), rows)
        target = (keep_ref if index < half else send_ref).at[index % half]
        target[start : start + rows, :] = grad_ref[source, :].astype(jnp.bfloat16)


def first_grads_kernel(
    place_ref,
    hidden_ref,
    update_grad_ref,
    normed_second_ref,
    up_pre_ref,
    carry_pre_ref,
    attended_ref,
    branch_grad_ref,
    normed_ref,
    gate_pre_ref,
    keep_ref,
    send_ref,
    up_grad,
    down_grad,
    square_grads,
):
    width = keep_ref.shape[2]
    rows = width // (2 * keep_ref.shape[0])
    start = 0
    for part in range(up_pre_ref.shape[1] // width):
        grad = up_grad.at[part]
        grad[...] = inner_rows(normed_second_ref[...], up_pre_ref[:, part * width : (part + 1) * width])
        spread_rows(place_ref, grad, keep_ref, send_ref, start, rows)
        start += rows
    for part in range(hidden_ref.shape[1] // width):
        here = slice(part * width, (part + 1) * width)
        down_grad[here, :] = inner_rows(hidden_ref[:, here], update_grad_ref[...])
    down_rows = hidden_ref.shape[1] // (2 * keep_ref.shape[0])
    spread_rows(place_ref, down_grad, keep_ref, send_ref, start, down_rows)
    start += down_rows
    pairs = ((normed_second_ref, carry_pre_ref), (attended_ref, branch_grad_ref), (normed_ref, gate_pre_ref))
    for index, (left_ref, right_ref) in enumerate(pairs):
        grad = square_grads.at[index]
        grad[...] = inner_rows(left_ref[...], right_ref[...])
        spread_rows(place_ref, grad, keep_ref, send_ref, start, rows)
        start += rows


def second_grads_kernel(
    place_ref,
    both_grads_ref,
    normed_ref,
    query_grad_ref,
    gate_pre_ref,
    lanes_ref,
    query_weight_ref,
    key_weight_ref,
    value_weight_ref,
    gate_weight_ref,
    vectors_ref,
    block_ref,
    keep_ref,
    send_ref,
    grads,
):
    width = keep_ref.shape[2]
    rows = width // (2 * keep_ref.shape[0])
    grads[0] = inner_rows(normed_ref[...], query_grad_ref[...])
    grads[1] = jnp.transpose(both_grads_ref[:width, :])
    grads[2] = jnp.transpose(both_grads_ref[width:, :])
    for index in range(3):
        spread_rows(place_ref, grads.at[index], keep_ref, send_ref, index * rows, rows)
    gate_grad = inner_rows(normed_ref[...], gate_pre_ref[...])

    def line_sums(ref):
        return jnp.sum(ref[...].astype(jnp.float32), axis=0, keepdims=True)

    def as_line(column):
        return jnp.transpose(jnp.broadcast_to(column, (width, BLK)))[:1, :]

    lines = (
        line_sums(query_grad_ref),
        jnp.sum(jnp.transpose(lanes_ref[:width, :]), axis=0, keepdims=True),
        jnp.sum(jnp.transpose(lanes_ref[width:, :]), axis=0, keepdims=True),
        line_sums(gate_pre_ref),
    )
    weighted = jnp.zeros((width, width), jnp.float32)
    shifted = jnp.zeros((width, width), jnp.float32)
    weight_refs = (query_weight_ref, key_weight_ref, value_weight_ref, gate_weight_ref)
    for weight_ref, line, grad in zip(weight_refs, lines, (grads[0], grads[1], grads[2], gate_grad)):
        weight = weight_ref[...].astype(jnp.float32)
        weighted += weight * grad
        shifted += weight * line
    shift_line = as_line(jnp.sum(shifted, axis=1, keepdims=True))
    gain_line = (
        as_line(jnp.sum(weighted, axis=1, keepdims=True)) - vectors_ref[SHIFT_ONE : SHIFT_ONE + 1, :] * shift_line
    ) / vectors_ref[GAIN_ONE : GAIN_ONE + 1, :]
    place = lax.broadcasted_iota(jnp.int32, block_ref.shape, 0)
    block = jnp.where(place == GAIN_ONE, gain_line, block_ref[...])
    block = jnp.where(place == SHIFT_ONE, shift_line, block).astype(jnp.bfloat16)
    for index in range(keep_ref.shape[0]):
        keep_ref[index, 3 * rows :, :] = block
        send_ref[index, 3 * rows :, :] = block


def input_grad_kernel(input_ref, local_ref, middle_grad_ref, vectors_ref, *refs):
    shared_refs, output_ref = refs[:-1], refs[-1]
    shared = sum(ref[...].astype(jnp.float32) for ref in shared_refs)
    values = input_ref[...].astype(jnp.float32)
    centered = values - jnp.mean(values, axis=-1, keepdims=True)
    scale = lax.rsqrt(jnp.mean(centered * centered, axis=-1, keepdims=True) + EPSILON)
    hat = centered * scale
    pull = (local_ref[...] + jnp.transpose(shared)) * vectors_ref[GAIN_ONE : GAIN_ONE + 1, :]
    output_ref[...] = middle_grad_ref[...] + scale * (
        pull - jnp.mean(pull, axis=-1, keepdims=True) - hat * jnp.mean(pull * hat, axis=-1, keepdims=True)
    )


def local_call(kernel, cost, outs, smem, args, scratch=()):
    return pl.pallas_call(
        kernel,
        cost_estimate=about(cost),
        out_shape=outs,
        in_specs=[in_smem()] + [in_vmem()] * len(args),
        out_specs=jax.tree.map(lambda out: in_vmem(), outs),
        scratch_shapes=list(scratch),
        compiler_params=pltpu.CompilerParams(vmem_limit_bytes=VMEM_BYTES),
    )(smem, *args)


def joined(pieces, axis):
    return pieces[0] if len(pieces) == 1 else jnp.concatenate(pieces, axis=axis)


def shards(
    inputs,
    cotangent,
    block_segment,
    segment_parent,
    query_weight,
    key_weight,
    value_weight,
    output_weight,
    gate_weight,
    gate_bias,
    up_weight,
    up_bias,
    down_weight,
    down_bias,
    carry_weight,
    carry_bias,
    first_gain,
    first_shift,
    second_gain,
    second_shift,
):
    width = inputs.shape[1]
    devices = lax.axis_size(BOTH)
    block_count = inputs.shape[0] // BLK
    group_blocks = block_segment.shape[0]

    axis_z, axis_x, axis_y, axis_core = axes()
    rows_each = query_weight.shape[0]
    sizes = (axis_z.size, axis_x.size, axis_y.size, axis_core.size)
    direct = sizes == (4, 2, 2, 2) and rows_each % 16 == 0
    places = relative_devices()
    targets = scatter_devices()
    device = lax.axis_index(BOTH)
    vectors = (gate_bias, down_bias, carry_bias, first_gain, first_shift, second_gain, second_shift, up_bias)
    early_set = (query_weight, key_weight, value_weight, gate_weight)
    late_set = (output_weight, up_weight, down_weight, carry_weight)
    low = jnp.bfloat16

    def struct(*shape, dtype=low):
        return jax.ShapeDtypeStruct(shape, dtype)

    def take(source, start, piece):
        rows = piece.shape[0]
        parts = piece.shape[1] // width
        blocks = [
            source[:, start + part * rows : start + (part + 1) * rows].reshape(devices * rows, width)
            for part in range(parts)
        ]
        return joined(blocks, 1), start + parts * rows

    def flat_rows(pieces):
        return [piece[:, start : start + width] for piece in pieces for start in range(0, piece.shape[1], width)]

    if direct:
        early_count = 4 * rows_each + VECTOR_ROWS
        late_count = sum(piece.shape[0] * piece.shape[1] // width for piece in late_set)
        early, late = local_call(
            functools.partial(pack_kernel, devices),
            2,
            (struct(early_count, width), struct(late_count, width)),
            device.reshape(1),
            early_set + late_set + tuple(vector.reshape(1, -1) for vector in vectors),
        )
        late_line = [late]
        z_one = axis_z.rotate(inputs, 1)
        x_zero = axis_x.rotate(inputs, 1)
        early_line = [axis_z.rotate(early, back) for back in range(1, 4)]
        late_line.append(axis_z.rotate(late, 1))
        early_line, z_one, x_zero, late_line[1] = lax.optimization_barrier((early_line, z_one, x_zero, late_line[1]))
        z_two = axis_z.rotate(z_one, 1)
        x_one = axis_x.rotate(z_one, 1)
        early_line = jnp.stack([early] + list(early_line))
        early_other = axis_x.rotate(early_line, 1)
        late_line.append(axis_z.rotate(late_line[1], 1))
        early_other, z_two, x_one, late_line[2] = lax.optimization_barrier((early_other, z_two, x_one, late_line[2]))
        z_three = axis_z.rotate(z_two, 1)
        x_two = axis_x.rotate(z_two, 1)
        early_plane = jnp.stack([early_line, early_other])
        early_other = axis_y.rotate(early_plane, 1)
        late_line.append(axis_z.rotate(late_line[2], 1))
        early_other, z_three, x_two, late_line[3] = lax.optimization_barrier(
            (early_other, z_three, x_two, late_line[3])
        )
        x_three = axis_x.rotate(z_three, 1)
        early_all = jnp.stack([early_plane, early_other]).reshape(devices // 2, early_count, width)
        early_other = axis_core.rotate(early_all, 1)
        late_half = late_count // 2
        late_x = jnp.stack([rows[:late_half] for rows in late_line])
        late_y = jnp.stack([rows[late_half:] for rows in late_line])
        late_x_other = axis_x.rotate(late_x, 1)
        late_y_other = axis_y.rotate(late_y, 1)
        input_pieces = [[inputs, x_zero], [z_one, x_one], [z_two, x_two], [z_three, x_three]]
        square = struct(width, width)
        full_query, full_key, full_value, full_gate, vector_rows = local_call(
            unpack_kernel,
            3,
            (square, square, square, square, struct(VECTOR_ROWS, width, dtype=jnp.float32)),
            places,
            (early_all, early_other),
        )
    else:
        early_rows = lax.all_gather(jnp.concatenate(early_set), BOTH)
        late_rows = lax.all_gather(jnp.concatenate(flat_rows(late_set)), BOTH)
        place = 0
        full_query, place = take(early_rows, place, query_weight)
        full_key, place = take(early_rows, place, key_weight)
        full_value, place = take(early_rows, place, value_weight)
        full_gate, place = take(early_rows, place, gate_weight)
        place = 0
        full_output, place = take(late_rows, place, output_weight)
        full_up, place = take(late_rows, place, up_weight)
        full_down, place = take(late_rows, place, down_weight)
        full_carry, place = take(late_rows, place, carry_weight)
        lines = [lax.all_gather(vector, BOTH, tiled=True).reshape(-1, width) for vector in vectors]
        lines = jnp.concatenate(lines).astype(jnp.float32)
        vector_rows = jnp.pad(lines, ((0, VECTOR_ROWS - lines.shape[0]), (0, 0)))
        input_pieces = []
        along_z = inputs
        for step_z in range(axis_z.size):
            along_x = along_z
            row = []
            for step_x in range(axis_x.size):
                row.append(along_x)
                along_x = axis_x.rotate(along_x, 1) if step_x + 1 < axis_x.size else None
            input_pieces.append(row)
            along_z = axis_z.rotate(along_z, 1) if step_z + 1 < axis_z.size else None

    carried = None
    for step, row in enumerate(input_pieces):
        if direct and step == 3:
            x_three, late_x_other, late_y_other, carried = lax.optimization_barrier(
                (row[1], late_x_other, late_y_other, carried)
            )
            row = [row[0], x_three]
            late_x = jnp.stack([late_x, late_x_other])
            late_y = jnp.stack([late_y, late_y_other])
            late_x_other = axis_y.rotate(late_x, 1)
            late_y_other = axis_x.rotate(late_y, 1)
        asked = full_query if step == 0 else None
        done = project(row, vector_rows, full_key, full_value, group_blocks * BLK, step, carried, asked)
        carried = done[:3]
        if step == 0:
            normed_low, query_low = done[3:]
    normed_group, key_group, value_group = carried

    gate_b, down_b, carry_b, gain_one, shift_one, gain_two, shift_two = [vector_rows[line] for line in range(UP_B)]
    up_b = vector_rows[UP_B : UP_B + up_weight.shape[1] // width].reshape(-1)

    own_start = lax.axis_index("seq") * block_count
    own_segments = lax.dynamic_slice_in_dim(block_segment, own_start, block_count)
    ancestor_slot, usable = ancestor_slots(block_segment, segment_parent, own_segments)
    owner = ancestor_slot // block_count
    away_z = (axis_z.position() - owner // axis_x.size) % axis_z.size
    away_x = (axis_x.position() - owner % axis_x.size) % axis_x.size
    relative_slot = (away_z * axis_x.size + away_x) * block_count + ancestor_slot % block_count
    slots = jnp.concatenate(
        [relative_slot, jnp.sum(usable, axis=-1, keepdims=True, dtype=jnp.int32)], axis=-1
    )

    values_in = inputs.astype(jnp.float32)
    gate_open = jax.nn.sigmoid(matmul(normed_low, full_gate) + gate_b)

    cuts = min(4, max(1, group_blocks // 40) ** 2)
    heads = [slice(cut * width // cuts, (cut + 1) * width // cuts) for cut in range(cuts)]
    forward = [
        attend(slots, query_low[:, cols], key_group[:, cols], value_group[:, cols]) for cols in heads
    ]
    attended_low = joined([mixed for mixed, logsum in forward], 1)

    if direct:
        attended_low, late_x_other, late_y_other = lax.optimization_barrier((attended_low, late_x_other, late_y_other))
        late_x = jnp.stack([late_x, late_x_other]).reshape(devices // 2, late_half, width)
        late_y = jnp.stack([late_y, late_y_other]).reshape(devices // 2, late_half, width)
        late_x_other = axis_core.rotate(late_x, 1)
        late_y_other = axis_core.rotate(late_y, 1)
        other_places = jnp.transpose(places.reshape(2, 2, 2, 4), (0, 2, 1, 3)).reshape(-1)
        full_output, full_up, full_down, full_carry = local_call(
            unpack_late_kernel,
            5,
            (struct(width, width), struct(width, up_weight.shape[1]), struct(up_weight.shape[1], width), struct(width, width)),
            jnp.stack([places, other_places]),
            (late_x, late_x_other, late_y, late_y_other),
        )
    branch = matmul(attended_low, full_output)
    middle = values_in + gate_open * branch
    normed_second = normalize(middle, gain_two, shift_two).astype(jnp.bfloat16)
    up_pre = matmul(normed_second, full_up) + up_b
    up_sigmoid = jax.nn.sigmoid(up_pre)
    hidden_low = (up_pre * up_sigmoid).astype(jnp.bfloat16)
    update = matmul(hidden_low, full_down) + down_b
    carry_open = jax.nn.sigmoid(matmul(normed_second, full_carry) + carry_b)
    output = (middle + carry_open * update).astype(jnp.bfloat16)

    grad_out = cotangent.astype(jnp.float32)
    update_grad = (carry_open * grad_out).astype(jnp.bfloat16)
    carry_pre_grad = (grad_out * update * carry_open * (1.0 - carry_open)).astype(jnp.bfloat16)
    grad_down_bias = column_sums(update_grad)
    grad_carry_bias = column_sums(carry_pre_grad)
    silu_slope = up_sigmoid * (1.0 + up_pre * (1.0 - up_sigmoid))
    up_pre_grad = (against(update_grad, full_down) * silu_slope).astype(jnp.bfloat16)
    grad_up_bias = column_sums(up_pre_grad)
    second_norm_grad = against(up_pre_grad, full_up) + against(carry_pre_grad, full_carry)
    second_pull = jax.vjp(normalize, middle, gain_two, shift_two)[1]
    middle_part, grad_second_gain, grad_second_shift = second_pull(second_norm_grad)
    middle_grad = grad_out + middle_part

    branch_grad = (gate_open * middle_grad).astype(jnp.bfloat16)
    gate_pre_grad = (middle_grad * branch * gate_open * (1.0 - gate_open)).astype(jnp.bfloat16)
    grad_gate_bias = column_sums(gate_pre_grad)
    attended_grad = against(branch_grad, full_output).astype(jnp.bfloat16)
    if direct:
        first_rows = late_count + rows_each
        half = struct(devices // 2, first_rows, width)
        first_keep, first_send = local_call(
            first_grads_kernel,
            9,
            (half, half),
            targets,
            (
                hidden_low,
                update_grad,
                normed_second,
                up_pre_grad,
                carry_pre_grad,
                attended_low,
                branch_grad,
                normed_low,
                gate_pre_grad,
            ),
            (
                pltpu.VMEM((up_weight.shape[1] // width, width, width), jnp.float32),
                pltpu.VMEM((up_weight.shape[1], width), jnp.float32),
                pltpu.VMEM((3, width, width), jnp.float32),
            ),
        )
        near = (2, 4, 2, first_rows, width)
        first_entry = pair_scatter(first_keep.reshape(near), first_send.reshape(near), axis_core)
        first_keep, first_send = first_entry(0), first_entry(1)
        attended_grad, first_keep, first_send = lax.optimization_barrier((attended_grad, first_keep, first_send))
        first_arrived = axis_y.rotate(first_send, -1)

    backward = [
        attend_backward(
            slots,
            query_low[:, cols],
            key_group[:, cols],
            value_group[:, cols],
            logsum,
            attended_low[:, cols],
            attended_grad[:, cols],
            normed_group,
            jnp.concatenate([full_key[:, cols], full_value[:, cols]], axis=1),
        )
        for cols, (mixed, logsum) in zip(heads, forward)
    ]
    if direct:
        backward, first_arrived = lax.optimization_barrier((backward, first_arrived))
    query_rows_grad = joined([parts[0] for parts in backward], 1)
    part = width // cuts
    both_grads, lanes = [
        joined([parts[index][:part] for parts in backward] + [parts[index][part:] for parts in backward], 0)
        if cuts > 1
        else backward[0][index]
        for index in (1, 2)
    ]

    shared_parts = [functools.reduce(add_low, pieces) for pieces in zip(*[parts[3:] for parts in backward])]

    zero_line = jnp.zeros((width,), jnp.float32)
    local_lines = (
        grad_gate_bias,
        grad_down_bias,
        grad_carry_bias,
        zero_line,
        zero_line,
        grad_second_gain,
        grad_second_shift,
        grad_up_bias,
    )
    block = jnp.concatenate([line.reshape(-1, width) for line in local_lines])
    block = jnp.pad(block, ((0, VECTOR_ROWS - block.shape[0]), (0, 0)))
    if direct:
        second_rows = 3 * rows_each + VECTOR_ROWS
        half = struct(devices // 2, second_rows, width)
        second_keep, second_send = local_call(
            second_grads_kernel,
            6,
            (half, half),
            targets,
            (
                both_grads,
                normed_low,
                query_rows_grad,
                gate_pre_grad,
                lanes,
                full_query,
                full_key,
                full_value,
                full_gate,
                vector_rows,
                block,
            ),
            (pltpu.VMEM((3, width, width), jnp.float32),),
        )
        near = (2, 4, 2, second_rows, width)
        second_entry = pair_scatter(second_keep.reshape(near), second_send.reshape(near), axis_core)
        barrier = lax.optimization_barrier

        def first_y(back):
            return add_low(first_arrived[back], first_keep[back])

        first_z = axis_z.rotate(first_y(3), -1)
        first_z = axis_z.rotate(add_low(first_z, first_y(2)), -1)
        x_three = axis_x.rotate(shared_parts[7], -1)
        second_keep, second_send = second_entry(0), second_entry(1)
        x_three, first_z, second_keep, second_send = barrier((x_three, first_z, second_keep, second_send))

        second_arrived = axis_y.rotate(second_send, -1)
        x_two = axis_x.rotate(tied(shared_parts[5], x_three), -1)
        z_three = axis_z.rotate(add_low(x_three, shared_parts[6]), -1)
        first_z = axis_z.rotate(add_low(first_z, first_y(1)), -1)
        x_two, z_three, first_z, second_arrived = barrier((x_two, z_three, first_z, second_arrived))

        second_y = add_low(second_arrived, second_keep)
        second_x = axis_x.rotate(second_y[:, 1], -1)
        x_one = axis_x.rotate(tied(shared_parts[3], x_two), -1)
        z_two = axis_z.rotate(add_three(x_two, shared_parts[4], z_three), -1)
        x_one, z_two, second_x = barrier((x_one, z_two, second_x))

        first_half = add_low(first_z, first_y(0))
        first_x = axis_x.rotate(tied(first_half[1], x_one), -1)
        second_half = add_low(second_x, second_y[:, 0])
        second_z = [axis_z.rotate(second_half[back], -back) for back in range(1, 4)]
        x_zero = axis_x.rotate(tied(shared_parts[1], x_one), -1)
        z_one = axis_z.rotate(add_three(x_one, shared_parts[2], z_two), -1)
        shared = (x_zero, z_one, shared_parts[0])
        first_sum = first_x.astype(jnp.float32) + first_half[0].astype(jnp.float32)
        second_sum = sum(piece.astype(jnp.float32) for piece in [second_half[0]] + second_z)
        weight_sum = jnp.concatenate([first_sum, second_sum])
    else:
        grad_key = jnp.transpose(both_grads[:width])
        grad_value = jnp.transpose(both_grads[width:])
        grad_query = inner_rows(normed_low, query_rows_grad)
        grad_gate = inner_rows(normed_low, gate_pre_grad)
        both_sums = jnp.sum(lanes, axis=1)
        weights = [weight.astype(jnp.float32) for weight in (full_query, full_key, full_value, full_gate)]
        line_sums = (column_sums(query_rows_grad), both_sums[:width], both_sums[width:], grad_gate_bias)
        shift_line = sum(jnp.sum(weight * line, axis=1) for weight, line in zip(weights, line_sums))
        weighted = sum(
            jnp.sum(weight * grad, axis=1)
            for weight, grad in zip(weights, (grad_query, grad_key, grad_value, grad_gate))
        )
        block = block.at[GAIN_ONE].set((weighted - shift_one * shift_line) / gain_one).at[SHIFT_ONE].set(shift_line)
        grads = (
            (inner_rows(normed_second, up_pre_grad), up_weight),
            (inner_rows(hidden_low, update_grad), down_weight),
            (inner_rows(normed_second, carry_pre_grad), carry_weight),
            (inner_rows(attended_low, branch_grad), output_weight),
            (grad_gate, gate_weight),
            (grad_query, query_weight),
            (grad_key, key_weight),
            (grad_value, value_weight),
        )
        pack = [
            cut.astype(low).reshape(devices, piece.shape[0], width)
            for grad, piece in grads
            for cut in flat_rows((grad,))
        ]
        pack.append(jnp.broadcast_to(block.astype(low), (devices, VECTOR_ROWS, width)))
        pack = jnp.concatenate(pack, axis=1)
        pack = jnp.pad(pack, ((0, 0), (0, -pack.shape[1] % 16), (0, 0)))
        weight_sum = lax.psum_scatter(pack, BOTH, scatter_dimension=0, tiled=True)[0].astype(jnp.float32)

        def over_x(step_z):
            return ring_scatter(lambda step_x: shared_parts[step_z * axis_x.size + step_x], axis_x)

        shared = (ring_scatter(over_x, axis_z),)

    def own(start, piece):
        rows = piece.shape[0]
        parts = piece.shape[1] // width
        blocks = [weight_sum[start + part * rows : start + (part + 1) * rows] for part in range(parts)]
        return joined(blocks, 1), start + parts * rows

    local_grad = against(query_rows_grad, full_query) + against(gate_pre_grad, full_gate)
    rows = inputs.shape[0]
    input_grad = pl.pallas_call(
        input_grad_kernel,
        cost_estimate=about(3),
        out_shape=struct(rows, width, dtype=jnp.float32),
        compiler_params=pltpu.CompilerParams(vmem_limit_bytes=VMEM_BYTES),
    )(inputs, local_grad, middle_grad, vector_rows, *shared)

    place = 0
    own_up, place = own(place, up_weight)
    own_down, place = own(place, down_weight)
    own_carry, place = own(place, carry_weight)
    own_output, place = own(place, output_weight)
    own_gate, place = own(place, gate_weight)
    own_query, place = own(place, query_weight)
    own_key, place = own(place, key_weight)
    own_value, place = own(place, value_weight)
    vector_out = []
    for index, vector in enumerate(vectors):
        count = vector.shape[0]
        lines = weight_sum[place + index : place + index + count * devices // width].reshape(-1)
        vector_out.append(lax.dynamic_slice_in_dim(lines, device * count, count))
    gate_bg, down_bg, carry_bg, gain_one_g, shift_one_g, gain_two_g, shift_two_g, up_bg = vector_out
    return (
        output,
        input_grad,
        own_query,
        own_key,
        own_value,
        own_output,
        own_gate,
        gate_bg,
        own_up,
        up_bg,
        own_down,
        down_bg,
        own_carry,
        carry_bg,
        gain_one_g,
        shift_one_g,
        gain_two_g,
        shift_two_g,
    )


def solution(mesh):
    rows = P(BOTH, None)
    line = P(BOTH)
    matrix_or_line = (rows,) * 5 + (line, rows, line, rows, line, rows) + (line,) * 5
    return jax.shard_map(
        shards,
        mesh=mesh,
        in_specs=(rows, rows, P("dp"), P("dp")) + matrix_or_line,
        out_specs=(rows, rows) + matrix_or_line,
        check_vma=False,
    )
```

```python
import functools

import jax
import jax.numpy as jnp
from jax import lax
from jax.experimental import pallas as pl
from jax.experimental.pallas import tpu as pltpu
from jax.sharding import PartitionSpec as P

HD = 64
BLK = 128
DEPTH = 10
PAIR = 2 * HD
PLACES = 4
TREE_BLOCKS = 20
TRUNK = 8

EPSILON = 1e-05
NEGATIVE = -1e30
BOTH = ("dp", "seq")
VMEM_BYTES = 60 * 1024 * 1024


def normalize(values, norm_gain, norm_shift):
    center = values - jnp.mean(values, axis=-1, keepdims=True)
    spread = jnp.mean(center * center, axis=-1, keepdims=True)
    return center * lax.rsqrt(spread + EPSILON) * norm_gain + norm_shift


def matmul(left_side, right_side):
    return jnp.dot(left_side, right_side, preferred_element_type=jnp.float32)


def inner_rows(left_side, right_side):
    return lax.dot_general(
        left_side, right_side, (((0,), (0,)), ((), ())), preferred_element_type=jnp.float32
    )


def against(left_side, right_side):
    return lax.dot_general(
        left_side, right_side, (((1,), (1,)), ((), ())), preferred_element_type=jnp.float32
    )


def column_sums(values):
    return jnp.sum(values.astype(jnp.float32), axis=0)


def lookup(lookup_table, wanted):
    entries = jnp.arange(lookup_table.shape[0], dtype=jnp.int32)
    matches = wanted[..., None] == entries
    located = jnp.sum(jnp.where(matches, lookup_table, jnp.int32(0)), axis=-1, dtype=jnp.int32)
    return jnp.where(wanted >= 0, located, jnp.int32(-1))


def ancestor_slots(block_segment, segment_parent, own_segments):
    entries = jnp.arange(block_segment.shape[0], dtype=jnp.int32)
    placed = block_segment[None, :] == entries[:, None]
    slot_of = jnp.sum(jnp.where(placed, entries[None, :], jnp.int32(0)), axis=1, dtype=jnp.int32)
    current = own_segments
    lineage = []
    for depth_step in range(DEPTH):
        lineage.append(current)
        current = lookup(segment_parent, current)
    lineage = jnp.stack(lineage, axis=-1)
    usable = lineage >= 0
    return (jnp.where(usable, lookup(slot_of, lineage), jnp.int32(0)), usable)


def stack_heads(rows):
    lane = lax.broadcasted_iota(jnp.int32, rows.shape, 1)
    low = lane < HD
    zero = jnp.zeros_like(rows)
    return jnp.concatenate([jnp.where(low, rows, zero), jnp.where(low, zero, rows)], axis=0)


def unstack_heads(rows):
    half = rows.shape[0] // 2
    lane = lax.broadcasted_iota(jnp.int32, (half, rows.shape[1]), 1)
    return jnp.where(lane < HD, rows[:half], rows[half:])


def make_bias(levels, bias_ref):
    row = lax.broadcasted_iota(jnp.int32, (BLK, DEPTH * BLK), 0)
    col = lax.broadcasted_iota(jnp.int32, (BLK, DEPTH * BLK), 1)
    limit = jnp.where(col < BLK, row + 1, levels * BLK)
    bias = jnp.where(col < limit, jnp.float32(0.0), jnp.float32(NEGATIVE))
    bias_ref[:BLK, :] = bias
    bias_ref[BLK:, :] = bias


class Levels:
    def __init__(self, slots_ref, sources, targets, arrivals):
        self.slots_ref = slots_ref
        self.pairs = tuple(zip(sources, targets))
        self.arrivals = arrivals

    def copies(self, slot):
        turn = slot % 2
        for level in range(DEPTH):
            start = pl.multiple_of(self.slots_ref[slot, level] * BLK, BLK)
            for index, (source, target) in enumerate(self.pairs):
                place = target.at[turn, level * BLK : (level + 1) * BLK, :]
                yield pltpu.make_async_copy(
                    source.at[pl.ds(start, BLK), :], place, self.arrivals.at[turn, index, level]
                )

    def start(self, slot):
        for copy in self.copies(slot):
            copy.start()

    def step(self, slot, count):
        @pl.when(slot + 1 < count)
        def ahead():
            self.start(slot + 1)

        for copy in self.copies(slot):
            copy.wait()


def forward_kernel(
    slots_ref, query_ref, key_source, value_source, mixed_ref, logsum_ref, key_here, value_here, bias_ref, arrivals
):
    width = query_ref.shape[1]
    count = query_ref.shape[0] // BLK
    levels = Levels(slots_ref, (key_source, value_source), (key_here, value_here), arrivals)
    levels.start(0)

    def one_slot(slot, carry):
        rows = pl.ds(pl.multiple_of(slot * BLK, BLK), BLK)
        make_bias(slots_ref[slot, DEPTH], bias_ref)
        levels.step(slot, count)
        turn = slot % 2
        lane = lax.broadcasted_iota(jnp.int32, (BLK, PAIR), 1)
        logsums = jnp.zeros((BLK, PAIR), jnp.float32)
        for pair in range(width // PAIR):
            cols = slice(pair * PAIR, (pair + 1) * PAIR)
            stacked = stack_heads(query_ref[rows, cols])
            scores = against(stacked, key_here[turn, :, cols]) + bias_ref[...]
            highest = jnp.max(scores, axis=-1, keepdims=True)
            raised = jnp.exp(scores - highest)
            total = jnp.sum(raised, axis=-1, keepdims=True)
            mixed = matmul(raised.astype(jnp.bfloat16), value_here[turn, :, cols]) / total
            mixed_ref[rows, cols] = unstack_heads(mixed).astype(jnp.bfloat16)
            logsum = highest + jnp.log(total)
            logsums = jnp.where(lane == 2 * pair, logsum[:BLK], logsums)
            logsums = jnp.where(lane == 2 * pair + 1, logsum[BLK:], logsums)
        logsum_ref[rows, :] = logsums
        return carry

    lax.fori_loop(0, count, one_slot, 0)


def backward_kernel(
    slots_ref,
    compact_ref,
    used_ref,
    seen_ref,
    query_ref,
    key_source,
    value_source,
    logsum_ref,
    mixed_ref,
    mixed_grad_ref,
    normed_source,
    weight_ref,
    query_grad_ref,
    grads_ref,
    lanes_ref,
    shared_ref,
    key_here,
    value_here,
    bias_ref,
    normed_here,
    key_sums,
    value_sums,
    stage,
    zero_block,
    arrivals,
    normed_arrivals,
    departures,
):
    width = query_ref.shape[1]
    count = query_ref.shape[0] // BLK
    places = used_ref.shape[1] - 1
    used_count = used_ref[0, places]
    levels = Levels(slots_ref, (key_source, value_source), (key_here, value_here), arrivals)
    levels.start(0)

    def normed_copy(place):
        source = pl.ds(pl.multiple_of(used_ref[0, place] * BLK, BLK), BLK)
        target = normed_here.at[place * BLK : (place + 1) * BLK, :]
        return pltpu.make_async_copy(normed_source.at[source, :], target, normed_arrivals.at[place])

    for place in range(places):

        @pl.when(place < used_count)
        def fetch():
            normed_copy(place).start()

        @pl.when(place >= used_count)
        def clear():
            normed_here[place * BLK : (place + 1) * BLK, :] = jnp.zeros((BLK, normed_here.shape[1]), jnp.bfloat16)

    zero_block[...] = jnp.zeros_like(zero_block)
    for slot in range(shared_ref.shape[0]):

        @pl.when(seen_ref[0, slot] == 0)
        def none():
            pltpu.make_async_copy(zero_block, shared_ref.at[slot], departures.at[slot]).start()

    key_sums[...] = jnp.zeros_like(key_sums)
    value_sums[...] = jnp.zeros_like(value_sums)

    def one_slot(slot, carry):
        rows = pl.ds(pl.multiple_of(slot * BLK, BLK), BLK)
        make_bias(slots_ref[slot, DEPTH], bias_ref)
        levels.step(slot, count)
        turn = slot % 2
        for pair in range(width // PAIR):
            cols = slice(pair * PAIR, (pair + 1) * PAIR)
            stacked = stack_heads(query_ref[rows, cols])
            grad_rows = mixed_grad_ref[rows, cols]
            grad_stacked = stack_heads(grad_rows)
            products = grad_rows.astype(jnp.float32) * mixed_ref[rows, cols].astype(jnp.float32)
            row_dot = jnp.sum(stack_heads(products), axis=-1, keepdims=True)
            logsum = jnp.concatenate(
                [logsum_ref[rows, 2 * pair : 2 * pair + 1], logsum_ref[rows, 2 * pair + 1 : 2 * pair + 2]], axis=0
            )
            key_rows = key_here[turn, :, cols]
            shares = jnp.exp(against(stacked, key_rows) + bias_ref[...] - logsum)
            share_grad = against(grad_stacked, value_here[turn, :, cols])
            score_grad = (shares * (share_grad - row_dot)).astype(jnp.bfloat16)
            query_grad = unstack_heads(matmul(score_grad, key_rows)) * (HD ** (-0.5))
            query_grad_ref[rows, cols] = query_grad.astype(jnp.bfloat16)
            key_part = inner_rows(stacked, score_grad)
            value_part = inner_rows(grad_stacked, shares.astype(jnp.bfloat16))
            for level in range(DEPTH):
                start = pl.multiple_of(compact_ref[slot, level] * BLK, BLK)
                here = slice(level * BLK, (level + 1) * BLK)
                key_sums[cols, pl.ds(start, BLK)] += key_part[:, here]
                value_sums[cols, pl.ds(start, BLK)] += value_part[:, here]
        return carry

    lax.fori_loop(0, count, one_slot, 0)

    for place in range(places):

        @pl.when(place < used_count)
        def arrived():
            normed_copy(place).wait()

    grads_ref[...] = jnp.zeros_like(grads_ref)
    lanes_ref[...] = jnp.zeros_like(lanes_ref)

    def some_places(step, carry):
        here = pl.ds(pl.multiple_of(step * (PLACES * BLK), PLACES * BLK), PLACES * BLK)
        shared = None
        for part, part_sums in enumerate((key_sums, value_sums)):
            lines = slice(part * width, (part + 1) * width)
            block = part_sums[:, here]
            tiles = [block[:, start : start + BLK] for start in range(0, PLACES * BLK, BLK)]
            lanes_ref[lines, :] += functools.reduce(lambda left, right: left + right, tiles)
            block = block.astype(jnp.bfloat16)
            product = matmul(weight_ref[:, lines], block)
            shared = product if shared is None else shared + product
            grads_ref[lines, :] += matmul(block, normed_here[here, :])
        for index in range(PLACES):
            place = step * PLACES + index
            stage[place] = shared[:, index * BLK : (index + 1) * BLK].astype(jnp.bfloat16)

            @pl.when(place < used_count)
            def leave():
                slot = used_ref[0, place]
                pltpu.make_async_copy(stage.at[place], shared_ref.at[slot], departures.at[slot]).start()

        return carry

    lax.fori_loop(0, (used_count + PLACES - 1) // PLACES, some_places, 0)
    for slot in range(shared_ref.shape[0]):
        pltpu.make_async_copy(zero_block, shared_ref.at[slot], departures.at[slot]).wait()


def about(cost):
    return pl.CostEstimate(flops=int(cost * 1e9), bytes_accessed=int(cost * 1e6), transcendentals=0)


def in_vmem():
    return pl.BlockSpec(memory_space=pltpu.VMEM)


def in_smem():
    return pl.BlockSpec(memory_space=pltpu.SMEM)


def anywhere():
    return pl.BlockSpec(memory_space=pl.ANY)


def level_scratch(width):
    return [
        pltpu.VMEM((2, DEPTH * BLK, width), jnp.bfloat16),
        pltpu.VMEM((2, DEPTH * BLK, width), jnp.bfloat16),
        pltpu.VMEM((2 * BLK, DEPTH * BLK), jnp.float32),
    ]


def attend(slots, query_rows, key_group, value_group):
    rows, width = query_rows.shape
    return pl.pallas_call(
        forward_kernel,
        cost_estimate=about(18),
        out_shape=(
            jax.ShapeDtypeStruct((rows, width), jnp.bfloat16),
            jax.ShapeDtypeStruct((rows, PAIR), jnp.float32),
        ),
        in_specs=[in_smem(), in_vmem(), anywhere(), anywhere()],
        out_specs=(in_vmem(), in_vmem()),
        scratch_shapes=level_scratch(width) + [pltpu.SemaphoreType.DMA((2, 2, DEPTH))],
        compiler_params=pltpu.CompilerParams(vmem_limit_bytes=VMEM_BYTES),
    )(slots, query_rows, key_group, value_group)


def attend_backward(tables, query_rows, key_group, value_group, logsum, mixed, mixed_grad, normed_group, both_weight):
    rows, width = query_rows.shape
    blocks = normed_group.shape[0] // BLK
    places = tables[2].shape[1] - 1
    return pl.pallas_call(
        backward_kernel,
        cost_estimate=about(32),
        out_shape=(
            jax.ShapeDtypeStruct((rows, width), jnp.bfloat16),
            jax.ShapeDtypeStruct((2 * width, width), jnp.float32),
            jax.ShapeDtypeStruct((2 * width, BLK), jnp.float32),
            jax.ShapeDtypeStruct((blocks, width, BLK), jnp.bfloat16),
        ),
        in_specs=[in_smem()] * 4
        + [in_vmem(), anywhere(), anywhere(), in_vmem(), in_vmem(), in_vmem(), anywhere(), in_vmem()],
        out_specs=(in_vmem(), in_vmem(), in_vmem(), anywhere()),
        scratch_shapes=level_scratch(width)
        + [
            pltpu.VMEM((places * BLK, width), jnp.bfloat16),
            pltpu.VMEM((width, places * BLK), jnp.float32),
            pltpu.VMEM((width, places * BLK), jnp.float32),
            pltpu.VMEM((places, width, BLK), jnp.bfloat16),
            pltpu.VMEM((width, BLK), jnp.bfloat16),
            pltpu.SemaphoreType.DMA((2, 2, DEPTH)),
            pltpu.SemaphoreType.DMA((places,)),
            pltpu.SemaphoreType.DMA((blocks,)),
        ],
        compiler_params=pltpu.CompilerParams(vmem_limit_bytes=VMEM_BYTES),
    )(*tables, query_rows, key_group, value_group, logsum, mixed, mixed_grad, normed_group, both_weight)


def used_places(relative_slot, usable, group_blocks):
    block_count = relative_slot.shape[0]
    most = group_blocks // TREE_BLOCKS * TRUNK + 2 * block_count
    places = min(-(-most // PLACES) * PLACES, -(-group_blocks // PLACES) * PLACES)
    entries = jnp.arange(group_blocks, dtype=jnp.int32)
    hits = (relative_slot[:, :, None] == entries) & usable[:, :, None]
    seen = jnp.any(hits, axis=(0, 1))
    earlier = (entries[None, :] < entries[:, None]) & seen[None, :]
    place_of = jnp.sum(earlier, axis=1, dtype=jnp.int32)
    compact = jnp.sum(jnp.where(hits, place_of, jnp.int32(0)), axis=-1, dtype=jnp.int32)
    wanted = jnp.arange(places, dtype=jnp.int32)
    matches = (place_of[None, :] == wanted[:, None]) & seen[None, :]
    used = jnp.sum(jnp.where(matches, entries, jnp.int32(0)), axis=1, dtype=jnp.int32)
    seen = seen.astype(jnp.int32)
    used = jnp.concatenate([used, jnp.sum(seen, dtype=jnp.int32).reshape(1)])
    return compact, used.reshape(1, -1), seen.reshape(1, -1)


def project(pieces, vectors, key_weight, value_weight, group_rows, step, carried, query_weight=None):
    count = len(pieces)
    rows, width = pieces[0].shape
    weights = [key_weight, value_weight] + ([] if query_weight is None else [query_weight])
    extra = [] if carried is None else list(carried)

    def body(*refs):
        piece_refs, vectors_ref = refs[:count], refs[count]
        weight_refs = refs[count + 1 : count + 1 + len(weights)]
        outs = refs[count + 1 + len(weights) + len(extra) :]
        normed_ref, key_ref, value_ref = outs[:3]
        gain = vectors_ref[GAIN_ONE : GAIN_ONE + 1, :]
        shift = vectors_ref[SHIFT_ONE : SHIFT_ONE + 1, :]
        for index, piece in enumerate(piece_refs):
            here = slice(index * rows, (index + 1) * rows)
            normed = normalize(piece[...].astype(jnp.float32), gain, shift).astype(jnp.bfloat16)
            normed_ref[here, :] = normed
            key_ref[here, :] = matmul(normed, weight_refs[0][...]).astype(jnp.bfloat16)
            value_ref[here, :] = matmul(normed, weight_refs[1][...]).astype(jnp.bfloat16)
            if index == 0 and len(outs) > 3:
                outs[3][...] = normed
                queries = matmul(normed, weight_refs[2][...]).astype(jnp.bfloat16)
                outs[4][...] = (queries.astype(jnp.float32) * (HD ** (-0.5))).astype(jnp.bfloat16)

    block = pl.BlockSpec((count * rows, width), lambda index: (step, 0))
    whole = jax.ShapeDtypeStruct((group_rows, width), jnp.bfloat16)
    own = [] if query_weight is None else [jax.ShapeDtypeStruct((rows, width), jnp.bfloat16)] * 2
    first = count + 1 + len(weights)
    return pl.pallas_call(
        body,
        cost_estimate=about(4),
        grid=(1,),
        out_shape=[whole] * 3 + own,
        in_specs=[in_vmem()] * first + [pl.BlockSpec(memory_space=pl.ANY)] * len(extra),
        out_specs=[block] * 3 + [in_vmem()] * len(own),
        input_output_aliases={first + index: index for index in range(len(extra))},
        compiler_params=pltpu.CompilerParams(vmem_limit_bytes=VMEM_BYTES),
    )(*pieces, vectors, *weights, *extra)


class Axis:
    def __init__(self, name, size, stride):
        self.name = name
        self.size = size
        self.stride = stride

    def position(self):
        return lax.axis_index(self.name) // self.stride % self.size

    def rotate(self, values, shift):
        pairs = []
        for index in range(lax.axis_size(self.name)):
            here = index // self.stride % self.size
            there = (here + shift) % self.size
            pairs.append((index, index + (there - here) * self.stride))
        return lax.ppermute(values, self.name, pairs)


def axes():
    seq = lax.axis_size("seq")
    dp = lax.axis_size("dp")
    along_z = 4 if seq % 4 == 0 else 1
    cores = 2 if dp % 2 == 0 else 1
    return (
        Axis("seq", along_z, seq // along_z),
        Axis("seq", seq // along_z, 1),
        Axis("dp", dp // cores, cores),
        Axis("dp", cores, 1),
    )


def relative_devices():
    axis_z, axis_x, axis_y, axis_core = axes()

    def place(axis, dim):
        back = lax.broadcasted_iota(jnp.int32, (axis_core.size, axis_y.size, axis_x.size, axis_z.size), dim)
        return (axis.position() - back + axis.size) % axis.size

    dp_index = place(axis_y, 1) * axis_core.size + place(axis_core, 0)
    seq_index = place(axis_z, 3) * axis_x.size + place(axis_x, 2)
    return (dp_index * lax.axis_size("seq") + seq_index).reshape(-1)


def scatter_devices():
    axis_z, axis_x, axis_y, axis_core = axes()
    entries = relative_devices().reshape(-1, axis_x.size, axis_z.size)
    return jnp.swapaxes(entries, 1, 2).reshape(-1)


def add_low(left_side, right_side):
    return (left_side.astype(jnp.float32) + right_side.astype(jnp.float32)).astype(jnp.bfloat16)


def add_three(first, second, third):
    total = first.astype(jnp.float32) + second.astype(jnp.float32) + third.astype(jnp.float32)
    return total.astype(jnp.bfloat16)


def tied(values, after):
    return lax.optimization_barrier((values, after))[0]


def ring_scatter(entry, axis):
    running = entry(axis.size - 1)
    for back in range(axis.size - 1, 0, -1):
        running = add_low(axis.rotate(running, -1), entry(back - 1))
    return running


def pair_scatter(keep, send, axis):
    arrived = axis.rotate(send, -1)
    return lambda index: add_low(arrived[index], keep[index])


GATE_B, DOWN_B, CARRY_B, GAIN_ONE, SHIFT_ONE, GAIN_TWO, SHIFT_TWO, UP_B = range(8)
VECTOR_ROWS = 16
MIDDLE_ROWS = 640


def pack_kernel(devices, place_ref, *refs):
    early_sources, late_sources, vector_refs, (early_ref, late_ref) = refs[:4], refs[4:8], refs[8:16], refs[16:]
    width = early_ref.shape[1]
    for target, sources in ((early_ref, early_sources), (late_ref, late_sources)):
        start = 0
        for source in sources:
            rows = source.shape[0]
            for column in range(0, source.shape[1], width):
                target[start : start + rows, :] = source[:, column : column + width]
                start += rows
    block = jnp.zeros((VECTOR_ROWS, width), jnp.float32)
    line = lax.broadcasted_iota(jnp.int32, block.shape, 0)
    for index, source in enumerate(vector_refs):
        count = source.shape[1]
        feature = lax.broadcasted_iota(jnp.int32, (count, width), 0) + place_ref[0] * count
        column = lax.broadcasted_iota(jnp.int32, (count, width), 1)
        for part in range(count * devices // width):
            spot = jnp.where(feature == column + part * width, jnp.float32(1.0), jnp.float32(0.0))
            spread = matmul(source[...], spot.astype(jnp.bfloat16))
            block += jnp.where(line == index + part, spread, jnp.float32(0.0))
    early_ref[early_ref.shape[0] - VECTOR_ROWS :, :] = block.astype(jnp.bfloat16)


def unpack_kernel(place_ref, mine_ref, other_ref, query_ref, key_ref, value_ref, gate_ref, vectors_ref):
    half = mine_ref.shape[0]
    rows = (mine_ref.shape[1] - VECTOR_ROWS) // 4
    vectors = jnp.zeros(vectors_ref.shape, jnp.float32)
    for index in range(2 * half):
        source = (mine_ref if index < half else other_ref).at[index % half]
        target = pl.ds(pl.multiple_of(place_ref[index] * rows, rows), rows)
        for part, weight_ref in enumerate((query_ref, key_ref, value_ref, gate_ref)):
            weight_ref[target, :] = source[part * rows : (part + 1) * rows, :]
        vectors += source[4 * rows :, :].astype(jnp.float32)
    vectors_ref[...] = vectors


def unpack_late(place_ref, line_sources, plane_sources, output_ref, up_ref, down_ref, carry_ref):
    part_size = line_sources[0].shape[0]
    devices = part_size * len(line_sources)
    width = output_ref.shape[1]
    rows = output_ref.shape[0] // devices
    down_rows = down_ref.shape[0] // devices
    for index in range(devices):
        source = line_sources[index // part_size].at[index % part_size]
        target = pl.ds(pl.multiple_of(place_ref[0, index] * rows, rows), rows)
        output_ref[target, :] = source[:rows, :]
        for part in range(up_ref.shape[1] // width):
            up_ref[target, part * width : (part + 1) * width] = source[(part + 1) * rows : (part + 2) * rows, :]
        source = plane_sources[index // part_size].at[index % part_size]
        target = pl.ds(pl.multiple_of(place_ref[1, index] * down_rows, down_rows), down_rows)
        down_ref[target, :] = source[:down_rows, :]
        target = pl.ds(pl.multiple_of(place_ref[1, index] * rows, rows), rows)
        carry_ref[target, :] = source[down_rows:, :]


def spread_rows(place_ref, grad_ref, keep_ref, send_ref, start, rows):
    half = keep_ref.shape[0]
    for index in range(2 * half):
        source = pl.ds(pl.multiple_of(place_ref[index] * rows, rows), rows)
        target = (keep_ref if index < half else send_ref).at[index % half]
        target[start : start + rows, :] = grad_ref[source, :].astype(jnp.bfloat16)


def middle_kernel(
    place_ref,
    attended_ref,
    input_ref,
    normed_ref,
    cotangent_ref,
    gate_weight_ref,
    vectors_ref,
    *refs,
):
    late_refs, refs = refs[:8], refs[8:]
    output_ref, middle_grad_ref, attended_grad_ref, gate_pre_ref, block_ref, keep_ref, send_ref = refs[:7]
    output_weight, up_weight, down_weight, carry_weight, hidden, up_pre_grads = refs[7:13]
    update_grads, normed_second, carry_pre_grads, branch_grads, up_grad, down_grad, square_grads = refs[13:]
    unpack_late(
        place_ref,
        late_refs[:4],
        late_refs[4:],
        output_weight,
        up_weight,
        down_weight,
        carry_weight,
    )
    width = output_ref.shape[1]
    hidden_width = up_weight.shape[1]
    wide = hidden_width // width

    def vector(line):
        return vectors_ref[line : line + 1, :]

    up_bias = jnp.concatenate([vector(UP_B + part) for part in range(wide)], axis=1)

    def column_lines(values):
        return jnp.sum(values.astype(jnp.float32), axis=0, keepdims=True)

    def some_rows(step, totals):
        rows = pl.ds(pl.multiple_of(step * MIDDLE_ROWS, MIDDLE_ROWS), MIDDLE_ROWS)
        gate_open = jax.nn.sigmoid(matmul(normed_ref[rows, :], gate_weight_ref[...]) + vector(GATE_B))
        branch = matmul(attended_ref[rows, :], output_weight[...])
        middle = input_ref[rows, :].astype(jnp.float32) + gate_open * branch
        centered = middle - jnp.mean(middle, axis=-1, keepdims=True)
        scale = lax.rsqrt(jnp.mean(centered * centered, axis=-1, keepdims=True) + EPSILON)
        hat = centered * scale
        normed = (hat * vector(GAIN_TWO) + vector(SHIFT_TWO)).astype(jnp.bfloat16)
        up_pre = matmul(normed, up_weight[...]) + up_bias
        up_open = jax.nn.sigmoid(up_pre)
        hidden_rows = (up_pre * up_open).astype(jnp.bfloat16)
        update = matmul(hidden_rows, down_weight[...]) + vector(DOWN_B)
        carry_open = jax.nn.sigmoid(matmul(normed, carry_weight[...]) + vector(CARRY_B))
        output_ref[rows, :] = (middle + carry_open * update).astype(jnp.bfloat16)

        grad_out = cotangent_ref[rows, :].astype(jnp.float32)
        update_grad = (carry_open * grad_out).astype(jnp.bfloat16)
        carry_pre_grad = (grad_out * update * carry_open * (1.0 - carry_open)).astype(jnp.bfloat16)
        slope = up_open * (1.0 + up_pre * (1.0 - up_open))
        up_pre_grad = (against(update_grad, down_weight[...]) * slope).astype(jnp.bfloat16)
        norm_grad = against(up_pre_grad, up_weight[...]) + against(carry_pre_grad, carry_weight[...])
        pull = norm_grad * vector(GAIN_TWO)
        middle_grad = grad_out + scale * (
            pull - jnp.mean(pull, axis=-1, keepdims=True) - hat * jnp.mean(pull * hat, axis=-1, keepdims=True)
        )
        middle_grad_ref[rows, :] = middle_grad
        branch_grad = (gate_open * middle_grad).astype(jnp.bfloat16)
        gate_pre_grad = (middle_grad * branch * gate_open * (1.0 - gate_open)).astype(jnp.bfloat16)
        gate_pre_ref[rows, :] = gate_pre_grad
        attended_grad_ref[rows, :] = against(branch_grad, output_weight[...]).astype(jnp.bfloat16)

        hidden[rows, :] = hidden_rows
        up_pre_grads[rows, :] = up_pre_grad
        update_grads[rows, :] = update_grad
        normed_second[rows, :] = normed
        carry_pre_grads[rows, :] = carry_pre_grad
        branch_grads[rows, :] = branch_grad
        lines = (gate_pre_grad, update_grad, carry_pre_grad, norm_grad * hat, norm_grad, up_pre_grad)
        return tuple(total + column_lines(line) for total, line in zip(totals, lines))

    start = (jnp.zeros((1, width), jnp.float32),) * 5 + (jnp.zeros((1, hidden_width), jnp.float32),)
    totals = lax.fori_loop(0, output_ref.shape[0] // MIDDLE_ROWS, some_rows, start)
    line = lax.broadcasted_iota(jnp.int32, block_ref.shape, 0)
    block = jnp.zeros(block_ref.shape, jnp.float32)
    for place, total in zip((GATE_B, DOWN_B, CARRY_B, GAIN_TWO, SHIFT_TWO), totals):
        block = jnp.where(line == place, total, block)
    for part in range(wide):
        block = jnp.where(line == UP_B + part, totals[5][:, part * width : (part + 1) * width], block)
    block_ref[...] = block

    target_ref = place_ref.at[2]
    rows = width // (2 * keep_ref.shape[0])
    place = 0
    for part in range(wide):
        grad = up_grad.at[part]
        grad[...] = inner_rows(normed_second[...], up_pre_grads[:, part * width : (part + 1) * width])
        spread_rows(target_ref, grad, keep_ref, send_ref, place, rows)
        place += rows
    for part in range(wide):
        here = slice(part * width, (part + 1) * width)
        down_grad[here, :] = inner_rows(hidden[:, here], update_grads[...])
    spread_rows(target_ref, down_grad, keep_ref, send_ref, place, wide * rows)
    place += wide * rows
    pairs = ((normed_second, carry_pre_grads), (attended_ref, branch_grads), (normed_ref, gate_pre_ref))
    for index, (left_ref, right_ref) in enumerate(pairs):
        grad = square_grads.at[index]
        grad[...] = inner_rows(left_ref[...], right_ref[...])
        spread_rows(target_ref, grad, keep_ref, send_ref, place, rows)
        place += rows


def second_grads_kernel(
    place_ref,
    both_grads_ref,
    normed_ref,
    query_grad_ref,
    gate_pre_ref,
    lanes_ref,
    query_weight_ref,
    key_weight_ref,
    value_weight_ref,
    gate_weight_ref,
    vectors_ref,
    block_ref,
    keep_ref,
    send_ref,
    grads,
):
    width = keep_ref.shape[2]
    rows = width // (2 * keep_ref.shape[0])
    grads[0] = inner_rows(normed_ref[...], query_grad_ref[...])
    grads[1] = jnp.transpose(both_grads_ref[:width, :])
    grads[2] = jnp.transpose(both_grads_ref[width:, :])
    for index in range(3):
        spread_rows(place_ref, grads.at[index], keep_ref, send_ref, index * rows, rows)
    gate_grad = inner_rows(normed_ref[...], gate_pre_ref[...])

    def line_sums(ref):
        return jnp.sum(ref[...].astype(jnp.float32), axis=0, keepdims=True)

    def as_line(column):
        return jnp.transpose(jnp.broadcast_to(column, (width, BLK)))[:1, :]

    lines = (
        line_sums(query_grad_ref),
        jnp.sum(jnp.transpose(lanes_ref[:width, :]), axis=0, keepdims=True),
        jnp.sum(jnp.transpose(lanes_ref[width:, :]), axis=0, keepdims=True),
        line_sums(gate_pre_ref),
    )
    weighted = jnp.zeros((width, width), jnp.float32)
    shifted = jnp.zeros((width, width), jnp.float32)
    weight_refs = (query_weight_ref, key_weight_ref, value_weight_ref, gate_weight_ref)
    for weight_ref, line, grad in zip(weight_refs, lines, (grads[0], grads[1], grads[2], gate_grad)):
        weight = weight_ref[...].astype(jnp.float32)
        weighted += weight * grad
        shifted += weight * line
    shift_line = as_line(jnp.sum(shifted, axis=1, keepdims=True))
    gain_line = (
        as_line(jnp.sum(weighted, axis=1, keepdims=True)) - vectors_ref[SHIFT_ONE : SHIFT_ONE + 1, :] * shift_line
    ) / vectors_ref[GAIN_ONE : GAIN_ONE + 1, :]
    place = lax.broadcasted_iota(jnp.int32, block_ref.shape, 0)
    block = jnp.where(place == GAIN_ONE, gain_line, block_ref[...])
    block = jnp.where(place == SHIFT_ONE, shift_line, block).astype(jnp.bfloat16)
    for index in range(keep_ref.shape[0]):
        keep_ref[index, 3 * rows :, :] = block
        send_ref[index, 3 * rows :, :] = block


def input_grad_kernel(input_ref, local_ref, middle_grad_ref, vectors_ref, *refs):
    shared_refs, output_ref = refs[:-1], refs[-1]
    blocks = [sum(ref[index].astype(jnp.float32) for ref in shared_refs) for index in range(shared_refs[0].shape[0])]
    shared = jnp.concatenate([jnp.transpose(block) for block in blocks])
    values = input_ref[...].astype(jnp.float32)
    centered = values - jnp.mean(values, axis=-1, keepdims=True)
    scale = lax.rsqrt(jnp.mean(centered * centered, axis=-1, keepdims=True) + EPSILON)
    hat = centered * scale
    pull = (local_ref[...] + shared) * vectors_ref[GAIN_ONE : GAIN_ONE + 1, :]
    output_ref[...] = middle_grad_ref[...] + scale * (
        pull - jnp.mean(pull, axis=-1, keepdims=True) - hat * jnp.mean(pull * hat, axis=-1, keepdims=True)
    )


def local_call(kernel, cost, outs, smem, args, scratch=()):
    return pl.pallas_call(
        kernel,
        cost_estimate=about(cost),
        out_shape=outs,
        in_specs=[in_smem()] + [in_vmem()] * len(args),
        out_specs=jax.tree.map(lambda out: in_vmem(), outs),
        scratch_shapes=list(scratch),
        compiler_params=pltpu.CompilerParams(vmem_limit_bytes=VMEM_BYTES),
    )(smem, *args)


def joined(pieces, axis):
    return pieces[0] if len(pieces) == 1 else jnp.concatenate(pieces, axis=axis)


def shards(
    inputs,
    cotangent,
    block_segment,
    segment_parent,
    query_weight,
    key_weight,
    value_weight,
    output_weight,
    gate_weight,
    gate_bias,
    up_weight,
    up_bias,
    down_weight,
    down_bias,
    carry_weight,
    carry_bias,
    first_gain,
    first_shift,
    second_gain,
    second_shift,
):
    width = inputs.shape[1]
    devices = lax.axis_size(BOTH)
    block_count = inputs.shape[0] // BLK
    group_blocks = block_segment.shape[0]

    axis_z, axis_x, axis_y, axis_core = axes()
    rows_each = query_weight.shape[0]
    sizes = (axis_z.size, axis_x.size, axis_y.size, axis_core.size)
    direct = sizes == (4, 2, 2, 2) and rows_each % 16 == 0
    places = relative_devices()
    targets = scatter_devices()
    device = lax.axis_index(BOTH)
    vectors = (gate_bias, down_bias, carry_bias, first_gain, first_shift, second_gain, second_shift, up_bias)
    early_set = (query_weight, key_weight, value_weight, gate_weight)
    late_set = (output_weight, up_weight, down_weight, carry_weight)
    low = jnp.bfloat16

    def struct(*shape, dtype=low):
        return jax.ShapeDtypeStruct(shape, dtype)

    def take(source, start, piece):
        rows = piece.shape[0]
        parts = piece.shape[1] // width
        blocks = [
            source[:, start + part * rows : start + (part + 1) * rows].reshape(devices * rows, width)
            for part in range(parts)
        ]
        return joined(blocks, 1), start + parts * rows

    def flat_rows(pieces):
        return [piece[:, start : start + width] for piece in pieces for start in range(0, piece.shape[1], width)]

    if direct:
        early_count = 4 * rows_each + VECTOR_ROWS
        late_count = sum(piece.shape[0] * piece.shape[1] // width for piece in late_set)
        early, late = local_call(
            functools.partial(pack_kernel, devices),
            0.1,
            (struct(early_count, width), struct(late_count, width)),
            device.reshape(1),
            early_set + late_set + tuple(vector.reshape(1, -1) for vector in vectors),
        )
        late_line = [late]
        late_line.append(axis_z.rotate(late, 1))
        early_line = [axis_z.rotate(early, back) for back in range(1, 4)]
        x_zero = axis_x.rotate(inputs, 1)
        z_one = axis_z.rotate(inputs, 1)
        late_line[1], early_line, x_zero, z_one = lax.optimization_barrier((late_line[1], early_line, x_zero, z_one))
        z_two = axis_z.rotate(z_one, 1)
        x_one = axis_x.rotate(z_one, 1)
        early_line = jnp.stack([early] + list(early_line))
        early_other = axis_x.rotate(early_line, 1)
        late_line.append(axis_z.rotate(late_line[1], 1))
        early_other, z_two, x_one, late_line[2] = lax.optimization_barrier((early_other, z_two, x_one, late_line[2]))
        z_three = axis_z.rotate(z_two, 1)
        x_two = axis_x.rotate(z_two, 1)
        early_plane = jnp.stack([early_line, early_other])
        early_other = axis_y.rotate(early_plane, 1)
        late_line.append(axis_z.rotate(late_line[2], 1))
        early_other, z_three, x_two, late_line[3] = lax.optimization_barrier(
            (early_other, z_three, x_two, late_line[3])
        )
        x_three = axis_x.rotate(z_three, 1)
        early_all = jnp.stack([early_plane, early_other]).reshape(devices // 2, early_count, width)
        early_other = axis_core.rotate(early_all, 1)
        late_half = late_count // 2
        late_x = jnp.stack([rows[:late_half] for rows in late_line])
        late_y = jnp.stack([rows[late_half:] for rows in late_line])
        late_x_other = axis_x.rotate(late_x, 1)
        late_y_other = axis_y.rotate(late_y, 1)
        input_pieces = [[inputs, x_zero], [z_one, x_one], [z_two, x_two], [z_three, x_three]]
        square = struct(width, width)
        full_query, full_key, full_value, full_gate, vector_rows = local_call(
            unpack_kernel,
            3,
            (square, square, square, square, struct(VECTOR_ROWS, width, dtype=jnp.float32)),
            places,
            (early_all, early_other),
        )
    else:
        early_rows = lax.all_gather(jnp.concatenate(early_set), BOTH)
        late_rows = lax.all_gather(jnp.concatenate(flat_rows(late_set)), BOTH)
        place = 0
        full_query, place = take(early_rows, place, query_weight)
        full_key, place = take(early_rows, place, key_weight)
        full_value, place = take(early_rows, place, value_weight)
        full_gate, place = take(early_rows, place, gate_weight)
        place = 0
        full_output, place = take(late_rows, place, output_weight)
        full_up, place = take(late_rows, place, up_weight)
        full_down, place = take(late_rows, place, down_weight)
        full_carry, place = take(late_rows, place, carry_weight)
        lines = [lax.all_gather(vector, BOTH, tiled=True).reshape(-1, width) for vector in vectors]
        lines = jnp.concatenate(lines).astype(jnp.float32)
        vector_rows = jnp.pad(lines, ((0, VECTOR_ROWS - lines.shape[0]), (0, 0)))
        input_pieces = []
        along_z = inputs
        for step_z in range(axis_z.size):
            along_x = along_z
            row = []
            for step_x in range(axis_x.size):
                row.append(along_x)
                along_x = axis_x.rotate(along_x, 1) if step_x + 1 < axis_x.size else None
            input_pieces.append(row)
            along_z = axis_z.rotate(along_z, 1) if step_z + 1 < axis_z.size else None

    carried = None
    for step, row in enumerate(input_pieces):
        if direct and step == 3:
            x_three, late_x_other, late_y_other, carried = lax.optimization_barrier(
                (row[1], late_x_other, late_y_other, carried)
            )
            row = [row[0], x_three]
            late_x = jnp.stack([late_x, late_x_other])
            late_y = jnp.stack([late_y, late_y_other])
            late_x_other = axis_y.rotate(late_x, 1)
            late_y_other = axis_x.rotate(late_y, 1)
        asked = full_query if step == 0 else None
        done = project(row, vector_rows, full_key, full_value, group_blocks * BLK, step, carried, asked)
        carried = done[:3]
        if step == 0:
            normed_low, query_low = done[3:]
    normed_group, key_group, value_group = carried

    gate_b, down_b, carry_b, gain_one, shift_one, gain_two, shift_two = [vector_rows[line] for line in range(UP_B)]
    up_b = vector_rows[UP_B : UP_B + up_weight.shape[1] // width].reshape(-1)

    own_start = lax.axis_index("seq") * block_count
    own_segments = lax.dynamic_slice_in_dim(block_segment, own_start, block_count)
    ancestor_slot, usable = ancestor_slots(block_segment, segment_parent, own_segments)
    owner = ancestor_slot // block_count
    away_z = (axis_z.position() - owner // axis_x.size) % axis_z.size
    away_x = (axis_x.position() - owner % axis_x.size) % axis_x.size
    relative_slot = (away_z * axis_x.size + away_x) * block_count + ancestor_slot % block_count
    tables = used_places(relative_slot, usable, group_blocks)
    slots = jnp.concatenate(
        [relative_slot, jnp.sum(usable, axis=-1, keepdims=True, dtype=jnp.int32)], axis=-1
    )

    values_in = inputs.astype(jnp.float32)
    attended_low, logsum = attend(slots, query_low, key_group, value_group)

    if direct:
        attended_low, late_x_other, late_y_other = lax.optimization_barrier((attended_low, late_x_other, late_y_other))
        late_parts = []
        for mine in ((late_x, late_x_other), (late_y, late_y_other)):
            for piece in list(mine) + [axis_core.rotate(part, 1) for part in mine]:
                late_parts.append(piece.reshape(devices // 4, late_half, width))
        other_places = jnp.transpose(places.reshape(2, 2, 2, 4), (0, 2, 1, 3)).reshape(-1)
        rows = inputs.shape[0]
        first_rows = late_count + rows_each
        hidden_width = up_weight.shape[1]
        half = struct(devices // 2, first_rows, width)
        tall, short = pltpu.VMEM((rows, hidden_width), low), pltpu.VMEM((rows, width), low)
        output, middle_grad, attended_grad, gate_pre_grad, block, first_keep, first_send = local_call(
            middle_kernel,
            28,
            (
                struct(rows, width),
                struct(rows, width, dtype=jnp.float32),
                struct(rows, width),
                struct(rows, width),
                struct(VECTOR_ROWS, width, dtype=jnp.float32),
                half,
                half,
            ),
            jnp.stack([places, other_places, targets]),
            (
                attended_low,
                inputs,
                normed_low,
                cotangent,
                full_gate,
                vector_rows,
            )
            + tuple(late_parts),
            (
                pltpu.VMEM((width, width), low),
                pltpu.VMEM((width, hidden_width), low),
                pltpu.VMEM((hidden_width, width), low),
                pltpu.VMEM((width, width), low),
                tall,
                tall,
                short,
                short,
                short,
                short,
                pltpu.VMEM((hidden_width // width, width, width), jnp.float32),
                pltpu.VMEM((hidden_width, width), jnp.float32),
                pltpu.VMEM((3, width, width), jnp.float32),
            ),
        )
        near = (2, 4, 2, first_rows, width)
        first_entry = pair_scatter(first_keep.reshape(near), first_send.reshape(near), axis_core)
        first_keep, first_send = first_entry(0), first_entry(1)
        attended_grad, first_keep, first_send = lax.optimization_barrier((attended_grad, first_keep, first_send))
        first_arrived = axis_y.rotate(first_send, -1)
    else:
        gate_open = jax.nn.sigmoid(matmul(normed_low, full_gate) + gate_b)
        branch = matmul(attended_low, full_output)
        middle = values_in + gate_open * branch
        normed_second = normalize(middle, gain_two, shift_two).astype(jnp.bfloat16)
        up_pre = matmul(normed_second, full_up) + up_b
        up_sigmoid = jax.nn.sigmoid(up_pre)
        hidden_low = (up_pre * up_sigmoid).astype(jnp.bfloat16)
        update = matmul(hidden_low, full_down) + down_b
        carry_open = jax.nn.sigmoid(matmul(normed_second, full_carry) + carry_b)
        output = (middle + carry_open * update).astype(jnp.bfloat16)

        grad_out = cotangent.astype(jnp.float32)
        update_grad = (carry_open * grad_out).astype(jnp.bfloat16)
        carry_pre_grad = (grad_out * update * carry_open * (1.0 - carry_open)).astype(jnp.bfloat16)
        grad_down_bias = column_sums(update_grad)
        grad_carry_bias = column_sums(carry_pre_grad)
        silu_slope = up_sigmoid * (1.0 + up_pre * (1.0 - up_sigmoid))
        up_pre_grad = (against(update_grad, full_down) * silu_slope).astype(jnp.bfloat16)
        grad_up_bias = column_sums(up_pre_grad)
        second_norm_grad = against(up_pre_grad, full_up) + against(carry_pre_grad, full_carry)
        second_pull = jax.vjp(normalize, middle, gain_two, shift_two)[1]
        middle_part, grad_second_gain, grad_second_shift = second_pull(second_norm_grad)
        middle_grad = grad_out + middle_part

        branch_grad = (gate_open * middle_grad).astype(jnp.bfloat16)
        gate_pre_grad = (middle_grad * branch * gate_open * (1.0 - gate_open)).astype(jnp.bfloat16)
        grad_gate_bias = column_sums(gate_pre_grad)
        attended_grad = against(branch_grad, full_output).astype(jnp.bfloat16)
        zero_line = jnp.zeros((width,), jnp.float32)
        local_lines = (
            grad_gate_bias,
            grad_down_bias,
            grad_carry_bias,
            zero_line,
            zero_line,
            grad_second_gain,
            grad_second_shift,
            grad_up_bias,
        )
        block = jnp.concatenate([line.reshape(-1, width) for line in local_lines])
        block = jnp.pad(block, ((0, VECTOR_ROWS - block.shape[0]), (0, 0)))
    backward = attend_backward(
        (slots,) + tables,
        query_low,
        key_group,
        value_group,
        logsum,
        attended_low,
        attended_grad,
        normed_group,
        jnp.concatenate([full_key, full_value], axis=1),
    )
    if direct:
        backward, first_arrived = lax.optimization_barrier((backward, first_arrived))

        def first_y(back):
            return add_low(first_arrived[back], first_keep[back])

        first_z = axis_z.rotate(first_y(3), -1)
    query_rows_grad, both_grads, lanes, shared_rows = backward

    shared_parts = [
        shared_rows[start : start + block_count] for start in range(0, group_blocks, block_count)
    ]

    if direct:
        second_rows = 3 * rows_each + VECTOR_ROWS
        half = struct(devices // 2, second_rows, width)
        second_keep, second_send = local_call(
            second_grads_kernel,
            0.1,
            (half, half),
            places,
            (
                both_grads,
                normed_low,
                query_rows_grad,
                gate_pre_grad,
                lanes,
                full_query,
                full_key,
                full_value,
                full_gate,
                vector_rows,
                block,
            ),
            (pltpu.VMEM((3, width, width), jnp.float32),),
        )
        near = (2, 2, 4, second_rows, width)
        second_entry = pair_scatter(second_keep.reshape(near), second_send.reshape(near), axis_core)
        barrier = lax.optimization_barrier
        first_z = axis_z.rotate(add_low(first_z, first_y(2)), -1)
        x_three = axis_x.rotate(shared_parts[7], -1)
        second_keep, second_send = second_entry(0), second_entry(1)
        x_three, first_z, second_keep, second_send = barrier((x_three, first_z, second_keep, second_send))

        second_arrived = axis_y.rotate(second_send, -1)
        x_two = axis_x.rotate(tied(shared_parts[5], x_three), -1)
        z_three = axis_z.rotate(add_low(x_three, shared_parts[6]), -1)
        first_z = axis_z.rotate(add_low(first_z, first_y(1)), -1)
        x_two, z_three, first_z, second_arrived = barrier((x_two, z_three, first_z, second_arrived))

        second_y = add_low(second_arrived, second_keep)
        second_x = axis_x.rotate(second_y[1], -1)
        x_one = axis_x.rotate(tied(shared_parts[3], x_two), -1)
        z_two = axis_z.rotate(add_three(x_two, shared_parts[4], z_three), -1)
        x_one, z_two, second_x = barrier((x_one, z_two, second_x))

        first_half = add_low(first_z, first_y(0))
        first_x = axis_x.rotate(tied(first_half[1], x_one), -1)
        second_half = add_low(second_x, second_y[0])
        second_z = [axis_z.rotate(second_half[back], -back) for back in range(1, 4)]
        x_zero = axis_x.rotate(tied(shared_parts[1], x_one), -1)
        z_one = axis_z.rotate(add_three(x_one, shared_parts[2], z_two), -1)
        shared = (x_zero, z_one, shared_parts[0])
        first_sum = first_x.astype(jnp.float32) + first_half[0].astype(jnp.float32)
        second_sum = sum(piece.astype(jnp.float32) for piece in [second_half[0]] + second_z)
        weight_sum = jnp.concatenate([first_sum, second_sum])
    else:
        grad_key = jnp.transpose(both_grads[:width])
        grad_value = jnp.transpose(both_grads[width:])
        grad_query = inner_rows(normed_low, query_rows_grad)
        grad_gate = inner_rows(normed_low, gate_pre_grad)
        both_sums = jnp.sum(lanes, axis=1)
        weights = [weight.astype(jnp.float32) for weight in (full_query, full_key, full_value, full_gate)]
        line_sums = (column_sums(query_rows_grad), both_sums[:width], both_sums[width:], grad_gate_bias)
        shift_line = sum(jnp.sum(weight * line, axis=1) for weight, line in zip(weights, line_sums))
        weighted = sum(
            jnp.sum(weight * grad, axis=1)
            for weight, grad in zip(weights, (grad_query, grad_key, grad_value, grad_gate))
        )
        block = block.at[GAIN_ONE].set((weighted - shift_one * shift_line) / gain_one).at[SHIFT_ONE].set(shift_line)
        grads = (
            (inner_rows(normed_second, up_pre_grad), up_weight),
            (inner_rows(hidden_low, update_grad), down_weight),
            (inner_rows(normed_second, carry_pre_grad), carry_weight),
            (inner_rows(attended_low, branch_grad), output_weight),
            (grad_gate, gate_weight),
            (grad_query, query_weight),
            (grad_key, key_weight),
            (grad_value, value_weight),
        )
        pack = [
            cut.astype(low).reshape(devices, piece.shape[0], width)
            for grad, piece in grads
            for cut in flat_rows((grad,))
        ]
        pack.append(jnp.broadcast_to(block.astype(low), (devices, VECTOR_ROWS, width)))
        pack = jnp.concatenate(pack, axis=1)
        pack = jnp.pad(pack, ((0, 0), (0, -pack.shape[1] % 16), (0, 0)))
        weight_sum = lax.psum_scatter(pack, BOTH, scatter_dimension=0, tiled=True)[0].astype(jnp.float32)

        def over_x(step_z):
            return ring_scatter(lambda step_x: shared_parts[step_z * axis_x.size + step_x], axis_x)

        shared = (ring_scatter(over_x, axis_z),)

    def own(start, piece):
        rows = piece.shape[0]
        parts = piece.shape[1] // width
        blocks = [weight_sum[start + part * rows : start + (part + 1) * rows] for part in range(parts)]
        return joined(blocks, 1), start + parts * rows

    local_grad = against(query_rows_grad, full_query) + against(gate_pre_grad, full_gate)
    rows = inputs.shape[0]
    input_grad = pl.pallas_call(
        input_grad_kernel,
        cost_estimate=about(3),
        out_shape=struct(rows, width, dtype=jnp.float32),
        compiler_params=pltpu.CompilerParams(vmem_limit_bytes=VMEM_BYTES),
    )(inputs, local_grad, middle_grad, vector_rows, *shared)

    place = 0
    own_up, place = own(place, up_weight)
    own_down, place = own(place, down_weight)
    own_carry, place = own(place, carry_weight)
    own_output, place = own(place, output_weight)
    own_gate, place = own(place, gate_weight)
    own_query, place = own(place, query_weight)
    own_key, place = own(place, key_weight)
    own_value, place = own(place, value_weight)
    vector_out = []
    for index, vector in enumerate(vectors):
        count = vector.shape[0]
        lines = weight_sum[place + index : place + index + count * devices // width].reshape(-1)
        vector_out.append(lax.dynamic_slice_in_dim(lines, device * count, count))
    gate_bg, down_bg, carry_bg, gain_one_g, shift_one_g, gain_two_g, shift_two_g, up_bg = vector_out
    return (
        output,
        input_grad,
        own_query,
        own_key,
        own_value,
        own_output,
        own_gate,
        gate_bg,
        own_up,
        up_bg,
        own_down,
        down_bg,
        own_carry,
        carry_bg,
        gain_one_g,
        shift_one_g,
        gain_two_g,
        shift_two_g,
    )


def solution(mesh):
    rows = P(BOTH, None)
    line = P(BOTH)
    matrix_or_line = (rows,) * 5 + (line, rows, line, rows, line, rows) + (line,) * 5
    return jax.shard_map(
        shards,
        mesh=mesh,
        in_specs=(rows, rows, P("dp"), P("dp")) + matrix_or_line,
        out_specs=(rows, rows) + matrix_or_line,
        check_vma=False,
    )
```

```python
import functools

import jax
import jax.numpy as jnp
from jax import lax
from jax.experimental import pallas as pl
from jax.experimental.pallas import tpu as pltpu
from jax.sharding import PartitionSpec as P

HD = 64
BLK = 128
DEPTH = 10
PAIR = 2 * HD
PLACES = 4
TREE_BLOCKS = 20
TRUNK = 8

EPSILON = 1e-05
NEGATIVE = -1e30
BOTH = ("dp", "seq")
VMEM_BYTES = 60 * 1024 * 1024


def normalize(values, norm_gain, norm_shift):
    center = values - jnp.mean(values, axis=-1, keepdims=True)
    spread = jnp.mean(center * center, axis=-1, keepdims=True)
    return center * lax.rsqrt(spread + EPSILON) * norm_gain + norm_shift


def matmul(left_side, right_side):
    return jnp.dot(left_side, right_side, preferred_element_type=jnp.float32)


def inner_rows(left_side, right_side):
    return lax.dot_general(
        left_side, right_side, (((0,), (0,)), ((), ())), preferred_element_type=jnp.float32
    )


def against(left_side, right_side):
    return lax.dot_general(
        left_side, right_side, (((1,), (1,)), ((), ())), preferred_element_type=jnp.float32
    )


def column_sums(values):
    return jnp.sum(values.astype(jnp.float32), axis=0)


def lookup(lookup_table, wanted):
    entries = jnp.arange(lookup_table.shape[0], dtype=jnp.int32)
    matches = wanted[..., None] == entries
    located = jnp.sum(jnp.where(matches, lookup_table, jnp.int32(0)), axis=-1, dtype=jnp.int32)
    return jnp.where(wanted >= 0, located, jnp.int32(-1))


def ancestor_slots(block_segment, segment_parent, own_segments):
    entries = jnp.arange(block_segment.shape[0], dtype=jnp.int32)
    placed = block_segment[None, :] == entries[:, None]
    slot_of = jnp.sum(jnp.where(placed, entries[None, :], jnp.int32(0)), axis=1, dtype=jnp.int32)
    current = own_segments
    lineage = []
    for depth_step in range(DEPTH):
        lineage.append(current)
        current = lookup(segment_parent, current)
    lineage = jnp.stack(lineage, axis=-1)
    usable = lineage >= 0
    return (jnp.where(usable, lookup(slot_of, lineage), jnp.int32(0)), usable)


def stack_heads(rows):
    lane = lax.broadcasted_iota(jnp.int32, rows.shape, 1)
    low = lane < HD
    zero = jnp.zeros_like(rows)
    return jnp.concatenate([jnp.where(low, rows, zero), jnp.where(low, zero, rows)], axis=0)


def unstack_heads(rows):
    half = rows.shape[0] // 2
    lane = lax.broadcasted_iota(jnp.int32, (half, rows.shape[1]), 1)
    return jnp.where(lane < HD, rows[:half], rows[half:])


def make_bias(levels, bias_ref):
    row = lax.broadcasted_iota(jnp.int32, (BLK, DEPTH * BLK), 0)
    col = lax.broadcasted_iota(jnp.int32, (BLK, DEPTH * BLK), 1)
    limit = jnp.where(col < BLK, row + 1, levels * BLK)
    bias = jnp.where(col < limit, jnp.float32(0.0), jnp.float32(NEGATIVE))
    bias_ref[:BLK, :] = bias
    bias_ref[BLK:, :] = bias


class Levels:
    def __init__(self, slots_ref, sources, targets, arrivals):
        self.slots_ref = slots_ref
        self.pairs = tuple(zip(sources, targets))
        self.arrivals = arrivals

    def copies(self, slot):
        turn = slot % 2
        for level in range(DEPTH):
            start = pl.multiple_of(self.slots_ref[slot, level] * BLK, BLK)
            for index, (source, target) in enumerate(self.pairs):
                place = target.at[turn, level * BLK : (level + 1) * BLK, :]
                yield pltpu.make_async_copy(
                    source.at[pl.ds(start, BLK), :], place, self.arrivals.at[turn, index, level]
                )

    def start(self, slot):
        for copy in self.copies(slot):
            copy.start()

    def step(self, slot, count):
        @pl.when(slot + 1 < count)
        def ahead():
            self.start(slot + 1)

        for copy in self.copies(slot):
            copy.wait()


def forward_kernel(
    slots_ref, query_ref, key_source, value_source, mixed_ref, logsum_ref, key_here, value_here, bias_ref, arrivals
):
    width = query_ref.shape[1]
    count = query_ref.shape[0] // BLK
    levels = Levels(slots_ref, (key_source, value_source), (key_here, value_here), arrivals)
    levels.start(0)

    def one_slot(slot, carry):
        rows = pl.ds(pl.multiple_of(slot * BLK, BLK), BLK)
        make_bias(slots_ref[slot, DEPTH], bias_ref)
        levels.step(slot, count)
        turn = slot % 2
        lane = lax.broadcasted_iota(jnp.int32, (BLK, PAIR), 1)
        logsums = jnp.zeros((BLK, PAIR), jnp.float32)
        for pair in range(width // PAIR):
            cols = slice(pair * PAIR, (pair + 1) * PAIR)
            stacked = stack_heads(query_ref[rows, cols])
            scores = against(stacked, key_here[turn, :, cols]) + bias_ref[...]
            highest = jnp.max(scores, axis=-1, keepdims=True)
            raised = jnp.exp(scores - highest)
            total = jnp.sum(raised, axis=-1, keepdims=True)
            mixed = matmul(raised.astype(jnp.bfloat16), value_here[turn, :, cols]) / total
            mixed_ref[rows, cols] = unstack_heads(mixed).astype(jnp.bfloat16)
            logsum = highest + jnp.log(total)
            logsums = jnp.where(lane == 2 * pair, logsum[:BLK], logsums)
            logsums = jnp.where(lane == 2 * pair + 1, logsum[BLK:], logsums)
        logsum_ref[rows, :] = logsums
        return carry

    lax.fori_loop(0, count, one_slot, 0)


def backward_kernel(
    slots_ref,
    compact_ref,
    used_ref,
    seen_ref,
    query_ref,
    key_source,
    value_source,
    logsum_ref,
    mixed_ref,
    mixed_grad_ref,
    normed_source,
    weight_ref,
    query_grad_ref,
    grads_ref,
    lanes_ref,
    *refs,
):
    width = query_ref.shape[1]
    count = query_ref.shape[0] // BLK
    shared_refs = refs[:-11]
    key_here, value_here, bias_ref, normed_here, key_sums, value_sums = refs[-11:-5]
    stage, zero_block, arrivals, normed_arrivals, departures = refs[-5:]
    places = used_ref.shape[1] - 1
    used_count = used_ref[0, places]
    levels = Levels(slots_ref, (key_source, value_source), (key_here, value_here), arrivals)
    levels.start(0)

    def normed_copy(place):
        source = pl.ds(pl.multiple_of(used_ref[0, place] * BLK, BLK), BLK)
        target = normed_here.at[place * BLK : (place + 1) * BLK, :]
        return pltpu.make_async_copy(normed_source.at[source, :], target, normed_arrivals.at[place])

    for place in range(places):

        @pl.when(place < used_count)
        def fetch():
            normed_copy(place).start()

        @pl.when(place >= used_count)
        def clear():
            normed_here[place * BLK : (place + 1) * BLK, :] = jnp.zeros((BLK, normed_here.shape[1]), jnp.bfloat16)

    zero_block[...] = jnp.zeros_like(zero_block)
    for slot in range(count * len(shared_refs)):

        @pl.when(seen_ref[0, slot] == 0)
        def none():
            target = shared_refs[slot // count].at[slot % count]
            pltpu.make_async_copy(zero_block, target, departures.at[slot]).start()

    key_sums[...] = jnp.zeros_like(key_sums)
    value_sums[...] = jnp.zeros_like(value_sums)

    def one_slot(slot, carry):
        rows = pl.ds(pl.multiple_of(slot * BLK, BLK), BLK)
        make_bias(slots_ref[slot, DEPTH], bias_ref)
        levels.step(slot, count)
        turn = slot % 2
        for pair in range(width // PAIR):
            cols = slice(pair * PAIR, (pair + 1) * PAIR)
            stacked = stack_heads(query_ref[rows, cols])
            grad_rows = mixed_grad_ref[rows, cols]
            grad_stacked = stack_heads(grad_rows)
            products = grad_rows.astype(jnp.float32) * mixed_ref[rows, cols].astype(jnp.float32)
            row_dot = jnp.sum(stack_heads(products), axis=-1, keepdims=True)
            logsum = jnp.concatenate(
                [logsum_ref[rows, 2 * pair : 2 * pair + 1], logsum_ref[rows, 2 * pair + 1 : 2 * pair + 2]], axis=0
            )
            key_rows = key_here[turn, :, cols]
            shares = jnp.exp(against(stacked, key_rows) + bias_ref[...] - logsum)
            share_grad = against(grad_stacked, value_here[turn, :, cols])
            score_grad = (shares * (share_grad - row_dot)).astype(jnp.bfloat16)
            query_grad = unstack_heads(matmul(score_grad, key_rows)) * (HD ** (-0.5))
            query_grad_ref[rows, cols] = query_grad.astype(jnp.bfloat16)
            key_part = inner_rows(stacked, score_grad)
            value_part = inner_rows(grad_stacked, shares.astype(jnp.bfloat16))
            for level in range(DEPTH):
                start = pl.multiple_of(compact_ref[slot, level] * BLK, BLK)
                here = slice(level * BLK, (level + 1) * BLK)
                key_sums[cols, pl.ds(start, BLK)] += key_part[:, here]
                value_sums[cols, pl.ds(start, BLK)] += value_part[:, here]
        return carry

    lax.fori_loop(0, count, one_slot, 0)

    for place in range(places):

        @pl.when(place < used_count)
        def arrived():
            normed_copy(place).wait()

    grads_ref[...] = jnp.zeros_like(grads_ref)
    lanes_ref[...] = jnp.zeros_like(lanes_ref)

    def some_places(step, carry):
        here = pl.ds(pl.multiple_of(step * (PLACES * BLK), PLACES * BLK), PLACES * BLK)
        shared = None
        for part, part_sums in enumerate((key_sums, value_sums)):
            lines = slice(part * width, (part + 1) * width)
            block = part_sums[:, here]
            tiles = [block[:, start : start + BLK] for start in range(0, PLACES * BLK, BLK)]
            lanes_ref[lines, :] += functools.reduce(lambda left, right: left + right, tiles)
            block = block.astype(jnp.bfloat16)
            product = matmul(weight_ref[:, lines], block)
            shared = product if shared is None else shared + product
            grads_ref[lines, :] += matmul(block, normed_here[here, :])
        for index in range(PLACES):
            place = step * PLACES + index
            stage[place] = shared[:, index * BLK : (index + 1) * BLK].astype(jnp.bfloat16)

            slot = used_ref[0, jnp.minimum(place, used_count - 1)]
            for piece, shared_ref in enumerate(shared_refs):

                @pl.when((place < used_count) & (slot // count == piece))
                def leave():
                    target = shared_ref.at[slot - piece * count]
                    pltpu.make_async_copy(stage.at[place], target, departures.at[slot]).start()

        return carry

    lax.fori_loop(0, (used_count + PLACES - 1) // PLACES, some_places, 0)
    for slot in range(count * len(shared_refs)):
        target = shared_refs[slot // count].at[slot % count]
        pltpu.make_async_copy(zero_block, target, departures.at[slot]).wait()


def about(cost):
    return pl.CostEstimate(flops=int(cost * 1e9), bytes_accessed=int(cost * 1e6), transcendentals=0)


def in_vmem():
    return pl.BlockSpec(memory_space=pltpu.VMEM)


def in_smem():
    return pl.BlockSpec(memory_space=pltpu.SMEM)


def anywhere():
    return pl.BlockSpec(memory_space=pl.ANY)


def level_scratch(width):
    return [
        pltpu.VMEM((2, DEPTH * BLK, width), jnp.bfloat16),
        pltpu.VMEM((2, DEPTH * BLK, width), jnp.bfloat16),
        pltpu.VMEM((2 * BLK, DEPTH * BLK), jnp.float32),
    ]


def attend(slots, query_rows, key_group, value_group):
    rows, width = query_rows.shape
    return pl.pallas_call(
        forward_kernel,
        cost_estimate=about(18),
        out_shape=(
            jax.ShapeDtypeStruct((rows, width), jnp.bfloat16),
            jax.ShapeDtypeStruct((rows, PAIR), jnp.float32),
        ),
        in_specs=[in_smem(), in_vmem(), anywhere(), anywhere()],
        out_specs=(in_vmem(), in_vmem()),
        scratch_shapes=level_scratch(width) + [pltpu.SemaphoreType.DMA((2, 2, DEPTH))],
        compiler_params=pltpu.CompilerParams(vmem_limit_bytes=VMEM_BYTES),
    )(slots, query_rows, key_group, value_group)


def attend_backward(tables, query_rows, key_group, value_group, logsum, mixed, mixed_grad, normed_group, both_weight):
    rows, width = query_rows.shape
    blocks = normed_group.shape[0] // BLK
    pieces = normed_group.shape[0] // rows
    places = tables[2].shape[1] - 1
    return pl.pallas_call(
        backward_kernel,
        cost_estimate=about(32),
        out_shape=(
            jax.ShapeDtypeStruct((rows, width), jnp.bfloat16),
            jax.ShapeDtypeStruct((2 * width, width), jnp.float32),
            jax.ShapeDtypeStruct((2 * width, BLK), jnp.float32),
        )
        + (jax.ShapeDtypeStruct((rows // BLK, width, BLK), jnp.bfloat16),) * pieces,
        in_specs=[in_smem()] * 4
        + [in_vmem(), anywhere(), anywhere(), in_vmem(), in_vmem(), in_vmem(), anywhere(), in_vmem()],
        out_specs=(in_vmem(),) * 3 + (anywhere(),) * pieces,
        scratch_shapes=level_scratch(width)
        + [
            pltpu.VMEM((places * BLK, width), jnp.bfloat16),
            pltpu.VMEM((width, places * BLK), jnp.float32),
            pltpu.VMEM((width, places * BLK), jnp.float32),
            pltpu.VMEM((places, width, BLK), jnp.bfloat16),
            pltpu.VMEM((width, BLK), jnp.bfloat16),
            pltpu.SemaphoreType.DMA((2, 2, DEPTH)),
            pltpu.SemaphoreType.DMA((places,)),
            pltpu.SemaphoreType.DMA((blocks,)),
        ],
        compiler_params=pltpu.CompilerParams(vmem_limit_bytes=VMEM_BYTES),
    )(*tables, query_rows, key_group, value_group, logsum, mixed, mixed_grad, normed_group, both_weight)


def used_places(relative_slot, usable, group_blocks):
    block_count = relative_slot.shape[0]
    most = group_blocks // TREE_BLOCKS * TRUNK + 2 * block_count
    places = min(-(-most // PLACES) * PLACES, -(-group_blocks // PLACES) * PLACES)
    entries = jnp.arange(group_blocks, dtype=jnp.int32)
    hits = (relative_slot[:, :, None] == entries) & usable[:, :, None]
    seen = jnp.any(hits, axis=(0, 1))
    earlier = (entries[None, :] < entries[:, None]) & seen[None, :]
    place_of = jnp.sum(earlier, axis=1, dtype=jnp.int32)
    compact = jnp.sum(jnp.where(hits, place_of, jnp.int32(0)), axis=-1, dtype=jnp.int32)
    wanted = jnp.arange(places, dtype=jnp.int32)
    matches = (place_of[None, :] == wanted[:, None]) & seen[None, :]
    used = jnp.sum(jnp.where(matches, entries, jnp.int32(0)), axis=1, dtype=jnp.int32)
    seen = seen.astype(jnp.int32)
    used = jnp.concatenate([used, jnp.sum(seen, dtype=jnp.int32).reshape(1)])
    return compact, used.reshape(1, -1), seen.reshape(1, -1)


def project(pieces, vectors, key_weight, value_weight, group_rows, first, carried, query_weight=None):
    count = len(pieces)
    rows, width = pieces[0].shape
    weights = [key_weight, value_weight] + ([] if query_weight is None else [query_weight])
    extra = [] if carried is None else list(carried)

    def body(*refs):
        piece_refs, vectors_ref = refs[:count], refs[count]
        weight_refs = refs[count + 1 : count + 1 + len(weights)]
        outs = refs[count + 1 + len(weights) + len(extra) : -4]
        piece_here, made, arrivals, departures = refs[-4:]
        gain = vectors_ref[GAIN_ONE : GAIN_ONE + 1, :]
        shift = vectors_ref[SHIFT_ONE : SHIFT_ONE + 1, :]

        def fetch(index):
            return pltpu.make_async_copy(piece_refs[index], piece_here.at[index % 2], arrivals.at[index])

        def leave(index, kind):
            target = outs[kind].at[(first + index) * rows : (first + index + 1) * rows, :]
            return pltpu.make_async_copy(made.at[index % 2, kind], target, departures.at[index, kind])

        for index in range(min(2, count)):
            fetch(index).start()
        for index in range(count):
            fetch(index).wait()
            normed = normalize(piece_here[index % 2].astype(jnp.float32), gain, shift).astype(jnp.bfloat16)
            if index + 2 < count:
                fetch(index + 2).start()
            if index >= 2:
                for kind in range(3):
                    leave(index - 2, kind).wait()
            made[index % 2, 0] = normed
            leave(index, 0).start()
            for kind in (1, 2):
                made[index % 2, kind] = matmul(normed, weight_refs[kind - 1][...]).astype(jnp.bfloat16)
                leave(index, kind).start()
            if index == 0 and len(outs) > 3:
                outs[3][...] = normed
                queries = matmul(normed, weight_refs[2][...]).astype(jnp.bfloat16)
                outs[4][...] = (queries.astype(jnp.float32) * (HD ** (-0.5))).astype(jnp.bfloat16)
        for index in range(max(0, count - 2), count):
            for kind in range(3):
                leave(index, kind).wait()

    whole = jax.ShapeDtypeStruct((group_rows, width), jnp.bfloat16)
    own = [] if query_weight is None else [jax.ShapeDtypeStruct((rows, width), jnp.bfloat16)] * 2
    inputs = count + 1 + len(weights)
    return pl.pallas_call(
        body,
        cost_estimate=about(1 + 1.6 * count),
        out_shape=[whole] * 3 + own,
        in_specs=[anywhere()] * count + [in_vmem()] * (1 + len(weights)) + [anywhere()] * len(extra),
        out_specs=[anywhere()] * 3 + [in_vmem()] * len(own),
        scratch_shapes=[
            pltpu.VMEM((2, rows, width), jnp.bfloat16),
            pltpu.VMEM((2, 3, rows, width), jnp.bfloat16),
            pltpu.SemaphoreType.DMA((count,)),
            pltpu.SemaphoreType.DMA((count, 3)),
        ],
        input_output_aliases={inputs + index: index for index in range(len(extra))},
        compiler_params=pltpu.CompilerParams(vmem_limit_bytes=VMEM_BYTES),
    )(*pieces, vectors, *weights, *extra)


class Axis:
    def __init__(self, name, size, stride):
        self.name = name
        self.size = size
        self.stride = stride

    def position(self):
        return lax.axis_index(self.name) // self.stride % self.size

    def rotate(self, values, shift):
        pairs = []
        for index in range(lax.axis_size(self.name)):
            here = index // self.stride % self.size
            there = (here + shift) % self.size
            pairs.append((index, index + (there - here) * self.stride))
        return lax.ppermute(values, self.name, pairs)


def axes():
    seq = lax.axis_size("seq")
    dp = lax.axis_size("dp")
    along_z = 4 if seq % 4 == 0 else 1
    cores = 2 if dp % 2 == 0 else 1
    return (
        Axis("seq", along_z, seq // along_z),
        Axis("seq", seq // along_z, 1),
        Axis("dp", dp // cores, cores),
        Axis("dp", cores, 1),
    )


def relative_devices():
    axis_z, axis_x, axis_y, axis_core = axes()

    def place(axis, dim):
        back = lax.broadcasted_iota(jnp.int32, (axis_core.size, axis_y.size, axis_x.size, axis_z.size), dim)
        return (axis.position() - back + axis.size) % axis.size

    dp_index = place(axis_y, 1) * axis_core.size + place(axis_core, 0)
    seq_index = place(axis_z, 3) * axis_x.size + place(axis_x, 2)
    return (dp_index * lax.axis_size("seq") + seq_index).reshape(-1)


def scatter_devices():
    axis_z, axis_x, axis_y, axis_core = axes()
    entries = relative_devices().reshape(-1, axis_x.size, axis_z.size)
    return jnp.swapaxes(entries, 1, 2).reshape(-1)


def add_low(left_side, right_side):
    return (left_side.astype(jnp.float32) + right_side.astype(jnp.float32)).astype(jnp.bfloat16)


def add_three(first, second, third):
    total = first.astype(jnp.float32) + second.astype(jnp.float32) + third.astype(jnp.float32)
    return total.astype(jnp.bfloat16)


def tied(values, after):
    return lax.optimization_barrier((values, after))[0]


def ring_scatter(entry, axis):
    running = entry(axis.size - 1)
    for back in range(axis.size - 1, 0, -1):
        running = add_low(axis.rotate(running, -1), entry(back - 1))
    return running


GATE_B, DOWN_B, CARRY_B, GAIN_ONE, SHIFT_ONE, GAIN_TWO, SHIFT_TWO, UP_B = range(8)
VECTOR_ROWS = 16
MIDDLE_ROWS = 640


def pack_kernel(devices, place_ref, *refs):
    early_sources, late_sources, vector_refs, (early_ref, all_ref) = refs[:4], refs[4:8], refs[8:16], refs[16:]
    width = early_ref.shape[1]
    early_count = early_ref.shape[0]
    for target, start, sources in (
        (early_ref, 0, early_sources),
        (all_ref, 0, early_sources),
        (all_ref, early_count, late_sources),
    ):
        for source in sources:
            rows = source.shape[0]
            for column in range(0, source.shape[1], width):
                target[start : start + rows, :] = source[:, column : column + width]
                start += rows
    block = jnp.zeros((VECTOR_ROWS, width), jnp.float32)
    line = lax.broadcasted_iota(jnp.int32, block.shape, 0)
    for index, source in enumerate(vector_refs):
        count = source.shape[1]
        feature = lax.broadcasted_iota(jnp.int32, (count, width), 0) + place_ref[0] * count
        column = lax.broadcasted_iota(jnp.int32, (count, width), 1)
        for part in range(count * devices // width):
            spot = jnp.where(feature == column + part * width, jnp.float32(1.0), jnp.float32(0.0))
            spread = matmul(source[...], spot.astype(jnp.bfloat16))
            block += jnp.where(line == index + part, spread, jnp.float32(0.0))
    early_ref[early_count - VECTOR_ROWS :, :] = block.astype(jnp.bfloat16)
    all_ref[early_count - VECTOR_ROWS : early_count, :] = block.astype(jnp.bfloat16)


def unpack_kernel(place_ref, mine_ref, other_ref, query_ref, key_ref, value_ref, gate_ref, vectors_ref):
    half = mine_ref.shape[0]
    rows = (mine_ref.shape[1] - VECTOR_ROWS) // 4
    vectors = jnp.zeros(vectors_ref.shape, jnp.float32)
    for index in range(2 * half):
        source = (mine_ref if index < half else other_ref).at[index % half]
        target = pl.ds(pl.multiple_of(place_ref[index] * rows, rows), rows)
        for part, weight_ref in enumerate((query_ref, key_ref, value_ref, gate_ref)):
            weight_ref[target, :] = source[part * rows : (part + 1) * rows, :]
        vectors += source[4 * rows :, :].astype(jnp.float32)
    vectors_ref[...] = vectors


def unpack_late(place_ref, line_sources, plane_sources, output_ref, up_ref, down_ref, carry_ref):
    part_size = line_sources[0].shape[0]
    devices = part_size * len(line_sources)
    width = output_ref.shape[1]
    rows = output_ref.shape[0] // devices
    down_rows = down_ref.shape[0] // devices
    for index in range(devices):
        source = line_sources[index // part_size].at[index % part_size]
        target = pl.ds(pl.multiple_of(place_ref[0, index] * rows, rows), rows)
        output_ref[target, :] = source[:rows, :]
        for part in range(up_ref.shape[1] // width):
            up_ref[target, part * width : (part + 1) * width] = source[(part + 1) * rows : (part + 2) * rows, :]
        source = plane_sources[index // part_size].at[index % part_size]
        target = pl.ds(pl.multiple_of(place_ref[1, index] * down_rows, down_rows), down_rows)
        down_ref[target, :] = source[:down_rows, :]
        target = pl.ds(pl.multiple_of(place_ref[1, index] * rows, rows), rows)
        carry_ref[target, :] = source[down_rows:, :]


def spread_rows(place_ref, grad_ref, pack_refs, start, rows):
    size = pack_refs[0].shape[0]
    for index in range(size * len(pack_refs)):
        source = pl.ds(pl.multiple_of(place_ref[index] * rows, rows), rows)
        target = pack_refs[index // size].at[index % size]
        target[start : start + rows, :] = grad_ref[source, :].astype(jnp.bfloat16)


def middle_kernel(
    place_ref,
    attended_ref,
    input_ref,
    normed_ref,
    cotangent_ref,
    gate_weight_ref,
    vectors_ref,
    *refs,
):
    late_refs, refs = refs[:8], refs[8:]
    output_ref, middle_grad_ref, attended_grad_ref, gate_pre_ref, block_ref = refs[:5]
    pack_refs = refs[5:9]
    output_weight, up_weight, down_weight, carry_weight, hidden, up_pre_grads = refs[9:15]
    update_grads, normed_second, carry_pre_grads, branch_grads, up_grad, down_grad, square_grads = refs[15:]
    unpack_late(
        place_ref,
        late_refs[:4],
        late_refs[4:],
        output_weight,
        up_weight,
        down_weight,
        carry_weight,
    )
    width = output_ref.shape[1]
    hidden_width = up_weight.shape[1]
    wide = hidden_width // width

    def vector(line):
        return vectors_ref[line : line + 1, :]

    up_bias = jnp.concatenate([vector(UP_B + part) for part in range(wide)], axis=1)

    def column_lines(values):
        return jnp.sum(values.astype(jnp.float32), axis=0, keepdims=True)

    def some_rows(step, totals):
        rows = pl.ds(pl.multiple_of(step * MIDDLE_ROWS, MIDDLE_ROWS), MIDDLE_ROWS)
        gate_open = jax.nn.sigmoid(matmul(normed_ref[rows, :], gate_weight_ref[...]) + vector(GATE_B))
        branch = matmul(attended_ref[rows, :], output_weight[...])
        middle = input_ref[rows, :].astype(jnp.float32) + gate_open * branch
        centered = middle - jnp.mean(middle, axis=-1, keepdims=True)
        scale = lax.rsqrt(jnp.mean(centered * centered, axis=-1, keepdims=True) + EPSILON)
        hat = centered * scale
        normed = (hat * vector(GAIN_TWO) + vector(SHIFT_TWO)).astype(jnp.bfloat16)
        up_pre = matmul(normed, up_weight[...]) + up_bias
        up_open = jax.nn.sigmoid(up_pre)
        hidden_rows = (up_pre * up_open).astype(jnp.bfloat16)
        update = matmul(hidden_rows, down_weight[...]) + vector(DOWN_B)
        carry_open = jax.nn.sigmoid(matmul(normed, carry_weight[...]) + vector(CARRY_B))
        output_ref[rows, :] = (middle + carry_open * update).astype(jnp.bfloat16)

        grad_out = cotangent_ref[rows, :].astype(jnp.float32)
        update_grad = (carry_open * grad_out).astype(jnp.bfloat16)
        carry_pre_grad = (grad_out * update * carry_open * (1.0 - carry_open)).astype(jnp.bfloat16)
        slope = up_open * (1.0 + up_pre * (1.0 - up_open))
        up_pre_grad = (against(update_grad, down_weight[...]) * slope).astype(jnp.bfloat16)
        norm_grad = against(up_pre_grad, up_weight[...]) + against(carry_pre_grad, carry_weight[...])
        pull = norm_grad * vector(GAIN_TWO)
        middle_grad = grad_out + scale * (
            pull - jnp.mean(pull, axis=-1, keepdims=True) - hat * jnp.mean(pull * hat, axis=-1, keepdims=True)
        )
        middle_grad_ref[rows, :] = middle_grad
        branch_grad = (gate_open * middle_grad).astype(jnp.bfloat16)
        gate_pre_grad = (middle_grad * branch * gate_open * (1.0 - gate_open)).astype(jnp.bfloat16)
        gate_pre_ref[rows, :] = gate_pre_grad
        attended_grad_ref[rows, :] = against(branch_grad, output_weight[...]).astype(jnp.bfloat16)

        hidden[rows, :] = hidden_rows
        up_pre_grads[rows, :] = up_pre_grad
        update_grads[rows, :] = update_grad
        normed_second[rows, :] = normed
        carry_pre_grads[rows, :] = carry_pre_grad
        branch_grads[rows, :] = branch_grad
        lines = (gate_pre_grad, update_grad, carry_pre_grad, norm_grad * hat, norm_grad, up_pre_grad)
        return tuple(total + column_lines(line) for total, line in zip(totals, lines))

    start = (jnp.zeros((1, width), jnp.float32),) * 5 + (jnp.zeros((1, hidden_width), jnp.float32),)
    totals = lax.fori_loop(0, output_ref.shape[0] // MIDDLE_ROWS, some_rows, start)
    line = lax.broadcasted_iota(jnp.int32, block_ref.shape, 0)
    block = jnp.zeros(block_ref.shape, jnp.float32)
    for place, total in zip((GATE_B, DOWN_B, CARRY_B, GAIN_TWO, SHIFT_TWO), totals):
        block = jnp.where(line == place, total, block)
    for part in range(wide):
        block = jnp.where(line == UP_B + part, totals[5][:, part * width : (part + 1) * width], block)
    block_ref[...] = block

    target_ref = place_ref.at[2]
    rows = width // (4 * pack_refs[0].shape[0])
    place = 0
    for part in range(wide):
        grad = up_grad.at[part]
        grad[...] = inner_rows(normed_second[...], up_pre_grads[:, part * width : (part + 1) * width])
        spread_rows(target_ref, grad, pack_refs, place, rows)
        place += rows
    for part in range(wide):
        here = slice(part * width, (part + 1) * width)
        down_grad[here, :] = inner_rows(hidden[:, here], update_grads[...])
    spread_rows(target_ref, down_grad, pack_refs, place, wide * rows)
    place += wide * rows
    pairs = ((normed_second, carry_pre_grads), (attended_ref, branch_grads), (normed_ref, gate_pre_ref))
    for index, (left_ref, right_ref) in enumerate(pairs):
        grad = square_grads.at[index]
        grad[...] = inner_rows(left_ref[...], right_ref[...])
        spread_rows(target_ref, grad, pack_refs, place, rows)
        place += rows


def second_grads_kernel(
    place_ref,
    both_grads_ref,
    normed_ref,
    query_grad_ref,
    gate_pre_ref,
    lanes_ref,
    query_weight_ref,
    key_weight_ref,
    value_weight_ref,
    gate_weight_ref,
    vectors_ref,
    block_ref,
    *refs,
):
    pack_refs, grads = refs[:4], refs[4]
    width = pack_refs[0].shape[2]
    rows = width // (4 * pack_refs[0].shape[0])
    grads[0] = inner_rows(normed_ref[...], query_grad_ref[...])
    grads[1] = jnp.transpose(both_grads_ref[:width, :])
    grads[2] = jnp.transpose(both_grads_ref[width:, :])
    for index in range(3):
        spread_rows(place_ref, grads.at[index], pack_refs, index * rows, rows)
    gate_grad = inner_rows(normed_ref[...], gate_pre_ref[...])

    def line_sums(ref):
        return jnp.sum(ref[...].astype(jnp.float32), axis=0, keepdims=True)

    def as_line(column):
        return jnp.transpose(jnp.broadcast_to(column, (width, BLK)))[:1, :]

    lines = (
        line_sums(query_grad_ref),
        jnp.sum(jnp.transpose(lanes_ref[:width, :]), axis=0, keepdims=True),
        jnp.sum(jnp.transpose(lanes_ref[width:, :]), axis=0, keepdims=True),
        line_sums(gate_pre_ref),
    )
    weighted = jnp.zeros((width, width), jnp.float32)
    shifted = jnp.zeros((width, width), jnp.float32)
    weight_refs = (query_weight_ref, key_weight_ref, value_weight_ref, gate_weight_ref)
    for weight_ref, line, grad in zip(weight_refs, lines, (grads[0], grads[1], grads[2], gate_grad)):
        weight = weight_ref[...].astype(jnp.float32)
        weighted += weight * grad
        shifted += weight * line
    shift_line = as_line(jnp.sum(shifted, axis=1, keepdims=True))
    gain_line = (
        as_line(jnp.sum(weighted, axis=1, keepdims=True)) - vectors_ref[SHIFT_ONE : SHIFT_ONE + 1, :] * shift_line
    ) / vectors_ref[GAIN_ONE : GAIN_ONE + 1, :]
    place = lax.broadcasted_iota(jnp.int32, block_ref.shape, 0)
    block = jnp.where(place == GAIN_ONE, gain_line, block_ref[...])
    block = jnp.where(place == SHIFT_ONE, shift_line, block).astype(jnp.bfloat16)
    for pack_ref in pack_refs:
        for index in range(pack_ref.shape[0]):
            pack_ref[index, 3 * rows :, :] = block


def input_grad_kernel(input_ref, local_ref, middle_grad_ref, vectors_ref, *refs):
    shared_refs, output_ref = refs[:-1], refs[-1]
    blocks = [sum(ref[index].astype(jnp.float32) for ref in shared_refs) for index in range(shared_refs[0].shape[0])]
    shared = jnp.concatenate([jnp.transpose(block) for block in blocks])
    values = input_ref[...].astype(jnp.float32)
    centered = values - jnp.mean(values, axis=-1, keepdims=True)
    scale = lax.rsqrt(jnp.mean(centered * centered, axis=-1, keepdims=True) + EPSILON)
    hat = centered * scale
    pull = (local_ref[...] + shared) * vectors_ref[GAIN_ONE : GAIN_ONE + 1, :]
    output_ref[...] = middle_grad_ref[...] + scale * (
        pull - jnp.mean(pull, axis=-1, keepdims=True) - hat * jnp.mean(pull * hat, axis=-1, keepdims=True)
    )


def local_call(kernel, cost, outs, smem, args, scratch=()):
    return pl.pallas_call(
        kernel,
        cost_estimate=about(cost),
        out_shape=outs,
        in_specs=[in_smem()] + [in_vmem()] * len(args),
        out_specs=jax.tree.map(lambda out: in_vmem(), outs),
        scratch_shapes=list(scratch),
        compiler_params=pltpu.CompilerParams(vmem_limit_bytes=VMEM_BYTES),
    )(smem, *args)


def joined(pieces, axis):
    return pieces[0] if len(pieces) == 1 else jnp.concatenate(pieces, axis=axis)


def shards(
    inputs,
    cotangent,
    block_segment,
    segment_parent,
    query_weight,
    key_weight,
    value_weight,
    output_weight,
    gate_weight,
    gate_bias,
    up_weight,
    up_bias,
    down_weight,
    down_bias,
    carry_weight,
    carry_bias,
    first_gain,
    first_shift,
    second_gain,
    second_shift,
):
    width = inputs.shape[1]
    devices = lax.axis_size(BOTH)
    block_count = inputs.shape[0] // BLK
    group_blocks = block_segment.shape[0]

    axis_z, axis_x, axis_y, axis_core = axes()
    rows_each = query_weight.shape[0]
    sizes = (axis_z.size, axis_x.size, axis_y.size, axis_core.size)
    direct = sizes == (4, 2, 2, 2) and rows_each % 16 == 0
    places = relative_devices()
    targets = scatter_devices()
    device = lax.axis_index(BOTH)
    vectors = (gate_bias, down_bias, carry_bias, first_gain, first_shift, second_gain, second_shift, up_bias)
    early_set = (query_weight, key_weight, value_weight, gate_weight)
    late_set = (output_weight, up_weight, down_weight, carry_weight)
    low = jnp.bfloat16

    def struct(*shape, dtype=low):
        return jax.ShapeDtypeStruct(shape, dtype)

    def take(source, start, piece):
        rows = piece.shape[0]
        parts = piece.shape[1] // width
        blocks = [
            source[:, start + part * rows : start + (part + 1) * rows].reshape(devices * rows, width)
            for part in range(parts)
        ]
        return joined(blocks, 1), start + parts * rows

    def flat_rows(pieces):
        return [piece[:, start : start + width] for piece in pieces for start in range(0, piece.shape[1], width)]

    own_start = lax.axis_index("seq") * block_count
    own_segments = lax.dynamic_slice_in_dim(block_segment, own_start, block_count)
    ancestor_slot, usable = ancestor_slots(block_segment, segment_parent, own_segments)
    owner = ancestor_slot // block_count
    away_z = (axis_z.position() - owner // axis_x.size) % axis_z.size
    away_x = (axis_x.position() - owner % axis_x.size) % axis_x.size
    relative_slot = (away_z * axis_x.size + away_x) * block_count + ancestor_slot % block_count
    tables = used_places(relative_slot, usable, group_blocks)
    slots = jnp.concatenate(
        [relative_slot, jnp.sum(usable, axis=-1, keepdims=True, dtype=jnp.int32)], axis=-1
    )

    if direct:
        early_count = 4 * rows_each + VECTOR_ROWS
        late_count = sum(piece.shape[0] * piece.shape[1] // width for piece in late_set)
        early, both = local_call(
            functools.partial(pack_kernel, devices),
            0.1,
            (struct(early_count, width), struct(early_count + late_count, width)),
            device.reshape(1),
            early_set + late_set + tuple(vector.reshape(1, -1) for vector in vectors),
        )
        both_one = axis_z.rotate(both, 1)
        early_line = [axis_z.rotate(early, back) for back in range(2, 4)]
        x_zero = axis_x.rotate(inputs, 1)
        z_one = axis_z.rotate(inputs, 1)
        both_one, early_line, x_zero, z_one = lax.optimization_barrier((both_one, early_line, x_zero, z_one))
        early_line = [both_one[:early_count]] + list(early_line)
        late_line = [both[early_count:], both_one[early_count:]]
        z_two = axis_z.rotate(z_one, 1)
        x_one = axis_x.rotate(z_one, 1)
        early_line = jnp.stack([early] + list(early_line))
        early_other = axis_x.rotate(early_line, 1)
        late_line.append(axis_z.rotate(late_line[1], 1))
        early_other, z_two, x_one, late_line[2], slots, tables = lax.optimization_barrier(
            (early_other, z_two, x_one, late_line[2], slots, tables)
        )
        z_three = axis_z.rotate(z_two, 1)
        x_two = axis_x.rotate(z_two, 1)
        early_plane = jnp.stack([early_line, early_other])
        early_other = axis_y.rotate(early_plane, 1)
        late_line.append(axis_z.rotate(late_line[2], 1))
        early_other, z_three, x_two, late_line[3] = lax.optimization_barrier(
            (early_other, z_three, x_two, late_line[3])
        )
        x_three = axis_x.rotate(z_three, 1)
        early_all = jnp.stack([early_plane, early_other]).reshape(devices // 2, early_count, width)
        early_other = axis_core.rotate(early_all, 1)
        input_pieces = [[inputs, x_zero], [z_one, x_one], [z_two, x_two], [z_three, x_three]]
        square = struct(width, width)
        full_query, full_key, full_value, full_gate, vector_rows = local_call(
            unpack_kernel,
            3,
            (square, square, square, square, struct(VECTOR_ROWS, width, dtype=jnp.float32)),
            places,
            (early_all, early_other),
        )
        late_line, full_key = lax.optimization_barrier((late_line, full_key))
        late_half = late_count // 2
        late_x = jnp.stack([rows[:late_half] for rows in late_line])
        late_y = jnp.stack([rows[late_half:] for rows in late_line])
        late_x_other = axis_x.rotate(late_x, 1)
        late_y_other = axis_y.rotate(late_y, 1)
    else:
        early_rows = lax.all_gather(jnp.concatenate(early_set), BOTH)
        late_rows = lax.all_gather(jnp.concatenate(flat_rows(late_set)), BOTH)
        place = 0
        full_query, place = take(early_rows, place, query_weight)
        full_key, place = take(early_rows, place, key_weight)
        full_value, place = take(early_rows, place, value_weight)
        full_gate, place = take(early_rows, place, gate_weight)
        place = 0
        full_output, place = take(late_rows, place, output_weight)
        full_up, place = take(late_rows, place, up_weight)
        full_down, place = take(late_rows, place, down_weight)
        full_carry, place = take(late_rows, place, carry_weight)
        lines = [lax.all_gather(vector, BOTH, tiled=True).reshape(-1, width) for vector in vectors]
        lines = jnp.concatenate(lines).astype(jnp.float32)
        vector_rows = jnp.pad(lines, ((0, VECTOR_ROWS - lines.shape[0]), (0, 0)))
        input_pieces = []
        along_z = inputs
        for step_z in range(axis_z.size):
            along_x = along_z
            row = []
            for step_x in range(axis_x.size):
                row.append(along_x)
                along_x = axis_x.rotate(along_x, 1) if step_x + 1 < axis_x.size else None
            input_pieces.append(row)
            along_z = axis_z.rotate(along_z, 1) if step_z + 1 < axis_z.size else None

    both_weight = jnp.concatenate([full_key, full_value], axis=1)

    group_rows = group_blocks * BLK
    pieces = [piece for row in input_pieces for piece in row]
    near = len(pieces) - 1 if direct else len(pieces)
    *carried, normed_low, query_low = project(
        pieces[:near], vector_rows, full_key, full_value, group_rows, 0, None, full_query
    )
    if direct:
        late_y_other, late_x_other, x_three, carried, both_weight = lax.optimization_barrier(
            (late_y_other, late_x_other, pieces[near], carried, both_weight)
        )
        late_x = jnp.stack([late_x, late_x_other])
        late_y = jnp.stack([late_y, late_y_other])
        late_x_other = axis_y.rotate(late_x, 1)
        late_y_other = axis_x.rotate(late_y, 1)
        carried = project([x_three], vector_rows, full_key, full_value, group_rows, near, carried)
    normed_group, key_group, value_group = carried

    gate_b, down_b, carry_b, gain_one, shift_one, gain_two, shift_two = [vector_rows[line] for line in range(UP_B)]
    up_b = vector_rows[UP_B : UP_B + up_weight.shape[1] // width].reshape(-1)

    values_in = inputs.astype(jnp.float32)
    attended_low, logsum = attend(slots, query_low, key_group, value_group)

    if direct:
        attended_low, late_x_other, late_y_other = lax.optimization_barrier((attended_low, late_x_other, late_y_other))
        late_parts = []
        for mine in ((late_x, late_x_other), (late_y, late_y_other)):
            for piece in list(mine) + [axis_core.rotate(part, 1) for part in mine]:
                late_parts.append(piece.reshape(devices // 4, late_half, width))
        other_places = jnp.transpose(places.reshape(2, 2, 2, 4), (0, 2, 1, 3)).reshape(-1)
        rows = inputs.shape[0]
        first_rows = late_count + rows_each
        hidden_width = up_weight.shape[1]
        quarter = struct(devices // 4, first_rows, width)
        tall, short = pltpu.VMEM((rows, hidden_width), low), pltpu.VMEM((rows, width), low)
        output, middle_grad, attended_grad, gate_pre_grad, block, *first = local_call(
            middle_kernel,
            28,
            (
                struct(rows, width),
                struct(rows, width, dtype=jnp.float32),
                struct(rows, width),
                struct(rows, width),
                struct(VECTOR_ROWS, width, dtype=jnp.float32),
            )
            + (quarter,) * 4,
            jnp.stack([places, other_places, targets]),
            (
                attended_low,
                inputs,
                normed_low,
                cotangent,
                full_gate,
                vector_rows,
            )
            + tuple(late_parts),
            (
                pltpu.VMEM((width, width), low),
                pltpu.VMEM((width, hidden_width), low),
                pltpu.VMEM((hidden_width, width), low),
                pltpu.VMEM((width, width), low),
                tall,
                tall,
                short,
                short,
                short,
                short,
                pltpu.VMEM((hidden_width // width, width, width), jnp.float32),
                pltpu.VMEM((hidden_width, width), jnp.float32),
                pltpu.VMEM((3, width, width), jnp.float32),
            ),
        )
        first = [pack.reshape(4, 2, first_rows, width) for pack in first]
        first_core = [axis_core.rotate(first[2 + index], -1) for index in range(2)]
        first_keep, first_send = [add_low(first_core[index], first[index]) for index in range(2)]
        attended_grad, first_keep, first_send = lax.optimization_barrier((attended_grad, first_keep, first_send))
        first_arrived = axis_y.rotate(first_send, -1)
    else:
        gate_open = jax.nn.sigmoid(matmul(normed_low, full_gate) + gate_b)
        branch = matmul(attended_low, full_output)
        middle = values_in + gate_open * branch
        normed_second = normalize(middle, gain_two, shift_two).astype(jnp.bfloat16)
        up_pre = matmul(normed_second, full_up) + up_b
        up_sigmoid = jax.nn.sigmoid(up_pre)
        hidden_low = (up_pre * up_sigmoid).astype(jnp.bfloat16)
        update = matmul(hidden_low, full_down) + down_b
        carry_open = jax.nn.sigmoid(matmul(normed_second, full_carry) + carry_b)
        output = (middle + carry_open * update).astype(jnp.bfloat16)

        grad_out = cotangent.astype(jnp.float32)
        update_grad = (carry_open * grad_out).astype(jnp.bfloat16)
        carry_pre_grad = (grad_out * update * carry_open * (1.0 - carry_open)).astype(jnp.bfloat16)
        grad_down_bias = column_sums(update_grad)
        grad_carry_bias = column_sums(carry_pre_grad)
        silu_slope = up_sigmoid * (1.0 + up_pre * (1.0 - up_sigmoid))
        up_pre_grad = (against(update_grad, full_down) * silu_slope).astype(jnp.bfloat16)
        grad_up_bias = column_sums(up_pre_grad)
        second_norm_grad = against(up_pre_grad, full_up) + against(carry_pre_grad, full_carry)
        second_pull = jax.vjp(normalize, middle, gain_two, shift_two)[1]
        middle_part, grad_second_gain, grad_second_shift = second_pull(second_norm_grad)
        middle_grad = grad_out + middle_part

        branch_grad = (gate_open * middle_grad).astype(jnp.bfloat16)
        gate_pre_grad = (middle_grad * branch * gate_open * (1.0 - gate_open)).astype(jnp.bfloat16)
        grad_gate_bias = column_sums(gate_pre_grad)
        attended_grad = against(branch_grad, full_output).astype(jnp.bfloat16)
        zero_line = jnp.zeros((width,), jnp.float32)
        local_lines = (
            grad_gate_bias,
            grad_down_bias,
            grad_carry_bias,
            zero_line,
            zero_line,
            grad_second_gain,
            grad_second_shift,
            grad_up_bias,
        )
        block = jnp.concatenate([line.reshape(-1, width) for line in local_lines])
        block = jnp.pad(block, ((0, VECTOR_ROWS - block.shape[0]), (0, 0)))
    backward = attend_backward(
        (slots,) + tables,
        query_low,
        key_group,
        value_group,
        logsum,
        attended_low,
        attended_grad,
        normed_group,
        both_weight,
    )
    if direct:
        backward, first_arrived = lax.optimization_barrier((backward, first_arrived))

        def first_y(back):
            return add_low(first_arrived[back], first_keep[back])

        first_z = axis_z.rotate(first_y(3), -1)
    query_rows_grad, both_grads, lanes = backward[:3]

    shared_parts = backward[3:]

    if direct:
        second_rows = 3 * rows_each + VECTOR_ROWS
        quarter = struct(devices // 4, second_rows, width)
        second = local_call(
            second_grads_kernel,
            0.1,
            (quarter,) * 4,
            places,
            (
                both_grads,
                normed_low,
                query_rows_grad,
                gate_pre_grad,
                lanes,
                full_query,
                full_key,
                full_value,
                full_gate,
                vector_rows,
                block,
            ),
            (pltpu.VMEM((3, width, width), jnp.float32),),
        )
        second = [pack.reshape(2, 4, second_rows, width) for pack in second]
        barrier = lax.optimization_barrier
        first_z = axis_z.rotate(add_low(first_z, first_y(2)), -1)
        x_three = axis_x.rotate(shared_parts[7], -1)
        x_three, first_z, second = barrier((x_three, first_z, second))

        second_core = [axis_core.rotate(second[2 + index], -1) for index in range(2)]
        second_keep = add_low(second_core[0], second[0])
        second_arrived = axis_y.rotate(add_low(second_core[1], second[1]), -1)
        x_two = axis_x.rotate(tied(shared_parts[5], x_three), -1)
        z_three = axis_z.rotate(add_low(x_three, shared_parts[6]), -1)
        first_z = axis_z.rotate(add_low(first_z, first_y(1)), -1)
        x_two, z_three, first_z, second_arrived = barrier((x_two, z_three, first_z, second_arrived))

        second_y = add_low(second_arrived, second_keep)
        second_x = axis_x.rotate(second_y[1], -1)
        x_one = axis_x.rotate(tied(shared_parts[3], x_two), -1)
        z_two = axis_z.rotate(add_three(x_two, shared_parts[4], z_three), -1)
        x_one, z_two, second_x = barrier((x_one, z_two, second_x))

        first_half = add_low(first_z, first_y(0))
        first_x = axis_x.rotate(tied(first_half[1], x_one), -1)
        second_half = add_low(second_x, second_y[0])
        second_z = [axis_z.rotate(second_half[back], -back) for back in range(1, 4)]
        x_zero = axis_x.rotate(tied(shared_parts[1], x_one), -1)
        z_one = axis_z.rotate(add_three(x_one, shared_parts[2], z_two), -1)
        shared = (x_zero, z_one, shared_parts[0])
        first_sum = first_x.astype(jnp.float32) + first_half[0].astype(jnp.float32)
        second_sum = sum(piece.astype(jnp.float32) for piece in [second_half[0]] + second_z)
        weight_sum = jnp.concatenate([first_sum, second_sum])
    else:
        grad_key = jnp.transpose(both_grads[:width])
        grad_value = jnp.transpose(both_grads[width:])
        grad_query = inner_rows(normed_low, query_rows_grad)
        grad_gate = inner_rows(normed_low, gate_pre_grad)
        both_sums = jnp.sum(lanes, axis=1)
        weights = [weight.astype(jnp.float32) for weight in (full_query, full_key, full_value, full_gate)]
        line_sums = (column_sums(query_rows_grad), both_sums[:width], both_sums[width:], grad_gate_bias)
        shift_line = sum(jnp.sum(weight * line, axis=1) for weight, line in zip(weights, line_sums))
        weighted = sum(
            jnp.sum(weight * grad, axis=1)
            for weight, grad in zip(weights, (grad_query, grad_key, grad_value, grad_gate))
        )
        block = block.at[GAIN_ONE].set((weighted - shift_one * shift_line) / gain_one).at[SHIFT_ONE].set(shift_line)
        grads = (
            (inner_rows(normed_second, up_pre_grad), up_weight),
            (inner_rows(hidden_low, update_grad), down_weight),
            (inner_rows(normed_second, carry_pre_grad), carry_weight),
            (inner_rows(attended_low, branch_grad), output_weight),
            (grad_gate, gate_weight),
            (grad_query, query_weight),
            (grad_key, key_weight),
            (grad_value, value_weight),
        )
        pack = [
            cut.astype(low).reshape(devices, piece.shape[0], width)
            for grad, piece in grads
            for cut in flat_rows((grad,))
        ]
        pack.append(jnp.broadcast_to(block.astype(low), (devices, VECTOR_ROWS, width)))
        pack = jnp.concatenate(pack, axis=1)
        pack = jnp.pad(pack, ((0, 0), (0, -pack.shape[1] % 16), (0, 0)))
        weight_sum = lax.psum_scatter(pack, BOTH, scatter_dimension=0, tiled=True)[0].astype(jnp.float32)

        def over_x(step_z):
            return ring_scatter(lambda step_x: shared_parts[step_z * axis_x.size + step_x], axis_x)

        shared = (ring_scatter(over_x, axis_z),)

    def own(start, piece):
        rows = piece.shape[0]
        parts = piece.shape[1] // width
        blocks = [weight_sum[start + part * rows : start + (part + 1) * rows] for part in range(parts)]
        return joined(blocks, 1), start + parts * rows

    local_grad = against(query_rows_grad, full_query) + against(gate_pre_grad, full_gate)
    input_grad = pl.pallas_call(
        input_grad_kernel,
        cost_estimate=about(3),
        out_shape=struct(block_count * BLK, width, dtype=jnp.float32),
        compiler_params=pltpu.CompilerParams(vmem_limit_bytes=VMEM_BYTES),
    )(inputs, local_grad, middle_grad, vector_rows, *shared)

    place = 0
    own_up, place = own(place, up_weight)
    own_down, place = own(place, down_weight)
    own_carry, place = own(place, carry_weight)
    own_output, place = own(place, output_weight)
    own_gate, place = own(place, gate_weight)
    own_query, place = own(place, query_weight)
    own_key, place = own(place, key_weight)
    own_value, place = own(place, value_weight)
    vector_out = []
    for index, vector in enumerate(vectors):
        count = vector.shape[0]
        lines = weight_sum[place + index : place + index + count * devices // width].reshape(-1)
        vector_out.append(lax.dynamic_slice_in_dim(lines, device * count, count))
    gate_bg, down_bg, carry_bg, gain_one_g, shift_one_g, gain_two_g, shift_two_g, up_bg = vector_out
    return (
        output,
        input_grad,
        own_query,
        own_key,
        own_value,
        own_output,
        own_gate,
        gate_bg,
        own_up,
        up_bg,
        own_down,
        down_bg,
        own_carry,
        carry_bg,
        gain_one_g,
        shift_one_g,
        gain_two_g,
        shift_two_g,
    )


def solution(mesh):
    rows = P(BOTH, None)
    line = P(BOTH)
    matrix_or_line = (rows,) * 5 + (line, rows, line, rows, line, rows) + (line,) * 5
    return jax.shard_map(
        shards,
        mesh=mesh,
        in_specs=(rows, rows, P("dp"), P("dp")) + matrix_or_line,
        out_specs=(rows, rows) + matrix_or_line,
        check_vma=False,
    )
```

```python
import functools

import jax
import jax.numpy as jnp
from jax import lax
from jax.experimental import pallas as pl
from jax.experimental.pallas import tpu as pltpu
from jax.sharding import PartitionSpec as P

HD = 64
BLK = 128
DEPTH = 10
PAIR = 2 * HD
PLACES = 4
TREE_BLOCKS = 20
TRUNK = 8

EPSILON = 1e-05
NEGATIVE = -1e30
BOTH = ("dp", "seq")
VMEM_BYTES = 60 * 1024 * 1024


def normalize(values, norm_gain, norm_shift):
    center = values - jnp.mean(values, axis=-1, keepdims=True)
    spread = jnp.mean(center * center, axis=-1, keepdims=True)
    return center * lax.rsqrt(spread + EPSILON) * norm_gain + norm_shift


def matmul(left_side, right_side):
    return jnp.dot(left_side, right_side, preferred_element_type=jnp.float32)


def inner_rows(left_side, right_side):
    return lax.dot_general(
        left_side, right_side, (((0,), (0,)), ((), ())), preferred_element_type=jnp.float32
    )


def against(left_side, right_side):
    return lax.dot_general(
        left_side, right_side, (((1,), (1,)), ((), ())), preferred_element_type=jnp.float32
    )


def column_sums(values):
    return jnp.sum(values.astype(jnp.float32), axis=0)


def lookup(lookup_table, wanted):
    entries = jnp.arange(lookup_table.shape[0], dtype=jnp.int32)
    matches = wanted[..., None] == entries
    located = jnp.sum(jnp.where(matches, lookup_table, jnp.int32(0)), axis=-1, dtype=jnp.int32)
    return jnp.where(wanted >= 0, located, jnp.int32(-1))


def ancestor_slots(block_segment, segment_parent, own_segments):
    entries = jnp.arange(block_segment.shape[0], dtype=jnp.int32)
    placed = block_segment[None, :] == entries[:, None]
    slot_of = jnp.sum(jnp.where(placed, entries[None, :], jnp.int32(0)), axis=1, dtype=jnp.int32)
    current = own_segments
    lineage = []
    for depth_step in range(DEPTH):
        lineage.append(current)
        current = lookup(segment_parent, current)
    lineage = jnp.stack(lineage, axis=-1)
    usable = lineage >= 0
    return (jnp.where(usable, lookup(slot_of, lineage), jnp.int32(0)), usable)


def stack_heads(rows):
    lane = lax.broadcasted_iota(jnp.int32, rows.shape, 1)
    low = lane < HD
    zero = jnp.zeros_like(rows)
    return jnp.concatenate([jnp.where(low, rows, zero), jnp.where(low, zero, rows)], axis=0)


def unstack_heads(rows):
    half = rows.shape[0] // 2
    lane = lax.broadcasted_iota(jnp.int32, (half, rows.shape[1]), 1)
    return jnp.where(lane < HD, rows[:half], rows[half:])


def make_bias(levels, bias_ref):
    row = lax.broadcasted_iota(jnp.int32, (BLK, DEPTH * BLK), 0)
    col = lax.broadcasted_iota(jnp.int32, (BLK, DEPTH * BLK), 1)
    limit = jnp.where(col < BLK, row + 1, levels * BLK)
    bias = jnp.where(col < limit, jnp.float32(0.0), jnp.float32(NEGATIVE))
    bias_ref[:BLK, :] = bias
    bias_ref[BLK:, :] = bias


class Levels:
    def __init__(self, slots_ref, sources, targets, arrivals):
        self.slots_ref = slots_ref
        self.pairs = tuple(zip(sources, targets))
        self.arrivals = arrivals

    def copies(self, slot):
        turn = slot % 2
        for level in range(DEPTH):
            start = pl.multiple_of(self.slots_ref[slot, level] * BLK, BLK)
            for index, (source, target) in enumerate(self.pairs):
                place = target.at[turn, level * BLK : (level + 1) * BLK, :]
                yield pltpu.make_async_copy(
                    source.at[pl.ds(start, BLK), :], place, self.arrivals.at[turn, index, level]
                )

    def start(self, slot):
        for copy in self.copies(slot):
            copy.start()

    def step(self, slot, count):
        @pl.when(slot + 1 < count)
        def ahead():
            self.start(slot + 1)

        for copy in self.copies(slot):
            copy.wait()


def forward_kernel(
    slots_ref, query_ref, key_source, value_source, mixed_ref, logsum_ref, key_here, value_here, bias_ref, arrivals
):
    width = query_ref.shape[1]
    count = query_ref.shape[0] // BLK
    levels = Levels(slots_ref, (key_source, value_source), (key_here, value_here), arrivals)
    levels.start(0)

    def one_slot(slot, carry):
        rows = pl.ds(pl.multiple_of(slot * BLK, BLK), BLK)
        make_bias(slots_ref[slot, DEPTH], bias_ref)
        levels.step(slot, count)
        turn = slot % 2
        lane = lax.broadcasted_iota(jnp.int32, (BLK, PAIR), 1)
        logsums = jnp.zeros((BLK, PAIR), jnp.float32)
        for pair in range(width // PAIR):
            cols = slice(pair * PAIR, (pair + 1) * PAIR)
            stacked = stack_heads(query_ref[rows, cols])
            scores = against(stacked, key_here[turn, :, cols]) + bias_ref[...]
            highest = jnp.max(scores, axis=-1, keepdims=True)
            raised = jnp.exp(scores - highest)
            total = jnp.sum(raised, axis=-1, keepdims=True)
            mixed = matmul(raised.astype(jnp.bfloat16), value_here[turn, :, cols]) / total
            mixed_ref[rows, cols] = unstack_heads(mixed).astype(jnp.bfloat16)
            logsum = highest + jnp.log(total)
            logsums = jnp.where(lane == 2 * pair, logsum[:BLK], logsums)
            logsums = jnp.where(lane == 2 * pair + 1, logsum[BLK:], logsums)
        logsum_ref[rows, :] = logsums
        return carry

    lax.fori_loop(0, count, one_slot, 0)


def backward_kernel(
    slots_ref,
    compact_ref,
    used_ref,
    seen_ref,
    query_ref,
    key_source,
    value_source,
    logsum_ref,
    mixed_ref,
    mixed_grad_ref,
    normed_source,
    weight_ref,
    query_grad_ref,
    grads_ref,
    lanes_ref,
    *refs,
):
    width = query_ref.shape[1]
    count = query_ref.shape[0] // BLK
    shared_refs = refs[:-11]
    key_here, value_here, bias_ref, normed_here, key_sums, value_sums = refs[-11:-5]
    stage, zero_block, arrivals, normed_arrivals, departures = refs[-5:]
    places = used_ref.shape[1] - 1
    used_count = used_ref[0, places]
    levels = Levels(slots_ref, (key_source, value_source), (key_here, value_here), arrivals)
    levels.start(0)

    def normed_copy(place):
        source = pl.ds(pl.multiple_of(used_ref[0, place] * BLK, BLK), BLK)
        target = normed_here.at[place * BLK : (place + 1) * BLK, :]
        return pltpu.make_async_copy(normed_source.at[source, :], target, normed_arrivals.at[place])

    for place in range(places):

        @pl.when(place < used_count)
        def fetch():
            normed_copy(place).start()

        @pl.when(place >= used_count)
        def clear():
            normed_here[place * BLK : (place + 1) * BLK, :] = jnp.zeros((BLK, normed_here.shape[1]), jnp.bfloat16)

    zero_block[...] = jnp.zeros_like(zero_block)
    for slot in range(count * len(shared_refs)):

        @pl.when(seen_ref[0, slot] == 0)
        def none():
            target = shared_refs[slot // count].at[slot % count]
            pltpu.make_async_copy(zero_block, target, departures.at[slot]).start()

    key_sums[...] = jnp.zeros_like(key_sums)
    value_sums[...] = jnp.zeros_like(value_sums)

    def one_slot(slot, carry):
        rows = pl.ds(pl.multiple_of(slot * BLK, BLK), BLK)
        make_bias(slots_ref[slot, DEPTH], bias_ref)
        levels.step(slot, count)
        turn = slot % 2
        for pair in range(width // PAIR):
            cols = slice(pair * PAIR, (pair + 1) * PAIR)
            stacked = stack_heads(query_ref[rows, cols])
            grad_rows = mixed_grad_ref[rows, cols]
            grad_stacked = stack_heads(grad_rows)
            products = grad_rows.astype(jnp.float32) * mixed_ref[rows, cols].astype(jnp.float32)
            row_dot = jnp.sum(stack_heads(products), axis=-1, keepdims=True)
            logsum = jnp.concatenate(
                [logsum_ref[rows, 2 * pair : 2 * pair + 1], logsum_ref[rows, 2 * pair + 1 : 2 * pair + 2]], axis=0
            )
            key_rows = key_here[turn, :, cols]
            shares = jnp.exp(against(stacked, key_rows) + bias_ref[...] - logsum)
            share_grad = against(grad_stacked, value_here[turn, :, cols])
            score_grad = (shares * (share_grad - row_dot)).astype(jnp.bfloat16)
            query_grad = unstack_heads(matmul(score_grad, key_rows)) * (HD ** (-0.5))
            query_grad_ref[rows, cols] = query_grad.astype(jnp.bfloat16)
            key_part = inner_rows(stacked, score_grad)
            value_part = inner_rows(grad_stacked, shares.astype(jnp.bfloat16))
            for level in range(DEPTH):
                start = pl.multiple_of(compact_ref[slot, level] * BLK, BLK)
                here = slice(level * BLK, (level + 1) * BLK)
                key_sums[cols, pl.ds(start, BLK)] += key_part[:, here]
                value_sums[cols, pl.ds(start, BLK)] += value_part[:, here]
        return carry

    lax.fori_loop(0, count, one_slot, 0)

    for place in range(places):

        @pl.when(place < used_count)
        def arrived():
            normed_copy(place).wait()

    grads_ref[...] = jnp.zeros_like(grads_ref)
    lanes_ref[...] = jnp.zeros_like(lanes_ref)

    def some_places(step, carry):
        here = pl.ds(pl.multiple_of(step * (PLACES * BLK), PLACES * BLK), PLACES * BLK)
        shared = None
        for part, part_sums in enumerate((key_sums, value_sums)):
            lines = slice(part * width, (part + 1) * width)
            block = part_sums[:, here]
            tiles = [block[:, start : start + BLK] for start in range(0, PLACES * BLK, BLK)]
            lanes_ref[lines, :] += functools.reduce(lambda left, right: left + right, tiles)
            block = block.astype(jnp.bfloat16)
            product = matmul(weight_ref[:, lines], block)
            shared = product if shared is None else shared + product
            grads_ref[lines, :] += matmul(block, normed_here[here, :])
        for index in range(PLACES):
            place = step * PLACES + index
            stage[place] = shared[:, index * BLK : (index + 1) * BLK].astype(jnp.bfloat16)

            slot = used_ref[0, jnp.minimum(place, used_count - 1)]
            for piece, shared_ref in enumerate(shared_refs):

                @pl.when((place < used_count) & (slot // count == piece))
                def leave():
                    target = shared_ref.at[slot - piece * count]
                    pltpu.make_async_copy(stage.at[place], target, departures.at[slot]).start()

        return carry

    lax.fori_loop(0, (used_count + PLACES - 1) // PLACES, some_places, 0)
    for slot in range(count * len(shared_refs)):
        target = shared_refs[slot // count].at[slot % count]
        pltpu.make_async_copy(zero_block, target, departures.at[slot]).wait()


def about(cost):
    return pl.CostEstimate(flops=int(cost * 1e9), bytes_accessed=int(cost * 1e6), transcendentals=0)


def in_vmem():
    return pl.BlockSpec(memory_space=pltpu.VMEM)


def in_smem():
    return pl.BlockSpec(memory_space=pltpu.SMEM)


def anywhere():
    return pl.BlockSpec(memory_space=pl.ANY)


def level_scratch(width):
    return [
        pltpu.VMEM((2, DEPTH * BLK, width), jnp.bfloat16),
        pltpu.VMEM((2, DEPTH * BLK, width), jnp.bfloat16),
        pltpu.VMEM((2 * BLK, DEPTH * BLK), jnp.float32),
    ]


def attend(slots, query_rows, key_group, value_group):
    rows, width = query_rows.shape
    return pl.pallas_call(
        forward_kernel,
        cost_estimate=about(18),
        out_shape=(
            jax.ShapeDtypeStruct((rows, width), jnp.bfloat16),
            jax.ShapeDtypeStruct((rows, PAIR), jnp.float32),
        ),
        in_specs=[in_smem(), in_vmem(), anywhere(), anywhere()],
        out_specs=(in_vmem(), in_vmem()),
        scratch_shapes=level_scratch(width) + [pltpu.SemaphoreType.DMA((2, 2, DEPTH))],
        compiler_params=pltpu.CompilerParams(vmem_limit_bytes=VMEM_BYTES),
    )(slots, query_rows, key_group, value_group)


def attend_backward(tables, query_rows, key_group, value_group, logsum, mixed, mixed_grad, normed_group, both_weight):
    rows, width = query_rows.shape
    blocks = normed_group.shape[0] // BLK
    pieces = normed_group.shape[0] // rows
    places = tables[2].shape[1] - 1
    return pl.pallas_call(
        backward_kernel,
        cost_estimate=about(32),
        out_shape=(
            jax.ShapeDtypeStruct((rows, width), jnp.bfloat16),
            jax.ShapeDtypeStruct((2 * width, width), jnp.float32),
            jax.ShapeDtypeStruct((2 * width, BLK), jnp.float32),
        )
        + (jax.ShapeDtypeStruct((rows // BLK, width, BLK), jnp.bfloat16),) * pieces,
        in_specs=[in_smem()] * 4
        + [in_vmem(), anywhere(), anywhere(), in_vmem(), in_vmem(), in_vmem(), anywhere(), in_vmem()],
        out_specs=(in_vmem(),) * 3 + (anywhere(),) * pieces,
        scratch_shapes=level_scratch(width)
        + [
            pltpu.VMEM((places * BLK, width), jnp.bfloat16),
            pltpu.VMEM((width, places * BLK), jnp.float32),
            pltpu.VMEM((width, places * BLK), jnp.float32),
            pltpu.VMEM((places, width, BLK), jnp.bfloat16),
            pltpu.VMEM((width, BLK), jnp.bfloat16),
            pltpu.SemaphoreType.DMA((2, 2, DEPTH)),
            pltpu.SemaphoreType.DMA((places,)),
            pltpu.SemaphoreType.DMA((blocks,)),
        ],
        compiler_params=pltpu.CompilerParams(vmem_limit_bytes=VMEM_BYTES),
    )(*tables, query_rows, key_group, value_group, logsum, mixed, mixed_grad, normed_group, both_weight)


def used_places(relative_slot, usable, group_blocks):
    block_count = relative_slot.shape[0]
    most = group_blocks // TREE_BLOCKS * TRUNK + 2 * block_count
    places = min(-(-most // PLACES) * PLACES, -(-group_blocks // PLACES) * PLACES)
    entries = jnp.arange(group_blocks, dtype=jnp.int32)
    hits = (relative_slot[:, :, None] == entries) & usable[:, :, None]
    seen = jnp.any(hits, axis=(0, 1))
    earlier = (entries[None, :] < entries[:, None]) & seen[None, :]
    place_of = jnp.sum(earlier, axis=1, dtype=jnp.int32)
    compact = jnp.sum(jnp.where(hits, place_of, jnp.int32(0)), axis=-1, dtype=jnp.int32)
    wanted = jnp.arange(places, dtype=jnp.int32)
    matches = (place_of[None, :] == wanted[:, None]) & seen[None, :]
    used = jnp.sum(jnp.where(matches, entries, jnp.int32(0)), axis=1, dtype=jnp.int32)
    seen = seen.astype(jnp.int32)
    used = jnp.concatenate([used, jnp.sum(seen, dtype=jnp.int32).reshape(1)])
    return compact, used.reshape(1, -1), seen.reshape(1, -1)


def project(pieces, vectors, key_weight, value_weight, group_rows, first, carried, query_weight=None):
    count = len(pieces)
    rows, width = pieces[0].shape
    weights = [key_weight, value_weight] + ([] if query_weight is None else [query_weight])
    extra = [] if carried is None else list(carried)

    def body(*refs):
        piece_refs, vectors_ref = refs[:count], refs[count]
        weight_refs = refs[count + 1 : count + 1 + len(weights)]
        outs = refs[count + 1 + len(weights) + len(extra) : -4]
        piece_here, made, arrivals, departures = refs[-4:]
        gain = vectors_ref[GAIN_ONE : GAIN_ONE + 1, :]
        shift = vectors_ref[SHIFT_ONE : SHIFT_ONE + 1, :]

        def fetch(index):
            return pltpu.make_async_copy(piece_refs[index], piece_here.at[index % 2], arrivals.at[index])

        def leave(index, kind):
            target = outs[kind].at[(first + index) * rows : (first + index + 1) * rows, :]
            return pltpu.make_async_copy(made.at[index % 2, kind], target, departures.at[index, kind])

        for index in range(min(2, count)):
            fetch(index).start()
        for index in range(count):
            fetch(index).wait()
            normed = normalize(piece_here[index % 2].astype(jnp.float32), gain, shift).astype(jnp.bfloat16)
            if index + 2 < count:
                fetch(index + 2).start()
            if index >= 2:
                for kind in range(3):
                    leave(index - 2, kind).wait()
            made[index % 2, 0] = normed
            leave(index, 0).start()
            for kind in (1, 2):
                made[index % 2, kind] = matmul(normed, weight_refs[kind - 1][...]).astype(jnp.bfloat16)
                leave(index, kind).start()
            if index == 0 and len(outs) > 3:
                outs[3][...] = normed
                queries = matmul(normed, weight_refs[2][...]).astype(jnp.bfloat16)
                outs[4][...] = (queries.astype(jnp.float32) * (HD ** (-0.5))).astype(jnp.bfloat16)
        for index in range(max(0, count - 2), count):
            for kind in range(3):
                leave(index, kind).wait()

    whole = jax.ShapeDtypeStruct((group_rows, width), jnp.bfloat16)
    own = [] if query_weight is None else [jax.ShapeDtypeStruct((rows, width), jnp.bfloat16)] * 2
    inputs = count + 1 + len(weights)
    return pl.pallas_call(
        body,
        cost_estimate=about(1 + 1.6 * count),
        out_shape=[whole] * 3 + own,
        in_specs=[anywhere()] * count + [in_vmem()] * (1 + len(weights)) + [anywhere()] * len(extra),
        out_specs=[anywhere()] * 3 + [in_vmem()] * len(own),
        scratch_shapes=[
            pltpu.VMEM((2, rows, width), jnp.bfloat16),
            pltpu.VMEM((2, 3, rows, width), jnp.bfloat16),
            pltpu.SemaphoreType.DMA((count,)),
            pltpu.SemaphoreType.DMA((count, 3)),
        ],
        input_output_aliases={inputs + index: index for index in range(len(extra))},
        compiler_params=pltpu.CompilerParams(vmem_limit_bytes=VMEM_BYTES),
    )(*pieces, vectors, *weights, *extra)


class Axis:
    def __init__(self, name, size, stride):
        self.name = name
        self.size = size
        self.stride = stride

    def position(self):
        return lax.axis_index(self.name) // self.stride % self.size

    def rotate(self, values, shift):
        pairs = []
        for index in range(lax.axis_size(self.name)):
            here = index // self.stride % self.size
            there = (here + shift) % self.size
            pairs.append((index, index + (there - here) * self.stride))
        return lax.ppermute(values, self.name, pairs)


def axes():
    seq = lax.axis_size("seq")
    dp = lax.axis_size("dp")
    along_z = 4 if seq % 4 == 0 else 1
    cores = 2 if dp % 2 == 0 else 1
    return (
        Axis("seq", along_z, seq // along_z),
        Axis("seq", seq // along_z, 1),
        Axis("dp", dp // cores, cores),
        Axis("dp", cores, 1),
    )


def relative_devices():
    axis_z, axis_x, axis_y, axis_core = axes()

    def place(axis, dim):
        back = lax.broadcasted_iota(jnp.int32, (axis_core.size, axis_y.size, axis_x.size, axis_z.size), dim)
        return (axis.position() - back + axis.size) % axis.size

    dp_index = place(axis_y, 1) * axis_core.size + place(axis_core, 0)
    seq_index = place(axis_z, 3) * axis_x.size + place(axis_x, 2)
    return (dp_index * lax.axis_size("seq") + seq_index).reshape(-1)


def scatter_devices():
    axis_z, axis_x, axis_y, axis_core = axes()
    entries = relative_devices().reshape(-1, axis_x.size, axis_z.size)
    return jnp.swapaxes(entries, 1, 2).reshape(-1)


def add_low(left_side, right_side):
    return (left_side.astype(jnp.float32) + right_side.astype(jnp.float32)).astype(jnp.bfloat16)


def add_three(first, second, third):
    total = first.astype(jnp.float32) + second.astype(jnp.float32) + third.astype(jnp.float32)
    return total.astype(jnp.bfloat16)


def tied(values, after):
    return lax.optimization_barrier((values, after))[0]


def ring_scatter(entry, axis):
    running = entry(axis.size - 1)
    for back in range(axis.size - 1, 0, -1):
        running = add_low(axis.rotate(running, -1), entry(back - 1))
    return running


GATE_B, DOWN_B, CARRY_B, GAIN_ONE, SHIFT_ONE, GAIN_TWO, SHIFT_TWO, UP_B = range(8)
VECTOR_ROWS = 16
MIDDLE_ROWS = 640


def pack_kernel(devices, place_ref, *refs):
    early_sources, late_sources, vector_refs, (early_ref, all_ref) = refs[:4], refs[4:8], refs[8:16], refs[16:]
    width = early_ref.shape[1]
    early_count = early_ref.shape[0]
    for target, start, sources in (
        (early_ref, 0, early_sources),
        (all_ref, 0, early_sources),
        (all_ref, early_count, late_sources),
    ):
        for source in sources:
            rows = source.shape[0]
            for column in range(0, source.shape[1], width):
                target[start : start + rows, :] = source[:, column : column + width]
                start += rows
    block = jnp.zeros((VECTOR_ROWS, width), jnp.float32)
    line = lax.broadcasted_iota(jnp.int32, block.shape, 0)
    for index, source in enumerate(vector_refs):
        count = source.shape[1]
        feature = lax.broadcasted_iota(jnp.int32, (count, width), 0) + place_ref[0] * count
        column = lax.broadcasted_iota(jnp.int32, (count, width), 1)
        for part in range(count * devices // width):
            spot = jnp.where(feature == column + part * width, jnp.float32(1.0), jnp.float32(0.0))
            spread = matmul(source[...], spot.astype(jnp.bfloat16))
            block += jnp.where(line == index + part, spread, jnp.float32(0.0))
    early_ref[early_count - VECTOR_ROWS :, :] = block.astype(jnp.bfloat16)
    all_ref[early_count - VECTOR_ROWS : early_count, :] = block.astype(jnp.bfloat16)


def unpack_kernel(place_ref, *refs):
    sources, (query_ref, key_ref, value_ref, gate_ref, vectors_ref) = refs[:4], refs[4:]
    size = sources[0].shape[0]
    rows = (sources[0].shape[1] - VECTOR_ROWS) // 4
    vectors = jnp.zeros(vectors_ref.shape, jnp.float32)
    for index in range(len(sources) * size):
        source = sources[index // size].at[index % size]
        target = pl.ds(pl.multiple_of(place_ref[index] * rows, rows), rows)
        for part, weight_ref in enumerate((query_ref, key_ref, value_ref, gate_ref)):
            weight_ref[target, :] = source[part * rows : (part + 1) * rows, :]
        vectors += source[4 * rows :, :].astype(jnp.float32)
    vectors_ref[...] = vectors


def unpack_late(place_ref, line_sources, plane_sources, output_ref, up_ref, down_ref, carry_ref):
    part_size = line_sources[0].shape[0]
    devices = part_size * len(line_sources)
    width = output_ref.shape[1]
    rows = output_ref.shape[0] // devices
    down_rows = down_ref.shape[0] // devices
    for index in range(devices):
        source = line_sources[index // part_size].at[index % part_size]
        target = pl.ds(pl.multiple_of(place_ref[0, index] * rows, rows), rows)
        output_ref[target, :] = source[:rows, :]
        for part in range(up_ref.shape[1] // width):
            up_ref[target, part * width : (part + 1) * width] = source[(part + 1) * rows : (part + 2) * rows, :]
        source = plane_sources[index // part_size].at[index % part_size]
        target = pl.ds(pl.multiple_of(place_ref[1, index] * down_rows, down_rows), down_rows)
        down_ref[target, :] = source[:down_rows, :]
        target = pl.ds(pl.multiple_of(place_ref[1, index] * rows, rows), rows)
        carry_ref[target, :] = source[down_rows:, :]


def spread_rows(place_ref, grad_ref, pack_refs, start, rows):
    size = pack_refs[0].shape[0]
    for index in range(size * len(pack_refs)):
        source = pl.ds(pl.multiple_of(place_ref[index] * rows, rows), rows)
        target = pack_refs[index // size].at[index % size]
        target[start : start + rows, :] = grad_ref[source, :].astype(jnp.bfloat16)


def middle_kernel(
    place_ref,
    attended_ref,
    input_ref,
    normed_ref,
    cotangent_ref,
    gate_weight_ref,
    vectors_ref,
    *refs,
):
    late_refs, refs = refs[:8], refs[8:]
    block_ref, row_targets, pack_targets, refs = refs[0], refs[1:5], refs[5:9], refs[9:]
    output_weight, up_weight, down_weight, carry_weight, hidden, up_pre_grads = refs[:6]
    update_grads, normed_second, carry_pre_grads, branch_grads, up_grad, down_grad, square_grads = refs[6:13]
    row_refs, pack_refs, row_departures, pack_departures = refs[13:17], refs[17:21], refs[21], refs[22]
    output_ref, middle_grad_ref, attended_grad_ref, gate_pre_ref = row_refs
    unpack_late(
        place_ref,
        late_refs[:4],
        late_refs[4:],
        output_weight,
        up_weight,
        down_weight,
        carry_weight,
    )
    width = output_ref.shape[1]
    hidden_width = up_weight.shape[1]
    wide = hidden_width // width

    def vector(line):
        return vectors_ref[line : line + 1, :]

    up_bias = jnp.concatenate([vector(UP_B + part) for part in range(wide)], axis=1)

    def column_lines(values):
        return jnp.sum(values.astype(jnp.float32), axis=0, keepdims=True)

    def some_rows(step, totals):
        rows = pl.ds(pl.multiple_of(step * MIDDLE_ROWS, MIDDLE_ROWS), MIDDLE_ROWS)
        gate_open = jax.nn.sigmoid(matmul(normed_ref[rows, :], gate_weight_ref[...]) + vector(GATE_B))
        branch = matmul(attended_ref[rows, :], output_weight[...])
        middle = input_ref[rows, :].astype(jnp.float32) + gate_open * branch
        centered = middle - jnp.mean(middle, axis=-1, keepdims=True)
        scale = lax.rsqrt(jnp.mean(centered * centered, axis=-1, keepdims=True) + EPSILON)
        hat = centered * scale
        normed = (hat * vector(GAIN_TWO) + vector(SHIFT_TWO)).astype(jnp.bfloat16)
        up_pre = matmul(normed, up_weight[...]) + up_bias
        up_open = jax.nn.sigmoid(up_pre)
        hidden_rows = (up_pre * up_open).astype(jnp.bfloat16)
        update = matmul(hidden_rows, down_weight[...]) + vector(DOWN_B)
        carry_open = jax.nn.sigmoid(matmul(normed, carry_weight[...]) + vector(CARRY_B))
        output_ref[rows, :] = (middle + carry_open * update).astype(jnp.bfloat16)

        grad_out = cotangent_ref[rows, :].astype(jnp.float32)
        update_grad = (carry_open * grad_out).astype(jnp.bfloat16)
        carry_pre_grad = (grad_out * update * carry_open * (1.0 - carry_open)).astype(jnp.bfloat16)
        slope = up_open * (1.0 + up_pre * (1.0 - up_open))
        up_pre_grad = (against(update_grad, down_weight[...]) * slope).astype(jnp.bfloat16)
        norm_grad = against(up_pre_grad, up_weight[...]) + against(carry_pre_grad, carry_weight[...])
        pull = norm_grad * vector(GAIN_TWO)
        middle_grad = grad_out + scale * (
            pull - jnp.mean(pull, axis=-1, keepdims=True) - hat * jnp.mean(pull * hat, axis=-1, keepdims=True)
        )
        middle_grad_ref[rows, :] = middle_grad
        branch_grad = (gate_open * middle_grad).astype(jnp.bfloat16)
        gate_pre_grad = (middle_grad * branch * gate_open * (1.0 - gate_open)).astype(jnp.bfloat16)
        gate_pre_ref[rows, :] = gate_pre_grad
        attended_grad_ref[rows, :] = against(branch_grad, output_weight[...]).astype(jnp.bfloat16)

        hidden[rows, :] = hidden_rows
        up_pre_grads[rows, :] = up_pre_grad
        update_grads[rows, :] = update_grad
        normed_second[rows, :] = normed
        carry_pre_grads[rows, :] = carry_pre_grad
        branch_grads[rows, :] = branch_grad
        lines = (gate_pre_grad, update_grad, carry_pre_grad, norm_grad * hat, norm_grad, up_pre_grad)
        return tuple(total + column_lines(line) for total, line in zip(totals, lines))

    start = (jnp.zeros((1, width), jnp.float32),) * 5 + (jnp.zeros((1, hidden_width), jnp.float32),)
    totals = lax.fori_loop(0, output_ref.shape[0] // MIDDLE_ROWS, some_rows, start)
    line = lax.broadcasted_iota(jnp.int32, block_ref.shape, 0)
    block = jnp.zeros(block_ref.shape, jnp.float32)
    for place, total in zip((GATE_B, DOWN_B, CARRY_B, GAIN_TWO, SHIFT_TWO), totals):
        block = jnp.where(line == place, total, block)
    for part in range(wide):
        block = jnp.where(line == UP_B + part, totals[5][:, part * width : (part + 1) * width], block)
    block_ref[...] = block
    leaving = []

    def leave(source, target, departure):
        leaving.append(pltpu.make_async_copy(source, target, departure))
        leaving[-1].start()

    def packs_leave(group, start, stop):
        for index, (source, target) in enumerate(zip(pack_refs, pack_targets)):
            here = (slice(None), slice(start, stop), slice(None))
            leave(source.at[here], target.at[here], pack_departures.at[group, index])

    for index, (source, target) in enumerate(zip(row_refs, row_targets)):
        leave(source, target, row_departures.at[index])

    target_ref = place_ref.at[2]
    rows = width // (4 * pack_refs[0].shape[0])
    place = 0
    for part in range(wide):
        grad = up_grad.at[part]
        grad[...] = inner_rows(normed_second[...], up_pre_grads[:, part * width : (part + 1) * width])
        spread_rows(target_ref, grad, pack_refs, place, rows)
        place += rows
    packs_leave(0, 0, place)
    for part in range(wide):
        here = slice(part * width, (part + 1) * width)
        down_grad[here, :] = inner_rows(hidden[:, here], update_grads[...])
    spread_rows(target_ref, down_grad, pack_refs, place, wide * rows)
    packs_leave(1, place, place + wide * rows)
    place += wide * rows
    pairs = ((normed_second, carry_pre_grads), (attended_ref, branch_grads), (normed_ref, gate_pre_ref))
    for index, (left_ref, right_ref) in enumerate(pairs):
        grad = square_grads.at[index]
        grad[...] = inner_rows(left_ref[...], right_ref[...])
        spread_rows(target_ref, grad, pack_refs, place, rows)
        place += rows
    packs_leave(2, 2 * wide * rows, place)
    for copy in leaving:
        copy.wait()


def second_grads_kernel(
    place_ref,
    both_grads_ref,
    normed_ref,
    query_grad_ref,
    gate_pre_ref,
    lanes_ref,
    query_weight_ref,
    key_weight_ref,
    value_weight_ref,
    gate_weight_ref,
    vectors_ref,
    block_ref,
    *refs,
):
    pack_refs, grads = refs[:4], refs[4]
    width = pack_refs[0].shape[2]
    rows = width // (4 * pack_refs[0].shape[0])
    grads[0] = inner_rows(normed_ref[...], query_grad_ref[...])
    grads[1] = jnp.transpose(both_grads_ref[:width, :])
    grads[2] = jnp.transpose(both_grads_ref[width:, :])
    for index in range(3):
        spread_rows(place_ref, grads.at[index], pack_refs, index * rows, rows)
    gate_grad = inner_rows(normed_ref[...], gate_pre_ref[...])

    def line_sums(ref):
        return jnp.sum(ref[...].astype(jnp.float32), axis=0, keepdims=True)

    def as_line(column):
        return jnp.transpose(jnp.broadcast_to(column, (width, BLK)))[:1, :]

    lines = (
        line_sums(query_grad_ref),
        jnp.sum(jnp.transpose(lanes_ref[:width, :]), axis=0, keepdims=True),
        jnp.sum(jnp.transpose(lanes_ref[width:, :]), axis=0, keepdims=True),
        line_sums(gate_pre_ref),
    )
    weighted = jnp.zeros((width, width), jnp.float32)
    shifted = jnp.zeros((width, width), jnp.float32)
    weight_refs = (query_weight_ref, key_weight_ref, value_weight_ref, gate_weight_ref)
    for weight_ref, line, grad in zip(weight_refs, lines, (grads[0], grads[1], grads[2], gate_grad)):
        weight = weight_ref[...].astype(jnp.float32)
        weighted += weight * grad
        shifted += weight * line
    shift_line = as_line(jnp.sum(shifted, axis=1, keepdims=True))
    gain_line = (
        as_line(jnp.sum(weighted, axis=1, keepdims=True)) - vectors_ref[SHIFT_ONE : SHIFT_ONE + 1, :] * shift_line
    ) / vectors_ref[GAIN_ONE : GAIN_ONE + 1, :]
    place = lax.broadcasted_iota(jnp.int32, block_ref.shape, 0)
    block = jnp.where(place == GAIN_ONE, gain_line, block_ref[...])
    block = jnp.where(place == SHIFT_ONE, shift_line, block).astype(jnp.bfloat16)
    for pack_ref in pack_refs:
        for index in range(pack_ref.shape[0]):
            pack_ref[index, 3 * rows :, :] = block


def input_grad_kernel(input_ref, local_ref, middle_grad_ref, vectors_ref, *refs):
    shared_refs, output_ref = refs[:-1], refs[-1]
    blocks = [sum(ref[index].astype(jnp.float32) for ref in shared_refs) for index in range(shared_refs[0].shape[0])]
    shared = jnp.concatenate([jnp.transpose(block) for block in blocks])
    values = input_ref[...].astype(jnp.float32)
    centered = values - jnp.mean(values, axis=-1, keepdims=True)
    scale = lax.rsqrt(jnp.mean(centered * centered, axis=-1, keepdims=True) + EPSILON)
    hat = centered * scale
    pull = (local_ref[...] + shared) * vectors_ref[GAIN_ONE : GAIN_ONE + 1, :]
    output_ref[...] = middle_grad_ref[...] + scale * (
        pull - jnp.mean(pull, axis=-1, keepdims=True) - hat * jnp.mean(pull * hat, axis=-1, keepdims=True)
    )


def local_call(kernel, cost, outs, smem, args, scratch=()):
    return pl.pallas_call(
        kernel,
        cost_estimate=about(cost),
        out_shape=outs,
        in_specs=[in_smem()] + [in_vmem()] * len(args),
        out_specs=jax.tree.map(lambda out: in_vmem(), outs),
        scratch_shapes=list(scratch),
        compiler_params=pltpu.CompilerParams(vmem_limit_bytes=VMEM_BYTES),
    )(smem, *args)


def joined(pieces, axis):
    return pieces[0] if len(pieces) == 1 else jnp.concatenate(pieces, axis=axis)


def shards(
    inputs,
    cotangent,
    block_segment,
    segment_parent,
    query_weight,
    key_weight,
    value_weight,
    output_weight,
    gate_weight,
    gate_bias,
    up_weight,
    up_bias,
    down_weight,
    down_bias,
    carry_weight,
    carry_bias,
    first_gain,
    first_shift,
    second_gain,
    second_shift,
):
    width = inputs.shape[1]
    devices = lax.axis_size(BOTH)
    block_count = inputs.shape[0] // BLK
    group_blocks = block_segment.shape[0]

    axis_z, axis_x, axis_y, axis_core = axes()
    rows_each = query_weight.shape[0]
    sizes = (axis_z.size, axis_x.size, axis_y.size, axis_core.size)
    direct = sizes == (4, 2, 2, 2) and rows_each % 16 == 0
    places = relative_devices()
    targets = scatter_devices()
    device = lax.axis_index(BOTH)
    vectors = (gate_bias, down_bias, carry_bias, first_gain, first_shift, second_gain, second_shift, up_bias)
    early_set = (query_weight, key_weight, value_weight, gate_weight)
    late_set = (output_weight, up_weight, down_weight, carry_weight)
    low = jnp.bfloat16

    def struct(*shape, dtype=low):
        return jax.ShapeDtypeStruct(shape, dtype)

    def take(source, start, piece):
        rows = piece.shape[0]
        parts = piece.shape[1] // width
        blocks = [
            source[:, start + part * rows : start + (part + 1) * rows].reshape(devices * rows, width)
            for part in range(parts)
        ]
        return joined(blocks, 1), start + parts * rows

    def flat_rows(pieces):
        return [piece[:, start : start + width] for piece in pieces for start in range(0, piece.shape[1], width)]

    own_start = lax.axis_index("seq") * block_count
    own_segments = lax.dynamic_slice_in_dim(block_segment, own_start, block_count)
    ancestor_slot, usable = ancestor_slots(block_segment, segment_parent, own_segments)
    owner = ancestor_slot // block_count
    away_z = (axis_z.position() - owner // axis_x.size) % axis_z.size
    away_x = (axis_x.position() - owner % axis_x.size) % axis_x.size
    relative_slot = (away_z * axis_x.size + away_x) * block_count + ancestor_slot % block_count
    tables = used_places(relative_slot, usable, group_blocks)
    slots = jnp.concatenate(
        [relative_slot, jnp.sum(usable, axis=-1, keepdims=True, dtype=jnp.int32)], axis=-1
    )

    if direct:
        early_count = 4 * rows_each + VECTOR_ROWS
        late_count = sum(piece.shape[0] * piece.shape[1] // width for piece in late_set)
        early, both = local_call(
            functools.partial(pack_kernel, devices),
            0.1,
            (struct(early_count, width), struct(early_count + late_count, width)),
            device.reshape(1),
            early_set + late_set + tuple(vector.reshape(1, -1) for vector in vectors),
        )
        both_one = axis_z.rotate(both, 1)
        early_line = [axis_z.rotate(early, back) for back in range(2, 4)]
        x_zero = axis_x.rotate(inputs, 1)
        z_one = axis_z.rotate(inputs, 1)
        both_one, early_line, x_zero, z_one = lax.optimization_barrier((both_one, early_line, x_zero, z_one))
        early_line = [both_one[:early_count]] + list(early_line)
        late_line = [both[early_count:], both_one[early_count:]]
        z_two = axis_z.rotate(z_one, 1)
        x_one = axis_x.rotate(z_one, 1)
        early_line = jnp.stack([early] + list(early_line))
        early_other = axis_x.rotate(early_line, 1)
        late_line.append(axis_z.rotate(late_line[1], 1))
        early_other, z_two, x_one, late_line[2], slots, tables = lax.optimization_barrier(
            (early_other, z_two, x_one, late_line[2], slots, tables)
        )
        z_three = axis_z.rotate(z_two, 1)
        x_two = axis_x.rotate(z_two, 1)
        early_plane = jnp.stack([early_line, early_other])
        early_other = axis_y.rotate(early_plane, 1)
        late_line.append(axis_z.rotate(late_line[2], 1))
        early_other, z_three, x_two, late_line[3] = lax.optimization_barrier(
            (early_other, z_three, x_two, late_line[3])
        )
        x_three = axis_x.rotate(z_three, 1)
        early_parts = [early_plane, early_other]
        early_parts += [axis_core.rotate(part, 1) for part in early_parts]
        early_parts = [part.reshape(devices // 4, early_count, width) for part in early_parts]
        input_pieces = [[inputs, x_zero], [z_one, x_one], [z_two, x_two], [z_three, x_three]]
        square = struct(width, width)
        full_query, full_key, full_value, full_gate, vector_rows = local_call(
            unpack_kernel,
            3,
            (square, square, square, square, struct(VECTOR_ROWS, width, dtype=jnp.float32)),
            places,
            early_parts,
        )
        late_line, full_key = lax.optimization_barrier((late_line, full_key))
        late_half = late_count // 2
        late_x = jnp.stack([rows[:late_half] for rows in late_line])
        late_y = jnp.stack([rows[late_half:] for rows in late_line])
        late_x_other = axis_x.rotate(late_x, 1)
        late_y_other = axis_y.rotate(late_y, 1)
    else:
        early_rows = lax.all_gather(jnp.concatenate(early_set), BOTH)
        late_rows = lax.all_gather(jnp.concatenate(flat_rows(late_set)), BOTH)
        place = 0
        full_query, place = take(early_rows, place, query_weight)
        full_key, place = take(early_rows, place, key_weight)
        full_value, place = take(early_rows, place, value_weight)
        full_gate, place = take(early_rows, place, gate_weight)
        place = 0
        full_output, place = take(late_rows, place, output_weight)
        full_up, place = take(late_rows, place, up_weight)
        full_down, place = take(late_rows, place, down_weight)
        full_carry, place = take(late_rows, place, carry_weight)
        lines = [lax.all_gather(vector, BOTH, tiled=True).reshape(-1, width) for vector in vectors]
        lines = jnp.concatenate(lines).astype(jnp.float32)
        vector_rows = jnp.pad(lines, ((0, VECTOR_ROWS - lines.shape[0]), (0, 0)))
        input_pieces = []
        along_z = inputs
        for step_z in range(axis_z.size):
            along_x = along_z
            row = []
            for step_x in range(axis_x.size):
                row.append(along_x)
                along_x = axis_x.rotate(along_x, 1) if step_x + 1 < axis_x.size else None
            input_pieces.append(row)
            along_z = axis_z.rotate(along_z, 1) if step_z + 1 < axis_z.size else None

    both_weight = jnp.concatenate([full_key, full_value], axis=1)

    group_rows = group_blocks * BLK
    pieces = [piece for row in input_pieces for piece in row]
    near = len(pieces) - 1 if direct else len(pieces)
    *carried, normed_low, query_low = project(
        pieces[:near], vector_rows, full_key, full_value, group_rows, 0, None, full_query
    )
    if direct:
        late_y_other, late_x_other, x_three, carried, both_weight = lax.optimization_barrier(
            (late_y_other, late_x_other, pieces[near], carried, both_weight)
        )
        late_x = jnp.stack([late_x, late_x_other])
        late_y = jnp.stack([late_y, late_y_other])
        late_x_other = axis_y.rotate(late_x, 1)
        late_y_other = axis_x.rotate(late_y, 1)
        carried = project([x_three], vector_rows, full_key, full_value, group_rows, near, carried)
    normed_group, key_group, value_group = carried

    gate_b, down_b, carry_b, gain_one, shift_one, gain_two, shift_two = [vector_rows[line] for line in range(UP_B)]
    up_b = vector_rows[UP_B : UP_B + up_weight.shape[1] // width].reshape(-1)

    values_in = inputs.astype(jnp.float32)
    attended_low, logsum = attend(slots, query_low, key_group, value_group)

    if direct:
        attended_low, late_x_other, late_y_other = lax.optimization_barrier((attended_low, late_x_other, late_y_other))
        late_parts = []
        for mine in ((late_x, late_x_other), (late_y, late_y_other)):
            for piece in list(mine) + [axis_core.rotate(part, 1) for part in mine]:
                late_parts.append(piece.reshape(devices // 4, late_half, width))
        other_places = jnp.transpose(places.reshape(2, 2, 2, 4), (0, 2, 1, 3)).reshape(-1)
        rows = inputs.shape[0]
        first_rows = late_count + rows_each
        hidden_width = up_weight.shape[1]
        quarter = struct(devices // 4, first_rows, width)
        tall, short = pltpu.VMEM((rows, hidden_width), low), pltpu.VMEM((rows, width), low)
        wide = (struct(rows, width), struct(rows, width, dtype=jnp.float32), struct(rows, width), struct(rows, width))
        leaving = wide + (quarter,) * 4
        block, output, middle_grad, attended_grad, gate_pre_grad, *first = pl.pallas_call(
            middle_kernel,
            cost_estimate=about(20),
            out_shape=(struct(VECTOR_ROWS, width, dtype=jnp.float32),) + leaving,
            in_specs=[in_smem()] + [in_vmem()] * 14,
            out_specs=(in_vmem(),) + (anywhere(),) * len(leaving),
            scratch_shapes=[
                pltpu.VMEM((width, width), low),
                pltpu.VMEM((width, hidden_width), low),
                pltpu.VMEM((hidden_width, width), low),
                pltpu.VMEM((width, width), low),
                tall,
                tall,
                short,
                short,
                short,
                short,
                pltpu.VMEM((hidden_width // width, width, width), jnp.float32),
                pltpu.VMEM((hidden_width, width), jnp.float32),
                pltpu.VMEM((3, width, width), jnp.float32),
            ]
            + [pltpu.VMEM(out.shape, out.dtype) for out in leaving]
            + [pltpu.SemaphoreType.DMA((4,)), pltpu.SemaphoreType.DMA((3, 4))],
            compiler_params=pltpu.CompilerParams(vmem_limit_bytes=VMEM_BYTES),
        )(
            jnp.stack([places, other_places, targets]),
            attended_low,
            inputs,
            normed_low,
            cotangent,
            full_gate,
            vector_rows,
            *late_parts,
        )
        first = [pack.reshape(4, 2, first_rows, width) for pack in first]
        first_core = [axis_core.rotate(first[2 + index], -1) for index in range(2)]
        first_keep, first_send = [add_low(first_core[index], first[index]) for index in range(2)]
        attended_grad, first_keep, first_send = lax.optimization_barrier((attended_grad, first_keep, first_send))
        first_arrived = axis_y.rotate(first_send, -1)
    else:
        gate_open = jax.nn.sigmoid(matmul(normed_low, full_gate) + gate_b)
        branch = matmul(attended_low, full_output)
        middle = values_in + gate_open * branch
        normed_second = normalize(middle, gain_two, shift_two).astype(jnp.bfloat16)
        up_pre = matmul(normed_second, full_up) + up_b
        up_sigmoid = jax.nn.sigmoid(up_pre)
        hidden_low = (up_pre * up_sigmoid).astype(jnp.bfloat16)
        update = matmul(hidden_low, full_down) + down_b
        carry_open = jax.nn.sigmoid(matmul(normed_second, full_carry) + carry_b)
        output = (middle + carry_open * update).astype(jnp.bfloat16)

        grad_out = cotangent.astype(jnp.float32)
        update_grad = (carry_open * grad_out).astype(jnp.bfloat16)
        carry_pre_grad = (grad_out * update * carry_open * (1.0 - carry_open)).astype(jnp.bfloat16)
        grad_down_bias = column_sums(update_grad)
        grad_carry_bias = column_sums(carry_pre_grad)
        silu_slope = up_sigmoid * (1.0 + up_pre * (1.0 - up_sigmoid))
        up_pre_grad = (against(update_grad, full_down) * silu_slope).astype(jnp.bfloat16)
        grad_up_bias = column_sums(up_pre_grad)
        second_norm_grad = against(up_pre_grad, full_up) + against(carry_pre_grad, full_carry)
        second_pull = jax.vjp(normalize, middle, gain_two, shift_two)[1]
        middle_part, grad_second_gain, grad_second_shift = second_pull(second_norm_grad)
        middle_grad = grad_out + middle_part

        branch_grad = (gate_open * middle_grad).astype(jnp.bfloat16)
        gate_pre_grad = (middle_grad * branch * gate_open * (1.0 - gate_open)).astype(jnp.bfloat16)
        grad_gate_bias = column_sums(gate_pre_grad)
        attended_grad = against(branch_grad, full_output).astype(jnp.bfloat16)
        zero_line = jnp.zeros((width,), jnp.float32)
        local_lines = (
            grad_gate_bias,
            grad_down_bias,
            grad_carry_bias,
            zero_line,
            zero_line,
            grad_second_gain,
            grad_second_shift,
            grad_up_bias,
        )
        block = jnp.concatenate([line.reshape(-1, width) for line in local_lines])
        block = jnp.pad(block, ((0, VECTOR_ROWS - block.shape[0]), (0, 0)))
    backward = attend_backward(
        (slots,) + tables,
        query_low,
        key_group,
        value_group,
        logsum,
        attended_low,
        attended_grad,
        normed_group,
        both_weight,
    )
    if direct:
        backward, first_arrived = lax.optimization_barrier((backward, first_arrived))

        def first_y(back):
            return add_low(first_arrived[back], first_keep[back])

        first_z = axis_z.rotate(first_y(3), -1)
    query_rows_grad, both_grads, lanes = backward[:3]

    shared_parts = backward[3:]

    if direct:
        second_rows = 3 * rows_each + VECTOR_ROWS
        quarter = struct(devices // 4, second_rows, width)
        second = local_call(
            second_grads_kernel,
            0.1,
            (quarter,) * 4,
            places,
            (
                both_grads,
                normed_low,
                query_rows_grad,
                gate_pre_grad,
                lanes,
                full_query,
                full_key,
                full_value,
                full_gate,
                vector_rows,
                block,
            ),
            (pltpu.VMEM((3, width, width), jnp.float32),),
        )
        second = [pack.reshape(2, 4, second_rows, width) for pack in second]
        barrier = lax.optimization_barrier
        first_z = axis_z.rotate(add_low(first_z, first_y(2)), -1)
        x_three = axis_x.rotate(shared_parts[7], -1)
        x_three, first_z, second = barrier((x_three, first_z, second))

        second_core = [axis_core.rotate(second[2 + index], -1) for index in range(2)]
        second_keep = add_low(second_core[0], second[0])
        second_arrived = axis_y.rotate(add_low(second_core[1], second[1]), -1)
        x_two = axis_x.rotate(tied(shared_parts[5], x_three), -1)
        z_three = axis_z.rotate(add_low(x_three, shared_parts[6]), -1)
        first_z = axis_z.rotate(add_low(first_z, first_y(1)), -1)
        x_two, z_three, first_z, second_arrived = barrier((x_two, z_three, first_z, second_arrived))

        second_y = add_low(second_arrived, second_keep)
        second_x = axis_x.rotate(second_y[1], -1)
        x_one = axis_x.rotate(tied(shared_parts[3], x_two), -1)
        z_two = axis_z.rotate(add_three(x_two, shared_parts[4], z_three), -1)
        x_one, z_two, second_x = barrier((x_one, z_two, second_x))

        first_half = add_low(first_z, first_y(0))
        first_x = axis_x.rotate(tied(first_half[1], x_one), -1)
        second_half = add_low(second_x, second_y[0])
        second_z = [axis_z.rotate(second_half[back], -back) for back in range(1, 4)]
        x_zero = axis_x.rotate(tied(shared_parts[1], x_one), -1)
        z_one = axis_z.rotate(add_three(x_one, shared_parts[2], z_two), -1)
        shared = (x_zero, z_one, shared_parts[0])
        first_sum = first_x.astype(jnp.float32) + first_half[0].astype(jnp.float32)
        second_sum = sum(piece.astype(jnp.float32) for piece in [second_half[0]] + second_z)
        weight_sum = jnp.concatenate([first_sum, second_sum])
    else:
        grad_key = jnp.transpose(both_grads[:width])
        grad_value = jnp.transpose(both_grads[width:])
        grad_query = inner_rows(normed_low, query_rows_grad)
        grad_gate = inner_rows(normed_low, gate_pre_grad)
        both_sums = jnp.sum(lanes, axis=1)
        weights = [weight.astype(jnp.float32) for weight in (full_query, full_key, full_value, full_gate)]
        line_sums = (column_sums(query_rows_grad), both_sums[:width], both_sums[width:], grad_gate_bias)
        shift_line = sum(jnp.sum(weight * line, axis=1) for weight, line in zip(weights, line_sums))
        weighted = sum(
            jnp.sum(weight * grad, axis=1)
            for weight, grad in zip(weights, (grad_query, grad_key, grad_value, grad_gate))
        )
        block = block.at[GAIN_ONE].set((weighted - shift_one * shift_line) / gain_one).at[SHIFT_ONE].set(shift_line)
        grads = (
            (inner_rows(normed_second, up_pre_grad), up_weight),
            (inner_rows(hidden_low, update_grad), down_weight),
            (inner_rows(normed_second, carry_pre_grad), carry_weight),
            (inner_rows(attended_low, branch_grad), output_weight),
            (grad_gate, gate_weight),
            (grad_query, query_weight),
            (grad_key, key_weight),
            (grad_value, value_weight),
        )
        pack = [
            cut.astype(low).reshape(devices, piece.shape[0], width)
            for grad, piece in grads
            for cut in flat_rows((grad,))
        ]
        pack.append(jnp.broadcast_to(block.astype(low), (devices, VECTOR_ROWS, width)))
        pack = jnp.concatenate(pack, axis=1)
        pack = jnp.pad(pack, ((0, 0), (0, -pack.shape[1] % 16), (0, 0)))
        weight_sum = lax.psum_scatter(pack, BOTH, scatter_dimension=0, tiled=True)[0].astype(jnp.float32)

        def over_x(step_z):
            return ring_scatter(lambda step_x: shared_parts[step_z * axis_x.size + step_x], axis_x)

        shared = (ring_scatter(over_x, axis_z),)

    def own(start, piece):
        rows = piece.shape[0]
        parts = piece.shape[1] // width
        blocks = [weight_sum[start + part * rows : start + (part + 1) * rows] for part in range(parts)]
        return joined(blocks, 1), start + parts * rows

    local_grad = against(query_rows_grad, full_query) + against(gate_pre_grad, full_gate)
    input_grad = pl.pallas_call(
        input_grad_kernel,
        cost_estimate=about(3),
        out_shape=struct(block_count * BLK, width, dtype=jnp.float32),
        compiler_params=pltpu.CompilerParams(vmem_limit_bytes=VMEM_BYTES),
    )(inputs, local_grad, middle_grad, vector_rows, *shared)

    place = 0
    own_up, place = own(place, up_weight)
    own_down, place = own(place, down_weight)
    own_carry, place = own(place, carry_weight)
    own_output, place = own(place, output_weight)
    own_gate, place = own(place, gate_weight)
    own_query, place = own(place, query_weight)
    own_key, place = own(place, key_weight)
    own_value, place = own(place, value_weight)
    vector_out = []
    for index, vector in enumerate(vectors):
        count = vector.shape[0]
        lines = weight_sum[place + index : place + index + count * devices // width].reshape(-1)
        vector_out.append(lax.dynamic_slice_in_dim(lines, device * count, count))
    gate_bg, down_bg, carry_bg, gain_one_g, shift_one_g, gain_two_g, shift_two_g, up_bg = vector_out
    return (
        output,
        input_grad,
        own_query,
        own_key,
        own_value,
        own_output,
        own_gate,
        gate_bg,
        own_up,
        up_bg,
        own_down,
        down_bg,
        own_carry,
        carry_bg,
        gain_one_g,
        shift_one_g,
        gain_two_g,
        shift_two_g,
    )


def solution(mesh):
    rows = P(BOTH, None)
    line = P(BOTH)
    matrix_or_line = (rows,) * 5 + (line, rows, line, rows, line, rows) + (line,) * 5
    return jax.shard_map(
        shards,
        mesh=mesh,
        in_specs=(rows, rows, P("dp"), P("dp")) + matrix_or_line,
        out_specs=(rows, rows) + matrix_or_line,
        check_vma=False,
    )
```

```python
import functools

import jax
import jax.numpy as jnp
from jax import lax
from jax.experimental import pallas as pl
from jax.experimental.pallas import tpu as pltpu
from jax.sharding import PartitionSpec as P

HD = 64
BLK = 128
DEPTH = 10
PAIR = 2 * HD
PLACES = 4
TREE_BLOCKS = 20
TRUNK = 8

EPSILON = 1e-05
NEGATIVE = -1e30
BOTH = ("dp", "seq")
VMEM_BYTES = 60 * 1024 * 1024


def normalize(values, norm_gain, norm_shift):
    center = values - jnp.mean(values, axis=-1, keepdims=True)
    spread = jnp.mean(center * center, axis=-1, keepdims=True)
    return center * lax.rsqrt(spread + EPSILON) * norm_gain + norm_shift


def matmul(left_side, right_side):
    return jnp.dot(left_side, right_side, preferred_element_type=jnp.float32)


def inner_rows(left_side, right_side):
    return lax.dot_general(
        left_side, right_side, (((0,), (0,)), ((), ())), preferred_element_type=jnp.float32
    )


def against(left_side, right_side):
    return lax.dot_general(
        left_side, right_side, (((1,), (1,)), ((), ())), preferred_element_type=jnp.float32
    )


def column_sums(values):
    return jnp.sum(values.astype(jnp.float32), axis=0)


def lookup(lookup_table, wanted):
    entries = jnp.arange(lookup_table.shape[0], dtype=jnp.int32)
    matches = wanted[..., None] == entries
    located = jnp.sum(jnp.where(matches, lookup_table, jnp.int32(0)), axis=-1, dtype=jnp.int32)
    return jnp.where(wanted >= 0, located, jnp.int32(-1))


def ancestor_slots(block_segment, segment_parent, own_segments):
    entries = jnp.arange(block_segment.shape[0], dtype=jnp.int32)
    placed = block_segment[None, :] == entries[:, None]
    slot_of = jnp.sum(jnp.where(placed, entries[None, :], jnp.int32(0)), axis=1, dtype=jnp.int32)
    current = own_segments
    lineage = []
    for depth_step in range(DEPTH):
        lineage.append(current)
        current = lookup(segment_parent, current)
    lineage = jnp.stack(lineage, axis=-1)
    usable = lineage >= 0
    return (jnp.where(usable, lookup(slot_of, lineage), jnp.int32(0)), usable)


def stack_heads(rows):
    lane = lax.broadcasted_iota(jnp.int32, rows.shape, 1)
    low = lane < HD
    zero = jnp.zeros_like(rows)
    return jnp.concatenate([jnp.where(low, rows, zero), jnp.where(low, zero, rows)], axis=0)


def unstack_heads(rows):
    half = rows.shape[0] // 2
    lane = lax.broadcasted_iota(jnp.int32, (half, rows.shape[1]), 1)
    return jnp.where(lane < HD, rows[:half], rows[half:])


def make_bias(levels, bias_ref):
    row = lax.broadcasted_iota(jnp.int32, (BLK, DEPTH * BLK), 0)
    col = lax.broadcasted_iota(jnp.int32, (BLK, DEPTH * BLK), 1)
    limit = jnp.where(col < BLK, row + 1, levels * BLK)
    bias = jnp.where(col < limit, jnp.float32(0.0), jnp.float32(NEGATIVE))
    bias_ref[:BLK, :] = bias
    bias_ref[BLK:, :] = bias


class Levels:
    def __init__(self, slots_ref, sources, targets, arrivals):
        self.slots_ref = slots_ref
        self.pairs = tuple(zip(sources, targets))
        self.arrivals = arrivals

    def copies(self, slot):
        turn = slot % 2
        for level in range(DEPTH):
            start = pl.multiple_of(self.slots_ref[slot, level] * BLK, BLK)
            for index, (source, target) in enumerate(self.pairs):
                place = target.at[turn, level * BLK : (level + 1) * BLK, :]
                yield pltpu.make_async_copy(
                    source.at[pl.ds(start, BLK), :], place, self.arrivals.at[turn, index, level]
                )

    def start(self, slot):
        for copy in self.copies(slot):
            copy.start()

    def step(self, slot, count):
        @pl.when(slot + 1 < count)
        def ahead():
            self.start(slot + 1)

        for copy in self.copies(slot):
            copy.wait()


def forward_kernel(
    slots_ref, query_ref, key_source, value_source, mixed_ref, logsum_ref, key_here, value_here, bias_ref, arrivals
):
    width = query_ref.shape[1]
    count = query_ref.shape[0] // BLK
    levels = Levels(slots_ref, (key_source, value_source), (key_here, value_here), arrivals)
    levels.start(0)

    def one_slot(slot, carry):
        rows = pl.ds(pl.multiple_of(slot * BLK, BLK), BLK)
        make_bias(slots_ref[slot, DEPTH], bias_ref)
        levels.step(slot, count)
        turn = slot % 2
        lane = lax.broadcasted_iota(jnp.int32, (BLK, PAIR), 1)
        logsums = jnp.zeros((BLK, PAIR), jnp.float32)
        for pair in range(width // PAIR):
            cols = slice(pair * PAIR, (pair + 1) * PAIR)
            stacked = stack_heads(query_ref[rows, cols])
            scores = against(stacked, key_here[turn, :, cols]) + bias_ref[...]
            highest = jnp.max(scores, axis=-1, keepdims=True)
            raised = jnp.exp(scores - highest)
            total = jnp.sum(raised, axis=-1, keepdims=True)
            mixed = matmul(raised.astype(jnp.bfloat16), value_here[turn, :, cols]) / total
            mixed_ref[rows, cols] = unstack_heads(mixed).astype(jnp.bfloat16)
            logsum = highest + jnp.log(total)
            logsums = jnp.where(lane == 2 * pair, logsum[:BLK], logsums)
            logsums = jnp.where(lane == 2 * pair + 1, logsum[BLK:], logsums)
        logsum_ref[rows, :] = logsums
        return carry

    lax.fori_loop(0, count, one_slot, 0)


def last_forward_kernel(
    slots_ref,
    query_ref,
    piece_ref,
    vectors_ref,
    key_weight_ref,
    value_weight_ref,
    *refs,
):
    mixed_ref, logsum_ref = refs[3:5]
    targets = refs[5:8]
    key_here, value_here, bias_ref, arrivals, made, departures = refs[8:]
    gain = vectors_ref[GAIN_ONE : GAIN_ONE + 1, :]
    shift = vectors_ref[SHIFT_ONE : SHIFT_ONE + 1, :]
    rows = piece_ref.shape[0]
    first = targets[0].shape[0] - rows

    def leave(kind):
        return pltpu.make_async_copy(made.at[kind], targets[kind].at[first : first + rows, :], departures.at[kind])

    normed = normalize(piece_ref[...].astype(jnp.float32), gain, shift).astype(jnp.bfloat16)
    made[1] = matmul(normed, key_weight_ref[...]).astype(jnp.bfloat16)
    leave(1).start()
    made[2] = matmul(normed, value_weight_ref[...]).astype(jnp.bfloat16)
    leave(2).start()
    made[0] = normed
    leave(0).start()
    leave(1).wait()
    leave(2).wait()
    forward_kernel(
        slots_ref, query_ref, targets[1], targets[2], mixed_ref, logsum_ref, key_here, value_here, bias_ref, arrivals
    )
    leave(0).wait()


def backward_kernel(
    slots_ref,
    compact_ref,
    used_ref,
    seen_ref,
    query_ref,
    key_source,
    value_source,
    logsum_ref,
    mixed_ref,
    mixed_grad_ref,
    normed_source,
    weight_ref,
    query_grad_ref,
    grads_ref,
    lanes_ref,
    *refs,
):
    width = query_ref.shape[1]
    count = query_ref.shape[0] // BLK
    shared_refs = refs[:-11]
    key_here, value_here, bias_ref, normed_here, key_sums, value_sums = refs[-11:-5]
    stage, zero_block, arrivals, normed_arrivals, departures = refs[-5:]
    places = used_ref.shape[1] - 1
    used_count = used_ref[0, places]
    levels = Levels(slots_ref, (key_source, value_source), (key_here, value_here), arrivals)
    levels.start(0)

    def normed_copy(place):
        source = pl.ds(pl.multiple_of(used_ref[0, place] * BLK, BLK), BLK)
        target = normed_here.at[place * BLK : (place + 1) * BLK, :]
        return pltpu.make_async_copy(normed_source.at[source, :], target, normed_arrivals.at[place])

    for place in range(places):

        @pl.when(place < used_count)
        def fetch():
            normed_copy(place).start()

        @pl.when(place >= used_count)
        def clear():
            normed_here[place * BLK : (place + 1) * BLK, :] = jnp.zeros((BLK, normed_here.shape[1]), jnp.bfloat16)

    zero_block[...] = jnp.zeros_like(zero_block)
    for slot in range(count * len(shared_refs)):

        @pl.when(seen_ref[0, slot] == 0)
        def none():
            target = shared_refs[slot // count].at[slot % count]
            pltpu.make_async_copy(zero_block, target, departures.at[slot]).start()

    key_sums[...] = jnp.zeros_like(key_sums)
    value_sums[...] = jnp.zeros_like(value_sums)

    def one_slot(slot, carry):
        rows = pl.ds(pl.multiple_of(slot * BLK, BLK), BLK)
        make_bias(slots_ref[slot, DEPTH], bias_ref)
        levels.step(slot, count)
        turn = slot % 2
        for pair in range(width // PAIR):
            cols = slice(pair * PAIR, (pair + 1) * PAIR)
            stacked = stack_heads(query_ref[rows, cols])
            grad_rows = mixed_grad_ref[rows, cols]
            grad_stacked = stack_heads(grad_rows)
            products = grad_rows.astype(jnp.float32) * mixed_ref[rows, cols].astype(jnp.float32)
            row_dot = jnp.sum(stack_heads(products), axis=-1, keepdims=True)
            logsum = jnp.concatenate(
                [logsum_ref[rows, 2 * pair : 2 * pair + 1], logsum_ref[rows, 2 * pair + 1 : 2 * pair + 2]], axis=0
            )
            key_rows = key_here[turn, :, cols]
            shares = jnp.exp(against(stacked, key_rows) + bias_ref[...] - logsum)
            share_grad = against(grad_stacked, value_here[turn, :, cols])
            score_grad = (shares * (share_grad - row_dot)).astype(jnp.bfloat16)
            query_grad = unstack_heads(matmul(score_grad, key_rows)) * (HD ** (-0.5))
            query_grad_ref[rows, cols] = query_grad.astype(jnp.bfloat16)
            key_part = inner_rows(stacked, score_grad)
            value_part = inner_rows(grad_stacked, shares.astype(jnp.bfloat16))
            for level in range(DEPTH):
                start = pl.multiple_of(compact_ref[slot, level] * BLK, BLK)
                here = slice(level * BLK, (level + 1) * BLK)
                key_sums[cols, pl.ds(start, BLK)] += key_part[:, here]
                value_sums[cols, pl.ds(start, BLK)] += value_part[:, here]
        return carry

    lax.fori_loop(0, count, one_slot, 0)

    for place in range(places):

        @pl.when(place < used_count)
        def arrived():
            normed_copy(place).wait()

    grads_ref[...] = jnp.zeros_like(grads_ref)
    lanes_ref[...] = jnp.zeros_like(lanes_ref)

    def some_places(step, carry):
        here = pl.ds(pl.multiple_of(step * (PLACES * BLK), PLACES * BLK), PLACES * BLK)
        shared = None
        for part, part_sums in enumerate((key_sums, value_sums)):
            lines = slice(part * width, (part + 1) * width)
            block = part_sums[:, here]
            tiles = [block[:, start : start + BLK] for start in range(0, PLACES * BLK, BLK)]
            lanes_ref[lines, :] += functools.reduce(lambda left, right: left + right, tiles)
            block = block.astype(jnp.bfloat16)
            product = matmul(weight_ref[:, lines], block)
            shared = product if shared is None else shared + product
            grads_ref[lines, :] += matmul(block, normed_here[here, :])
        for index in range(PLACES):
            place = step * PLACES + index
            stage[place] = shared[:, index * BLK : (index + 1) * BLK].astype(jnp.bfloat16)

            slot = used_ref[0, jnp.minimum(place, used_count - 1)]
            for piece, shared_ref in enumerate(shared_refs):

                @pl.when((place < used_count) & (slot // count == piece))
                def leave():
                    target = shared_ref.at[slot - piece * count]
                    pltpu.make_async_copy(stage.at[place], target, departures.at[slot]).start()

        return carry

    lax.fori_loop(0, (used_count + PLACES - 1) // PLACES, some_places, 0)
    for slot in range(count * len(shared_refs)):
        target = shared_refs[slot // count].at[slot % count]
        pltpu.make_async_copy(zero_block, target, departures.at[slot]).wait()


def about(cost):
    return pl.CostEstimate(flops=int(cost * 1e9), bytes_accessed=int(cost * 1e6), transcendentals=0)


def in_vmem():
    return pl.BlockSpec(memory_space=pltpu.VMEM)


def in_smem():
    return pl.BlockSpec(memory_space=pltpu.SMEM)


def anywhere():
    return pl.BlockSpec(memory_space=pl.ANY)


def level_scratch(width):
    return [
        pltpu.VMEM((2, DEPTH * BLK, width), jnp.bfloat16),
        pltpu.VMEM((2, DEPTH * BLK, width), jnp.bfloat16),
        pltpu.VMEM((2 * BLK, DEPTH * BLK), jnp.float32),
    ]


def attend(slots, query_rows, key_group, value_group):
    rows, width = query_rows.shape
    return pl.pallas_call(
        forward_kernel,
        cost_estimate=about(18),
        out_shape=(
            jax.ShapeDtypeStruct((rows, width), jnp.bfloat16),
            jax.ShapeDtypeStruct((rows, PAIR), jnp.float32),
        ),
        in_specs=[in_smem(), in_vmem(), anywhere(), anywhere()],
        out_specs=(in_vmem(), in_vmem()),
        scratch_shapes=level_scratch(width) + [pltpu.SemaphoreType.DMA((2, 2, DEPTH))],
        compiler_params=pltpu.CompilerParams(vmem_limit_bytes=VMEM_BYTES),
    )(slots, query_rows, key_group, value_group)


def project_and_attend(slots, query_rows, piece, vectors, key_weight, value_weight, carried):
    rows, width = query_rows.shape
    whole = jax.ShapeDtypeStruct(carried[0].shape, jnp.bfloat16)
    return pl.pallas_call(
        last_forward_kernel,
        cost_estimate=about(20),
        out_shape=(
            jax.ShapeDtypeStruct((rows, width), jnp.bfloat16),
            jax.ShapeDtypeStruct((rows, PAIR), jnp.float32),
            whole,
            whole,
            whole,
        ),
        in_specs=[in_smem()] + [in_vmem()] * 5 + [anywhere()] * 3,
        out_specs=(in_vmem(), in_vmem(), anywhere(), anywhere(), anywhere()),
        scratch_shapes=level_scratch(width)
        + [
            pltpu.SemaphoreType.DMA((2, 2, DEPTH)),
            pltpu.VMEM((3, rows, width), jnp.bfloat16),
            pltpu.SemaphoreType.DMA((3,)),
        ],
        input_output_aliases={6: 2, 7: 3, 8: 4},
        compiler_params=pltpu.CompilerParams(vmem_limit_bytes=VMEM_BYTES),
    )(slots, query_rows, piece, vectors, key_weight, value_weight, *carried)


def attend_backward(tables, query_rows, key_group, value_group, logsum, mixed, mixed_grad, normed_group, both_weight):
    rows, width = query_rows.shape
    blocks = normed_group.shape[0] // BLK
    pieces = normed_group.shape[0] // rows
    places = tables[2].shape[1] - 1
    return pl.pallas_call(
        backward_kernel,
        cost_estimate=about(32),
        out_shape=(
            jax.ShapeDtypeStruct((rows, width), jnp.bfloat16),
            jax.ShapeDtypeStruct((2 * width, width), jnp.float32),
            jax.ShapeDtypeStruct((2 * width, BLK), jnp.float32),
        )
        + (jax.ShapeDtypeStruct((rows // BLK, width, BLK), jnp.bfloat16),) * pieces,
        in_specs=[in_smem()] * 4
        + [in_vmem(), anywhere(), anywhere(), in_vmem(), in_vmem(), in_vmem(), anywhere(), in_vmem()],
        out_specs=(in_vmem(),) * 3 + (anywhere(),) * pieces,
        scratch_shapes=level_scratch(width)
        + [
            pltpu.VMEM((places * BLK, width), jnp.bfloat16),
            pltpu.VMEM((width, places * BLK), jnp.float32),
            pltpu.VMEM((width, places * BLK), jnp.float32),
            pltpu.VMEM((places, width, BLK), jnp.bfloat16),
            pltpu.VMEM((width, BLK), jnp.bfloat16),
            pltpu.SemaphoreType.DMA((2, 2, DEPTH)),
            pltpu.SemaphoreType.DMA((places,)),
            pltpu.SemaphoreType.DMA((blocks,)),
        ],
        compiler_params=pltpu.CompilerParams(vmem_limit_bytes=VMEM_BYTES),
    )(*tables, query_rows, key_group, value_group, logsum, mixed, mixed_grad, normed_group, both_weight)


def used_places(relative_slot, usable, group_blocks):
    block_count = relative_slot.shape[0]
    most = group_blocks // TREE_BLOCKS * TRUNK + 2 * block_count
    places = min(-(-most // PLACES) * PLACES, -(-group_blocks // PLACES) * PLACES)
    entries = jnp.arange(group_blocks, dtype=jnp.int32)
    hits = (relative_slot[:, :, None] == entries) & usable[:, :, None]
    seen = jnp.any(hits, axis=(0, 1))
    earlier = (entries[None, :] < entries[:, None]) & seen[None, :]
    place_of = jnp.sum(earlier, axis=1, dtype=jnp.int32)
    compact = jnp.sum(jnp.where(hits, place_of, jnp.int32(0)), axis=-1, dtype=jnp.int32)
    wanted = jnp.arange(places, dtype=jnp.int32)
    matches = (place_of[None, :] == wanted[:, None]) & seen[None, :]
    used = jnp.sum(jnp.where(matches, entries, jnp.int32(0)), axis=1, dtype=jnp.int32)
    seen = seen.astype(jnp.int32)
    used = jnp.concatenate([used, jnp.sum(seen, dtype=jnp.int32).reshape(1)])
    return compact, used.reshape(1, -1), seen.reshape(1, -1)


def project(pieces, vectors, key_weight, value_weight, group_rows, first, carried, query_weight=None):
    count = len(pieces)
    rows, width = pieces[0].shape
    weights = [key_weight, value_weight] + ([] if query_weight is None else [query_weight])
    extra = [] if carried is None else list(carried)

    def body(*refs):
        piece_refs, vectors_ref = refs[:count], refs[count]
        weight_refs = refs[count + 1 : count + 1 + len(weights)]
        outs = refs[count + 1 + len(weights) + len(extra) : -4]
        piece_here, made, arrivals, departures = refs[-4:]
        gain = vectors_ref[GAIN_ONE : GAIN_ONE + 1, :]
        shift = vectors_ref[SHIFT_ONE : SHIFT_ONE + 1, :]

        def fetch(index):
            return pltpu.make_async_copy(piece_refs[index], piece_here.at[index % 2], arrivals.at[index])

        def leave(index, kind):
            target = outs[kind].at[(first + index) * rows : (first + index + 1) * rows, :]
            return pltpu.make_async_copy(made.at[index % 2, kind], target, departures.at[index, kind])

        for index in range(min(2, count)):
            fetch(index).start()
        for index in range(count):
            fetch(index).wait()
            normed = normalize(piece_here[index % 2].astype(jnp.float32), gain, shift).astype(jnp.bfloat16)
            if index + 2 < count:
                fetch(index + 2).start()
            if index >= 2:
                for kind in range(3):
                    leave(index - 2, kind).wait()
            made[index % 2, 0] = normed
            leave(index, 0).start()
            for kind in (1, 2):
                made[index % 2, kind] = matmul(normed, weight_refs[kind - 1][...]).astype(jnp.bfloat16)
                leave(index, kind).start()
            if index == 0 and len(outs) > 3:
                outs[3][...] = normed
                queries = matmul(normed, weight_refs[2][...]).astype(jnp.bfloat16)
                outs[4][...] = (queries.astype(jnp.float32) * (HD ** (-0.5))).astype(jnp.bfloat16)
        for index in range(max(0, count - 2), count):
            for kind in range(3):
                leave(index, kind).wait()

    whole = jax.ShapeDtypeStruct((group_rows, width), jnp.bfloat16)
    own = [] if query_weight is None else [jax.ShapeDtypeStruct((rows, width), jnp.bfloat16)] * 2
    inputs = count + 1 + len(weights)
    return pl.pallas_call(
        body,
        cost_estimate=about(1 + 1.6 * count),
        out_shape=[whole] * 3 + own,
        in_specs=[anywhere()] * count + [in_vmem()] * (1 + len(weights)) + [anywhere()] * len(extra),
        out_specs=[anywhere()] * 3 + [in_vmem()] * len(own),
        scratch_shapes=[
            pltpu.VMEM((2, rows, width), jnp.bfloat16),
            pltpu.VMEM((2, 3, rows, width), jnp.bfloat16),
            pltpu.SemaphoreType.DMA((count,)),
            pltpu.SemaphoreType.DMA((count, 3)),
        ],
        input_output_aliases={inputs + index: index for index in range(len(extra))},
        compiler_params=pltpu.CompilerParams(vmem_limit_bytes=VMEM_BYTES),
    )(*pieces, vectors, *weights, *extra)


class Axis:
    def __init__(self, name, size, stride):
        self.name = name
        self.size = size
        self.stride = stride

    def position(self):
        return lax.axis_index(self.name) // self.stride % self.size

    def rotate(self, values, shift):
        pairs = []
        for index in range(lax.axis_size(self.name)):
            here = index // self.stride % self.size
            there = (here + shift) % self.size
            pairs.append((index, index + (there - here) * self.stride))
        return lax.ppermute(values, self.name, pairs)


def axes():
    seq = lax.axis_size("seq")
    dp = lax.axis_size("dp")
    along_z = 4 if seq % 4 == 0 else 1
    cores = 2 if dp % 2 == 0 else 1
    return (
        Axis("seq", along_z, seq // along_z),
        Axis("seq", seq // along_z, 1),
        Axis("dp", dp // cores, cores),
        Axis("dp", cores, 1),
    )


def relative_devices():
    axis_z, axis_x, axis_y, axis_core = axes()

    def place(axis, dim):
        back = lax.broadcasted_iota(jnp.int32, (axis_core.size, axis_y.size, axis_x.size, axis_z.size), dim)
        return (axis.position() - back + axis.size) % axis.size

    dp_index = place(axis_y, 1) * axis_core.size + place(axis_core, 0)
    seq_index = place(axis_z, 3) * axis_x.size + place(axis_x, 2)
    return (dp_index * lax.axis_size("seq") + seq_index).reshape(-1)


def scatter_devices():
    axis_z, axis_x, axis_y, axis_core = axes()
    entries = relative_devices().reshape(-1, axis_x.size, axis_z.size)
    return jnp.swapaxes(entries, 1, 2).reshape(-1)


def add_low(left_side, right_side):
    return (left_side.astype(jnp.float32) + right_side.astype(jnp.float32)).astype(jnp.bfloat16)


def add_three(first, second, third):
    total = first.astype(jnp.float32) + second.astype(jnp.float32) + third.astype(jnp.float32)
    return total.astype(jnp.bfloat16)


def tied(values, after):
    return lax.optimization_barrier((values, after))[0]


def ring_scatter(entry, axis):
    running = entry(axis.size - 1)
    for back in range(axis.size - 1, 0, -1):
        running = add_low(axis.rotate(running, -1), entry(back - 1))
    return running


GATE_B, DOWN_B, CARRY_B, GAIN_ONE, SHIFT_ONE, GAIN_TWO, SHIFT_TWO, UP_B = range(8)
VECTOR_ROWS = 16
MIDDLE_ROWS = 640


def pack_kernel(devices, place_ref, *refs):
    early_sources, late_sources, vector_refs, (early_ref, all_ref) = refs[:4], refs[4:8], refs[8:16], refs[16:]
    width = early_ref.shape[1]
    early_count = early_ref.shape[0]
    for target, start, sources in (
        (early_ref, 0, early_sources),
        (all_ref, 0, early_sources),
        (all_ref, early_count, late_sources),
    ):
        for source in sources:
            rows = source.shape[0]
            for column in range(0, source.shape[1], width):
                target[start : start + rows, :] = source[:, column : column + width]
                start += rows
    block = jnp.zeros((VECTOR_ROWS, width), jnp.float32)
    line = lax.broadcasted_iota(jnp.int32, block.shape, 0)
    for index, source in enumerate(vector_refs):
        count = source.shape[1]
        feature = lax.broadcasted_iota(jnp.int32, (count, width), 0) + place_ref[0] * count
        column = lax.broadcasted_iota(jnp.int32, (count, width), 1)
        for part in range(count * devices // width):
            spot = jnp.where(feature == column + part * width, jnp.float32(1.0), jnp.float32(0.0))
            spread = matmul(source[...], spot.astype(jnp.bfloat16))
            block += jnp.where(line == index + part, spread, jnp.float32(0.0))
    early_ref[early_count - VECTOR_ROWS :, :] = block.astype(jnp.bfloat16)
    all_ref[early_count - VECTOR_ROWS : early_count, :] = block.astype(jnp.bfloat16)


def unpack_kernel(place_ref, *refs):
    sources, (query_ref, key_ref, value_ref, gate_ref, vectors_ref) = refs[:4], refs[4:]
    size = sources[0].shape[0]
    rows = (sources[0].shape[1] - VECTOR_ROWS) // 4
    vectors = jnp.zeros(vectors_ref.shape, jnp.float32)
    for index in range(len(sources) * size):
        source = sources[index // size].at[index % size]
        target = pl.ds(pl.multiple_of(place_ref[index] * rows, rows), rows)
        for part, weight_ref in enumerate((query_ref, key_ref, value_ref, gate_ref)):
            weight_ref[target, :] = source[part * rows : (part + 1) * rows, :]
        vectors += source[4 * rows :, :].astype(jnp.float32)
    vectors_ref[...] = vectors


def unpack_late(place_ref, line_sources, plane_sources, output_ref, up_ref, down_ref, carry_ref):
    part_size = line_sources[0].shape[0]
    devices = part_size * len(line_sources)
    width = output_ref.shape[1]
    rows = output_ref.shape[0] // devices
    down_rows = down_ref.shape[0] // devices
    for index in range(devices):
        source = line_sources[index // part_size].at[index % part_size]
        target = pl.ds(pl.multiple_of(place_ref[0, index] * rows, rows), rows)
        output_ref[target, :] = source[:rows, :]
        for part in range(up_ref.shape[1] // width):
            up_ref[target, part * width : (part + 1) * width] = source[(part + 1) * rows : (part + 2) * rows, :]
        source = plane_sources[index // part_size].at[index % part_size]
        target = pl.ds(pl.multiple_of(place_ref[1, index] * down_rows, down_rows), down_rows)
        down_ref[target, :] = source[:down_rows, :]
        target = pl.ds(pl.multiple_of(place_ref[1, index] * rows, rows), rows)
        carry_ref[target, :] = source[down_rows:, :]


def spread_rows(place_ref, grad_ref, pack_refs, start, rows):
    size = pack_refs[0].shape[0]
    for index in range(size * len(pack_refs)):
        source = pl.ds(pl.multiple_of(place_ref[index] * rows, rows), rows)
        target = pack_refs[index // size].at[index % size]
        target[start : start + rows, :] = grad_ref[source, :].astype(jnp.bfloat16)


def middle_kernel(
    place_ref,
    attended_ref,
    input_ref,
    normed_ref,
    cotangent_ref,
    gate_weight_ref,
    vectors_ref,
    *refs,
):
    late_refs, refs = refs[:8], refs[8:]
    block_ref, row_targets, pack_targets, refs = refs[0], refs[1:5], refs[5:9], refs[9:]
    output_weight, up_weight, down_weight, carry_weight, hidden, up_pre_grads = refs[:6]
    update_grads, normed_second, carry_pre_grads, branch_grads, up_grad, down_grad, square_grads = refs[6:13]
    row_refs, pack_refs, row_departures, pack_departures = refs[13:17], refs[17:21], refs[21], refs[22]
    output_ref, middle_grad_ref, attended_grad_ref, gate_pre_ref = row_refs
    unpack_late(
        place_ref,
        late_refs[:4],
        late_refs[4:],
        output_weight,
        up_weight,
        down_weight,
        carry_weight,
    )
    width = output_ref.shape[1]
    hidden_width = up_weight.shape[1]
    wide = hidden_width // width

    def vector(line):
        return vectors_ref[line : line + 1, :]

    up_bias = jnp.concatenate([vector(UP_B + part) for part in range(wide)], axis=1)

    def column_lines(values):
        return jnp.sum(values.astype(jnp.float32), axis=0, keepdims=True)

    def some_rows(step, totals):
        rows = pl.ds(pl.multiple_of(step * MIDDLE_ROWS, MIDDLE_ROWS), MIDDLE_ROWS)
        gate_open = jax.nn.sigmoid(matmul(normed_ref[rows, :], gate_weight_ref[...]) + vector(GATE_B))
        branch = matmul(attended_ref[rows, :], output_weight[...])
        middle = input_ref[rows, :].astype(jnp.float32) + gate_open * branch
        centered = middle - jnp.mean(middle, axis=-1, keepdims=True)
        scale = lax.rsqrt(jnp.mean(centered * centered, axis=-1, keepdims=True) + EPSILON)
        hat = centered * scale
        normed = (hat * vector(GAIN_TWO) + vector(SHIFT_TWO)).astype(jnp.bfloat16)
        up_pre = matmul(normed, up_weight[...]) + up_bias
        up_open = jax.nn.sigmoid(up_pre)
        hidden_rows = (up_pre * up_open).astype(jnp.bfloat16)
        update = matmul(hidden_rows, down_weight[...]) + vector(DOWN_B)
        carry_open = jax.nn.sigmoid(matmul(normed, carry_weight[...]) + vector(CARRY_B))
        output_ref[rows, :] = (middle + carry_open * update).astype(jnp.bfloat16)

        grad_out = cotangent_ref[rows, :].astype(jnp.float32)
        update_grad = (carry_open * grad_out).astype(jnp.bfloat16)
        carry_pre_grad = (grad_out * update * carry_open * (1.0 - carry_open)).astype(jnp.bfloat16)
        slope = up_open * (1.0 + up_pre * (1.0 - up_open))
        up_pre_grad = (against(update_grad, down_weight[...]) * slope).astype(jnp.bfloat16)
        norm_grad = against(up_pre_grad, up_weight[...]) + against(carry_pre_grad, carry_weight[...])
        pull = norm_grad * vector(GAIN_TWO)
        middle_grad = grad_out + scale * (
            pull - jnp.mean(pull, axis=-1, keepdims=True) - hat * jnp.mean(pull * hat, axis=-1, keepdims=True)
        )
        middle_grad_ref[rows, :] = middle_grad
        branch_grad = (gate_open * middle_grad).astype(jnp.bfloat16)
        gate_pre_grad = (middle_grad * branch * gate_open * (1.0 - gate_open)).astype(jnp.bfloat16)
        gate_pre_ref[rows, :] = gate_pre_grad
        attended_grad_ref[rows, :] = against(branch_grad, output_weight[...]).astype(jnp.bfloat16)

        hidden[rows, :] = hidden_rows
        up_pre_grads[rows, :] = up_pre_grad
        update_grads[rows, :] = update_grad
        normed_second[rows, :] = normed
        carry_pre_grads[rows, :] = carry_pre_grad
        branch_grads[rows, :] = branch_grad
        lines = (gate_pre_grad, update_grad, carry_pre_grad, norm_grad * hat, norm_grad, up_pre_grad)
        return tuple(total + column_lines(line) for total, line in zip(totals, lines))

    start = (jnp.zeros((1, width), jnp.float32),) * 5 + (jnp.zeros((1, hidden_width), jnp.float32),)
    totals = lax.fori_loop(0, output_ref.shape[0] // MIDDLE_ROWS, some_rows, start)
    line = lax.broadcasted_iota(jnp.int32, block_ref.shape, 0)
    block = jnp.zeros(block_ref.shape, jnp.float32)
    for place, total in zip((GATE_B, DOWN_B, CARRY_B, GAIN_TWO, SHIFT_TWO), totals):
        block = jnp.where(line == place, total, block)
    for part in range(wide):
        block = jnp.where(line == UP_B + part, totals[5][:, part * width : (part + 1) * width], block)
    block_ref[...] = block
    leaving = []

    def leave(source, target, departure):
        leaving.append(pltpu.make_async_copy(source, target, departure))
        leaving[-1].start()

    def packs_leave(group, start, stop):
        for index, (source, target) in enumerate(zip(pack_refs, pack_targets)):
            here = (slice(None), slice(start, stop), slice(None))
            leave(source.at[here], target.at[here], pack_departures.at[group, index])

    for index, (source, target) in enumerate(zip(row_refs, row_targets)):
        leave(source, target, row_departures.at[index])

    target_ref = place_ref.at[2]
    rows = width // (4 * pack_refs[0].shape[0])
    place = 0
    for part in range(wide):
        grad = up_grad.at[part]
        grad[...] = inner_rows(normed_second[...], up_pre_grads[:, part * width : (part + 1) * width])
        spread_rows(target_ref, grad, pack_refs, place, rows)
        place += rows
    packs_leave(0, 0, place)
    for part in range(wide):
        here = slice(part * width, (part + 1) * width)
        down_grad[here, :] = inner_rows(hidden[:, here], update_grads[...])
    spread_rows(target_ref, down_grad, pack_refs, place, wide * rows)
    packs_leave(1, place, place + wide * rows)
    place += wide * rows
    pairs = ((normed_second, carry_pre_grads), (attended_ref, branch_grads), (normed_ref, gate_pre_ref))
    for index, (left_ref, right_ref) in enumerate(pairs):
        grad = square_grads.at[index]
        grad[...] = inner_rows(left_ref[...], right_ref[...])
        spread_rows(target_ref, grad, pack_refs, place, rows)
        place += rows
    packs_leave(2, 2 * wide * rows, place)
    for copy in leaving:
        copy.wait()


def second_grads_kernel(
    place_ref,
    both_grads_ref,
    normed_ref,
    query_grad_ref,
    gate_pre_ref,
    lanes_ref,
    query_weight_ref,
    key_weight_ref,
    value_weight_ref,
    gate_weight_ref,
    vectors_ref,
    block_ref,
    *refs,
):
    pack_refs, grads = refs[:4], refs[4]
    width = pack_refs[0].shape[2]
    rows = width // (4 * pack_refs[0].shape[0])
    grads[0] = inner_rows(normed_ref[...], query_grad_ref[...])
    grads[1] = jnp.transpose(both_grads_ref[:width, :])
    grads[2] = jnp.transpose(both_grads_ref[width:, :])
    for index in range(3):
        spread_rows(place_ref, grads.at[index], pack_refs, index * rows, rows)
    gate_grad = inner_rows(normed_ref[...], gate_pre_ref[...])

    def line_sums(ref):
        return jnp.sum(ref[...].astype(jnp.float32), axis=0, keepdims=True)

    def as_line(column):
        return jnp.transpose(jnp.broadcast_to(column, (width, BLK)))[:1, :]

    lines = (
        line_sums(query_grad_ref),
        jnp.sum(jnp.transpose(lanes_ref[:width, :]), axis=0, keepdims=True),
        jnp.sum(jnp.transpose(lanes_ref[width:, :]), axis=0, keepdims=True),
        line_sums(gate_pre_ref),
    )
    weighted = jnp.zeros((width, width), jnp.float32)
    shifted = jnp.zeros((width, width), jnp.float32)
    weight_refs = (query_weight_ref, key_weight_ref, value_weight_ref, gate_weight_ref)
    for weight_ref, line, grad in zip(weight_refs, lines, (grads[0], grads[1], grads[2], gate_grad)):
        weight = weight_ref[...].astype(jnp.float32)
        weighted += weight * grad
        shifted += weight * line
    shift_line = as_line(jnp.sum(shifted, axis=1, keepdims=True))
    gain_line = (
        as_line(jnp.sum(weighted, axis=1, keepdims=True)) - vectors_ref[SHIFT_ONE : SHIFT_ONE + 1, :] * shift_line
    ) / vectors_ref[GAIN_ONE : GAIN_ONE + 1, :]
    place = lax.broadcasted_iota(jnp.int32, block_ref.shape, 0)
    block = jnp.where(place == GAIN_ONE, gain_line, block_ref[...])
    block = jnp.where(place == SHIFT_ONE, shift_line, block).astype(jnp.bfloat16)
    for pack_ref in pack_refs:
        for index in range(pack_ref.shape[0]):
            pack_ref[index, 3 * rows :, :] = block


def own_kernel(device_ref, arrived_ref, kept_ref, *refs):
    second_refs, weight_refs, line_refs = refs[:4], refs[4:12], refs[12:]
    width = arrived_ref.shape[1]
    first = arrived_ref[...].astype(jnp.float32) + kept_ref[...].astype(jnp.float32)
    second = sum(ref[...].astype(jnp.float32) for ref in second_refs)
    start = 0
    source = first
    for index, ref in enumerate(weight_refs):
        if index == 5:
            start, source = 0, second
        rows = ref.shape[0]
        for column in range(0, ref.shape[1], width):
            ref[:, column : column + width] = source[start : start + rows, :]
            start += rows
    lines = second[start:, :]
    place = lax.broadcasted_iota(jnp.int32, lines.shape, 0)
    for index, ref in enumerate(line_refs):
        count = ref.shape[1]
        offset = device_ref[0] * count
        line = jnp.where(place == index + offset // width, lines, jnp.float32(0.0))
        line = jnp.broadcast_to(jnp.sum(line, axis=0, keepdims=True), (8, width))
        ref[...] = pltpu.roll(line, (width - offset % width) % width, 1)[:1, :count]


def input_grad_kernel(input_ref, local_ref, middle_grad_ref, vectors_ref, *refs):
    shared_refs, output_ref = refs[:-1], refs[-1]
    blocks = [sum(ref[index].astype(jnp.float32) for ref in shared_refs) for index in range(shared_refs[0].shape[0])]
    shared = jnp.concatenate([jnp.transpose(block) for block in blocks])
    values = input_ref[...].astype(jnp.float32)
    centered = values - jnp.mean(values, axis=-1, keepdims=True)
    scale = lax.rsqrt(jnp.mean(centered * centered, axis=-1, keepdims=True) + EPSILON)
    hat = centered * scale
    pull = (local_ref[...] + shared) * vectors_ref[GAIN_ONE : GAIN_ONE + 1, :]
    output_ref[...] = middle_grad_ref[...] + scale * (
        pull - jnp.mean(pull, axis=-1, keepdims=True) - hat * jnp.mean(pull * hat, axis=-1, keepdims=True)
    )


def local_call(kernel, cost, outs, smem, args, scratch=()):
    return pl.pallas_call(
        kernel,
        cost_estimate=about(cost),
        out_shape=outs,
        in_specs=[in_smem()] + [in_vmem()] * len(args),
        out_specs=jax.tree.map(lambda out: in_vmem(), outs),
        scratch_shapes=list(scratch),
        compiler_params=pltpu.CompilerParams(vmem_limit_bytes=VMEM_BYTES),
    )(smem, *args)


def joined(pieces, axis):
    return pieces[0] if len(pieces) == 1 else jnp.concatenate(pieces, axis=axis)


def shards(
    inputs,
    cotangent,
    block_segment,
    segment_parent,
    query_weight,
    key_weight,
    value_weight,
    output_weight,
    gate_weight,
    gate_bias,
    up_weight,
    up_bias,
    down_weight,
    down_bias,
    carry_weight,
    carry_bias,
    first_gain,
    first_shift,
    second_gain,
    second_shift,
):
    width = inputs.shape[1]
    devices = lax.axis_size(BOTH)
    block_count = inputs.shape[0] // BLK
    group_blocks = block_segment.shape[0]

    axis_z, axis_x, axis_y, axis_core = axes()
    rows_each = query_weight.shape[0]
    sizes = (axis_z.size, axis_x.size, axis_y.size, axis_core.size)
    direct = sizes == (4, 2, 2, 2) and rows_each % 16 == 0
    places = relative_devices()
    targets = scatter_devices()
    device = lax.axis_index(BOTH)
    vectors = (gate_bias, down_bias, carry_bias, first_gain, first_shift, second_gain, second_shift, up_bias)
    early_set = (query_weight, key_weight, value_weight, gate_weight)
    late_set = (output_weight, up_weight, down_weight, carry_weight)
    low = jnp.bfloat16

    def struct(*shape, dtype=low):
        return jax.ShapeDtypeStruct(shape, dtype)

    def take(source, start, piece):
        rows = piece.shape[0]
        parts = piece.shape[1] // width
        blocks = [
            source[:, start + part * rows : start + (part + 1) * rows].reshape(devices * rows, width)
            for part in range(parts)
        ]
        return joined(blocks, 1), start + parts * rows

    def flat_rows(pieces):
        return [piece[:, start : start + width] for piece in pieces for start in range(0, piece.shape[1], width)]

    own_start = lax.axis_index("seq") * block_count
    own_segments = lax.dynamic_slice_in_dim(block_segment, own_start, block_count)
    ancestor_slot, usable = ancestor_slots(block_segment, segment_parent, own_segments)
    owner = ancestor_slot // block_count
    away_z = (axis_z.position() - owner // axis_x.size) % axis_z.size
    away_x = (axis_x.position() - owner % axis_x.size) % axis_x.size
    relative_slot = (away_z * axis_x.size + away_x) * block_count + ancestor_slot % block_count
    tables = used_places(relative_slot, usable, group_blocks)
    slots = jnp.concatenate(
        [relative_slot, jnp.sum(usable, axis=-1, keepdims=True, dtype=jnp.int32)], axis=-1
    )

    if direct:
        early_count = 4 * rows_each + VECTOR_ROWS
        late_count = sum(piece.shape[0] * piece.shape[1] // width for piece in late_set)
        early, both = local_call(
            functools.partial(pack_kernel, devices),
            0.1,
            (struct(early_count, width), struct(early_count + late_count, width)),
            device.reshape(1),
            early_set + late_set + tuple(vector.reshape(1, -1) for vector in vectors),
        )
        both_one = axis_z.rotate(both, 1)
        early_line = [axis_z.rotate(early, back) for back in range(2, 4)]
        x_zero = axis_x.rotate(inputs, 1)
        z_one = axis_z.rotate(inputs, 1)
        both_one, early_line, x_zero, z_one = lax.optimization_barrier((both_one, early_line, x_zero, z_one))
        early_line = [both_one[:early_count]] + list(early_line)
        late_line = [both[early_count:], both_one[early_count:]]
        z_two = axis_z.rotate(z_one, 1)
        x_one = axis_x.rotate(z_one, 1)
        early_line = jnp.stack([early] + list(early_line))
        early_other = axis_x.rotate(early_line, 1)
        late_line.append(axis_z.rotate(late_line[1], 1))
        early_other, z_two, x_one, late_line[2], slots, tables = lax.optimization_barrier(
            (early_other, z_two, x_one, late_line[2], slots, tables)
        )
        z_three = axis_z.rotate(z_two, 1)
        x_two = axis_x.rotate(z_two, 1)
        early_plane = jnp.stack([early_line, early_other])
        early_other = axis_y.rotate(early_plane, 1)
        late_line.append(axis_z.rotate(late_line[2], 1))
        early_other, z_three, x_two, late_line[3] = lax.optimization_barrier(
            (early_other, z_three, x_two, late_line[3])
        )
        x_three = axis_x.rotate(z_three, 1)
        early_parts = [early_plane, early_other]
        early_parts += [axis_core.rotate(part, 1) for part in early_parts]
        early_parts = [part.reshape(devices // 4, early_count, width) for part in early_parts]
        input_pieces = [[inputs, x_zero], [z_one, x_one], [z_two, x_two], [z_three, x_three]]
        square = struct(width, width)
        full_query, full_key, full_value, full_gate, vector_rows = local_call(
            unpack_kernel,
            3,
            (square, square, square, square, struct(VECTOR_ROWS, width, dtype=jnp.float32)),
            places,
            early_parts,
        )
        late_line, full_key = lax.optimization_barrier((late_line, full_key))
        late_half = late_count // 2
        late_x = jnp.stack([rows[:late_half] for rows in late_line])
        late_y = jnp.stack([rows[late_half:] for rows in late_line])
        late_x_other = axis_x.rotate(late_x, 1)
        late_y_other = axis_y.rotate(late_y, 1)
    else:
        early_rows = lax.all_gather(jnp.concatenate(early_set), BOTH)
        late_rows = lax.all_gather(jnp.concatenate(flat_rows(late_set)), BOTH)
        place = 0
        full_query, place = take(early_rows, place, query_weight)
        full_key, place = take(early_rows, place, key_weight)
        full_value, place = take(early_rows, place, value_weight)
        full_gate, place = take(early_rows, place, gate_weight)
        place = 0
        full_output, place = take(late_rows, place, output_weight)
        full_up, place = take(late_rows, place, up_weight)
        full_down, place = take(late_rows, place, down_weight)
        full_carry, place = take(late_rows, place, carry_weight)
        lines = [lax.all_gather(vector, BOTH, tiled=True).reshape(-1, width) for vector in vectors]
        lines = jnp.concatenate(lines).astype(jnp.float32)
        vector_rows = jnp.pad(lines, ((0, VECTOR_ROWS - lines.shape[0]), (0, 0)))
        input_pieces = []
        along_z = inputs
        for step_z in range(axis_z.size):
            along_x = along_z
            row = []
            for step_x in range(axis_x.size):
                row.append(along_x)
                along_x = axis_x.rotate(along_x, 1) if step_x + 1 < axis_x.size else None
            input_pieces.append(row)
            along_z = axis_z.rotate(along_z, 1) if step_z + 1 < axis_z.size else None

    both_weight = jnp.concatenate([full_key, full_value], axis=1)

    group_rows = group_blocks * BLK
    pieces = [piece for row in input_pieces for piece in row]
    near = len(pieces) - 1 if direct else len(pieces)
    *carried, normed_low, query_low = project(
        pieces[:near], vector_rows, full_key, full_value, group_rows, 0, None, full_query
    )
    if direct:
        late_y_other, late_x_other, x_three, carried, both_weight = lax.optimization_barrier(
            (late_y_other, late_x_other, pieces[near], carried, both_weight)
        )
        late_x = jnp.stack([late_x, late_x_other])
        late_y = jnp.stack([late_y, late_y_other])
        late_x_other = axis_y.rotate(late_x, 1)
        late_y_other = axis_x.rotate(late_y, 1)
        attended_low, logsum, *carried = project_and_attend(
            slots, query_low, x_three, vector_rows, full_key, full_value, carried
        )
    normed_group, key_group, value_group = carried

    gate_b, down_b, carry_b, gain_one, shift_one, gain_two, shift_two = [vector_rows[line] for line in range(UP_B)]
    up_b = vector_rows[UP_B : UP_B + up_weight.shape[1] // width].reshape(-1)

    values_in = inputs.astype(jnp.float32)
    if not direct:
        attended_low, logsum = attend(slots, query_low, key_group, value_group)

    if direct:
        attended_low, late_x_other, late_y_other = lax.optimization_barrier((attended_low, late_x_other, late_y_other))
        late_parts = []
        for mine in ((late_x, late_x_other), (late_y, late_y_other)):
            for piece in list(mine) + [axis_core.rotate(part, 1) for part in mine]:
                late_parts.append(piece.reshape(devices // 4, late_half, width))
        other_places = jnp.transpose(places.reshape(2, 2, 2, 4), (0, 2, 1, 3)).reshape(-1)
        rows = inputs.shape[0]
        first_rows = late_count + rows_each
        hidden_width = up_weight.shape[1]
        quarter = struct(devices // 4, first_rows, width)
        tall, short = pltpu.VMEM((rows, hidden_width), low), pltpu.VMEM((rows, width), low)
        wide = (struct(rows, width), struct(rows, width, dtype=jnp.float32), struct(rows, width), struct(rows, width))
        leaving = wide + (quarter,) * 4
        block, output, middle_grad, attended_grad, gate_pre_grad, *first = pl.pallas_call(
            middle_kernel,
            cost_estimate=about(20),
            out_shape=(struct(VECTOR_ROWS, width, dtype=jnp.float32),) + leaving,
            in_specs=[in_smem()] + [in_vmem()] * 14,
            out_specs=(in_vmem(),) + (anywhere(),) * len(leaving),
            scratch_shapes=[
                pltpu.VMEM((width, width), low),
                pltpu.VMEM((width, hidden_width), low),
                pltpu.VMEM((hidden_width, width), low),
                pltpu.VMEM((width, width), low),
                tall,
                tall,
                short,
                short,
                short,
                short,
                pltpu.VMEM((hidden_width // width, width, width), jnp.float32),
                pltpu.VMEM((hidden_width, width), jnp.float32),
                pltpu.VMEM((3, width, width), jnp.float32),
            ]
            + [pltpu.VMEM(out.shape, out.dtype) for out in leaving]
            + [pltpu.SemaphoreType.DMA((4,)), pltpu.SemaphoreType.DMA((3, 4))],
            compiler_params=pltpu.CompilerParams(vmem_limit_bytes=VMEM_BYTES),
        )(
            jnp.stack([places, other_places, targets]),
            attended_low,
            inputs,
            normed_low,
            cotangent,
            full_gate,
            vector_rows,
            *late_parts,
        )
        first = [pack.reshape(4, 2, first_rows, width) for pack in first]
        first_core = [axis_core.rotate(first[2 + index], -1) for index in range(2)]
        first_keep, first_send = [add_low(first_core[index], first[index]) for index in range(2)]
        attended_grad, first_keep, first_send = lax.optimization_barrier((attended_grad, first_keep, first_send))
        first_arrived = axis_y.rotate(first_send, -1)
    else:
        gate_open = jax.nn.sigmoid(matmul(normed_low, full_gate) + gate_b)
        branch = matmul(attended_low, full_output)
        middle = values_in + gate_open * branch
        normed_second = normalize(middle, gain_two, shift_two).astype(jnp.bfloat16)
        up_pre = matmul(normed_second, full_up) + up_b
        up_sigmoid = jax.nn.sigmoid(up_pre)
        hidden_low = (up_pre * up_sigmoid).astype(jnp.bfloat16)
        update = matmul(hidden_low, full_down) + down_b
        carry_open = jax.nn.sigmoid(matmul(normed_second, full_carry) + carry_b)
        output = (middle + carry_open * update).astype(jnp.bfloat16)

        grad_out = cotangent.astype(jnp.float32)
        update_grad = (carry_open * grad_out).astype(jnp.bfloat16)
        carry_pre_grad = (grad_out * update * carry_open * (1.0 - carry_open)).astype(jnp.bfloat16)
        grad_down_bias = column_sums(update_grad)
        grad_carry_bias = column_sums(carry_pre_grad)
        silu_slope = up_sigmoid * (1.0 + up_pre * (1.0 - up_sigmoid))
        up_pre_grad = (against(update_grad, full_down) * silu_slope).astype(jnp.bfloat16)
        grad_up_bias = column_sums(up_pre_grad)
        second_norm_grad = against(up_pre_grad, full_up) + against(carry_pre_grad, full_carry)
        second_pull = jax.vjp(normalize, middle, gain_two, shift_two)[1]
        middle_part, grad_second_gain, grad_second_shift = second_pull(second_norm_grad)
        middle_grad = grad_out + middle_part

        branch_grad = (gate_open * middle_grad).astype(jnp.bfloat16)
        gate_pre_grad = (middle_grad * branch * gate_open * (1.0 - gate_open)).astype(jnp.bfloat16)
        grad_gate_bias = column_sums(gate_pre_grad)
        attended_grad = against(branch_grad, full_output).astype(jnp.bfloat16)
        zero_line = jnp.zeros((width,), jnp.float32)
        local_lines = (
            grad_gate_bias,
            grad_down_bias,
            grad_carry_bias,
            zero_line,
            zero_line,
            grad_second_gain,
            grad_second_shift,
            grad_up_bias,
        )
        block = jnp.concatenate([line.reshape(-1, width) for line in local_lines])
        block = jnp.pad(block, ((0, VECTOR_ROWS - block.shape[0]), (0, 0)))
    backward = attend_backward(
        (slots,) + tables,
        query_low,
        key_group,
        value_group,
        logsum,
        attended_low,
        attended_grad,
        normed_group,
        both_weight,
    )
    if direct:
        backward, first_arrived = lax.optimization_barrier((backward, first_arrived))

        def first_y(back):
            return add_low(first_arrived[back], first_keep[back])

        first_z = axis_z.rotate(first_y(3), -1)
    query_rows_grad, both_grads, lanes = backward[:3]

    shared_parts = backward[3:]

    if direct:
        second_rows = 3 * rows_each + VECTOR_ROWS
        quarter = struct(devices // 4, second_rows, width)
        second = local_call(
            second_grads_kernel,
            0.1,
            (quarter,) * 4,
            places,
            (
                both_grads,
                normed_low,
                query_rows_grad,
                gate_pre_grad,
                lanes,
                full_query,
                full_key,
                full_value,
                full_gate,
                vector_rows,
                block,
            ),
            (pltpu.VMEM((3, width, width), jnp.float32),),
        )
        second = [pack.reshape(2, 4, second_rows, width) for pack in second]
        barrier = lax.optimization_barrier
        first_z = axis_z.rotate(add_low(first_z, first_y(2)), -1)
        x_three = axis_x.rotate(shared_parts[7], -1)
        x_three, first_z, second = barrier((x_three, first_z, second))

        second_core = [axis_core.rotate(second[2 + index], -1) for index in range(2)]
        second_keep = add_low(second_core[0], second[0])
        second_arrived = axis_y.rotate(add_low(second_core[1], second[1]), -1)
        x_two = axis_x.rotate(tied(shared_parts[5], x_three), -1)
        z_three = axis_z.rotate(add_low(x_three, shared_parts[6]), -1)
        x_two, z_three, second_arrived = barrier((x_two, z_three, second_arrived))

        second_y = add_low(second_arrived, second_keep)
        second_x = axis_x.rotate(second_y[1], -1)
        x_one = axis_x.rotate(tied(shared_parts[3], x_two), -1)
        z_two = axis_z.rotate(add_three(x_two, shared_parts[4], z_three), -1)
        first_z = axis_z.rotate(add_low(tied(first_z, x_two), first_y(1)), -1)
        x_one, z_two, second_x, first_z = barrier((x_one, z_two, second_x, first_z))

        first_half = add_low(first_z, first_y(0))
        first_x = axis_x.rotate(tied(first_half[1], x_one), -1)
        second_half = add_low(second_x, second_y[0])
        second_z = [axis_z.rotate(second_half[back], -back) for back in range(1, 4)]
        x_zero = axis_x.rotate(tied(shared_parts[1], x_one), -1)
        z_one = axis_z.rotate(add_three(x_one, shared_parts[2], z_two), -1)
        shared = (x_zero, z_one, shared_parts[0])
    else:
        grad_key = jnp.transpose(both_grads[:width])
        grad_value = jnp.transpose(both_grads[width:])
        grad_query = inner_rows(normed_low, query_rows_grad)
        grad_gate = inner_rows(normed_low, gate_pre_grad)
        both_sums = jnp.sum(lanes, axis=1)
        weights = [weight.astype(jnp.float32) for weight in (full_query, full_key, full_value, full_gate)]
        line_sums = (column_sums(query_rows_grad), both_sums[:width], both_sums[width:], grad_gate_bias)
        shift_line = sum(jnp.sum(weight * line, axis=1) for weight, line in zip(weights, line_sums))
        weighted = sum(
            jnp.sum(weight * grad, axis=1)
            for weight, grad in zip(weights, (grad_query, grad_key, grad_value, grad_gate))
        )
        block = block.at[GAIN_ONE].set((weighted - shift_one * shift_line) / gain_one).at[SHIFT_ONE].set(shift_line)
        grads = (
            (inner_rows(normed_second, up_pre_grad), up_weight),
            (inner_rows(hidden_low, update_grad), down_weight),
            (inner_rows(normed_second, carry_pre_grad), carry_weight),
            (inner_rows(attended_low, branch_grad), output_weight),
            (grad_gate, gate_weight),
            (grad_query, query_weight),
            (grad_key, key_weight),
            (grad_value, value_weight),
        )
        pack = [
            cut.astype(low).reshape(devices, piece.shape[0], width)
            for grad, piece in grads
            for cut in flat_rows((grad,))
        ]
        pack.append(jnp.broadcast_to(block.astype(low), (devices, VECTOR_ROWS, width)))
        pack = jnp.concatenate(pack, axis=1)
        pack = jnp.pad(pack, ((0, 0), (0, -pack.shape[1] % 16), (0, 0)))
        weight_sum = lax.psum_scatter(pack, BOTH, scatter_dimension=0, tiled=True)[0].astype(jnp.float32)

        def over_x(step_z):
            return ring_scatter(lambda step_x: shared_parts[step_z * axis_x.size + step_x], axis_x)

        shared = (ring_scatter(over_x, axis_z),)

    local_grad = against(query_rows_grad, full_query) + against(gate_pre_grad, full_gate)
    input_grad = pl.pallas_call(
        input_grad_kernel,
        cost_estimate=about(3),
        out_shape=struct(block_count * BLK, width, dtype=jnp.float32),
        compiler_params=pltpu.CompilerParams(vmem_limit_bytes=VMEM_BYTES),
    )(inputs, local_grad, middle_grad, vector_rows, *shared)

    if direct:
        input_grad, first_x, second_z = lax.optimization_barrier((input_grad, first_x, second_z))
        square = struct(rows_each, width, dtype=jnp.float32)
        tall = struct(down_weight.shape[0], width, dtype=jnp.float32)
        broad = struct(rows_each, up_weight.shape[1], dtype=jnp.float32)
        weight_outs = (broad, tall, square, square, square, square, square, square)
        line_outs = tuple(struct(1, vector.shape[0], dtype=jnp.float32) for vector in vectors)
        own_grads = local_call(
            own_kernel,
            2,
            weight_outs + line_outs,
            device.reshape(1),
            (first_x, first_half[0], second_half[0], *second_z),
        )
        own_up, own_down, own_carry, own_output, own_gate, own_query, own_key, own_value = own_grads[:8]
        vector_out = [line.reshape(-1) for line in own_grads[8:]]
    else:
        def own(start, piece):
            rows = piece.shape[0]
            parts = piece.shape[1] // width
            blocks = [weight_sum[start + part * rows : start + (part + 1) * rows] for part in range(parts)]
            return joined(blocks, 1), start + parts * rows

        place = 0
        own_up, place = own(place, up_weight)
        own_down, place = own(place, down_weight)
        own_carry, place = own(place, carry_weight)
        own_output, place = own(place, output_weight)
        own_gate, place = own(place, gate_weight)
        own_query, place = own(place, query_weight)
        own_key, place = own(place, key_weight)
        own_value, place = own(place, value_weight)
        vector_out = []
        for index, vector in enumerate(vectors):
            count = vector.shape[0]
            lines = weight_sum[place + index : place + index + count * devices // width].reshape(-1)
            vector_out.append(lax.dynamic_slice_in_dim(lines, device * count, count))
    gate_bg, down_bg, carry_bg, gain_one_g, shift_one_g, gain_two_g, shift_two_g, up_bg = vector_out
    return (
        output,
        input_grad,
        own_query,
        own_key,
        own_value,
        own_output,
        own_gate,
        gate_bg,
        own_up,
        up_bg,
        own_down,
        down_bg,
        own_carry,
        carry_bg,
        gain_one_g,
        shift_one_g,
        gain_two_g,
        shift_two_g,
    )


def solution(mesh):
    rows = P(BOTH, None)
    line = P(BOTH)
    matrix_or_line = (rows,) * 5 + (line, rows, line, rows, line, rows) + (line,) * 5
    return jax.shard_map(
        shards,
        mesh=mesh,
        in_specs=(rows, rows, P("dp"), P("dp")) + matrix_or_line,
        out_specs=(rows, rows) + matrix_or_line,
        check_vma=False,
    )
```

```python
import functools

import jax
import jax.numpy as jnp
from jax import lax
from jax.experimental import pallas as pl
from jax.experimental.pallas import tpu as pltpu
from jax.sharding import PartitionSpec as P

HD = 64
BLK = 128
DEPTH = 10
PAIR = 2 * HD
PLACES = 4
TREE_BLOCKS = 20
TRUNK = 8

EPSILON = 1e-05
NEGATIVE = -1e30
BOTH = ("dp", "seq")
VMEM_BYTES = 60 * 1024 * 1024


def normalize(values, norm_gain, norm_shift):
    center = values - jnp.mean(values, axis=-1, keepdims=True)
    spread = jnp.mean(center * center, axis=-1, keepdims=True)
    return center * lax.rsqrt(spread + EPSILON) * norm_gain + norm_shift


def matmul(left_side, right_side):
    return jnp.dot(left_side, right_side, preferred_element_type=jnp.float32)


def inner_rows(left_side, right_side):
    return lax.dot_general(
        left_side, right_side, (((0,), (0,)), ((), ())), preferred_element_type=jnp.float32
    )


def against(left_side, right_side):
    return lax.dot_general(
        left_side, right_side, (((1,), (1,)), ((), ())), preferred_element_type=jnp.float32
    )


def column_sums(values):
    return jnp.sum(values.astype(jnp.float32), axis=0)


def lookup(lookup_table, wanted):
    entries = jnp.arange(lookup_table.shape[0], dtype=jnp.int32)
    matches = wanted[..., None] == entries
    located = jnp.sum(jnp.where(matches, lookup_table, jnp.int32(0)), axis=-1, dtype=jnp.int32)
    return jnp.where(wanted >= 0, located, jnp.int32(-1))


def ancestor_slots(block_segment, segment_parent, own_segments):
    entries = jnp.arange(block_segment.shape[0], dtype=jnp.int32)
    placed = block_segment[None, :] == entries[:, None]
    slot_of = jnp.sum(jnp.where(placed, entries[None, :], jnp.int32(0)), axis=1, dtype=jnp.int32)
    current = own_segments
    lineage = []
    for depth_step in range(DEPTH):
        lineage.append(current)
        current = lookup(segment_parent, current)
    lineage = jnp.stack(lineage, axis=-1)
    usable = lineage >= 0
    return (jnp.where(usable, lookup(slot_of, lineage), jnp.int32(0)), usable)


def stack_heads(rows):
    lane = lax.broadcasted_iota(jnp.int32, rows.shape, 1)
    low = lane < HD
    zero = jnp.zeros_like(rows)
    return jnp.concatenate([jnp.where(low, rows, zero), jnp.where(low, zero, rows)], axis=0)


def unstack_heads(rows):
    half = rows.shape[0] // 2
    lane = lax.broadcasted_iota(jnp.int32, (half, rows.shape[1]), 1)
    return jnp.where(lane < HD, rows[:half], rows[half:])


def make_bias(bias_ref):
    row = lax.broadcasted_iota(jnp.int32, bias_ref.shape, 0) % BLK
    col = lax.broadcasted_iota(jnp.int32, bias_ref.shape, 1)
    bias_ref[...] = jnp.where(col <= row, jnp.float32(0.0), jnp.float32(NEGATIVE))


def masked(scores, levels, bias_ref):
    col = lax.broadcasted_iota(jnp.int32, (1, (DEPTH - 1) * BLK), 1)
    line = jnp.where(col < (levels - 1) * BLK, jnp.float32(0.0), jnp.float32(NEGATIVE))
    return jnp.concatenate([scores[:, :BLK] + bias_ref[...], scores[:, BLK:] + line], axis=1)


class Levels:
    def __init__(self, slots_ref, sources, targets, arrivals):
        self.slots_ref = slots_ref
        self.pairs = tuple(zip(sources, targets))
        self.arrivals = arrivals

    def copies(self, slot):
        turn = slot % 2
        for level in range(DEPTH):
            start = pl.multiple_of(self.slots_ref[slot, level] * BLK, BLK)
            for index, (source, target) in enumerate(self.pairs):
                place = target.at[turn, level * BLK : (level + 1) * BLK, :]
                yield pltpu.make_async_copy(
                    source.at[pl.ds(start, BLK), :], place, self.arrivals.at[turn, index, level]
                )

    def start(self, slot):
        for copy in self.copies(slot):
            copy.start()

    def step(self, slot, count):
        @pl.when(slot + 1 < count)
        def ahead():
            self.start(slot + 1)

        for copy in self.copies(slot):
            copy.wait()


def forward_kernel(
    slots_ref, query_ref, key_source, value_source, mixed_ref, logsum_ref, key_here, value_here, bias_ref, arrivals
):
    width = query_ref.shape[1]
    count = query_ref.shape[0] // BLK
    levels = Levels(slots_ref, (key_source, value_source), (key_here, value_here), arrivals)
    levels.start(0)
    make_bias(bias_ref)

    def one_slot(slot, carry):
        rows = pl.ds(pl.multiple_of(slot * BLK, BLK), BLK)
        levels.step(slot, count)
        turn = slot % 2
        lane = lax.broadcasted_iota(jnp.int32, (BLK, PAIR), 1)
        logsums = jnp.zeros((BLK, PAIR), jnp.float32)
        for pair in range(width // PAIR):
            cols = slice(pair * PAIR, (pair + 1) * PAIR)
            stacked = stack_heads(query_ref[rows, cols])
            scores = masked(against(stacked, key_here[turn, :, cols]), slots_ref[slot, DEPTH], bias_ref)
            highest = jnp.max(scores, axis=-1, keepdims=True)
            raised = jnp.exp(scores - highest)
            total = jnp.sum(raised, axis=-1, keepdims=True)
            mixed = matmul(raised.astype(jnp.bfloat16), value_here[turn, :, cols]) / total
            mixed_ref[rows, cols] = unstack_heads(mixed).astype(jnp.bfloat16)
            logsum = highest + jnp.log(total)
            logsums = jnp.where(lane == 2 * pair, logsum[:BLK], logsums)
            logsums = jnp.where(lane == 2 * pair + 1, logsum[BLK:], logsums)
        logsum_ref[rows, :] = logsums
        return carry

    lax.fori_loop(0, count, one_slot, 0)


def last_forward_kernel(
    slots_ref,
    query_ref,
    piece_ref,
    vectors_ref,
    key_weight_ref,
    value_weight_ref,
    *refs,
):
    mixed_ref, logsum_ref = refs[3:5]
    targets = refs[5:8]
    key_here, value_here, bias_ref, arrivals, made, departures = refs[8:]
    gain = vectors_ref[GAIN_ONE : GAIN_ONE + 1, :]
    shift = vectors_ref[SHIFT_ONE : SHIFT_ONE + 1, :]
    rows = piece_ref.shape[0]
    first = targets[0].shape[0] - rows

    def leave(kind):
        return pltpu.make_async_copy(made.at[kind], targets[kind].at[first : first + rows, :], departures.at[kind])

    normed = normalize(piece_ref[...].astype(jnp.float32), gain, shift).astype(jnp.bfloat16)
    made[1] = matmul(normed, key_weight_ref[...]).astype(jnp.bfloat16)
    leave(1).start()
    made[2] = matmul(normed, value_weight_ref[...]).astype(jnp.bfloat16)
    leave(2).start()
    made[0] = normed
    leave(0).start()
    leave(1).wait()
    leave(2).wait()
    forward_kernel(
        slots_ref, query_ref, targets[1], targets[2], mixed_ref, logsum_ref, key_here, value_here, bias_ref, arrivals
    )
    leave(0).wait()


def backward_kernel(
    slots_ref,
    compact_ref,
    used_ref,
    seen_ref,
    query_ref,
    key_source,
    value_source,
    logsum_ref,
    mixed_ref,
    mixed_grad_ref,
    normed_source,
    weight_ref,
    query_grad_ref,
    grads_ref,
    lanes_ref,
    *refs,
):
    width = query_ref.shape[1]
    count = query_ref.shape[0] // BLK
    shared_refs = refs[:-11]
    key_here, value_here, bias_ref, normed_here, key_sums, value_sums = refs[-11:-5]
    stage, zero_block, arrivals, normed_arrivals, departures = refs[-5:]
    places = used_ref.shape[1] - 1
    used_count = used_ref[0, places]
    levels = Levels(slots_ref, (key_source, value_source), (key_here, value_here), arrivals)
    levels.start(0)

    def normed_copy(place):
        source = pl.ds(pl.multiple_of(used_ref[0, place] * BLK, BLK), BLK)
        target = normed_here.at[place * BLK : (place + 1) * BLK, :]
        return pltpu.make_async_copy(normed_source.at[source, :], target, normed_arrivals.at[place])

    for place in range(places):

        @pl.when(place < used_count)
        def fetch():
            normed_copy(place).start()

        @pl.when(place >= used_count)
        def clear():
            normed_here[place * BLK : (place + 1) * BLK, :] = jnp.zeros((BLK, normed_here.shape[1]), jnp.bfloat16)

    zero_block[...] = jnp.zeros_like(zero_block)
    for slot in range(count * len(shared_refs)):

        @pl.when(seen_ref[0, slot] == 0)
        def none():
            target = shared_refs[slot // count].at[slot % count]
            pltpu.make_async_copy(zero_block, target, departures.at[slot]).start()

    make_bias(bias_ref)
    key_sums[...] = jnp.zeros_like(key_sums)
    value_sums[...] = jnp.zeros_like(value_sums)

    def one_slot(slot, carry):
        rows = pl.ds(pl.multiple_of(slot * BLK, BLK), BLK)
        levels.step(slot, count)
        turn = slot % 2
        for pair in range(width // PAIR):
            cols = slice(pair * PAIR, (pair + 1) * PAIR)
            stacked = stack_heads(query_ref[rows, cols])
            grad_rows = mixed_grad_ref[rows, cols]
            grad_stacked = stack_heads(grad_rows)
            products = grad_rows.astype(jnp.float32) * mixed_ref[rows, cols].astype(jnp.float32)
            row_dot = jnp.sum(stack_heads(products), axis=-1, keepdims=True)
            logsum = jnp.concatenate(
                [logsum_ref[rows, 2 * pair : 2 * pair + 1], logsum_ref[rows, 2 * pair + 1 : 2 * pair + 2]], axis=0
            )
            key_rows = key_here[turn, :, cols]
            shares = jnp.exp(masked(against(stacked, key_rows), slots_ref[slot, DEPTH], bias_ref) - logsum)
            share_grad = against(grad_stacked, value_here[turn, :, cols])
            score_grad = (shares * (share_grad - row_dot)).astype(jnp.bfloat16)
            query_grad = unstack_heads(matmul(score_grad, key_rows)) * (HD ** (-0.5))
            query_grad_ref[rows, cols] = query_grad.astype(jnp.bfloat16)
            key_part = inner_rows(stacked, score_grad)
            value_part = inner_rows(grad_stacked, shares.astype(jnp.bfloat16))
            for level in range(DEPTH):
                start = pl.multiple_of(compact_ref[slot, level] * BLK, BLK)
                here = slice(level * BLK, (level + 1) * BLK)
                key_sums[cols, pl.ds(start, BLK)] += key_part[:, here]
                value_sums[cols, pl.ds(start, BLK)] += value_part[:, here]
        return carry

    lax.fori_loop(0, count, one_slot, 0)

    for place in range(places):

        @pl.when(place < used_count)
        def arrived():
            normed_copy(place).wait()

    grads_ref[...] = jnp.zeros_like(grads_ref)
    lanes_ref[...] = jnp.zeros_like(lanes_ref)

    def some_places(step, carry):
        here = pl.ds(pl.multiple_of(step * (PLACES * BLK), PLACES * BLK), PLACES * BLK)
        shared = None
        for part, part_sums in enumerate((key_sums, value_sums)):
            lines = slice(part * width, (part + 1) * width)
            block = part_sums[:, here]
            tiles = [block[:, start : start + BLK] for start in range(0, PLACES * BLK, BLK)]
            lanes_ref[lines, :] += functools.reduce(lambda left, right: left + right, tiles)
            block = block.astype(jnp.bfloat16)
            product = matmul(weight_ref[:, lines], block)
            shared = product if shared is None else shared + product
            grads_ref[lines, :] += matmul(block, normed_here[here, :])
        for index in range(PLACES):
            place = step * PLACES + index
            stage[place] = shared[:, index * BLK : (index + 1) * BLK].astype(jnp.bfloat16)

            slot = used_ref[0, jnp.minimum(place, used_count - 1)]
            for piece, shared_ref in enumerate(shared_refs):

                @pl.when((place < used_count) & (slot // count == piece))
                def leave():
                    target = shared_ref.at[slot - piece * count]
                    pltpu.make_async_copy(stage.at[place], target, departures.at[slot]).start()

        return carry

    lax.fori_loop(0, (used_count + PLACES - 1) // PLACES, some_places, 0)
    for slot in range(count * len(shared_refs)):
        target = shared_refs[slot // count].at[slot % count]
        pltpu.make_async_copy(zero_block, target, departures.at[slot]).wait()


def about(cost):
    return pl.CostEstimate(flops=int(cost * 1e9), bytes_accessed=int(cost * 1e6), transcendentals=0)


def in_vmem():
    return pl.BlockSpec(memory_space=pltpu.VMEM)


def in_smem():
    return pl.BlockSpec(memory_space=pltpu.SMEM)


def anywhere():
    return pl.BlockSpec(memory_space=pl.ANY)


def level_scratch(width):
    return [
        pltpu.VMEM((2, DEPTH * BLK, width), jnp.bfloat16),
        pltpu.VMEM((2, DEPTH * BLK, width), jnp.bfloat16),
        pltpu.VMEM((2 * BLK, BLK), jnp.float32),
    ]


def attend(slots, query_rows, key_group, value_group):
    rows, width = query_rows.shape
    return pl.pallas_call(
        forward_kernel,
        cost_estimate=about(18),
        out_shape=(
            jax.ShapeDtypeStruct((rows, width), jnp.bfloat16),
            jax.ShapeDtypeStruct((rows, PAIR), jnp.float32),
        ),
        in_specs=[in_smem(), in_vmem(), anywhere(), anywhere()],
        out_specs=(in_vmem(), in_vmem()),
        scratch_shapes=level_scratch(width) + [pltpu.SemaphoreType.DMA((2, 2, DEPTH))],
        compiler_params=pltpu.CompilerParams(vmem_limit_bytes=VMEM_BYTES),
    )(slots, query_rows, key_group, value_group)


def project_and_attend(slots, query_rows, piece, vectors, key_weight, value_weight, carried):
    rows, width = query_rows.shape
    whole = jax.ShapeDtypeStruct(carried[0].shape, jnp.bfloat16)
    return pl.pallas_call(
        last_forward_kernel,
        cost_estimate=about(20),
        out_shape=(
            jax.ShapeDtypeStruct((rows, width), jnp.bfloat16),
            jax.ShapeDtypeStruct((rows, PAIR), jnp.float32),
            whole,
            whole,
            whole,
        ),
        in_specs=[in_smem()] + [in_vmem()] * 5 + [anywhere()] * 3,
        out_specs=(in_vmem(), in_vmem(), anywhere(), anywhere(), anywhere()),
        scratch_shapes=level_scratch(width)
        + [
            pltpu.SemaphoreType.DMA((2, 2, DEPTH)),
            pltpu.VMEM((3, rows, width), jnp.bfloat16),
            pltpu.SemaphoreType.DMA((3,)),
        ],
        input_output_aliases={6: 2, 7: 3, 8: 4},
        compiler_params=pltpu.CompilerParams(vmem_limit_bytes=VMEM_BYTES),
    )(slots, query_rows, piece, vectors, key_weight, value_weight, *carried)


def attend_backward(tables, query_rows, key_group, value_group, logsum, mixed, mixed_grad, normed_group, both_weight):
    rows, width = query_rows.shape
    blocks = normed_group.shape[0] // BLK
    pieces = normed_group.shape[0] // rows
    places = tables[2].shape[1] - 1
    return pl.pallas_call(
        backward_kernel,
        cost_estimate=about(32),
        out_shape=(
            jax.ShapeDtypeStruct((rows, width), jnp.bfloat16),
            jax.ShapeDtypeStruct((2 * width, width), jnp.float32),
            jax.ShapeDtypeStruct((2 * width, BLK), jnp.float32),
        )
        + (jax.ShapeDtypeStruct((rows // BLK, width, BLK), jnp.bfloat16),) * pieces,
        in_specs=[in_smem()] * 4
        + [in_vmem(), anywhere(), anywhere(), in_vmem(), in_vmem(), in_vmem(), anywhere(), in_vmem()],
        out_specs=(in_vmem(),) * 3 + (anywhere(),) * pieces,
        scratch_shapes=level_scratch(width)
        + [
            pltpu.VMEM((places * BLK, width), jnp.bfloat16),
            pltpu.VMEM((width, places * BLK), jnp.float32),
            pltpu.VMEM((width, places * BLK), jnp.float32),
            pltpu.VMEM((places, width, BLK), jnp.bfloat16),
            pltpu.VMEM((width, BLK), jnp.bfloat16),
            pltpu.SemaphoreType.DMA((2, 2, DEPTH)),
            pltpu.SemaphoreType.DMA((places,)),
            pltpu.SemaphoreType.DMA((blocks,)),
        ],
        compiler_params=pltpu.CompilerParams(vmem_limit_bytes=VMEM_BYTES),
    )(*tables, query_rows, key_group, value_group, logsum, mixed, mixed_grad, normed_group, both_weight)


def used_places(relative_slot, usable, group_blocks):
    block_count = relative_slot.shape[0]
    most = group_blocks // TREE_BLOCKS * TRUNK + 2 * block_count
    places = min(-(-most // PLACES) * PLACES, -(-group_blocks // PLACES) * PLACES)
    entries = jnp.arange(group_blocks, dtype=jnp.int32)
    hits = (relative_slot[:, :, None] == entries) & usable[:, :, None]
    seen = jnp.any(hits, axis=(0, 1))
    earlier = (entries[None, :] < entries[:, None]) & seen[None, :]
    place_of = jnp.sum(earlier, axis=1, dtype=jnp.int32)
    compact = jnp.sum(jnp.where(hits, place_of, jnp.int32(0)), axis=-1, dtype=jnp.int32)
    wanted = jnp.arange(places, dtype=jnp.int32)
    matches = (place_of[None, :] == wanted[:, None]) & seen[None, :]
    used = jnp.sum(jnp.where(matches, entries, jnp.int32(0)), axis=1, dtype=jnp.int32)
    seen = seen.astype(jnp.int32)
    used = jnp.concatenate([used, jnp.sum(seen, dtype=jnp.int32).reshape(1)])
    return compact, used.reshape(1, -1), seen.reshape(1, -1)


def project(pieces, vectors, key_weight, value_weight, group_rows, first, carried, query_weight=None):
    count = len(pieces)
    rows, width = pieces[0].shape
    weights = [key_weight, value_weight] + ([] if query_weight is None else [query_weight])
    extra = [] if carried is None else list(carried)

    def body(*refs):
        piece_refs, vectors_ref = refs[:count], refs[count]
        weight_refs = refs[count + 1 : count + 1 + len(weights)]
        outs = refs[count + 1 + len(weights) + len(extra) : -4]
        piece_here, made, arrivals, departures = refs[-4:]
        gain = vectors_ref[GAIN_ONE : GAIN_ONE + 1, :]
        shift = vectors_ref[SHIFT_ONE : SHIFT_ONE + 1, :]

        def fetch(index):
            return pltpu.make_async_copy(piece_refs[index], piece_here.at[index % 2], arrivals.at[index])

        def leave(index, kind):
            target = outs[kind].at[(first + index) * rows : (first + index + 1) * rows, :]
            return pltpu.make_async_copy(made.at[index % 2, kind], target, departures.at[index, kind])

        for index in range(min(2, count)):
            fetch(index).start()
        for index in range(count):
            fetch(index).wait()
            normed = normalize(piece_here[index % 2].astype(jnp.float32), gain, shift).astype(jnp.bfloat16)
            if index + 2 < count:
                fetch(index + 2).start()
            if index >= 2:
                for kind in range(3):
                    leave(index - 2, kind).wait()
            made[index % 2, 0] = normed
            leave(index, 0).start()
            for kind in (1, 2):
                made[index % 2, kind] = matmul(normed, weight_refs[kind - 1][...]).astype(jnp.bfloat16)
                leave(index, kind).start()
            if index == 0 and len(outs) > 3:
                outs[3][...] = normed
                queries = matmul(normed, weight_refs[2][...]).astype(jnp.bfloat16)
                outs[4][...] = (queries.astype(jnp.float32) * (HD ** (-0.5))).astype(jnp.bfloat16)
        for index in range(max(0, count - 2), count):
            for kind in range(3):
                leave(index, kind).wait()

    whole = jax.ShapeDtypeStruct((group_rows, width), jnp.bfloat16)
    own = [] if query_weight is None else [jax.ShapeDtypeStruct((rows, width), jnp.bfloat16)] * 2
    inputs = count + 1 + len(weights)
    return pl.pallas_call(
        body,
        cost_estimate=about(1 + 1.6 * count),
        out_shape=[whole] * 3 + own,
        in_specs=[anywhere()] * count + [in_vmem()] * (1 + len(weights)) + [anywhere()] * len(extra),
        out_specs=[anywhere()] * 3 + [in_vmem()] * len(own),
        scratch_shapes=[
            pltpu.VMEM((2, rows, width), jnp.bfloat16),
            pltpu.VMEM((2, 3, rows, width), jnp.bfloat16),
            pltpu.SemaphoreType.DMA((count,)),
            pltpu.SemaphoreType.DMA((count, 3)),
        ],
        input_output_aliases={inputs + index: index for index in range(len(extra))},
        compiler_params=pltpu.CompilerParams(vmem_limit_bytes=VMEM_BYTES),
    )(*pieces, vectors, *weights, *extra)


class Axis:
    def __init__(self, name, size, stride):
        self.name = name
        self.size = size
        self.stride = stride

    def position(self):
        return lax.axis_index(self.name) // self.stride % self.size

    def rotate(self, values, shift):
        pairs = []
        for index in range(lax.axis_size(self.name)):
            here = index // self.stride % self.size
            there = (here + shift) % self.size
            pairs.append((index, index + (there - here) * self.stride))
        return lax.ppermute(values, self.name, pairs)


def axes():
    seq = lax.axis_size("seq")
    dp = lax.axis_size("dp")
    along_z = 4 if seq % 4 == 0 else 1
    cores = 2 if dp % 2 == 0 else 1
    return (
        Axis("seq", along_z, seq // along_z),
        Axis("seq", seq // along_z, 1),
        Axis("dp", dp // cores, cores),
        Axis("dp", cores, 1),
    )


def relative_devices():
    axis_z, axis_x, axis_y, axis_core = axes()

    def place(axis, dim):
        back = lax.broadcasted_iota(jnp.int32, (axis_core.size, axis_y.size, axis_x.size, axis_z.size), dim)
        return (axis.position() - back + axis.size) % axis.size

    dp_index = place(axis_y, 1) * axis_core.size + place(axis_core, 0)
    seq_index = place(axis_z, 3) * axis_x.size + place(axis_x, 2)
    return (dp_index * lax.axis_size("seq") + seq_index).reshape(-1)


def scatter_devices():
    axis_z, axis_x, axis_y, axis_core = axes()
    entries = relative_devices().reshape(-1, axis_x.size, axis_z.size)
    return jnp.swapaxes(entries, 1, 2).reshape(-1)


def add_low(left_side, right_side):
    return (left_side.astype(jnp.float32) + right_side.astype(jnp.float32)).astype(jnp.bfloat16)


def add_three(first, second, third):
    total = first.astype(jnp.float32) + second.astype(jnp.float32) + third.astype(jnp.float32)
    return total.astype(jnp.bfloat16)


def tied(values, after):
    return lax.optimization_barrier((values, after))[0]


def ring_scatter(entry, axis):
    running = entry(axis.size - 1)
    for back in range(axis.size - 1, 0, -1):
        running = add_low(axis.rotate(running, -1), entry(back - 1))
    return running


GATE_B, DOWN_B, CARRY_B, GAIN_ONE, SHIFT_ONE, GAIN_TWO, SHIFT_TWO, UP_B = range(8)
VECTOR_ROWS = 16
MIDDLE_ROWS = 640


def pack_kernel(devices, place_ref, *refs):
    early_sources, late_sources, vector_refs, (early_ref, all_ref) = refs[:4], refs[4:8], refs[8:16], refs[16:]
    width = early_ref.shape[1]
    early_count = early_ref.shape[0]
    for target, start, sources in (
        (early_ref, 0, early_sources),
        (all_ref, 0, early_sources),
        (all_ref, early_count, late_sources),
    ):
        for source in sources:
            rows = source.shape[0]
            for column in range(0, source.shape[1], width):
                target[start : start + rows, :] = source[:, column : column + width]
                start += rows
    block = jnp.zeros((VECTOR_ROWS, width), jnp.float32)
    line = lax.broadcasted_iota(jnp.int32, block.shape, 0)
    for index, source in enumerate(vector_refs):
        count = source.shape[1]
        feature = lax.broadcasted_iota(jnp.int32, (count, width), 0) + place_ref[0] * count
        column = lax.broadcasted_iota(jnp.int32, (count, width), 1)
        for part in range(count * devices // width):
            spot = jnp.where(feature == column + part * width, jnp.float32(1.0), jnp.float32(0.0))
            spread = matmul(source[...], spot.astype(jnp.bfloat16))
            block += jnp.where(line == index + part, spread, jnp.float32(0.0))
    early_ref[early_count - VECTOR_ROWS :, :] = block.astype(jnp.bfloat16)
    all_ref[early_count - VECTOR_ROWS : early_count, :] = block.astype(jnp.bfloat16)


def unpack_kernel(place_ref, *refs):
    sources, (query_ref, key_ref, value_ref, gate_ref, vectors_ref) = refs[:4], refs[4:]
    size = sources[0].shape[0]
    rows = (sources[0].shape[1] - VECTOR_ROWS) // 4
    vectors = jnp.zeros(vectors_ref.shape, jnp.float32)
    for index in range(len(sources) * size):
        source = sources[index // size].at[index % size]
        target = pl.ds(pl.multiple_of(place_ref[index] * rows, rows), rows)
        for part, weight_ref in enumerate((query_ref, key_ref, value_ref, gate_ref)):
            weight_ref[target, :] = source[part * rows : (part + 1) * rows, :]
        vectors += source[4 * rows :, :].astype(jnp.float32)
    vectors_ref[...] = vectors


def unpack_late(place_ref, line_sources, plane_sources, output_ref, up_ref, down_ref, carry_ref):
    part_size = line_sources[0].shape[0]
    devices = part_size * len(line_sources)
    width = output_ref.shape[1]
    rows = output_ref.shape[0] // devices
    down_rows = down_ref.shape[0] // devices
    for index in range(devices):
        source = line_sources[index // part_size].at[index % part_size]
        target = pl.ds(pl.multiple_of(place_ref[0, index] * rows, rows), rows)
        output_ref[target, :] = source[:rows, :]
        for part in range(up_ref.shape[1] // width):
            up_ref[target, part * width : (part + 1) * width] = source[(part + 1) * rows : (part + 2) * rows, :]
        source = plane_sources[index // part_size].at[index % part_size]
        target = pl.ds(pl.multiple_of(place_ref[1, index] * down_rows, down_rows), down_rows)
        down_ref[target, :] = source[:down_rows, :]
        target = pl.ds(pl.multiple_of(place_ref[1, index] * rows, rows), rows)
        carry_ref[target, :] = source[down_rows:, :]


def spread_rows(place_ref, grad_ref, pack_refs, start, rows):
    size = pack_refs[0].shape[0]
    for index in range(size * len(pack_refs)):
        source = pl.ds(pl.multiple_of(place_ref[index] * rows, rows), rows)
        target = pack_refs[index // size].at[index % size]
        target[start : start + rows, :] = grad_ref[source, :].astype(jnp.bfloat16)


def middle_kernel(
    place_ref,
    attended_ref,
    input_ref,
    normed_ref,
    cotangent_ref,
    gate_weight_ref,
    vectors_ref,
    *refs,
):
    late_refs, refs = refs[:8], refs[8:]
    block_ref, row_targets, pack_targets, refs = refs[0], refs[1:5], refs[5:9], refs[9:]
    output_weight, up_weight, down_weight, carry_weight, hidden, up_pre_grads = refs[:6]
    update_grads, normed_second, carry_pre_grads, branch_grads, up_grad, down_grad, square_grads = refs[6:13]
    row_refs, pack_refs, row_departures, pack_departures = refs[13:17], refs[17:21], refs[21], refs[22]
    output_ref, middle_grad_ref, attended_grad_ref, gate_pre_ref = row_refs
    unpack_late(
        place_ref,
        late_refs[:4],
        late_refs[4:],
        output_weight,
        up_weight,
        down_weight,
        carry_weight,
    )
    width = output_ref.shape[1]
    hidden_width = up_weight.shape[1]
    wide = hidden_width // width

    def vector(line):
        return vectors_ref[line : line + 1, :]

    up_bias = jnp.concatenate([vector(UP_B + part) for part in range(wide)], axis=1)

    def column_lines(values):
        return jnp.sum(values.astype(jnp.float32), axis=0, keepdims=True)

    def some_rows(step, totals):
        rows = pl.ds(pl.multiple_of(step * MIDDLE_ROWS, MIDDLE_ROWS), MIDDLE_ROWS)
        gate_open = jax.nn.sigmoid(matmul(normed_ref[rows, :], gate_weight_ref[...]) + vector(GATE_B))
        branch = matmul(attended_ref[rows, :], output_weight[...])
        middle = input_ref[rows, :].astype(jnp.float32) + gate_open * branch
        centered = middle - jnp.mean(middle, axis=-1, keepdims=True)
        scale = lax.rsqrt(jnp.mean(centered * centered, axis=-1, keepdims=True) + EPSILON)
        hat = centered * scale
        normed = (hat * vector(GAIN_TWO) + vector(SHIFT_TWO)).astype(jnp.bfloat16)
        up_pre = matmul(normed, up_weight[...]) + up_bias
        up_open = jax.nn.sigmoid(up_pre)
        hidden_rows = (up_pre * up_open).astype(jnp.bfloat16)
        update = matmul(hidden_rows, down_weight[...]) + vector(DOWN_B)
        carry_open = jax.nn.sigmoid(matmul(normed, carry_weight[...]) + vector(CARRY_B))
        output_ref[rows, :] = (middle + carry_open * update).astype(jnp.bfloat16)

        grad_out = cotangent_ref[rows, :].astype(jnp.float32)
        update_grad = (carry_open * grad_out).astype(jnp.bfloat16)
        carry_pre_grad = (grad_out * update * carry_open * (1.0 - carry_open)).astype(jnp.bfloat16)
        slope = up_open * (1.0 + up_pre * (1.0 - up_open))
        up_pre_grad = (against(update_grad, down_weight[...]) * slope).astype(jnp.bfloat16)
        norm_grad = against(up_pre_grad, up_weight[...]) + against(carry_pre_grad, carry_weight[...])
        pull = norm_grad * vector(GAIN_TWO)
        middle_grad = grad_out + scale * (
            pull - jnp.mean(pull, axis=-1, keepdims=True) - hat * jnp.mean(pull * hat, axis=-1, keepdims=True)
        )
        middle_grad_ref[rows, :] = middle_grad
        branch_grad = (gate_open * middle_grad).astype(jnp.bfloat16)
        gate_pre_grad = (middle_grad * branch * gate_open * (1.0 - gate_open)).astype(jnp.bfloat16)
        gate_pre_ref[rows, :] = gate_pre_grad
        attended_grad_ref[rows, :] = against(branch_grad, output_weight[...]).astype(jnp.bfloat16)

        hidden[rows, :] = hidden_rows
        up_pre_grads[rows, :] = up_pre_grad
        update_grads[rows, :] = update_grad
        normed_second[rows, :] = normed
        carry_pre_grads[rows, :] = carry_pre_grad
        branch_grads[rows, :] = branch_grad
        lines = (gate_pre_grad, update_grad, carry_pre_grad, norm_grad * hat, norm_grad, up_pre_grad)
        return tuple(total + column_lines(line) for total, line in zip(totals, lines))

    start = (jnp.zeros((1, width), jnp.float32),) * 5 + (jnp.zeros((1, hidden_width), jnp.float32),)
    totals = lax.fori_loop(0, output_ref.shape[0] // MIDDLE_ROWS, some_rows, start)
    line = lax.broadcasted_iota(jnp.int32, block_ref.shape, 0)
    block = jnp.zeros(block_ref.shape, jnp.float32)
    for place, total in zip((GATE_B, DOWN_B, CARRY_B, GAIN_TWO, SHIFT_TWO), totals):
        block = jnp.where(line == place, total, block)
    for part in range(wide):
        block = jnp.where(line == UP_B + part, totals[5][:, part * width : (part + 1) * width], block)
    block_ref[...] = block
    leaving = []

    def leave(source, target, departure):
        leaving.append(pltpu.make_async_copy(source, target, departure))
        leaving[-1].start()

    def packs_leave(group, start, stop):
        for index, (source, target) in enumerate(zip(pack_refs, pack_targets)):
            here = (slice(None), slice(start, stop), slice(None))
            leave(source.at[here], target.at[here], pack_departures.at[group, index])

    for index, (source, target) in enumerate(zip(row_refs, row_targets)):
        leave(source, target, row_departures.at[index])

    target_ref = place_ref.at[2]
    rows = width // (4 * pack_refs[0].shape[0])
    place = 0
    for part in range(wide):
        grad = up_grad.at[part]
        grad[...] = inner_rows(normed_second[...], up_pre_grads[:, part * width : (part + 1) * width])
        spread_rows(target_ref, grad, pack_refs, place, rows)
        place += rows
    packs_leave(0, 0, place)
    for part in range(wide):
        here = slice(part * width, (part + 1) * width)
        down_grad[here, :] = inner_rows(hidden[:, here], update_grads[...])
    spread_rows(target_ref, down_grad, pack_refs, place, wide * rows)
    packs_leave(1, place, place + wide * rows)
    place += wide * rows
    pairs = ((normed_second, carry_pre_grads), (attended_ref, branch_grads), (normed_ref, gate_pre_ref))
    for index, (left_ref, right_ref) in enumerate(pairs):
        grad = square_grads.at[index]
        grad[...] = inner_rows(left_ref[...], right_ref[...])
        spread_rows(target_ref, grad, pack_refs, place, rows)
        place += rows
    packs_leave(2, 2 * wide * rows, place)
    for copy in leaving:
        copy.wait()


def second_grads_kernel(
    place_ref,
    both_grads_ref,
    normed_ref,
    query_grad_ref,
    gate_pre_ref,
    lanes_ref,
    query_weight_ref,
    key_weight_ref,
    value_weight_ref,
    gate_weight_ref,
    vectors_ref,
    block_ref,
    *refs,
):
    pack_refs, grads = refs[:4], refs[4]
    width = pack_refs[0].shape[2]
    rows = width // (4 * pack_refs[0].shape[0])
    grads[0] = inner_rows(normed_ref[...], query_grad_ref[...])
    grads[1] = jnp.transpose(both_grads_ref[:width, :])
    grads[2] = jnp.transpose(both_grads_ref[width:, :])
    for index in range(3):
        spread_rows(place_ref, grads.at[index], pack_refs, index * rows, rows)
    gate_grad = inner_rows(normed_ref[...], gate_pre_ref[...])

    def line_sums(ref):
        return jnp.sum(ref[...].astype(jnp.float32), axis=0, keepdims=True)

    def as_line(column):
        return jnp.transpose(jnp.broadcast_to(column, (width, BLK)))[:1, :]

    lines = (
        line_sums(query_grad_ref),
        jnp.sum(jnp.transpose(lanes_ref[:width, :]), axis=0, keepdims=True),
        jnp.sum(jnp.transpose(lanes_ref[width:, :]), axis=0, keepdims=True),
        line_sums(gate_pre_ref),
    )
    weighted = jnp.zeros((width, width), jnp.float32)
    shifted = jnp.zeros((width, width), jnp.float32)
    weight_refs = (query_weight_ref, key_weight_ref, value_weight_ref, gate_weight_ref)
    for weight_ref, line, grad in zip(weight_refs, lines, (grads[0], grads[1], grads[2], gate_grad)):
        weight = weight_ref[...].astype(jnp.float32)
        weighted += weight * grad
        shifted += weight * line
    shift_line = as_line(jnp.sum(shifted, axis=1, keepdims=True))
    gain_line = (
        as_line(jnp.sum(weighted, axis=1, keepdims=True)) - vectors_ref[SHIFT_ONE : SHIFT_ONE + 1, :] * shift_line
    ) / vectors_ref[GAIN_ONE : GAIN_ONE + 1, :]
    place = lax.broadcasted_iota(jnp.int32, block_ref.shape, 0)
    block = jnp.where(place == GAIN_ONE, gain_line, block_ref[...])
    block = jnp.where(place == SHIFT_ONE, shift_line, block).astype(jnp.bfloat16)
    for pack_ref in pack_refs:
        for index in range(pack_ref.shape[0]):
            pack_ref[index, 3 * rows :, :] = block


def own_kernel(device_ref, arrived_ref, kept_ref, *refs):
    second_refs, weight_refs, line_refs = refs[:4], refs[4:12], refs[12:]
    width = arrived_ref.shape[1]
    first = arrived_ref[...].astype(jnp.float32) + kept_ref[...].astype(jnp.float32)
    second = sum(ref[...].astype(jnp.float32) for ref in second_refs)
    start = 0
    source = first
    for index, ref in enumerate(weight_refs):
        if index == 5:
            start, source = 0, second
        rows = ref.shape[0]
        for column in range(0, ref.shape[1], width):
            ref[:, column : column + width] = source[start : start + rows, :]
            start += rows
    lines = second[start:, :]
    place = lax.broadcasted_iota(jnp.int32, lines.shape, 0)
    for index, ref in enumerate(line_refs):
        count = ref.shape[1]
        offset = device_ref[0] * count
        line = jnp.where(place == index + offset // width, lines, jnp.float32(0.0))
        line = jnp.broadcast_to(jnp.sum(line, axis=0, keepdims=True), (8, width))
        ref[...] = pltpu.roll(line, (width - offset % width) % width, 1)[:1, :count]


def input_grad_kernel(input_ref, local_ref, middle_grad_ref, vectors_ref, *refs):
    shared_refs, output_ref = refs[:-1], refs[-1]
    blocks = [sum(ref[index].astype(jnp.float32) for ref in shared_refs) for index in range(shared_refs[0].shape[0])]
    shared = jnp.concatenate([jnp.transpose(block) for block in blocks])
    values = input_ref[...].astype(jnp.float32)
    centered = values - jnp.mean(values, axis=-1, keepdims=True)
    scale = lax.rsqrt(jnp.mean(centered * centered, axis=-1, keepdims=True) + EPSILON)
    hat = centered * scale
    pull = (local_ref[...] + shared) * vectors_ref[GAIN_ONE : GAIN_ONE + 1, :]
    output_ref[...] = middle_grad_ref[...] + scale * (
        pull - jnp.mean(pull, axis=-1, keepdims=True) - hat * jnp.mean(pull * hat, axis=-1, keepdims=True)
    )


def local_call(kernel, cost, outs, smem, args, scratch=()):
    return pl.pallas_call(
        kernel,
        cost_estimate=about(cost),
        out_shape=outs,
        in_specs=[in_smem()] + [in_vmem()] * len(args),
        out_specs=jax.tree.map(lambda out: in_vmem(), outs),
        scratch_shapes=list(scratch),
        compiler_params=pltpu.CompilerParams(vmem_limit_bytes=VMEM_BYTES),
    )(smem, *args)


def joined(pieces, axis):
    return pieces[0] if len(pieces) == 1 else jnp.concatenate(pieces, axis=axis)


def shards(
    inputs,
    cotangent,
    block_segment,
    segment_parent,
    query_weight,
    key_weight,
    value_weight,
    output_weight,
    gate_weight,
    gate_bias,
    up_weight,
    up_bias,
    down_weight,
    down_bias,
    carry_weight,
    carry_bias,
    first_gain,
    first_shift,
    second_gain,
    second_shift,
):
    width = inputs.shape[1]
    devices = lax.axis_size(BOTH)
    block_count = inputs.shape[0] // BLK
    group_blocks = block_segment.shape[0]

    axis_z, axis_x, axis_y, axis_core = axes()
    rows_each = query_weight.shape[0]
    sizes = (axis_z.size, axis_x.size, axis_y.size, axis_core.size)
    direct = sizes == (4, 2, 2, 2) and rows_each % 16 == 0
    places = relative_devices()
    targets = scatter_devices()
    device = lax.axis_index(BOTH)
    vectors = (gate_bias, down_bias, carry_bias, first_gain, first_shift, second_gain, second_shift, up_bias)
    early_set = (query_weight, key_weight, value_weight, gate_weight)
    late_set = (output_weight, up_weight, down_weight, carry_weight)
    low = jnp.bfloat16

    def struct(*shape, dtype=low):
        return jax.ShapeDtypeStruct(shape, dtype)

    def take(source, start, piece):
        rows = piece.shape[0]
        parts = piece.shape[1] // width
        blocks = [
            source[:, start + part * rows : start + (part + 1) * rows].reshape(devices * rows, width)
            for part in range(parts)
        ]
        return joined(blocks, 1), start + parts * rows

    def flat_rows(pieces):
        return [piece[:, start : start + width] for piece in pieces for start in range(0, piece.shape[1], width)]

    own_start = lax.axis_index("seq") * block_count
    own_segments = lax.dynamic_slice_in_dim(block_segment, own_start, block_count)
    ancestor_slot, usable = ancestor_slots(block_segment, segment_parent, own_segments)
    owner = ancestor_slot // block_count
    away_z = (axis_z.position() - owner // axis_x.size) % axis_z.size
    away_x = (axis_x.position() - owner % axis_x.size) % axis_x.size
    relative_slot = (away_z * axis_x.size + away_x) * block_count + ancestor_slot % block_count
    tables = used_places(relative_slot, usable, group_blocks)
    slots = jnp.concatenate(
        [relative_slot, jnp.sum(usable, axis=-1, keepdims=True, dtype=jnp.int32)], axis=-1
    )

    if direct:
        early_count = 4 * rows_each + VECTOR_ROWS
        late_count = sum(piece.shape[0] * piece.shape[1] // width for piece in late_set)
        early, both = local_call(
            functools.partial(pack_kernel, devices),
            0.1,
            (struct(early_count, width), struct(early_count + late_count, width)),
            device.reshape(1),
            early_set + late_set + tuple(vector.reshape(1, -1) for vector in vectors),
        )
        both_one = axis_z.rotate(both, 1)
        early_line = [axis_z.rotate(early, back) for back in range(2, 4)]
        x_zero = axis_x.rotate(inputs, 1)
        z_one = axis_z.rotate(inputs, 1)
        both_one, early_line, x_zero, z_one = lax.optimization_barrier((both_one, early_line, x_zero, z_one))
        early_line = [both_one[:early_count]] + list(early_line)
        late_line = [both[early_count:], both_one[early_count:]]
        z_two = axis_z.rotate(z_one, 1)
        x_one = axis_x.rotate(z_one, 1)
        early_line = jnp.stack([early] + list(early_line))
        early_other = axis_x.rotate(early_line, 1)
        late_line.append(axis_z.rotate(late_line[1], 1))
        early_other, z_two, x_one, late_line[2], slots, tables = lax.optimization_barrier(
            (early_other, z_two, x_one, late_line[2], slots, tables)
        )
        z_three = axis_z.rotate(z_two, 1)
        x_two = axis_x.rotate(z_two, 1)
        early_plane = jnp.stack([early_line, early_other])
        early_other = axis_y.rotate(early_plane, 1)
        late_line.append(axis_z.rotate(late_line[2], 1))
        early_other, z_three, x_two, late_line[3] = lax.optimization_barrier(
            (early_other, z_three, x_two, late_line[3])
        )
        x_three = axis_x.rotate(z_three, 1)
        early_parts = [early_plane, early_other]
        early_parts += [axis_core.rotate(part, 1) for part in early_parts]
        early_parts = [part.reshape(devices // 4, early_count, width) for part in early_parts]
        input_pieces = [[inputs, x_zero], [z_one, x_one], [z_two, x_two], [z_three, x_three]]
        square = struct(width, width)
        full_query, full_key, full_value, full_gate, vector_rows = local_call(
            unpack_kernel,
            3,
            (square, square, square, square, struct(VECTOR_ROWS, width, dtype=jnp.float32)),
            places,
            early_parts,
        )
        late_line, full_key = lax.optimization_barrier((late_line, full_key))
        late_half = late_count // 2
        late_x = jnp.stack([rows[:late_half] for rows in late_line])
        late_y = jnp.stack([rows[late_half:] for rows in late_line])
        late_x_other = axis_x.rotate(late_x, 1)
        late_y_other = axis_y.rotate(late_y, 1)
    else:
        early_rows = lax.all_gather(jnp.concatenate(early_set), BOTH)
        late_rows = lax.all_gather(jnp.concatenate(flat_rows(late_set)), BOTH)
        place = 0
        full_query, place = take(early_rows, place, query_weight)
        full_key, place = take(early_rows, place, key_weight)
        full_value, place = take(early_rows, place, value_weight)
        full_gate, place = take(early_rows, place, gate_weight)
        place = 0
        full_output, place = take(late_rows, place, output_weight)
        full_up, place = take(late_rows, place, up_weight)
        full_down, place = take(late_rows, place, down_weight)
        full_carry, place = take(late_rows, place, carry_weight)
        lines = [lax.all_gather(vector, BOTH, tiled=True).reshape(-1, width) for vector in vectors]
        lines = jnp.concatenate(lines).astype(jnp.float32)
        vector_rows = jnp.pad(lines, ((0, VECTOR_ROWS - lines.shape[0]), (0, 0)))
        input_pieces = []
        along_z = inputs
        for step_z in range(axis_z.size):
            along_x = along_z
            row = []
            for step_x in range(axis_x.size):
                row.append(along_x)
                along_x = axis_x.rotate(along_x, 1) if step_x + 1 < axis_x.size else None
            input_pieces.append(row)
            along_z = axis_z.rotate(along_z, 1) if step_z + 1 < axis_z.size else None

    both_weight = jnp.concatenate([full_key, full_value], axis=1)

    group_rows = group_blocks * BLK
    pieces = [piece for row in input_pieces for piece in row]
    near = len(pieces) - 1 if direct else len(pieces)
    *carried, normed_low, query_low = project(
        pieces[:near], vector_rows, full_key, full_value, group_rows, 0, None, full_query
    )
    if direct:
        late_y_other, late_x_other, x_three, carried, both_weight = lax.optimization_barrier(
            (late_y_other, late_x_other, pieces[near], carried, both_weight)
        )
        late_x = jnp.stack([late_x, late_x_other])
        late_y = jnp.stack([late_y, late_y_other])
        late_x_other = axis_y.rotate(late_x, 1)
        late_y_other = axis_x.rotate(late_y, 1)
        attended_low, logsum, *carried = project_and_attend(
            slots, query_low, x_three, vector_rows, full_key, full_value, carried
        )
    normed_group, key_group, value_group = carried

    gate_b, down_b, carry_b, gain_one, shift_one, gain_two, shift_two = [vector_rows[line] for line in range(UP_B)]
    up_b = vector_rows[UP_B : UP_B + up_weight.shape[1] // width].reshape(-1)

    values_in = inputs.astype(jnp.float32)
    if not direct:
        attended_low, logsum = attend(slots, query_low, key_group, value_group)

    if direct:
        attended_low, late_x_other, late_y_other = lax.optimization_barrier((attended_low, late_x_other, late_y_other))
        late_parts = []
        for mine in ((late_x, late_x_other), (late_y, late_y_other)):
            for piece in list(mine) + [axis_core.rotate(part, 1) for part in mine]:
                late_parts.append(piece.reshape(devices // 4, late_half, width))
        other_places = jnp.transpose(places.reshape(2, 2, 2, 4), (0, 2, 1, 3)).reshape(-1)
        rows = inputs.shape[0]
        first_rows = late_count + rows_each
        hidden_width = up_weight.shape[1]
        quarter = struct(devices // 4, first_rows, width)
        tall, short = pltpu.VMEM((rows, hidden_width), low), pltpu.VMEM((rows, width), low)
        wide = (struct(rows, width), struct(rows, width, dtype=jnp.float32), struct(rows, width), struct(rows, width))
        leaving = wide + (quarter,) * 4
        block, output, middle_grad, attended_grad, gate_pre_grad, *first = pl.pallas_call(
            middle_kernel,
            cost_estimate=about(20),
            out_shape=(struct(VECTOR_ROWS, width, dtype=jnp.float32),) + leaving,
            in_specs=[in_smem()] + [in_vmem()] * 14,
            out_specs=(in_vmem(),) + (anywhere(),) * len(leaving),
            scratch_shapes=[
                pltpu.VMEM((width, width), low),
                pltpu.VMEM((width, hidden_width), low),
                pltpu.VMEM((hidden_width, width), low),
                pltpu.VMEM((width, width), low),
                tall,
                tall,
                short,
                short,
                short,
                short,
                pltpu.VMEM((hidden_width // width, width, width), jnp.float32),
                pltpu.VMEM((hidden_width, width), jnp.float32),
                pltpu.VMEM((3, width, width), jnp.float32),
            ]
            + [pltpu.VMEM(out.shape, out.dtype) for out in leaving]
            + [pltpu.SemaphoreType.DMA((4,)), pltpu.SemaphoreType.DMA((3, 4))],
            compiler_params=pltpu.CompilerParams(vmem_limit_bytes=VMEM_BYTES),
        )(
            jnp.stack([places, other_places, targets]),
            attended_low,
            inputs,
            normed_low,
            cotangent,
            full_gate,
            vector_rows,
            *late_parts,
        )
        first = [pack.reshape(4, 2, first_rows, width) for pack in first]
        first_core = [axis_core.rotate(first[2 + index], -1) for index in range(2)]
        first_keep, first_send = [add_low(first_core[index], first[index]) for index in range(2)]
        attended_grad, first_keep, first_send = lax.optimization_barrier((attended_grad, first_keep, first_send))
        first_arrived = axis_y.rotate(first_send, -1)
    else:
        gate_open = jax.nn.sigmoid(matmul(normed_low, full_gate) + gate_b)
        branch = matmul(attended_low, full_output)
        middle = values_in + gate_open * branch
        normed_second = normalize(middle, gain_two, shift_two).astype(jnp.bfloat16)
        up_pre = matmul(normed_second, full_up) + up_b
        up_sigmoid = jax.nn.sigmoid(up_pre)
        hidden_low = (up_pre * up_sigmoid).astype(jnp.bfloat16)
        update = matmul(hidden_low, full_down) + down_b
        carry_open = jax.nn.sigmoid(matmul(normed_second, full_carry) + carry_b)
        output = (middle + carry_open * update).astype(jnp.bfloat16)

        grad_out = cotangent.astype(jnp.float32)
        update_grad = (carry_open * grad_out).astype(jnp.bfloat16)
        carry_pre_grad = (grad_out * update * carry_open * (1.0 - carry_open)).astype(jnp.bfloat16)
        grad_down_bias = column_sums(update_grad)
        grad_carry_bias = column_sums(carry_pre_grad)
        silu_slope = up_sigmoid * (1.0 + up_pre * (1.0 - up_sigmoid))
        up_pre_grad = (against(update_grad, full_down) * silu_slope).astype(jnp.bfloat16)
        grad_up_bias = column_sums(up_pre_grad)
        second_norm_grad = against(up_pre_grad, full_up) + against(carry_pre_grad, full_carry)
        second_pull = jax.vjp(normalize, middle, gain_two, shift_two)[1]
        middle_part, grad_second_gain, grad_second_shift = second_pull(second_norm_grad)
        middle_grad = grad_out + middle_part

        branch_grad = (gate_open * middle_grad).astype(jnp.bfloat16)
        gate_pre_grad = (middle_grad * branch * gate_open * (1.0 - gate_open)).astype(jnp.bfloat16)
        grad_gate_bias = column_sums(gate_pre_grad)
        attended_grad = against(branch_grad, full_output).astype(jnp.bfloat16)
        zero_line = jnp.zeros((width,), jnp.float32)
        local_lines = (
            grad_gate_bias,
            grad_down_bias,
            grad_carry_bias,
            zero_line,
            zero_line,
            grad_second_gain,
            grad_second_shift,
            grad_up_bias,
        )
        block = jnp.concatenate([line.reshape(-1, width) for line in local_lines])
        block = jnp.pad(block, ((0, VECTOR_ROWS - block.shape[0]), (0, 0)))
    backward = attend_backward(
        (slots,) + tables,
        query_low,
        key_group,
        value_group,
        logsum,
        attended_low,
        attended_grad,
        normed_group,
        both_weight,
    )
    if direct:
        backward, first_arrived = lax.optimization_barrier((backward, first_arrived))

        def first_y(back):
            return add_low(first_arrived[back], first_keep[back])

        first_z = axis_z.rotate(first_y(3), -1)
    query_rows_grad, both_grads, lanes = backward[:3]

    shared_parts = backward[3:]

    if direct:
        second_rows = 3 * rows_each + VECTOR_ROWS
        quarter = struct(devices // 4, second_rows, width)
        second = local_call(
            second_grads_kernel,
            0.1,
            (quarter,) * 4,
            places,
            (
                both_grads,
                normed_low,
                query_rows_grad,
                gate_pre_grad,
                lanes,
                full_query,
                full_key,
                full_value,
                full_gate,
                vector_rows,
                block,
            ),
            (pltpu.VMEM((3, width, width), jnp.float32),),
        )
        second = [pack.reshape(2, 4, second_rows, width) for pack in second]
        barrier = lax.optimization_barrier
        first_z = axis_z.rotate(add_low(first_z, first_y(2)), -1)
        x_three = axis_x.rotate(shared_parts[7], -1)
        x_three, first_z, second = barrier((x_three, first_z, second))

        second_core = [axis_core.rotate(second[2 + index], -1) for index in range(2)]
        second_keep = add_low(second_core[0], second[0])
        second_arrived = axis_y.rotate(add_low(second_core[1], second[1]), -1)
        x_two = axis_x.rotate(tied(shared_parts[5], x_three), -1)
        z_three = axis_z.rotate(add_low(x_three, shared_parts[6]), -1)
        x_two, z_three, second_arrived = barrier((x_two, z_three, second_arrived))

        second_y = add_low(second_arrived, second_keep)
        second_x = axis_x.rotate(second_y[1], -1)
        x_one = axis_x.rotate(tied(shared_parts[3], x_two), -1)
        z_two = axis_z.rotate(add_three(x_two, shared_parts[4], z_three), -1)
        first_z = axis_z.rotate(add_low(tied(first_z, x_two), first_y(1)), -1)
        x_one, z_two, second_x, first_z = barrier((x_one, z_two, second_x, first_z))

        first_half = add_low(first_z, first_y(0))
        first_x = axis_x.rotate(tied(first_half[1], x_one), -1)
        second_half = add_low(second_x, second_y[0])
        second_z = [axis_z.rotate(second_half[back], -back) for back in range(1, 4)]
        x_zero = axis_x.rotate(tied(shared_parts[1], x_one), -1)
        z_one = axis_z.rotate(add_three(x_one, shared_parts[2], z_two), -1)
        shared = (x_zero, z_one, shared_parts[0])
    else:
        grad_key = jnp.transpose(both_grads[:width])
        grad_value = jnp.transpose(both_grads[width:])
        grad_query = inner_rows(normed_low, query_rows_grad)
        grad_gate = inner_rows(normed_low, gate_pre_grad)
        both_sums = jnp.sum(lanes, axis=1)
        weights = [weight.astype(jnp.float32) for weight in (full_query, full_key, full_value, full_gate)]
        line_sums = (column_sums(query_rows_grad), both_sums[:width], both_sums[width:], grad_gate_bias)
        shift_line = sum(jnp.sum(weight * line, axis=1) for weight, line in zip(weights, line_sums))
        weighted = sum(
            jnp.sum(weight * grad, axis=1)
            for weight, grad in zip(weights, (grad_query, grad_key, grad_value, grad_gate))
        )
        block = block.at[GAIN_ONE].set((weighted - shift_one * shift_line) / gain_one).at[SHIFT_ONE].set(shift_line)
        grads = (
            (inner_rows(normed_second, up_pre_grad), up_weight),
            (inner_rows(hidden_low, update_grad), down_weight),
            (inner_rows(normed_second, carry_pre_grad), carry_weight),
            (inner_rows(attended_low, branch_grad), output_weight),
            (grad_gate, gate_weight),
            (grad_query, query_weight),
            (grad_key, key_weight),
            (grad_value, value_weight),
        )
        pack = [
            cut.astype(low).reshape(devices, piece.shape[0], width)
            for grad, piece in grads
            for cut in flat_rows((grad,))
        ]
        pack.append(jnp.broadcast_to(block.astype(low), (devices, VECTOR_ROWS, width)))
        pack = jnp.concatenate(pack, axis=1)
        pack = jnp.pad(pack, ((0, 0), (0, -pack.shape[1] % 16), (0, 0)))
        weight_sum = lax.psum_scatter(pack, BOTH, scatter_dimension=0, tiled=True)[0].astype(jnp.float32)

        def over_x(step_z):
            return ring_scatter(lambda step_x: shared_parts[step_z * axis_x.size + step_x], axis_x)

        shared = (ring_scatter(over_x, axis_z),)

    local_grad = against(query_rows_grad, full_query) + against(gate_pre_grad, full_gate)
    input_grad = pl.pallas_call(
        input_grad_kernel,
        cost_estimate=about(3),
        out_shape=struct(block_count * BLK, width, dtype=jnp.float32),
        compiler_params=pltpu.CompilerParams(vmem_limit_bytes=VMEM_BYTES),
    )(inputs, local_grad, middle_grad, vector_rows, *shared)

    if direct:
        input_grad, first_x, second_z = lax.optimization_barrier((input_grad, first_x, second_z))
        square = struct(rows_each, width, dtype=jnp.float32)
        tall = struct(down_weight.shape[0], width, dtype=jnp.float32)
        broad = struct(rows_each, up_weight.shape[1], dtype=jnp.float32)
        weight_outs = (broad, tall, square, square, square, square, square, square)
        line_outs = tuple(struct(1, vector.shape[0], dtype=jnp.float32) for vector in vectors)
        own_grads = local_call(
            own_kernel,
            2,
            weight_outs + line_outs,
            device.reshape(1),
            (first_x, first_half[0], second_half[0], *second_z),
        )
        own_up, own_down, own_carry, own_output, own_gate, own_query, own_key, own_value = own_grads[:8]
        vector_out = [line.reshape(-1) for line in own_grads[8:]]
    else:
        def own(start, piece):
            rows = piece.shape[0]
            parts = piece.shape[1] // width
            blocks = [weight_sum[start + part * rows : start + (part + 1) * rows] for part in range(parts)]
            return joined(blocks, 1), start + parts * rows

        place = 0
        own_up, place = own(place, up_weight)
        own_down, place = own(place, down_weight)
        own_carry, place = own(place, carry_weight)
        own_output, place = own(place, output_weight)
        own_gate, place = own(place, gate_weight)
        own_query, place = own(place, query_weight)
        own_key, place = own(place, key_weight)
        own_value, place = own(place, value_weight)
        vector_out = []
        for index, vector in enumerate(vectors):
            count = vector.shape[0]
            lines = weight_sum[place + index : place + index + count * devices // width].reshape(-1)
            vector_out.append(lax.dynamic_slice_in_dim(lines, device * count, count))
    gate_bg, down_bg, carry_bg, gain_one_g, shift_one_g, gain_two_g, shift_two_g, up_bg = vector_out
    return (
        output,
        input_grad,
        own_query,
        own_key,
        own_value,
        own_output,
        own_gate,
        gate_bg,
        own_up,
        up_bg,
        own_down,
        down_bg,
        own_carry,
        carry_bg,
        gain_one_g,
        shift_one_g,
        gain_two_g,
        shift_two_g,
    )


def solution(mesh):
    rows = P(BOTH, None)
    line = P(BOTH)
    matrix_or_line = (rows,) * 5 + (line, rows, line, rows, line, rows) + (line,) * 5
    return jax.shard_map(
        shards,
        mesh=mesh,
        in_specs=(rows, rows, P("dp"), P("dp")) + matrix_or_line,
        out_specs=(rows, rows) + matrix_or_line,
        check_vma=False,
    )
```
